128 devices in a mesh: prompt: 8 (over y, core), sample: 16 (over z, x).
Axes of the slice: x: 4, y: 4, z: 4, core: 2. Of those that a mesh axis runs over, the one named last changes fastest.
Arguments:
- prompt_states: bfloat16 [8, 4096, 8192], P('prompt', None, 'sample'), may hold values from -6 to 6
- kv_weight: bfloat16 [8192, 2048], P('sample', 'prompt'), may hold values from -0.0625 to 0.0625
- queries: bfloat16 [8, 16, 8192], P('prompt', 'sample'), may hold values from -10 to 10
- new_kv: bfloat16 [8, 16, 2048], P('prompt', 'sample'), may hold values from -8 to 8
- local_pages: bfloat16 [8, 16, 16, 128, 2048], P('prompt', 'sample'), may hold values from -6 to 6
- pool_pages: bfloat16 [8, 16, 16, 128, 2048], P('prompt', 'sample'), may hold values from -6 to 6
- prompt_pages: int32 [8], P('prompt'), may hold values from 1 to 32, as said below
- comp_pages: int32 [8, 16], P('prompt', 'sample'), may hold values from 8 to 16, as said below
- preempted: int32 [8, 16], P('prompt', 'sample'), may hold values from 0 to 1, as said below
- page_where: int32 [8, 16, 16], P('prompt', 'sample'), may hold values from 0 to 255, as said below
Outputs:
- prefix_cache: bfloat16 [8, 4096, 2048], P('prompt', 'sample')
- attended: bfloat16 [8, 16, 8192], P('prompt', 'sample')
The draws below stay inside these ranges and needn't reach their ends.
Inputs may be any that keep to these rules, and one draw needn't show every extreme that they name: `prompt_pages`: some prompt has 32 pages. `comp_pages`: every prompt has a sample of 16 pages. A preempted sample's pages c < comp_pages are read from the pool, the others' from local_pages; every prompt has a preempted sample of 16 pages. `page_where`: within one prompt every pool device and slot is named by exactly one page of one sample, and no pool device holds two pages of the same sample; entries of pages that are not read name slots of unrelated content.
All inputs are finite; a program needn't handle non-finite values.
Results may differ from the reference program's by a relative error of at most 0.039.
Values may be sent and summed in bfloat16 or wider, within the bound.
No kernel may reach another device: no remote copies, remote signals or barrier semaphores. Data moves between devices by JAX's collectives and lax.ppermute only.
A program may use at most 192 MiB of HBM per device.

```python
import math
import jax
import jax.numpy as jnp
from jax import lax

D = 8192
QUERY_HEADS = 64
KEY_VALUE_HEADS = 8
HEAD_SIZE = 128
PAGE = 128
PREF_PAGES = 32
PROMPT_TOTAL = 8
SAMPLES_EACH = 16
CMAX = 16
PREFIX = 4096
KVW = 2048
N_SAMPLE = 16


def distinct_order(key, shape, count):
    scores = jax.random.randint(key, shape + (count,), 0, 1 << 20) * count + jnp.arange(count, dtype=jnp.int32)
    return jnp.argsort(scores, axis=-1).astype(jnp.int32)


def page_plan(key):
    random_subkeys = jax.random.split(jax.random.fold_in(key, 11), 6)
    lowest = max(1, CMAX // 2)
    lengths = jax.random.randint(random_subkeys[0], (PROMPT_TOTAL, SAMPLES_EACH), lowest, CMAX + 1)
    flagged = (jax.random.randint(random_subkeys[1], (PROMPT_TOTAL, SAMPLES_EACH), 0, 4) > 0).astype(jnp.int32)
    longest = jax.random.randint(random_subkeys[2], (PROMPT_TOTAL, 1), 0, SAMPLES_EACH)
    chosen = jnp.arange(SAMPLES_EACH, dtype=jnp.int32)[None, :] == longest
    lengths = jnp.where(chosen, CMAX, lengths).astype(jnp.int32)
    flagged = jnp.where(chosen, 1, flagged).astype(jnp.int32)
    pool_order = distinct_order(random_subkeys[3], (PROMPT_TOTAL,), SAMPLES_EACH)
    offset = jax.random.randint(random_subkeys[4], (PROMPT_TOTAL, 1, 1), 0, SAMPLES_EACH)
    slot_order = distinct_order(random_subkeys[5], (PROMPT_TOTAL, SAMPLES_EACH), CMAX)
    page_ids = jnp.arange(CMAX, dtype=jnp.int32)[None, None, :]
    rotation = (jnp.arange(SAMPLES_EACH, dtype=jnp.int32)[None, :, None] + page_ids + offset) % SAMPLES_EACH
    pool_index = jnp.take_along_axis(pool_order, rotation.reshape(PROMPT_TOTAL, -1), axis=1).reshape(PROMPT_TOTAL, SAMPLES_EACH, CMAX)
    flat_index = (pool_index * CMAX + page_ids).reshape(PROMPT_TOTAL, -1)
    slot_index = jnp.take_along_axis(slot_order.reshape(PROMPT_TOTAL, -1), flat_index, axis=1).reshape(PROMPT_TOTAL, SAMPLES_EACH, CMAX)
    return (lengths, flagged, (pool_index * CMAX + slot_index).astype(jnp.int32))


def query_base(key):
    base_offset = 2.5 * jax.random.normal(jax.random.fold_in(key, 202), (PROMPT_TOTAL, SAMPLES_EACH, QUERY_HEADS * HEAD_SIZE), jnp.float32)
    return jnp.clip(base_offset, -10.0, 10.0)


def page_contents(key):
    logical_index = jax.random.normal(jax.random.fold_in(key, 303), (PROMPT_TOTAL, SAMPLES_EACH, CMAX, PAGE, KVW), jnp.float32)
    return jnp.clip(logical_index, -6.0, 6.0)


def draw_queries(key, part):
    base_offset = query_base(key)
    return base_offset.astype(jnp.bfloat16)


def draw_new_kv(key, part):
    base_offset = query_base(key)
    key = jax.random.fold_in(key, 2)
    first_random_key, second_random_key = jax.random.split(key)
    summed_total = base_offset.reshape(PROMPT_TOTAL, SAMPLES_EACH, KEY_VALUE_HEADS, QUERY_HEADS // KEY_VALUE_HEADS, HEAD_SIZE).sum(axis=3).reshape(PROMPT_TOTAL, SAMPLES_EACH, KEY_VALUE_HEADS * HEAD_SIZE)
    random_noise = jax.random.normal(first_random_key, (PROMPT_TOTAL, SAMPLES_EACH, KEY_VALUE_HEADS * HEAD_SIZE), jnp.float32)
    key_portion = jnp.clip(1.6 * HEAD_SIZE ** (-0.5) * summed_total + 0.5 * random_noise, -8.0, 8.0)
    value_portion = jnp.clip(jax.random.normal(second_random_key, (PROMPT_TOTAL, SAMPLES_EACH, KEY_VALUE_HEADS * HEAD_SIZE), jnp.float32), -6.0, 6.0)
    return jnp.concatenate([key_portion, value_portion], axis=-1).astype(jnp.bfloat16)


def draw_local_pages(key, part):
    lengths, flagged, locations = page_plan(key)
    logical_index = page_contents(key)
    key = jax.random.fold_in(key, 3)
    stale = jnp.clip(jax.random.normal(key, logical_index.shape, jnp.float32), -6.0, 6.0)
    page_ids = jnp.arange(CMAX, dtype=jnp.int32)[None, None, :]
    resident = (page_ids < lengths[:, :, None]) & (flagged[:, :, None] == 0)
    return jnp.where(resident[..., None, None], logical_index, stale).astype(jnp.bfloat16)


def draw_pool_pages(key, part):
    lengths, flagged, locations = page_plan(key)
    logical_index = page_contents(key)
    key = jax.random.fold_in(key, 4)
    stale = jnp.clip(jax.random.normal(key, (PROMPT_TOTAL, SAMPLES_EACH * CMAX, PAGE, KVW), jnp.float32), -6.0, 6.0)
    page_ids = jnp.arange(CMAX, dtype=jnp.int32)[None, None, :]
    moved = ((page_ids < lengths[:, :, None]) & (flagged[:, :, None] > 0)).reshape(PROMPT_TOTAL, -1)
    inverse = jnp.argsort(locations.reshape(PROMPT_TOTAL, -1), axis=1).astype(jnp.int32)
    placed = jnp.take_along_axis(logical_index.reshape(PROMPT_TOTAL, SAMPLES_EACH * CMAX, PAGE, KVW), inverse[:, :, None, None], axis=1)
    placed_live = jnp.take_along_axis(moved, inverse, axis=1)
    result = jnp.where(placed_live[:, :, None, None], placed, stale)
    return result.reshape(PROMPT_TOTAL, SAMPLES_EACH, CMAX, PAGE, KVW).astype(jnp.bfloat16)


def draw_prompt_pages(key, part):
    key = jax.random.fold_in(key, 5)
    first_random_key, second_random_key = jax.random.split(key)
    lengths = jax.random.randint(first_random_key, (PROMPT_TOTAL,), 1, PREF_PAGES + 1)
    longest = jax.random.randint(second_random_key, (), 0, PROMPT_TOTAL)
    return jnp.where(jnp.arange(PROMPT_TOTAL, dtype=jnp.int32) == longest, PREF_PAGES, lengths).astype(jnp.int32)


def draw_comp_pages(key, part):
    lengths, flagged, locations = page_plan(key)
    return lengths


def draw_preempted(key, part):
    lengths, flagged, locations = page_plan(key)
    return flagged


def draw_page_where(key, part):
    lengths, flagged, locations = page_plan(key)
    return locations


def level_of(key, shape, cuts, least, high):
    factor_of = 1.0
    for axis_at, blocks in cuts:
        heights = jax.random.uniform(jax.random.fold_in(jax.random.fold_in(key, 6), axis_at), (blocks,), jnp.float32, least / len(cuts), high / len(cuts))
        factor_of = factor_of * jnp.repeat(jnp.exp(heights), shape[axis_at] // blocks).reshape((-1,) + (1,) * (len(shape) - 1 - axis_at))
    return factor_of


def gaussian(rng, extent, spread, reach, cuts=(), kind=jnp.bfloat16):
    values = spread * jax.random.normal(rng, extent, jnp.float32)
    if cuts:
        values = values * level_of(rng, extent, cuts, -0.22, 0.18)
    return jnp.clip(values, -reach, reach).astype(kind)


def setup_inputs(seed: int = 0) -> dict:
    key_list = jax.random.split(jax.random.key(seed), 11)
    prompt_states = gaussian(key_list[0], (PROMPT_TOTAL, PREFIX, D), 1.0, 6.0, ((0, 8), (2, 16)))
    kv_weight = gaussian(key_list[1], (D, KVW), D ** -0.5, 0.0625, ((0, 16), (1, 8)))
    queries = draw_queries(jax.random.fold_in(key_list[10], 71), 0)
    new_kv = draw_new_kv(jax.random.fold_in(key_list[10], 71), 0)
    local_pages = draw_local_pages(jax.random.fold_in(key_list[10], 71), 0)
    pool_pages = draw_pool_pages(jax.random.fold_in(key_list[10], 71), 0)
    prompt_pages = draw_prompt_pages(jax.random.fold_in(key_list[10], 71), 0)
    comp_pages = draw_comp_pages(jax.random.fold_in(key_list[10], 71), 0)
    preempted = draw_preempted(jax.random.fold_in(key_list[10], 71), 0)
    page_where = draw_page_where(jax.random.fold_in(key_list[10], 71), 0)
    return dict(prompt_states=prompt_states, kv_weight=kv_weight, queries=queries, new_kv=new_kv, local_pages=local_pages, pool_pages=pool_pages, prompt_pages=prompt_pages, comp_pages=comp_pages, preempted=preempted, page_where=page_where)


def reference(prompt_states, kv_weight, queries, new_kv, local_pages, pool_pages, prompt_pages, comp_pages, preempted, page_where):
    slice_width = D // N_SAMPLE
    weight_parts = kv_weight.reshape(N_SAMPLE, slice_width, KVW)
    group_width = QUERY_HEADS // KEY_VALUE_HEADS

    def one_prompt(operands):
        states, query_rows, new_rows, local_rows, pool_rows, prompt_len, lengths, flagged, locations = operands
        state_parts = states.reshape(PREFIX, N_SAMPLE, slice_width)

        def add_part(running, part_index):
            left_part = lax.dynamic_index_in_dim(state_parts, part_index, 1, keepdims=False)
            right_part = lax.dynamic_index_in_dim(weight_parts, part_index, 0, keepdims=False)
            partial_value = jnp.dot(left_part, right_part, preferred_element_type=jnp.float32)
            rounded = lax.optimization_barrier(partial_value.astype(jnp.bfloat16))
            return (running + rounded.astype(jnp.float32), None)
        projected, _ = lax.scan(add_part, jnp.zeros((PREFIX, KVW), jnp.float32), jnp.arange(N_SAMPLE, dtype=jnp.int32))
        cached = projected.astype(jnp.bfloat16)
        pooled = pool_rows.reshape(SAMPLES_EACH * CMAX, PAGE, KVW)
        fetched = jnp.take(pooled, locations.reshape(-1), axis=0).reshape(SAMPLES_EACH, CMAX, PAGE, KVW)
        private = jnp.where((flagged > 0)[:, None, None, None], fetched, local_rows)
        prefix_alive = jnp.arange(PREFIX, dtype=jnp.int32) < prompt_len * PAGE

        def one_sample(sample_operands):
            single_query, new_row, page_rows, length = sample_operands
            key_row_block = jnp.concatenate([cached, page_rows.reshape(CMAX * PAGE, KVW), new_row[None, :]], axis=0)
            page_alive = jnp.repeat(jnp.arange(CMAX, dtype=jnp.int32) < length, PAGE)
            alive = jnp.concatenate([prefix_alive, page_alive, jnp.arange(1, dtype=jnp.int32) < 1])
            key_portion = key_row_block[:, :KEY_VALUE_HEADS * HEAD_SIZE].reshape(-1, KEY_VALUE_HEADS, HEAD_SIZE).astype(jnp.float32)
            value_portion = key_row_block[:, KEY_VALUE_HEADS * HEAD_SIZE:].reshape(-1, KEY_VALUE_HEADS, HEAD_SIZE).astype(jnp.float32)
            grouped_rows = single_query.reshape(KEY_VALUE_HEADS, group_width, HEAD_SIZE).astype(jnp.float32)
            scores = jnp.einsum('kgd,tkd->kgt', grouped_rows, key_portion, precision=lax.Precision.HIGHEST) / math.sqrt(HEAD_SIZE)
            scores = jnp.where(alive, scores, -jnp.inf)
            row_max = lax.optimization_barrier(jnp.max(scores, axis=-1, keepdims=True))
            exponent = jnp.where(alive, jnp.exp(scores - row_max), 0.0)
            row_total = lax.optimization_barrier(jnp.sum(exponent, axis=-1))
            weights = lax.optimization_barrier(exponent.astype(jnp.bfloat16)).astype(jnp.float32)
            mixture = jnp.einsum('kgt,tkd->kgd', weights, value_portion, precision=lax.Precision.HIGHEST)
            mixture = mixture / row_total[..., None]
            return mixture.reshape(QUERY_HEADS * HEAD_SIZE).astype(jnp.bfloat16)
        outputs = lax.map(one_sample, (query_rows, new_rows, private, lengths))
        return (cached, outputs)
    prefix_cache, attended = lax.map(one_prompt, (prompt_states, queries, new_kv, local_pages, pool_pages, prompt_pages, comp_pages, preempted, page_where))
    return (prefix_cache, attended)
```

```python
import functools
import math

import jax
import jax.numpy as jnp
from jax import lax
from jax.experimental import pallas as pl
from jax.experimental.pallas import tpu as pltpu
from jax.sharding import PartitionSpec as P

QUERY_HEADS = 64
GROUPS = 8
HEADS = 8
HEAD_SIZE = 128
PAGE = 128
SAMPLES = 16
CMAX = 16
ROWS = 256
SLICE = 512
COLUMNS = 256
KVW = 2048
KEYS = GROUPS * HEAD_SIZE
PACK = QUERY_HEADS + HEADS
LOW = -1e30
SCALE = 1.0 / math.sqrt(HEAD_SIZE)
MIB = 1 << 20
F32 = jnp.float32
BF16 = jnp.bfloat16

X_RIGHT = [(z * 4 + x, z * 4 + (x + 1) % 4) for z in range(4) for x in range(4)]
X_LEFT = [(z * 4 + x, z * 4 + (x + 3) % 4) for z in range(4) for x in range(4)]
X_FAR = [(z * 4 + x, z * 4 + (x + 2) % 4) for z in range(4) for x in range(4)]
Z_UP = [(z * 4 + x, (z + 1) % 4 * 4 + x) for z in range(4) for x in range(4)]
Z_DOWN = [(z * 4 + x, (z + 3) % 4 * 4 + x) for z in range(4) for x in range(4)]
SWAP = [(y * 2 + c, y * 2 + 1 - c) for y in range(4) for c in range(2)]
Y_SPLIT = [(y * 2 + c, (y + (1 if c == 0 else 3)) % 4 * 2 + c) for y in range(4) for c in range(2)]


def params(mib):
    return pltpu.CompilerParams(vmem_limit_bytes=mib * MIB)


def cost(flops, bytes_accessed):
    return pl.CostEstimate(flops=flops, bytes_accessed=bytes_accessed, transcendentals=0)


def nt_dot(a, b):
    return lax.dot_general(a, b, (((1,), (1,)), ((), ())), preferred_element_type=F32)


def put_lane(running, lane, column):
    at = lax.broadcasted_iota(jnp.int32, running.shape, len(running.shape) - 1)
    return jnp.where(at == lane, column, running)


def weight_copies(pieces, held, sems):
    return [pltpu.make_async_copy(pieces[j], held.at[j], sems.at[j]) for j in range(8)]


def product_kernel(count, table, *refs):
    states, pieces = refs[:4], refs[4:12]
    outs, (held, sems) = refs[12:-2], refs[-2:]
    copies = weight_copies(pieces, held, sems)
    for copy in copies:
        copy.start()
    for j in range(8):
        copies[j].wait()
        for k in range(count):
            row_block = table[k]
            total = jnp.zeros((ROWS, COLUMNS), F32)
            for d in range(4):
                total += jnp.dot(states[d][row_block], held[j, d], preferred_element_type=F32)
            out = outs[2 * k + j // 4]
            out[:, (j % 4) * COLUMNS : (j % 4 + 1) * COLUMNS] = total.astype(out.dtype)


def product(states, pieces, row_blocks, types, name):
    count = len(types)
    outs = [jax.ShapeDtypeStruct((ROWS, KVW // 2), t) for t in types for _ in range(2)]
    return pl.pallas_call(
        functools.partial(product_kernel, count),
        out_shape=outs,
        in_specs=[pl.BlockSpec(memory_space=pltpu.SMEM)]
        + [pl.BlockSpec(memory_space=pltpu.VMEM)] * 4
        + [pl.BlockSpec(memory_space=pl.ANY)] * 8,
        out_specs=[pl.BlockSpec(memory_space=pltpu.VMEM)] * len(outs),
        scratch_shapes=[
            pltpu.VMEM((8, 4, SLICE, COLUMNS), BF16),
            pltpu.SemaphoreType.DMA((8,)),
        ],
        compiler_params=params(48),
        cost_estimate=cost(2 * count * ROWS * KVW * KVW, 12 * MIB),
        name=name,
    )(row_blocks, *states, *pieces)


def page_kernel(slots, alive, query, page, out):
    s = pl.program_id(0)

    @pl.when(alive[s] == 0)
    def _():
        out[0, :QUERY_HEADS] = jnp.zeros((QUERY_HEADS, HEAD_SIZE), F32)
        out[0, QUERY_HEADS:] = jnp.full((HEADS, HEAD_SIZE), LOW, F32)

    @pl.when(alive[s] != 0)
    def _():
        logs = jnp.full((HEADS, HEAD_SIZE), LOW, F32)
        for g in range(GROUPS):
            keys = page[0, :, g * HEAD_SIZE : (g + 1) * HEAD_SIZE]
            values = page[0, :, KEYS + g * HEAD_SIZE : KEYS + (g + 1) * HEAD_SIZE]
            scores = nt_dot(query[0, g * HEADS : (g + 1) * HEADS], keys) * SCALE
            top = jnp.max(scores, axis=-1, keepdims=True)
            exponent = jnp.exp(scores - top)
            total = jnp.sum(exponent, axis=-1, keepdims=True)
            mixture = jnp.dot(exponent.astype(BF16), values, preferred_element_type=F32)
            out[0, g * HEADS : (g + 1) * HEADS] = mixture / total
            logs = put_lane(logs, g, top + jnp.log(total))
        out[0, QUERY_HEADS:] = logs


def pool_attention(slots, alive, queries_all, pool):
    return pl.pallas_call(
        page_kernel,
        out_shape=jax.ShapeDtypeStruct((SAMPLES, PACK, HEAD_SIZE), F32),
        grid_spec=pltpu.PrefetchScalarGridSpec(
            num_scalar_prefetch=2,
            grid=(SAMPLES,),
            in_specs=[
                pl.BlockSpec((1,) + queries_all.shape[1:], lambda s, slots, alive: (s, 0, 0)),
                pl.BlockSpec((1, PAGE, KVW), lambda s, slots, alive: (slots[s], 0, 0)),
            ],
            out_specs=pl.BlockSpec((1, PACK, HEAD_SIZE), lambda s, slots, alive: (s, 0, 0)),
        ),
        compiler_params=params(32),
        cost_estimate=cost(200_000_000, 8 * MIB),
        name="pool_attention",
    )(slots, alive, queries_all, pool)


LOCAL_PAGES = 4


def local_kernel(pages_alive, query, new, pages, out, top_ref, sum_ref, mix_ref):
    step = pl.program_id(0)
    width = LOCAL_PAGES * PAGE

    @pl.when(step == 0)
    def _():
        for g in range(GROUPS):
            rows = slice(g * HEADS, (g + 1) * HEADS)
            lanes = slice(g * HEAD_SIZE, (g + 1) * HEAD_SIZE)
            value_lanes = slice(KEYS + g * HEAD_SIZE, KEYS + (g + 1) * HEAD_SIZE)
            products = query[rows].astype(F32) * new[0:1, lanes].astype(F32)
            top_ref[rows] = jnp.sum(products, axis=-1, keepdims=True) * SCALE
            sum_ref[rows] = jnp.ones((HEADS, 1), F32)
            mix_ref[rows] = jnp.broadcast_to(new[0:1, value_lanes].astype(F32), (HEADS, HEAD_SIZE))

    @pl.when(step * LOCAL_PAGES < pages_alive[0])
    def _():
        block = pages.reshape(width, KVW)
        at = step * width + lax.broadcasted_iota(jnp.int32, (HEADS, width), 1)
        live = at < pages_alive[0] * PAGE
        for g in range(GROUPS):
            rows = slice(g * HEADS, (g + 1) * HEADS)
            keys = block[:, g * HEAD_SIZE : (g + 1) * HEAD_SIZE]
            values = block[:, KEYS + g * HEAD_SIZE : KEYS + (g + 1) * HEAD_SIZE]
            scores = jnp.where(live, nt_dot(query[rows], keys) * SCALE, LOW)
            old = top_ref[rows]
            top = jnp.maximum(old, jnp.max(scores, axis=-1, keepdims=True))
            shrink = jnp.exp(old - top)
            exponent = jnp.where(live, jnp.exp(scores - top), 0.0)
            top_ref[rows] = top
            sum_ref[rows] = sum_ref[rows] * shrink + jnp.sum(exponent, axis=-1, keepdims=True)
            mix_ref[rows] = mix_ref[rows] * shrink + jnp.dot(
                exponent.astype(BF16), values, preferred_element_type=F32
            )

    @pl.when(step == CMAX // LOCAL_PAGES - 1)
    def _():
        logs = jnp.full((HEADS, HEAD_SIZE), LOW, F32)
        for g in range(GROUPS):
            rows = slice(g * HEADS, (g + 1) * HEADS)
            out[rows] = mix_ref[rows] / sum_ref[rows]
            logs = put_lane(logs, g, top_ref[rows] + jnp.log(sum_ref[rows]))
        out[QUERY_HEADS:] = logs


def local_attention(pages_alive, query, new, pages):
    def block_of(step, alive):
        last = jnp.maximum(alive[0] - 1, 0) // LOCAL_PAGES
        return (jnp.minimum(step, last), 0, 0)

    return pl.pallas_call(
        local_kernel,
        out_shape=jax.ShapeDtypeStruct((PACK, HEAD_SIZE), F32),
        grid_spec=pltpu.PrefetchScalarGridSpec(
            num_scalar_prefetch=1,
            grid=(CMAX // LOCAL_PAGES,),
            in_specs=[
                pl.BlockSpec((QUERY_HEADS, HEAD_SIZE), lambda step, alive: (0, 0)),
                pl.BlockSpec((1, KVW), lambda step, alive: (0, 0)),
                pl.BlockSpec((LOCAL_PAGES, PAGE, KVW), block_of),
            ],
            out_specs=pl.BlockSpec((PACK, HEAD_SIZE), lambda step, alive: (0, 0)),
            scratch_shapes=[
                pltpu.VMEM((QUERY_HEADS, 1), F32),
                pltpu.VMEM((QUERY_HEADS, 1), F32),
                pltpu.VMEM((QUERY_HEADS, HEAD_SIZE), F32),
            ],
        ),
        compiler_params=params(32),
        cost_estimate=cost(200_000_000, 8 * MIB),
        name="local_attention",
    )(pages_alive, query, new, pages)


def prefix_kernel(
    columns, live_rows, own_l, own_r, up_l, up_r, down_l, down_r, queries, pool, cache, packed
):
    for j in range(8):
        lanes = slice((j % 4) * COLUMNS, (j % 4 + 1) * COLUMNS)
        own, up, down = (own_l, up_l, down_l) if j < 4 else (own_r, up_r, down_r)
        total = own[:, lanes] + up[:, lanes].astype(F32) + down[:, lanes].astype(F32)
        target = pl.ds(pl.multiple_of(columns[j] * COLUMNS, COLUMNS), COLUMNS)
        cache[0, :, target] = total.astype(BF16)
    live = lax.broadcasted_iota(jnp.int32, (SAMPLES * HEADS, ROWS), 1) < live_rows[0]
    logs = jnp.full((SAMPLES * HEADS, HEAD_SIZE), LOW, F32)
    for g in range(GROUPS):
        keys = cache[0, :, g * HEAD_SIZE : (g + 1) * HEAD_SIZE]
        values = cache[0, :, KEYS + g * HEAD_SIZE : KEYS + (g + 1) * HEAD_SIZE]
        scores = jnp.where(live, nt_dot(queries[g], keys) * SCALE, LOW)
        top = jnp.max(scores, axis=-1, keepdims=True)
        exponent = jnp.where(live, jnp.exp(scores - top), 0.0)
        total = jnp.sum(exponent, axis=-1, keepdims=True)
        mixture = jnp.dot(exponent.astype(BF16), values, preferred_element_type=F32)
        some = total > 0.0
        total = jnp.where(some, total, 1.0)
        log = jnp.where(some, top + jnp.log(total), LOW)
        rows = slice(g * HEADS, (g + 1) * HEADS)
        pool_log = pool[:, QUERY_HEADS:, g : g + 1].reshape(SAMPLES * HEADS, 1)
        pool_mixture = pool[:, rows].reshape(SAMPLES * HEADS, HEAD_SIZE)
        high = jnp.maximum(log, pool_log)
        here, there = jnp.exp(log - high), jnp.exp(pool_log - high)
        both = here + there
        merged = mixture * (here / (total * both)) + pool_mixture * (there / both)
        packed[:, rows] = merged.reshape(SAMPLES, HEADS, HEAD_SIZE)
        logs = put_lane(logs, g, high + jnp.log(both))
    packed[:, QUERY_HEADS:] = logs.reshape(SAMPLES, HEADS, HEAD_SIZE)


def prefix_attention(columns, live_rows, parts, queries, pool):
    smem, vmem = pl.BlockSpec(memory_space=pltpu.SMEM), pl.BlockSpec(memory_space=pltpu.VMEM)
    return pl.pallas_call(
        prefix_kernel,
        out_shape=[
            jax.ShapeDtypeStruct((1, ROWS, KVW), BF16),
            jax.ShapeDtypeStruct((SAMPLES, PACK, HEAD_SIZE), F32),
        ],
        in_specs=[smem, smem] + [vmem] * 8,
        out_specs=[vmem, vmem],
        compiler_params=params(32),
        cost_estimate=cost(300_000_000, 6 * MIB),
        name="prefix_attention",
    )(columns, live_rows, *parts, queries, pool)


def combine_kernel(arrived, local, out):
    for g in range(GROUPS):
        rows = slice(g * HEADS, (g + 1) * HEADS)
        logs = arrived[:, QUERY_HEADS:, g : g + 1]
        local_log = local[QUERY_HEADS:, g : g + 1]
        high = jnp.maximum(jnp.max(logs, axis=0), local_log)
        shares = jnp.exp(logs - high[None])
        local_share = jnp.exp(local_log - high)
        total = jnp.sum(shares, axis=0) + local_share
        mixture = jnp.sum(arrived[:, rows] * shares, axis=0) + local[rows] * local_share
        out[rows] = (mixture / total).astype(BF16)


def combine(arrived, local):
    vmem = pl.BlockSpec(memory_space=pltpu.VMEM)
    return pl.pallas_call(
        combine_kernel,
        out_shape=jax.ShapeDtypeStruct((QUERY_HEADS, HEAD_SIZE), BF16),
        in_specs=[vmem, vmem],
        out_specs=vmem,
        compiler_params=params(32),
        cost_estimate=cost(1_000_000, MIB),
        name="combine",
    )(arrived, local)


def per_device(
    prompt_states,
    kv_weight,
    queries,
    new_kv,
    local_pages,
    pool_pages,
    prompt_pages,
    comp_pages,
    preempted,
    page_where,
):
    own_index = lax.axis_index("sample")
    z, x = own_index // 4, own_index % 4
    prompt_index = lax.axis_index("prompt")
    y, core = prompt_index // 2, prompt_index % 2

    gathered = [
        kv_weight,
        lax.ppermute(kv_weight, "sample", X_RIGHT),
        lax.ppermute(kv_weight, "sample", X_LEFT),
        lax.ppermute(kv_weight, "sample", X_FAR),
    ]
    here = jnp.stack(gathered)
    states = prompt_states.reshape(4, 4, ROWS, SLICE)

    def rows_for(step):
        return lax.dynamic_index_in_dim(states, (x + step) % 4, 1, keepdims=False)

    arrived_states = [
        rows_for(0),
        lax.ppermute(rows_for(1), "sample", X_RIGHT),
        lax.ppermute(rows_for(3), "sample", X_LEFT),
        lax.ppermute(rows_for(2), "sample", X_FAR),
    ]
    here_other = lax.ppermute(here, "prompt", SWAP)
    near = lax.ppermute(here, "prompt", Y_SPLIT)
    near_other = lax.ppermute(here_other, "prompt", Y_SPLIT)
    far = lax.ppermute(near, "prompt", Y_SPLIT)
    near_swapped = lax.ppermute(near, "prompt", SWAP)
    near_other_swapped = lax.ppermute(near_other, "prompt", SWAP)
    far_other = lax.ppermute(far, "prompt", SWAP)
    pieces = [
        here, here_other, near, near_other,
        near_swapped, near_other_swapped, far, far_other,
    ]
    towards = jnp.where(core == 0, 3, 1)
    near_y, other_y, far_y = (y + towards) % 4, (y + 4 - towards) % 4, (y + 2) % 4
    columns = jnp.stack(
        [
            2 * y + core, 2 * y + 1 - core, 2 * near_y + core, 2 * near_y + 1 - core,
            2 * other_y + 1 - core, 2 * other_y + core, 2 * far_y + core, 2 * far_y + 1 - core,
        ]
    ).astype(jnp.int32)

    first = ((z + 2) % 4).reshape(1).astype(jnp.int32)
    rest = jnp.stack([(z + 1) % 4, (z + 3) % 4, z]).astype(jnp.int32)
    far_l, far_r = product(arrived_states, pieces, first, [BF16], "product_far")
    up_l, up_r, down_l, down_r, own_l, own_r = product(
        arrived_states, pieces, rest, [BF16, BF16, F32], "product_near"
    )
    from_down = lax.ppermute(far_l, "sample", Z_UP)
    from_up = lax.ppermute(far_r, "sample", Z_DOWN)
    up_l = (up_l.astype(F32) + from_down.astype(F32)).astype(BF16)
    down_r = (down_r.astype(F32) + from_up.astype(F32)).astype(BF16)
    sums = [
        own_l,
        own_r,
        lax.ppermute(up_l, "sample", Z_UP),
        lax.ppermute(up_r, "sample", Z_UP),
        lax.ppermute(down_l, "sample", Z_DOWN),
        lax.ppermute(down_r, "sample", Z_DOWN),
    ]

    plan = jnp.concatenate([page_where[0, 0], comp_pages[0], preempted[0]]).astype(BF16)
    plan = jnp.pad(plan.reshape(1, -1), ((0, 15), (0, HEAD_SIZE - CMAX - 2)))
    query = queries.reshape(QUERY_HEADS, HEAD_SIZE)
    sent, _ = lax.optimization_barrier((jnp.concatenate([query, plan]), gathered[1]))
    everyone = lax.all_gather(sent, "sample", axis=0)
    plans = everyone[:, QUERY_HEADS, : CMAX + 2].astype(jnp.int32)
    where_all, lens_all, flags_all = plans[:, :CMAX], plans[:, CMAX], plans[:, CMAX + 1]
    page_ids = jnp.arange(CMAX, dtype=jnp.int32)
    here_page = where_all // CMAX == own_index
    slots = jnp.sum(jnp.where(here_page, where_all % CMAX, 0), axis=1)
    live_all = (page_ids[None, :] < lens_all[:, None]) & (flags_all[:, None] > 0)
    alive = jnp.any(here_page & live_all, axis=1).astype(jnp.int32)
    pool = pool_attention(slots, alive, everyone, pool_pages[0, 0])
    local_alive = jnp.where(preempted[0] > 0, 0, comp_pages[0])
    local = local_attention(local_alive, query, new_kv[0], local_pages[0, 0])

    by_group = everyone[:, :QUERY_HEADS].reshape(SAMPLES, GROUPS, HEADS, HEAD_SIZE)
    by_group = by_group.transpose(1, 0, 2, 3).reshape(GROUPS, SAMPLES * HEADS, HEAD_SIZE)
    live_rows = (prompt_pages * PAGE - own_index * ROWS).astype(jnp.int32)
    cache, packed = prefix_attention(columns, live_rows, sums, by_group, pool)
    arrived = lax.all_to_all(packed, "sample", split_axis=0, concat_axis=0, tiled=True)
    attended = combine(arrived, local)
    return (cache, attended.reshape(1, 1, -1))


def solution(mesh):
    return jax.shard_map(
        per_device,
        mesh=mesh,
        in_specs=(
            P("prompt", None, "sample"),
            P("sample", "prompt"),
            P("prompt", "sample", None),
            P("prompt", "sample", None),
            P("prompt", "sample", None, None, None),
            P("prompt", "sample", None, None, None),
            P("prompt"),
            P("prompt", "sample"),
            P("prompt", "sample"),
            P("prompt", "sample", None),
        ),
        out_specs=(P("prompt", "sample", None), P("prompt", "sample", None)),
        check_vma=False,
    )
```

```python
import functools
import math

import jax
import jax.numpy as jnp
from jax import lax
from jax.experimental import pallas as pl
from jax.experimental.pallas import tpu as pltpu
from jax.sharding import PartitionSpec as P

QUERY_HEADS = 64
GROUPS = 8
HEADS = 8
HEAD_SIZE = 128
PAGE = 128
SAMPLES = 16
CMAX = 16
ROWS = 256
SLICE = 512
COLUMNS = 256
KVW = 2048
KEYS = GROUPS * HEAD_SIZE
PACK = QUERY_HEADS + HEADS
LOW = -1e30
SCALE = 1.0 / math.sqrt(HEAD_SIZE)
MIB = 1 << 20
F32 = jnp.float32
BF16 = jnp.bfloat16

X_RIGHT = [(z * 4 + x, z * 4 + (x + 1) % 4) for z in range(4) for x in range(4)]
X_LEFT = [(z * 4 + x, z * 4 + (x + 3) % 4) for z in range(4) for x in range(4)]
X_FAR = [(z * 4 + x, z * 4 + (x + 2) % 4) for z in range(4) for x in range(4)]
Z_UP = [(z * 4 + x, (z + 1) % 4 * 4 + x) for z in range(4) for x in range(4)]
Z_DOWN = [(z * 4 + x, (z + 3) % 4 * 4 + x) for z in range(4) for x in range(4)]
Z_FAR = [(z * 4 + x, (z + 2) % 4 * 4 + x) for z in range(4) for x in range(4)]
SWAP = [(y * 2 + c, y * 2 + 1 - c) for y in range(4) for c in range(2)]
Y_SPLIT = [(y * 2 + c, (y + (1 if c == 0 else 3)) % 4 * 2 + c) for y in range(4) for c in range(2)]


def params(mib):
    return pltpu.CompilerParams(vmem_limit_bytes=mib * MIB)


def cost(flops, bytes_accessed):
    return pl.CostEstimate(flops=flops, bytes_accessed=bytes_accessed, transcendentals=0)


def nt_dot(a, b):
    return lax.dot_general(a, b, (((1,), (1,)), ((), ())), preferred_element_type=F32)


def put_lane(running, lane, column):
    at = lax.broadcasted_iota(jnp.int32, running.shape, len(running.shape) - 1)
    return jnp.where(at == lane, column, running)


def pick_kernel(states, *refs):
    outs, sems = refs[:6], refs[6]
    me = lax.axis_index("sample")
    z, x = me // 4, lax.rem(me, 4)
    copies = []
    for i, step in enumerate((1, 3, 2)):
        column = lax.rem(x + step, 4)
        for k, up in enumerate((2, 1, 3)):
            copies.append((states.at[lax.rem(z + up, 4), column], outs[2 * i].at[k]))
        copies.append((states.at[z, column], outs[2 * i + 1]))
    copies = [pltpu.make_async_copy(src, dst, sems.at[n]) for n, (src, dst) in enumerate(copies)]
    for copy in copies:
        copy.start()
    for copy in copies:
        copy.wait()


def pick(states):
    far = jax.ShapeDtypeStruct((3, ROWS, SLICE), BF16)
    near = jax.ShapeDtypeStruct((ROWS, SLICE), BF16)
    hbm = pl.BlockSpec(memory_space=pl.ANY)
    return pl.pallas_call(
        pick_kernel,
        out_shape=[far, near] * 3,
        in_specs=[hbm],
        out_specs=[hbm] * 6,
        scratch_shapes=[pltpu.SemaphoreType.DMA((12,))],
        compiler_params=params(16),
        cost_estimate=cost(0, 6 * MIB),
        name="pick_rows",
    )(states)


def product_kernel(blocks, *refs):
    states, pieces, outs = refs[:4], refs[4:12], refs[12:]
    for j in range(8):
        for k, block in enumerate(blocks):
            total = jnp.zeros((ROWS, COLUMNS), F32)
            for d in range(4):
                left = states[d][...] if block is None else states[d][block]
                total += jnp.dot(left, pieces[j][d], preferred_element_type=F32)
            out = outs[2 * k + j // 4]
            out[:, (j % 4) * COLUMNS : (j % 4 + 1) * COLUMNS] = total.astype(out.dtype)


def product(states, pieces, blocks, kind, name):
    vmem = pl.BlockSpec(memory_space=pltpu.VMEM)
    outs = [jax.ShapeDtypeStruct((ROWS, KVW // 2), kind)] * (2 * len(blocks))
    return pl.pallas_call(
        functools.partial(product_kernel, blocks),
        out_shape=outs,
        in_specs=[vmem] * 12,
        out_specs=[vmem] * len(outs),
        compiler_params=params(40),
        cost_estimate=cost(2 * len(blocks) * ROWS * KVW * KVW, 2 * MIB),
        name=name,
    )(*states, *pieces)


def log_rows(logs):
    out = jnp.full((HEADS, HEAD_SIZE), LOW, F32)
    for g in range(GROUPS):
        out = put_lane(out, g, logs[g * HEADS : (g + 1) * HEADS])
    return out


POOL_PAGES = 4


def page_kernel(slots, alive, query, *refs):
    pages, out = refs[:POOL_PAGES], refs[POOL_PAGES]
    step = pl.program_id(0)
    scores = []
    for k in range(POOL_PAGES):
        for g in range(GROUPS):
            keys = pages[k][0, :, g * HEAD_SIZE : (g + 1) * HEAD_SIZE]
            scores.append(nt_dot(query[k, g * HEADS : (g + 1) * HEADS], keys))
    scores = jnp.concatenate(scores) * SCALE
    top = jnp.max(scores, axis=-1, keepdims=True)
    exponent = jnp.exp(scores - top)
    total = jnp.sum(exponent, axis=-1, keepdims=True)
    logs, share = top + jnp.log(total), 1.0 / total
    for k in range(POOL_PAGES):
        live = alive[step * POOL_PAGES + k] != 0
        for g in range(GROUPS):
            rows = slice(k * QUERY_HEADS + g * HEADS, k * QUERY_HEADS + (g + 1) * HEADS)
            values = pages[k][0, :, KEYS + g * HEAD_SIZE : KEYS + (g + 1) * HEAD_SIZE]
            mixture = jnp.dot(exponent[rows].astype(BF16), values, preferred_element_type=F32)
            out[k, g * HEADS : (g + 1) * HEADS] = jnp.where(live, mixture * share[rows], 0.0)
        mine = log_rows(logs[k * QUERY_HEADS : (k + 1) * QUERY_HEADS])
        out[k, QUERY_HEADS:] = jnp.where(live, mine, LOW)


def pool_attention(slots, alive, queries_all, pool):
    def page_of(k):
        return lambda s, slots, alive: (slots[s * POOL_PAGES + k], 0, 0)

    return pl.pallas_call(
        page_kernel,
        out_shape=jax.ShapeDtypeStruct((SAMPLES, PACK, HEAD_SIZE), F32),
        grid_spec=pltpu.PrefetchScalarGridSpec(
            num_scalar_prefetch=2,
            grid=(SAMPLES // POOL_PAGES,),
            in_specs=[
                pl.BlockSpec(
                    (POOL_PAGES, QUERY_HEADS, HEAD_SIZE), lambda s, slots, alive: (s, 0, 0)
                )
            ]
            + [pl.BlockSpec((1, PAGE, KVW), page_of(k)) for k in range(POOL_PAGES)],
            out_specs=pl.BlockSpec(
                (POOL_PAGES, PACK, HEAD_SIZE), lambda s, slots, alive: (s, 0, 0)
            ),
        ),
        compiler_params=params(32),
        cost_estimate=cost(10_000_000_000, 8 * MIB),
        name="pool_attention",
    )(slots, alive, queries_all, *[pool] * POOL_PAGES)


LOCAL_PAGES = 4


def local_kernel(pages_alive, query, new, pages, out, top_ref, sum_ref, mix_ref):
    step = pl.program_id(0)
    width = LOCAL_PAGES * PAGE

    @pl.when(step == 0)
    def _():
        for g in range(GROUPS):
            rows = slice(g * HEADS, (g + 1) * HEADS)
            lanes = slice(g * HEAD_SIZE, (g + 1) * HEAD_SIZE)
            value_lanes = slice(KEYS + g * HEAD_SIZE, KEYS + (g + 1) * HEAD_SIZE)
            products = query[rows].astype(F32) * new[0:1, lanes].astype(F32)
            top_ref[rows] = jnp.sum(products, axis=-1, keepdims=True) * SCALE
            sum_ref[rows] = jnp.ones((HEADS, 1), F32)
            mix_ref[rows] = jnp.broadcast_to(new[0:1, value_lanes].astype(F32), (HEADS, HEAD_SIZE))

    @pl.when(step * LOCAL_PAGES < pages_alive[0])
    def _():
        block = pages.reshape(width, KVW)
        at = step * width + lax.broadcasted_iota(jnp.int32, (QUERY_HEADS, width), 1)
        live = at < pages_alive[0] * PAGE
        scores = jnp.concatenate(
            [
                nt_dot(
                    query[g * HEADS : (g + 1) * HEADS],
                    block[:, g * HEAD_SIZE : (g + 1) * HEAD_SIZE],
                )
                for g in range(GROUPS)
            ]
        )
        scores = jnp.where(live, scores * SCALE, LOW)
        old = top_ref[...]
        top = jnp.maximum(old, jnp.max(scores, axis=-1, keepdims=True))
        shrink = jnp.exp(old - top)
        exponent = jnp.where(live, jnp.exp(scores - top), 0.0)
        top_ref[...] = top
        sum_ref[...] = sum_ref[...] * shrink + jnp.sum(exponent, axis=-1, keepdims=True)
        for g in range(GROUPS):
            rows = slice(g * HEADS, (g + 1) * HEADS)
            values = block[:, KEYS + g * HEAD_SIZE : KEYS + (g + 1) * HEAD_SIZE]
            mix_ref[rows] = mix_ref[rows] * shrink[rows] + jnp.dot(
                exponent[rows].astype(BF16), values, preferred_element_type=F32
            )

    @pl.when(step == CMAX // LOCAL_PAGES - 1)
    def _():
        out[:QUERY_HEADS] = mix_ref[...] / sum_ref[...]
        out[QUERY_HEADS:] = log_rows(top_ref[...] + jnp.log(sum_ref[...]))


def local_attention(pages_alive, query, new, pages):
    def block_of(step, alive):
        last = jnp.maximum(alive[0] - 1, 0) // LOCAL_PAGES
        return (jnp.minimum(step, last), 0, 0)

    return pl.pallas_call(
        local_kernel,
        out_shape=jax.ShapeDtypeStruct((PACK, HEAD_SIZE), F32),
        grid_spec=pltpu.PrefetchScalarGridSpec(
            num_scalar_prefetch=1,
            grid=(CMAX // LOCAL_PAGES,),
            in_specs=[
                pl.BlockSpec((QUERY_HEADS, HEAD_SIZE), lambda step, alive: (0, 0)),
                pl.BlockSpec((1, KVW), lambda step, alive: (0, 0)),
                pl.BlockSpec((LOCAL_PAGES, PAGE, KVW), block_of),
            ],
            out_specs=pl.BlockSpec((PACK, HEAD_SIZE), lambda step, alive: (0, 0)),
            scratch_shapes=[
                pltpu.VMEM((QUERY_HEADS, 1), F32),
                pltpu.VMEM((QUERY_HEADS, 1), F32),
                pltpu.VMEM((QUERY_HEADS, HEAD_SIZE), F32),
            ],
        ),
        compiler_params=params(32),
        cost_estimate=cost(10_000_000_000, 8 * MIB),
        name="local_attention",
    )(pages_alive, query, new, pages)


def prefix_kernel(
    prompt_pages, own_l, own_r, up_l, up_r, down_l, down_r, queries, pool, cache, packed
):
    me, prompt = lax.axis_index("sample"), lax.axis_index("prompt")
    z, x = me // 4, lax.rem(me, 4)
    y, core = prompt // 2, lax.rem(prompt, 2)
    near = lax.rem(y + 3 - 2 * core, 4)
    other = lax.rem(y + 1 + 2 * core, 4)
    far = lax.rem(y + 2, 4)
    columns = (
        2 * y + core, 2 * y + 1 - core, 2 * near + core, 2 * near + 1 - core,
        2 * other + 1 - core, 2 * other + core, 2 * far + core, 2 * far + 1 - core,
    )
    for j in range(8):
        lanes = slice((j % 4) * COLUMNS, (j % 4 + 1) * COLUMNS)
        own, up, down = (own_l, up_l, down_l) if j < 4 else (own_r, up_r, down_r)
        total = own[:, lanes] + up[:, lanes].astype(F32) + down[:, lanes].astype(F32)
        target = pl.ds(pl.multiple_of(columns[j] * COLUMNS, COLUMNS), COLUMNS)
        cache[0, :, target] = total.astype(BF16)
    sources = [
        lax.rem(z + 4 - dz, 4) * 4 + lax.rem(x + 4 - dx, 4) for dz in (0, 1, 3, 2) for dx in (0, 1, 3, 2)
    ]
    live = lax.broadcasted_iota(jnp.int32, (SAMPLES * HEADS, ROWS), 1) < prompt_pages[0] * PAGE - me * ROWS
    logs = jnp.full((SAMPLES * HEADS, HEAD_SIZE), LOW, F32)
    for g in range(GROUPS):
        keys = cache[0, :, g * HEAD_SIZE : (g + 1) * HEAD_SIZE]
        values = cache[0, :, KEYS + g * HEAD_SIZE : KEYS + (g + 1) * HEAD_SIZE]
        scores = jnp.where(live, nt_dot(queries[g], keys) * SCALE, LOW)
        top = jnp.max(scores, axis=-1, keepdims=True)
        exponent = jnp.where(live, jnp.exp(scores - top), 0.0)
        total = jnp.sum(exponent, axis=-1, keepdims=True)
        mixture = jnp.dot(exponent.astype(BF16), values, preferred_element_type=F32)
        some = total > 0.0
        total = jnp.where(some, total, 1.0)
        log = jnp.where(some, top + jnp.log(total), LOW)
        rows = slice(g * HEADS, (g + 1) * HEADS)
        pool_log = pool[:, QUERY_HEADS:, g : g + 1].reshape(SAMPLES * HEADS, 1)
        pool_mixture = pool[:, rows].reshape(SAMPLES * HEADS, HEAD_SIZE)
        high = jnp.maximum(log, pool_log)
        here, there = jnp.exp(log - high), jnp.exp(pool_log - high)
        both = here + there
        merged = mixture * (here / (total * both)) + pool_mixture * (there / both)
        for r, source in enumerate(sources):
            packed[source, rows] = merged[r * HEADS : (r + 1) * HEADS]
        logs = put_lane(logs, g, high + jnp.log(both))
    for r, source in enumerate(sources):
        packed[source, QUERY_HEADS:] = logs[r * HEADS : (r + 1) * HEADS]


def prefix_attention(prompt_pages, parts, queries, pool):
    smem, vmem = pl.BlockSpec(memory_space=pltpu.SMEM), pl.BlockSpec(memory_space=pltpu.VMEM)
    return pl.pallas_call(
        prefix_kernel,
        out_shape=[
            jax.ShapeDtypeStruct((1, ROWS, KVW), BF16),
            jax.ShapeDtypeStruct((SAMPLES, PACK, HEAD_SIZE), F32),
        ],
        in_specs=[smem] + [vmem] * 8,
        out_specs=[vmem, vmem],
        compiler_params=params(32),
        cost_estimate=cost(300_000_000, 6 * MIB),
        name="prefix_attention",
    )(prompt_pages, *parts, queries, pool)


def combine_kernel(arrived, local, out):
    for g in range(GROUPS):
        rows = slice(g * HEADS, (g + 1) * HEADS)
        logs = arrived[:, QUERY_HEADS:, g : g + 1]
        local_log = local[QUERY_HEADS:, g : g + 1]
        high = jnp.maximum(jnp.max(logs, axis=0), local_log)
        shares = jnp.exp(logs - high[None])
        local_share = jnp.exp(local_log - high)
        total = jnp.sum(shares, axis=0) + local_share
        mixture = jnp.sum(arrived[:, rows] * shares, axis=0) + local[rows] * local_share
        out[rows] = (mixture / total).astype(BF16)


def combine(arrived, local):
    vmem = pl.BlockSpec(memory_space=pltpu.VMEM)
    return pl.pallas_call(
        combine_kernel,
        out_shape=jax.ShapeDtypeStruct((QUERY_HEADS, HEAD_SIZE), BF16),
        in_specs=[vmem, vmem],
        out_specs=vmem,
        compiler_params=params(32),
        cost_estimate=cost(1_000_000, MIB),
        name="combine",
    )(arrived, local)


def per_device(
    prompt_states,
    kv_weight,
    queries,
    new_kv,
    local_pages,
    pool_pages,
    prompt_pages,
    comp_pages,
    preempted,
    page_where,
):
    own_index = lax.axis_index("sample")
    tie = lax.optimization_barrier

    plan = jnp.concatenate([page_where[0, 0], comp_pages[0], preempted[0]]).astype(BF16)
    plan = jnp.pad(plan.reshape(1, -1), ((0, 7), (0, COLUMNS - CMAX - 2)))
    query = queries.reshape(QUERY_HEADS, HEAD_SIZE)
    sent = jnp.concatenate([kv_weight, queries.reshape(-1, COLUMNS), plan])
    along_x = [sent] + [lax.ppermute(sent, "sample", to) for to in (X_RIGHT, X_LEFT, X_FAR)]

    states = prompt_states.reshape(4, 4, ROWS, SLICE)
    to_right, last_right, to_left, last_left, to_far, last_far = pick(states)
    rows_right = lax.ppermute(to_right, "sample", X_RIGHT)
    rows_left = lax.ppermute(to_left, "sample", X_LEFT)
    rows_far = lax.ppermute(to_far, "sample", X_FAR)
    last_right, last_left, last_far, rows_right = tie((last_right, last_left, last_far, rows_right))
    own_states = [
        lax.ppermute(last_right, "sample", X_RIGHT),
        lax.ppermute(last_left, "sample", X_LEFT),
        lax.ppermute(last_far, "sample", X_FAR),
    ]

    here = jnp.stack([a[:SLICE] for a in along_x])
    here_other = lax.ppermute(here, "prompt", SWAP)
    near = lax.ppermute(here, "prompt", Y_SPLIT)
    near_other = lax.ppermute(here_other, "prompt", Y_SPLIT)
    far = lax.ppermute(near, "prompt", Y_SPLIT)
    near_swapped = lax.ppermute(near, "prompt", SWAP)
    near_other_swapped = lax.ppermute(near_other, "prompt", SWAP)
    far_other = lax.ppermute(far, "prompt", SWAP)
    pieces = [
        here, here_other, near, near_other,
        near_swapped, near_other_swapped, far, far_other,
    ]

    of_row = jnp.stack([a[SLICE:] for a in along_x])
    everyone = jnp.concatenate(
        [of_row] + [lax.ppermute(of_row, "sample", to) for to in (Z_UP, Z_DOWN, Z_FAR)]
    )
    queries_all = everyone[:, : QUERY_HEADS // 2].reshape(SAMPLES, QUERY_HEADS, HEAD_SIZE)
    queries_all, rows_right = tie((queries_all, rows_right))
    plans = everyone[:, QUERY_HEADS // 2, : CMAX + 2].astype(jnp.int32)
    where_all, lens_all, flags_all = plans[:, :CMAX], plans[:, CMAX], plans[:, CMAX + 1]
    page_ids = jnp.arange(CMAX, dtype=jnp.int32)
    here_page = where_all // CMAX == own_index
    slots = jnp.sum(jnp.where(here_page, where_all % CMAX, 0), axis=1)
    live_all = (page_ids[None, :] < lens_all[:, None]) & (flags_all[:, None] > 0)
    alive = jnp.any(here_page & live_all, axis=1).astype(jnp.int32)
    pool = pool_attention(slots, alive, queries_all, pool_pages[0, 0])
    local_alive = jnp.where(preempted[0] > 0, 0, comp_pages[0])
    query, here_other = tie((query, here_other))
    local = local_attention(local_alive, query, new_kv[0], local_pages[0, 0])
    by_group = queries_all.reshape(SAMPLES, GROUPS, HEADS, HEAD_SIZE)
    by_group = by_group.transpose(1, 0, 2, 3).reshape(GROUPS, SAMPLES * HEADS, HEAD_SIZE)

    z, x = own_index // 4, own_index % 4
    mine = lax.dynamic_index_in_dim(states, x, 1, keepdims=False)
    mine_rows = jnp.stack(
        [lax.dynamic_index_in_dim(mine, (z + up) % 4, 0, keepdims=False) for up in (2, 1, 3)]
    )
    mine_last = lax.dynamic_index_in_dim(mine, z, 0, keepdims=False)
    mine_rows, pool, local = tie((mine_rows, pool, local))
    rows = [mine_rows, rows_right, rows_left, rows_far]
    far_l, far_r = product(rows, pieces, (0,), BF16, "product_far")
    up_l, up_r, down_l, down_r = product(rows, pieces, (1, 2), BF16, "product_near")
    own_l, own_r = product([mine_last] + own_states, pieces, (None,), F32, "product_own")
    from_down = lax.ppermute(far_l, "sample", Z_UP)
    from_up = lax.ppermute(far_r, "sample", Z_DOWN)
    up_l = (up_l.astype(F32) + from_down.astype(F32)).astype(BF16)
    down_r = (down_r.astype(F32) + from_up.astype(F32)).astype(BF16)
    sums = [
        own_l,
        own_r,
        lax.ppermute(up_l, "sample", Z_UP),
        lax.ppermute(up_r, "sample", Z_UP),
        lax.ppermute(down_l, "sample", Z_DOWN),
        lax.ppermute(down_r, "sample", Z_DOWN),
    ]

    cache, packed = prefix_attention(prompt_pages, sums, by_group, pool)
    arrived = lax.all_to_all(packed, "sample", split_axis=0, concat_axis=0, tiled=True)
    attended = combine(arrived, local)
    return (cache, attended.reshape(1, 1, -1))


def solution(mesh):
    return jax.shard_map(
        per_device,
        mesh=mesh,
        in_specs=(
            P("prompt", None, "sample"),
            P("sample", "prompt"),
            P("prompt", "sample", None),
            P("prompt", "sample", None),
            P("prompt", "sample", None, None, None),
            P("prompt", "sample", None, None, None),
            P("prompt"),
            P("prompt", "sample"),
            P("prompt", "sample"),
            P("prompt", "sample", None),
        ),
        out_specs=(P("prompt", "sample", None), P("prompt", "sample", None)),
        check_vma=False,
    )
```

```python
import functools
import math

import jax
import jax.numpy as jnp
from jax import lax
from jax.experimental import pallas as pl
from jax.experimental.pallas import tpu as pltpu
from jax.sharding import PartitionSpec as P

QUERY_HEADS = 64
GROUPS = 8
HEADS = 8
HEAD_SIZE = 128
PAGE = 128
SAMPLES = 16
CMAX = 16
ROWS = 256
SLICE = 512
COLUMNS = 256
KVW = 2048
KEYS = GROUPS * HEAD_SIZE
PACK = QUERY_HEADS + HEADS
LOW = -1e30
SCALE = 1.0 / math.sqrt(HEAD_SIZE)
MIB = 1 << 20
F32 = jnp.float32
BF16 = jnp.bfloat16

X_RIGHT = [(z * 4 + x, z * 4 + (x + 1) % 4) for z in range(4) for x in range(4)]
X_LEFT = [(z * 4 + x, z * 4 + (x + 3) % 4) for z in range(4) for x in range(4)]
X_FAR = [(z * 4 + x, z * 4 + (x + 2) % 4) for z in range(4) for x in range(4)]
Z_UP = [(z * 4 + x, (z + 1) % 4 * 4 + x) for z in range(4) for x in range(4)]
Z_DOWN = [(z * 4 + x, (z + 3) % 4 * 4 + x) for z in range(4) for x in range(4)]
Z_FAR = [(z * 4 + x, (z + 2) % 4 * 4 + x) for z in range(4) for x in range(4)]
SWAP = [(y * 2 + c, y * 2 + 1 - c) for y in range(4) for c in range(2)]
Y_SPLIT = [(y * 2 + c, (y + (1 if c == 0 else 3)) % 4 * 2 + c) for y in range(4) for c in range(2)]


def params(mib):
    return pltpu.CompilerParams(vmem_limit_bytes=mib * MIB)


def cost(flops, bytes_accessed):
    return pl.CostEstimate(flops=flops, bytes_accessed=bytes_accessed, transcendentals=0)


def nt_dot(a, b):
    return lax.dot_general(a, b, (((1,), (1,)), ((), ())), preferred_element_type=F32)


def put_lane(running, lane, column):
    at = lax.broadcasted_iota(jnp.int32, running.shape, len(running.shape) - 1)
    return jnp.where(at == lane, column, running)


SENT = SLICE + QUERY_HEADS // 2 + 8
HALF = QUERY_HEADS // 2


def prepare_kernel(where, length, flag, weight, query, sent, own):
    sent[:SLICE] = weight[...]
    heads = [query[0, 0:1, h * HEAD_SIZE : (h + 1) * HEAD_SIZE].astype(F32) for h in range(QUERY_HEADS)]
    low, high = jnp.concatenate(heads[:HALF]), jnp.concatenate(heads[HALF:])
    own[:HALF] = low.astype(BF16)
    own[HALF:] = high.astype(BF16)
    sent[SLICE : SLICE + HALF, :HEAD_SIZE] = low.astype(BF16)
    sent[SLICE : SLICE + HALF, HEAD_SIZE:] = high.astype(BF16)
    plan = jnp.zeros((8, COLUMNS), F32)
    for c in range(CMAX):
        plan = put_lane(plan, c, where[0, 0, c].astype(F32))
    plan = put_lane(plan, CMAX, length[0, 0].astype(F32))
    plan = put_lane(plan, CMAX + 1, flag[0, 0].astype(F32))
    sent[SLICE + HALF :] = plan.astype(BF16)


def prepare(weight, query, where, length, flag):
    smem, vmem = pl.BlockSpec(memory_space=pltpu.SMEM), pl.BlockSpec(memory_space=pltpu.VMEM)
    return pl.pallas_call(
        prepare_kernel,
        out_shape=[
            jax.ShapeDtypeStruct((SENT, COLUMNS), BF16),
            jax.ShapeDtypeStruct((QUERY_HEADS, HEAD_SIZE), BF16),
        ],
        in_specs=[smem] * 3 + [vmem] * 2,
        out_specs=[vmem, vmem],
        compiler_params=params(16),
        cost_estimate=cost(1000, 1000),
        name="prepare",
    )(where, length, flag, weight, query)


def unpack_kernel(*refs):
    arrived, (queries, by_group, slots, alive) = refs[:4], refs[4:]
    me = lax.axis_index("sample")
    plans = []
    for r in range(SAMPLES):
        block = arrived[r // 4][r % 4].astype(F32)
        for half in range(2):
            lanes = slice(half * HEAD_SIZE, (half + 1) * HEAD_SIZE)
            queries[r, half * HALF : (half + 1) * HALF] = block[:HALF, lanes].astype(BF16)
        plans.append(block[HALF : HALF + 1])
    for g in range(GROUPS):
        lanes = slice(g // 4 * HEAD_SIZE, (g // 4 + 1) * HEAD_SIZE)
        rows = slice(g % 4 * HEADS, (g % 4 + 1) * HEADS)
        parts = [arrived[r // 4][r % 4].astype(F32)[rows, lanes] for r in range(SAMPLES)]
        by_group[g] = jnp.concatenate(parts).astype(BF16)
    plan = jnp.concatenate(plans)
    lane = lax.broadcasted_iota(jnp.int32, plan.shape, 1)
    first = (me * CMAX).astype(F32)
    here = (lane < CMAX) & (plan >= first) & (plan < first + CMAX)
    live = here & (lane.astype(F32) < plan[:, CMAX : CMAX + 1]) & (plan[:, CMAX + 1 : CMAX + 2] > 0.5)
    slot = jnp.sum(jnp.where(here, plan - first, 0.0), axis=1, keepdims=True).astype(jnp.int32)
    some = jnp.max(jnp.where(live, 1.0, 0.0), axis=1, keepdims=True).astype(jnp.int32)
    for r in range(SAMPLES):
        slots[r] = slot[r, 0]
        alive[r] = some[r, 0]


def unpack(arrived):
    smem, vmem = pl.BlockSpec(memory_space=pltpu.SMEM), pl.BlockSpec(memory_space=pltpu.VMEM)
    return pl.pallas_call(
        unpack_kernel,
        out_shape=[
            jax.ShapeDtypeStruct((SAMPLES, QUERY_HEADS, HEAD_SIZE), BF16),
            jax.ShapeDtypeStruct((GROUPS, SAMPLES * HEADS, HEAD_SIZE), BF16),
            jax.ShapeDtypeStruct((SAMPLES,), jnp.int32),
            jax.ShapeDtypeStruct((SAMPLES,), jnp.int32),
        ],
        in_specs=[vmem] * 4,
        out_specs=[vmem, vmem, smem, smem],
        compiler_params=params(16),
        cost_estimate=cost(1000, 1000),
        name="unpack",
    )(*arrived)


def pick_kernel(steps, states, *refs):
    outs, sems = refs[:-1], refs[-1]
    me = lax.axis_index("sample")
    z, x = me // 4, lax.rem(me, 4)
    copies = []
    for i, step in enumerate(steps):
        column = lax.rem(x + step, 4)
        for k, up in enumerate((2, 1, 3)):
            copies.append((states.at[lax.rem(z + up, 4), column], outs[2 * i].at[k]))
        copies.append((states.at[z, column], outs[2 * i + 1]))
    copies = [pltpu.make_async_copy(src, dst, sems.at[n]) for n, (src, dst) in enumerate(copies)]
    for copy in copies:
        copy.start()
    for copy in copies:
        copy.wait()


def pick(states, steps, space, mib, name):
    rest = jax.ShapeDtypeStruct((3, ROWS, SLICE), BF16)
    own = jax.ShapeDtypeStruct((ROWS, SLICE), BF16)
    return pl.pallas_call(
        functools.partial(pick_kernel, steps),
        out_shape=[rest, own] * len(steps),
        in_specs=[pl.BlockSpec(memory_space=pl.ANY)],
        out_specs=[pl.BlockSpec(memory_space=space)] * (2 * len(steps)),
        scratch_shapes=[pltpu.SemaphoreType.DMA((4 * len(steps),))],
        compiler_params=params(mib),
        cost_estimate=cost(1000, 1000),
        name=name,
    )(states)


def product_kernel(blocks, *refs):
    states, pieces, outs = refs[:4], refs[4:12], refs[12:]
    for j in range(8):
        for k, block in enumerate(blocks):
            total = jnp.zeros((ROWS, COLUMNS), F32)
            for d in range(4):
                left = states[d][...] if block is None else states[d][block]
                total += jnp.dot(left, pieces[j][d], preferred_element_type=F32)
            out = outs[2 * k + j // 4]
            out[:, (j % 4) * COLUMNS : (j % 4 + 1) * COLUMNS] = total.astype(out.dtype)


def product(states, pieces, blocks, kind, name):
    vmem = pl.BlockSpec(memory_space=pltpu.VMEM)
    outs = [jax.ShapeDtypeStruct((ROWS, KVW // 2), kind)] * (2 * len(blocks))
    return pl.pallas_call(
        functools.partial(product_kernel, blocks),
        out_shape=outs,
        in_specs=[vmem] * 12,
        out_specs=[vmem] * len(outs),
        compiler_params=params(20),
        cost_estimate=cost(1000, 1000),
        name=name,
    )(*states, *pieces)


def log_rows(logs):
    out = jnp.full((HEADS, HEAD_SIZE), LOW, F32)
    for g in range(GROUPS):
        out = put_lane(out, g, logs[g * HEADS : (g + 1) * HEADS])
    return out


POOL_PAGES = 4


def page_kernel(slots, alive, query, *refs):
    pages, out = refs[:POOL_PAGES], refs[POOL_PAGES]
    step = pl.program_id(0)
    scores = []
    for k in range(POOL_PAGES):
        for g in range(GROUPS):
            keys = pages[k][0, :, g * HEAD_SIZE : (g + 1) * HEAD_SIZE]
            scores.append(nt_dot(query[k, g * HEADS : (g + 1) * HEADS], keys))
    scores = jnp.concatenate(scores) * SCALE
    top = jnp.max(scores, axis=-1, keepdims=True)
    exponent = jnp.exp(scores - top)
    total = jnp.sum(exponent, axis=-1, keepdims=True)
    logs, share = top + jnp.log(total), 1.0 / total
    for k in range(POOL_PAGES):
        live = alive[step * POOL_PAGES + k] != 0
        for g in range(GROUPS):
            rows = slice(k * QUERY_HEADS + g * HEADS, k * QUERY_HEADS + (g + 1) * HEADS)
            values = pages[k][0, :, KEYS + g * HEAD_SIZE : KEYS + (g + 1) * HEAD_SIZE]
            mixture = jnp.dot(exponent[rows].astype(BF16), values, preferred_element_type=F32)
            out[k, g * HEADS : (g + 1) * HEADS] = jnp.where(live, mixture * share[rows], 0.0)
        mine = log_rows(logs[k * QUERY_HEADS : (k + 1) * QUERY_HEADS])
        out[k, QUERY_HEADS:] = jnp.where(live, mine, LOW)


def pool_attention(slots, alive, queries_all, pool):
    def page_of(k):
        return lambda s, slots, alive: (slots[s * POOL_PAGES + k], 0, 0)

    return pl.pallas_call(
        page_kernel,
        out_shape=jax.ShapeDtypeStruct((SAMPLES, PACK, HEAD_SIZE), F32),
        grid_spec=pltpu.PrefetchScalarGridSpec(
            num_scalar_prefetch=2,
            grid=(SAMPLES // POOL_PAGES,),
            in_specs=[
                pl.BlockSpec(
                    (POOL_PAGES, QUERY_HEADS, HEAD_SIZE), lambda s, slots, alive: (s, 0, 0)
                )
            ]
            + [pl.BlockSpec((1, PAGE, KVW), page_of(k)) for k in range(POOL_PAGES)],
            out_specs=pl.BlockSpec(
                (POOL_PAGES, PACK, HEAD_SIZE), lambda s, slots, alive: (s, 0, 0)
            ),
        ),
        compiler_params=params(16),
        cost_estimate=cost(1000, 1000),
        name="pool_attention",
    )(slots, alive, queries_all, *[pool] * POOL_PAGES)


LOCAL_PAGES = 4


def local_kernel(pages_alive, query, new, pages, out, top_ref, sum_ref, mix_ref):
    step = pl.program_id(0)
    width = LOCAL_PAGES * PAGE

    @pl.when(step == 0)
    def _():
        for g in range(GROUPS):
            rows = slice(g * HEADS, (g + 1) * HEADS)
            lanes = slice(g * HEAD_SIZE, (g + 1) * HEAD_SIZE)
            value_lanes = slice(KEYS + g * HEAD_SIZE, KEYS + (g + 1) * HEAD_SIZE)
            products = query[rows].astype(F32) * new[0:1, lanes].astype(F32)
            top_ref[rows] = jnp.sum(products, axis=-1, keepdims=True) * SCALE
            sum_ref[rows] = jnp.ones((HEADS, 1), F32)
            mix_ref[rows] = jnp.broadcast_to(new[0:1, value_lanes].astype(F32), (HEADS, HEAD_SIZE))

    @pl.when(step * LOCAL_PAGES < pages_alive[0])
    def _():
        block = pages.reshape(width, KVW)
        at = step * width + lax.broadcasted_iota(jnp.int32, (QUERY_HEADS, width), 1)
        live = at < pages_alive[0] * PAGE
        scores = jnp.concatenate(
            [
                nt_dot(
                    query[g * HEADS : (g + 1) * HEADS],
                    block[:, g * HEAD_SIZE : (g + 1) * HEAD_SIZE],
                )
                for g in range(GROUPS)
            ]
        )
        scores = jnp.where(live, scores * SCALE, LOW)
        old = top_ref[...]
        top = jnp.maximum(old, jnp.max(scores, axis=-1, keepdims=True))
        shrink = jnp.exp(old - top)
        exponent = jnp.where(live, jnp.exp(scores - top), 0.0)
        top_ref[...] = top
        sum_ref[...] = sum_ref[...] * shrink + jnp.sum(exponent, axis=-1, keepdims=True)
        for g in range(GROUPS):
            rows = slice(g * HEADS, (g + 1) * HEADS)
            values = block[:, KEYS + g * HEAD_SIZE : KEYS + (g + 1) * HEAD_SIZE]
            mix_ref[rows] = mix_ref[rows] * shrink[rows] + jnp.dot(
                exponent[rows].astype(BF16), values, preferred_element_type=F32
            )

    @pl.when(step == CMAX // LOCAL_PAGES - 1)
    def _():
        out[:QUERY_HEADS] = mix_ref[...] / sum_ref[...]
        out[QUERY_HEADS:] = log_rows(top_ref[...] + jnp.log(sum_ref[...]))


def local_attention(pages_alive, query, new, pages):
    def block_of(step, alive):
        last = jnp.maximum(alive[0] - 1, 0) // LOCAL_PAGES
        return (jnp.minimum(step, last), 0, 0)

    return pl.pallas_call(
        local_kernel,
        out_shape=jax.ShapeDtypeStruct((PACK, HEAD_SIZE), F32),
        grid_spec=pltpu.PrefetchScalarGridSpec(
            num_scalar_prefetch=1,
            grid=(CMAX // LOCAL_PAGES,),
            in_specs=[
                pl.BlockSpec((QUERY_HEADS, HEAD_SIZE), lambda step, alive: (0, 0)),
                pl.BlockSpec((1, KVW), lambda step, alive: (0, 0)),
                pl.BlockSpec((LOCAL_PAGES, PAGE, KVW), block_of),
            ],
            out_specs=pl.BlockSpec((PACK, HEAD_SIZE), lambda step, alive: (0, 0)),
            scratch_shapes=[
                pltpu.VMEM((QUERY_HEADS, 1), F32),
                pltpu.VMEM((QUERY_HEADS, 1), F32),
                pltpu.VMEM((QUERY_HEADS, HEAD_SIZE), F32),
            ],
        ),
        compiler_params=params(16),
        cost_estimate=cost(1000, 1000),
        name="local_attention",
    )(pages_alive, query, new, pages)


def prefix_kernel(
    prompt_pages, own_l, own_r, up_l, up_r, down_l, down_r, queries, pool, cache, packed
):
    me, prompt = lax.axis_index("sample"), lax.axis_index("prompt")
    z, x = me // 4, lax.rem(me, 4)
    y, core = prompt // 2, lax.rem(prompt, 2)
    near = lax.rem(y + 3 - 2 * core, 4)
    other = lax.rem(y + 1 + 2 * core, 4)
    far = lax.rem(y + 2, 4)
    columns = (
        2 * y + core, 2 * y + 1 - core, 2 * near + core, 2 * near + 1 - core,
        2 * other + 1 - core, 2 * other + core, 2 * far + core, 2 * far + 1 - core,
    )
    for j in range(8):
        lanes = slice((j % 4) * COLUMNS, (j % 4 + 1) * COLUMNS)
        own, up, down = (own_l, up_l, down_l) if j < 4 else (own_r, up_r, down_r)
        total = own[:, lanes] + up[:, lanes].astype(F32) + down[:, lanes].astype(F32)
        target = pl.ds(pl.multiple_of(columns[j] * COLUMNS, COLUMNS), COLUMNS)
        cache[0, :, target] = total.astype(BF16)
    sources = [
        lax.rem(z + 4 - dz, 4) * 4 + lax.rem(x + 4 - dx, 4) for dz in (0, 1, 3, 2) for dx in (0, 1, 3, 2)
    ]
    live = lax.broadcasted_iota(jnp.int32, (SAMPLES * HEADS, ROWS), 1) < prompt_pages[0] * PAGE - me * ROWS
    logs = jnp.full((SAMPLES * HEADS, HEAD_SIZE), LOW, F32)
    for g in range(GROUPS):
        keys = cache[0, :, g * HEAD_SIZE : (g + 1) * HEAD_SIZE]
        values = cache[0, :, KEYS + g * HEAD_SIZE : KEYS + (g + 1) * HEAD_SIZE]
        scores = jnp.where(live, nt_dot(queries[g], keys) * SCALE, LOW)
        top = jnp.max(scores, axis=-1, keepdims=True)
        exponent = jnp.where(live, jnp.exp(scores - top), 0.0)
        total = jnp.sum(exponent, axis=-1, keepdims=True)
        mixture = jnp.dot(exponent.astype(BF16), values, preferred_element_type=F32)
        some = total > 0.0
        total = jnp.where(some, total, 1.0)
        log = jnp.where(some, top + jnp.log(total), LOW)
        rows = slice(g * HEADS, (g + 1) * HEADS)
        pool_log = pool[:, QUERY_HEADS:, g : g + 1].reshape(SAMPLES * HEADS, 1)
        pool_mixture = pool[:, rows].reshape(SAMPLES * HEADS, HEAD_SIZE)
        high = jnp.maximum(log, pool_log)
        here, there = jnp.exp(log - high), jnp.exp(pool_log - high)
        both = here + there
        merged = mixture * (here / (total * both)) + pool_mixture * (there / both)
        for r, source in enumerate(sources):
            packed[source, rows] = merged[r * HEADS : (r + 1) * HEADS]
        logs = put_lane(logs, g, high + jnp.log(both))
    for r, source in enumerate(sources):
        packed[source, QUERY_HEADS:] = logs[r * HEADS : (r + 1) * HEADS]


def prefix_attention(prompt_pages, parts, queries, pool):
    smem, vmem = pl.BlockSpec(memory_space=pltpu.SMEM), pl.BlockSpec(memory_space=pltpu.VMEM)
    return pl.pallas_call(
        prefix_kernel,
        out_shape=[
            jax.ShapeDtypeStruct((1, ROWS, KVW), BF16),
            jax.ShapeDtypeStruct((SAMPLES, PACK, HEAD_SIZE), F32),
        ],
        in_specs=[smem] + [vmem] * 8,
        out_specs=[vmem, vmem],
        compiler_params=params(20),
        cost_estimate=cost(300_000_000, 6 * MIB),
        name="prefix_attention",
    )(prompt_pages, *parts, queries, pool)


def combine_kernel(arrived, local, out):
    for g in range(GROUPS):
        rows = slice(g * HEADS, (g + 1) * HEADS)
        logs = arrived[:, QUERY_HEADS:, g : g + 1]
        local_log = local[QUERY_HEADS:, g : g + 1]
        high = jnp.maximum(jnp.max(logs, axis=0), local_log)
        shares = jnp.exp(logs - high[None])
        local_share = jnp.exp(local_log - high)
        total = jnp.sum(shares, axis=0) + local_share
        mixture = jnp.sum(arrived[:, rows] * shares, axis=0) + local[rows] * local_share
        out[rows] = (mixture / total).astype(BF16)


def combine(arrived, local):
    vmem = pl.BlockSpec(memory_space=pltpu.VMEM)
    return pl.pallas_call(
        combine_kernel,
        out_shape=jax.ShapeDtypeStruct((QUERY_HEADS, HEAD_SIZE), BF16),
        in_specs=[vmem, vmem],
        out_specs=vmem,
        compiler_params=params(16),
        cost_estimate=cost(1_000_000, MIB),
        name="combine",
    )(arrived, local)


def per_device(
    prompt_states,
    kv_weight,
    queries,
    new_kv,
    local_pages,
    pool_pages,
    prompt_pages,
    comp_pages,
    preempted,
    page_where,
):
    tie = lax.optimization_barrier

    sent, query = prepare(kv_weight, queries, page_where, comp_pages, preempted)
    along_x = [sent] + [lax.ppermute(sent, "sample", to) for to in (X_RIGHT, X_LEFT, X_FAR)]

    states = prompt_states.reshape(4, 4, ROWS, SLICE)
    to_right, last_right, to_left, last_left, to_far, last_far = pick(
        states, (1, 3, 2), pl.ANY, 56, "pick_sent"
    )
    to_far, *along_x = tie((to_far, *along_x))
    rows_far = lax.ppermute(to_far, "sample", X_FAR)
    to_right, to_left, query, rows_far = tie((to_right, to_left, query, rows_far))
    rows_right = lax.ppermute(to_right, "sample", X_RIGHT)
    rows_left = lax.ppermute(to_left, "sample", X_LEFT)
    last_right, last_left, last_far, rows_right = tie((last_right, last_left, last_far, rows_right))
    own_states = [
        lax.ppermute(last_right, "sample", X_RIGHT),
        lax.ppermute(last_left, "sample", X_LEFT),
        lax.ppermute(last_far, "sample", X_FAR),
    ]

    of_row = jnp.stack([a[SLICE:] for a in along_x])
    everyone = [of_row] + [lax.ppermute(of_row, "sample", to) for to in (Z_UP, Z_DOWN, Z_FAR)]

    here = jnp.stack([a[:SLICE] for a in along_x])
    here_other = lax.ppermute(here, "prompt", SWAP)
    near = lax.ppermute(here, "prompt", Y_SPLIT)
    near_other = lax.ppermute(here_other, "prompt", Y_SPLIT)
    near, *everyone = tie((near, *everyone))
    far = lax.ppermute(near, "prompt", Y_SPLIT)
    near_swapped = lax.ppermute(near, "prompt", SWAP)
    near_other_swapped = lax.ppermute(near_other, "prompt", SWAP)

    queries_all, by_group, slots, alive = unpack(everyone)
    queries_all, rows_far = tie((queries_all, rows_far))
    pool = pool_attention(slots, alive, queries_all, pool_pages[0, 0])
    local_alive = jnp.where(preempted[0] > 0, 0, comp_pages[0])
    query, here_other = tie((query, here_other))
    local = local_attention(local_alive, query, new_kv[0], local_pages[0, 0])

    far, pool, local, rows_right, rows_left = tie((far, pool, local, rows_right, rows_left))
    far_other = lax.ppermute(far, "prompt", SWAP)
    pieces = [
        here, here_other, near, near_other,
        near_swapped, near_other_swapped, far, far_other,
    ]

    mine_rows, mine_last = pick(states, (0,), pltpu.VMEM, 16, "pick_own")
    rows = [mine_rows, rows_right, rows_left, rows_far]
    far_l, far_r = product(rows, pieces, (0,), BF16, "product_far")
    up_l, up_r, down_l, down_r = product(rows, pieces, (1, 2), BF16, "product_near")
    own_l, own_r = product([mine_last] + own_states, pieces, (None,), F32, "product_own")
    from_down = lax.ppermute(far_l, "sample", Z_UP)
    from_up = lax.ppermute(far_r, "sample", Z_DOWN)
    up_l = (up_l.astype(F32) + from_down.astype(F32)).astype(BF16)
    down_r = (down_r.astype(F32) + from_up.astype(F32)).astype(BF16)
    sums = [
        own_l,
        own_r,
        lax.ppermute(up_l, "sample", Z_UP),
        lax.ppermute(up_r, "sample", Z_UP),
        lax.ppermute(down_l, "sample", Z_DOWN),
        lax.ppermute(down_r, "sample", Z_DOWN),
    ]

    cache, packed = prefix_attention(prompt_pages, sums, by_group, pool)
    arrived = lax.all_to_all(packed, "sample", split_axis=0, concat_axis=0, tiled=True)
    attended = combine(arrived, local)
    return (cache, attended.reshape(1, 1, -1))


def solution(mesh):
    return jax.shard_map(
        per_device,
        mesh=mesh,
        in_specs=(
            P("prompt", None, "sample"),
            P("sample", "prompt"),
            P("prompt", "sample", None),
            P("prompt", "sample", None),
            P("prompt", "sample", None, None, None),
            P("prompt", "sample", None, None, None),
            P("prompt"),
            P("prompt", "sample"),
            P("prompt", "sample"),
            P("prompt", "sample", None),
        ),
        out_specs=(P("prompt", "sample", None), P("prompt", "sample", None)),
        check_vma=False,
    )
```

```python
import functools
import math

import jax
import jax.numpy as jnp
from jax import lax
from jax.experimental import pallas as pl
from jax.experimental.pallas import tpu as pltpu
from jax.sharding import PartitionSpec as P

QUERY_HEADS = 64
GROUPS = 8
HEADS = 8
HEAD_SIZE = 128
PAGE = 128
SAMPLES = 16
CMAX = 16
ROWS = 256
SLICE = 512
COLUMNS = 256
KVW = 2048
KEYS = GROUPS * HEAD_SIZE
PACK = QUERY_HEADS + HEADS
LOW = -1e30
SCALE = 1.0 / math.sqrt(HEAD_SIZE)
MIB = 1 << 20
F32 = jnp.float32
BF16 = jnp.bfloat16

X_RIGHT = [(z * 4 + x, z * 4 + (x + 1) % 4) for z in range(4) for x in range(4)]
X_LEFT = [(z * 4 + x, z * 4 + (x + 3) % 4) for z in range(4) for x in range(4)]
X_FAR = [(z * 4 + x, z * 4 + (x + 2) % 4) for z in range(4) for x in range(4)]
Z_UP = [(z * 4 + x, (z + 1) % 4 * 4 + x) for z in range(4) for x in range(4)]
Z_DOWN = [(z * 4 + x, (z + 3) % 4 * 4 + x) for z in range(4) for x in range(4)]
Z_FAR = [(z * 4 + x, (z + 2) % 4 * 4 + x) for z in range(4) for x in range(4)]
SWAP = [(y * 2 + c, y * 2 + 1 - c) for y in range(4) for c in range(2)]
Y_SPLIT = [(y * 2 + c, (y + (1 if c == 0 else 3)) % 4 * 2 + c) for y in range(4) for c in range(2)]


def params(mib):
    return pltpu.CompilerParams(vmem_limit_bytes=mib * MIB)


def cost(flops, bytes_accessed):
    return pl.CostEstimate(flops=flops, bytes_accessed=bytes_accessed, transcendentals=0)


def nt_dot(a, b):
    return lax.dot_general(a, b, (((1,), (1,)), ((), ())), preferred_element_type=F32)


def put_lane(running, lane, column):
    at = lax.broadcasted_iota(jnp.int32, running.shape, len(running.shape) - 1)
    return jnp.where(at == lane, column, running)


SENT = SLICE + QUERY_HEADS // 2 + 8
HALF = QUERY_HEADS // 2


def prepare_kernel(where, length, flag, weight, query_hbm, sent, own, query, sems):
    weight_copy = pltpu.make_async_copy(weight, sent.at[pl.ds(0, SLICE)], sems.at[0])
    query_copy = pltpu.make_async_copy(query_hbm, query, sems.at[1])
    query_copy.start()
    weight_copy.start()
    query_copy.wait()
    heads = [query[0, 0:1, h * HEAD_SIZE : (h + 1) * HEAD_SIZE].astype(F32) for h in range(QUERY_HEADS)]
    low, high = jnp.concatenate(heads[:HALF]), jnp.concatenate(heads[HALF:])
    own[:HALF] = low.astype(BF16)
    own[HALF:] = high.astype(BF16)
    sent[SLICE : SLICE + HALF, :HEAD_SIZE] = low.astype(BF16)
    sent[SLICE : SLICE + HALF, HEAD_SIZE:] = high.astype(BF16)
    plan = jnp.zeros((8, COLUMNS), F32)
    for c in range(CMAX):
        plan = put_lane(plan, c, where[0, 0, c].astype(F32))
    plan = put_lane(plan, CMAX, length[0, 0].astype(F32))
    plan = put_lane(plan, CMAX + 1, flag[0, 0].astype(F32))
    sent[SLICE + HALF :] = plan.astype(BF16)
    weight_copy.wait()


def prepare(weight, query, where, length, flag):
    smem, vmem = pl.BlockSpec(memory_space=pltpu.SMEM), pl.BlockSpec(memory_space=pltpu.VMEM)
    return pl.pallas_call(
        prepare_kernel,
        out_shape=[
            jax.ShapeDtypeStruct((SENT, COLUMNS), BF16),
            jax.ShapeDtypeStruct((QUERY_HEADS, HEAD_SIZE), BF16),
        ],
        in_specs=[smem] * 3 + [pl.BlockSpec(memory_space=pl.ANY)] * 2,
        out_specs=[vmem, vmem],
        scratch_shapes=[
            pltpu.VMEM((1, 1, QUERY_HEADS * HEAD_SIZE), BF16),
            pltpu.SemaphoreType.DMA((2,)),
        ],
        compiler_params=params(58),
        cost_estimate=cost(1000, 1000),
        name="prepare",
    )(where, length, flag, weight, query)


def unpack_kernel(*refs):
    arrived, (queries, by_group, slots, alive) = refs[:4], refs[4:]
    me = lax.axis_index("sample")
    plans = []
    for r in range(SAMPLES):
        block = arrived[r // 4][r % 4].astype(F32)
        for half in range(2):
            lanes = slice(half * HEAD_SIZE, (half + 1) * HEAD_SIZE)
            queries[r, half * HALF : (half + 1) * HALF] = block[:HALF, lanes].astype(BF16)
        plans.append(block[HALF : HALF + 1])
    for g in range(GROUPS):
        lanes = slice(g // 4 * HEAD_SIZE, (g // 4 + 1) * HEAD_SIZE)
        rows = slice(g % 4 * HEADS, (g % 4 + 1) * HEADS)
        parts = [arrived[r // 4][r % 4].astype(F32)[rows, lanes] for r in range(SAMPLES)]
        by_group[g] = jnp.concatenate(parts).astype(BF16)
    plan = jnp.concatenate(plans)
    lane = lax.broadcasted_iota(jnp.int32, plan.shape, 1)
    first = (me * CMAX).astype(F32)
    here = (lane < CMAX) & (plan >= first) & (plan < first + CMAX)
    live = here & (lane.astype(F32) < plan[:, CMAX : CMAX + 1]) & (plan[:, CMAX + 1 : CMAX + 2] > 0.5)
    slot = jnp.sum(jnp.where(here, plan - first, 0.0), axis=1, keepdims=True).astype(jnp.int32)
    some = jnp.max(jnp.where(live, 1.0, 0.0), axis=1, keepdims=True).astype(jnp.int32)
    for r in range(SAMPLES):
        slots[r] = slot[r, 0]
        alive[r] = some[r, 0]


def unpack(arrived):
    smem, vmem = pl.BlockSpec(memory_space=pltpu.SMEM), pl.BlockSpec(memory_space=pltpu.VMEM)
    return pl.pallas_call(
        unpack_kernel,
        out_shape=[
            jax.ShapeDtypeStruct((SAMPLES, QUERY_HEADS, HEAD_SIZE), BF16),
            jax.ShapeDtypeStruct((GROUPS, SAMPLES * HEADS, HEAD_SIZE), BF16),
            jax.ShapeDtypeStruct((SAMPLES,), jnp.int32),
            jax.ShapeDtypeStruct((SAMPLES,), jnp.int32),
        ],
        in_specs=[vmem] * 4,
        out_specs=[vmem, vmem, smem, smem],
        compiler_params=params(16),
        cost_estimate=cost(1000, 1000),
        name="unpack",
    )(*arrived)


def pick_kernel(steps, states, *refs):
    outs, sems = refs[:-1], refs[-1]
    me = lax.axis_index("sample")
    z, x = me // 4, lax.rem(me, 4)
    copies = []
    for i, step in enumerate(steps):
        column = lax.rem(x + step, 4)
        copies.append((states.at[lax.rem(z + 2, 4), column], outs[3 * i]))
        copies.append((states.at[lax.rem(z + 1, 4), column], outs[3 * i + 1].at[0]))
        copies.append((states.at[lax.rem(z + 3, 4), column], outs[3 * i + 1].at[1]))
        copies.append((states.at[z, column], outs[3 * i + 2]))
    copies = [pltpu.make_async_copy(src, dst, sems.at[n]) for n, (src, dst) in enumerate(copies)]
    for copy in copies:
        copy.start()
    for copy in copies:
        copy.wait()


def pick(states, steps, mib, name):
    one = jax.ShapeDtypeStruct((ROWS, SLICE), BF16)
    two = jax.ShapeDtypeStruct((2, ROWS, SLICE), BF16)
    return pl.pallas_call(
        functools.partial(pick_kernel, steps),
        out_shape=[one, two, one] * len(steps),
        in_specs=[pl.BlockSpec(memory_space=pl.ANY)],
        out_specs=[pl.BlockSpec(memory_space=pltpu.VMEM)] * (3 * len(steps)),
        scratch_shapes=[pltpu.SemaphoreType.DMA((4 * len(steps),))],
        compiler_params=params(mib),
        cost_estimate=cost(1000, 1000),
        name=name,
    )(states)


def product_kernel(blocks, count, *refs):
    states, pieces, outs = refs[:4], refs[4 : 4 + count], refs[4 + count :]
    for j in range(count):
        for k, block in enumerate(blocks):
            total = jnp.zeros((ROWS, COLUMNS), F32)
            for d in range(4):
                left = states[d][...] if block is None else states[d][block]
                total += jnp.dot(left, pieces[j][d], preferred_element_type=F32)
            out = outs[k * count // 4 + j // 4]
            out[:, (j % 4) * COLUMNS : (j % 4 + 1) * COLUMNS] = total.astype(out.dtype)


def product(states, pieces, blocks, kind, name):
    vmem = pl.BlockSpec(memory_space=pltpu.VMEM)
    count = len(pieces)
    outs = [jax.ShapeDtypeStruct((ROWS, KVW // 2), kind)] * (len(blocks) * count // 4)
    return pl.pallas_call(
        functools.partial(product_kernel, blocks, count),
        out_shape=outs,
        in_specs=[vmem] * (4 + count),
        out_specs=[vmem] * len(outs),
        compiler_params=params(20),
        cost_estimate=cost(1000, 1000),
        name=name,
    )(*states, *pieces)


def log_rows(logs):
    out = jnp.full((HEADS, HEAD_SIZE), LOW, F32)
    for g in range(GROUPS):
        out = put_lane(out, g, logs[g * HEADS : (g + 1) * HEADS])
    return out


POOL_PAGES = 4


def page_kernel(slots, alive, query, *refs):
    pages, out = refs[:POOL_PAGES], refs[POOL_PAGES]
    step = pl.program_id(0)
    scores = []
    for k in range(POOL_PAGES):
        for g in range(GROUPS):
            keys = pages[k][0, :, g * HEAD_SIZE : (g + 1) * HEAD_SIZE]
            scores.append(nt_dot(query[k, g * HEADS : (g + 1) * HEADS], keys))
    scores = jnp.concatenate(scores) * SCALE
    top = jnp.max(scores, axis=-1, keepdims=True)
    exponent = jnp.exp(scores - top)
    total = jnp.sum(exponent, axis=-1, keepdims=True)
    logs, share = top + jnp.log(total), 1.0 / total
    for k in range(POOL_PAGES):
        live = alive[step * POOL_PAGES + k] != 0
        for g in range(GROUPS):
            rows = slice(k * QUERY_HEADS + g * HEADS, k * QUERY_HEADS + (g + 1) * HEADS)
            values = pages[k][0, :, KEYS + g * HEAD_SIZE : KEYS + (g + 1) * HEAD_SIZE]
            mixture = jnp.dot(exponent[rows].astype(BF16), values, preferred_element_type=F32)
            out[k, g * HEADS : (g + 1) * HEADS] = jnp.where(live, mixture * share[rows], 0.0)
        mine = log_rows(logs[k * QUERY_HEADS : (k + 1) * QUERY_HEADS])
        out[k, QUERY_HEADS:] = jnp.where(live, mine, LOW)


def pool_attention(slots, alive, queries_all, pool):
    def page_of(k):
        return lambda s, slots, alive: (slots[s * POOL_PAGES + k], 0, 0)

    return pl.pallas_call(
        page_kernel,
        out_shape=jax.ShapeDtypeStruct((SAMPLES, PACK, HEAD_SIZE), F32),
        grid_spec=pltpu.PrefetchScalarGridSpec(
            num_scalar_prefetch=2,
            grid=(SAMPLES // POOL_PAGES,),
            in_specs=[
                pl.BlockSpec(
                    (POOL_PAGES, QUERY_HEADS, HEAD_SIZE), lambda s, slots, alive: (s, 0, 0)
                )
            ]
            + [pl.BlockSpec((1, PAGE, KVW), page_of(k)) for k in range(POOL_PAGES)],
            out_specs=pl.BlockSpec(
                (POOL_PAGES, PACK, HEAD_SIZE), lambda s, slots, alive: (s, 0, 0)
            ),
        ),
        compiler_params=params(16),
        cost_estimate=cost(1000, 1000),
        name="pool_attention",
    )(slots, alive, queries_all, *[pool] * POOL_PAGES)


LOCAL_PAGES = 4


def local_kernel(pages_alive, query, new, pages, out, top_ref, sum_ref, mix_ref):
    step = pl.program_id(0)
    width = LOCAL_PAGES * PAGE

    @pl.when(step == 0)
    def _():
        for g in range(GROUPS):
            rows = slice(g * HEADS, (g + 1) * HEADS)
            lanes = slice(g * HEAD_SIZE, (g + 1) * HEAD_SIZE)
            value_lanes = slice(KEYS + g * HEAD_SIZE, KEYS + (g + 1) * HEAD_SIZE)
            products = query[rows].astype(F32) * new[0:1, lanes].astype(F32)
            top_ref[rows] = jnp.sum(products, axis=-1, keepdims=True) * SCALE
            sum_ref[rows] = jnp.ones((HEADS, 1), F32)
            mix_ref[rows] = jnp.broadcast_to(new[0:1, value_lanes].astype(F32), (HEADS, HEAD_SIZE))

    @pl.when(step * LOCAL_PAGES < pages_alive[0])
    def _():
        block = pages.reshape(width, KVW)
        at = step * width + lax.broadcasted_iota(jnp.int32, (QUERY_HEADS, width), 1)
        live = at < pages_alive[0] * PAGE
        scores = jnp.concatenate(
            [
                nt_dot(
                    query[g * HEADS : (g + 1) * HEADS],
                    block[:, g * HEAD_SIZE : (g + 1) * HEAD_SIZE],
                )
                for g in range(GROUPS)
            ]
        )
        scores = jnp.where(live, scores * SCALE, LOW)
        old = top_ref[...]
        top = jnp.maximum(old, jnp.max(scores, axis=-1, keepdims=True))
        shrink = jnp.exp(old - top)
        exponent = jnp.where(live, jnp.exp(scores - top), 0.0)
        top_ref[...] = top
        sum_ref[...] = sum_ref[...] * shrink + jnp.sum(exponent, axis=-1, keepdims=True)
        for g in range(GROUPS):
            rows = slice(g * HEADS, (g + 1) * HEADS)
            values = block[:, KEYS + g * HEAD_SIZE : KEYS + (g + 1) * HEAD_SIZE]
            mix_ref[rows] = mix_ref[rows] * shrink[rows] + jnp.dot(
                exponent[rows].astype(BF16), values, preferred_element_type=F32
            )

    @pl.when(step == CMAX // LOCAL_PAGES - 1)
    def _():
        out[:QUERY_HEADS] = mix_ref[...] / sum_ref[...]
        out[QUERY_HEADS:] = log_rows(top_ref[...] + jnp.log(sum_ref[...]))


def local_attention(pages_alive, query, new, pages):
    def block_of(step, alive):
        last = jnp.maximum(alive[0] - 1, 0) // LOCAL_PAGES
        return (jnp.minimum(step, last), 0, 0)

    return pl.pallas_call(
        local_kernel,
        out_shape=jax.ShapeDtypeStruct((PACK, HEAD_SIZE), F32),
        grid_spec=pltpu.PrefetchScalarGridSpec(
            num_scalar_prefetch=1,
            grid=(CMAX // LOCAL_PAGES,),
            in_specs=[
                pl.BlockSpec((QUERY_HEADS, HEAD_SIZE), lambda step, alive: (0, 0)),
                pl.BlockSpec((1, KVW), lambda step, alive: (0, 0)),
                pl.BlockSpec((LOCAL_PAGES, PAGE, KVW), block_of),
            ],
            out_specs=pl.BlockSpec((PACK, HEAD_SIZE), lambda step, alive: (0, 0)),
            scratch_shapes=[
                pltpu.VMEM((QUERY_HEADS, 1), F32),
                pltpu.VMEM((QUERY_HEADS, 1), F32),
                pltpu.VMEM((QUERY_HEADS, HEAD_SIZE), F32),
            ],
        ),
        compiler_params=params(16),
        cost_estimate=cost(1000, 1000),
        name="local_attention",
    )(pages_alive, query, new, pages)


def prefix_kernel(
    prompt_pages, own_l, own_r, up_l, up_r, down_l, down_r, far_l, far_r, queries, pool, cache, packed
):
    me, prompt = lax.axis_index("sample"), lax.axis_index("prompt")
    z, x = me // 4, lax.rem(me, 4)
    y, core = prompt // 2, lax.rem(prompt, 2)
    near = lax.rem(y + 3 - 2 * core, 4)
    other = lax.rem(y + 1 + 2 * core, 4)
    far = lax.rem(y + 2, 4)
    columns = (
        2 * y + core, 2 * y + 1 - core, 2 * near + core, 2 * near + 1 - core,
        2 * other + 1 - core, 2 * other + core, 2 * far + core, 2 * far + 1 - core,
    )
    for j in range(8):
        lanes = slice((j % 4) * COLUMNS, (j % 4 + 1) * COLUMNS)
        terms = (up_l, down_l, far_l) if j < 4 else (up_r, down_r, far_r)
        total = (own_l if j < 4 else own_r)[:, lanes]
        for term in terms:
            total = total + term[:, lanes].astype(F32)
        target = pl.ds(pl.multiple_of(columns[j] * COLUMNS, COLUMNS), COLUMNS)
        cache[0, :, target] = total.astype(BF16)
    sources = [
        lax.rem(z + 4 - dz, 4) * 4 + lax.rem(x + 4 - dx, 4) for dz in (0, 1, 3, 2) for dx in (0, 1, 3, 2)
    ]
    live = lax.broadcasted_iota(jnp.int32, (SAMPLES * HEADS, ROWS), 1) < prompt_pages[0] * PAGE - me * ROWS
    logs = jnp.full((SAMPLES * HEADS, HEAD_SIZE), LOW, F32)
    for g in range(GROUPS):
        keys = cache[0, :, g * HEAD_SIZE : (g + 1) * HEAD_SIZE]
        values = cache[0, :, KEYS + g * HEAD_SIZE : KEYS + (g + 1) * HEAD_SIZE]
        scores = jnp.where(live, nt_dot(queries[g], keys) * SCALE, LOW)
        top = jnp.max(scores, axis=-1, keepdims=True)
        exponent = jnp.where(live, jnp.exp(scores - top), 0.0)
        total = jnp.sum(exponent, axis=-1, keepdims=True)
        mixture = jnp.dot(exponent.astype(BF16), values, preferred_element_type=F32)
        some = total > 0.0
        total = jnp.where(some, total, 1.0)
        log = jnp.where(some, top + jnp.log(total), LOW)
        rows = slice(g * HEADS, (g + 1) * HEADS)
        pool_log = pool[:, QUERY_HEADS:, g : g + 1].reshape(SAMPLES * HEADS, 1)
        pool_mixture = pool[:, rows].reshape(SAMPLES * HEADS, HEAD_SIZE)
        high = jnp.maximum(log, pool_log)
        here, there = jnp.exp(log - high), jnp.exp(pool_log - high)
        both = here + there
        merged = mixture * (here / (total * both)) + pool_mixture * (there / both)
        for r, source in enumerate(sources):
            packed[source, rows] = merged[r * HEADS : (r + 1) * HEADS]
        logs = put_lane(logs, g, high + jnp.log(both))
    for r, source in enumerate(sources):
        packed[source, QUERY_HEADS:] = logs[r * HEADS : (r + 1) * HEADS]


def prefix_attention(prompt_pages, parts, queries, pool):
    smem, vmem = pl.BlockSpec(memory_space=pltpu.SMEM), pl.BlockSpec(memory_space=pltpu.VMEM)
    return pl.pallas_call(
        prefix_kernel,
        out_shape=[
            jax.ShapeDtypeStruct((1, ROWS, KVW), BF16),
            jax.ShapeDtypeStruct((SAMPLES, PACK, HEAD_SIZE), F32),
        ],
        in_specs=[smem] + [vmem] * 10,
        out_specs=[vmem, vmem],
        compiler_params=params(20),
        cost_estimate=cost(300_000_000, 6 * MIB),
        name="prefix_attention",
    )(prompt_pages, *parts, queries, pool)


def combine_kernel(arrived, local, out):
    for g in range(GROUPS):
        rows = slice(g * HEADS, (g + 1) * HEADS)
        logs = arrived[:, QUERY_HEADS:, g : g + 1]
        local_log = local[QUERY_HEADS:, g : g + 1]
        high = jnp.maximum(jnp.max(logs, axis=0), local_log)
        shares = jnp.exp(logs - high[None])
        local_share = jnp.exp(local_log - high)
        total = jnp.sum(shares, axis=0) + local_share
        mixture = jnp.sum(arrived[:, rows] * shares, axis=0) + local[rows] * local_share
        out[rows] = (mixture / total).astype(BF16)


def combine(arrived, local):
    vmem = pl.BlockSpec(memory_space=pltpu.VMEM)
    return pl.pallas_call(
        combine_kernel,
        out_shape=jax.ShapeDtypeStruct((QUERY_HEADS, HEAD_SIZE), BF16),
        in_specs=[vmem, vmem],
        out_specs=vmem,
        compiler_params=params(16),
        cost_estimate=cost(1_000_000, MIB),
        name="combine",
    )(arrived, local)


def per_device(
    prompt_states,
    kv_weight,
    queries,
    new_kv,
    local_pages,
    pool_pages,
    prompt_pages,
    comp_pages,
    preempted,
    page_where,
):
    tie = lax.optimization_barrier

    sent, query = prepare(kv_weight, queries, page_where, comp_pages, preempted)
    along_x = [sent] + [lax.ppermute(sent, "sample", to) for to in (X_RIGHT, X_LEFT, X_FAR)]

    states = prompt_states.reshape(4, 4, ROWS, SLICE)
    picked = pick(states, (1, 3, 2), 52, "pick_sent")
    towards = (X_RIGHT, X_LEFT, X_FAR)

    def across(batch):
        return [lax.ppermute(a, "sample", to) for a, to in zip(batch, towards)]

    first, second, third = (list(picked[k::3]) for k in range(3))
    *first, along_x[0], along_x[1], along_x[2], along_x[3] = tie((*first, *along_x))
    mine = list(pick(states, (0,), 16, "pick_own"))
    here = jnp.stack([a[:SLICE] for a in along_x])
    of_row = jnp.stack([a[SLICE:] for a in along_x])

    near = lax.ppermute(here, "prompt", Y_SPLIT)
    here_other = lax.ppermute(here, "prompt", SWAP)
    first = across(first)

    near, here_other, second[0], second[1], of_row, *rest = tie(
        (near, here_other, second[0], second[1], of_row, *first)
    )
    first = rest
    near_other = lax.ppermute(here_other, "prompt", Y_SPLIT)
    near_swapped = lax.ppermute(near, "prompt", SWAP)
    right_left = across(second[:2])
    everyone = [of_row] + [lax.ppermute(of_row, "sample", to) for to in (Z_UP, Z_DOWN, Z_FAR)]

    near, near_other, second[2], *rest = tie(
        (near, near_other, second[2], *right_left, *everyone, *mine)
    )
    right_left, everyone, mine = rest[:2], rest[2:6], rest[6:]
    far = lax.ppermute(near, "prompt", Y_SPLIT)
    near_other_swapped = lax.ppermute(near_other, "prompt", SWAP)
    second = [*right_left, lax.ppermute(second[2], "sample", X_FAR)]
    left_half = [here, here_other, near, near_other]
    (far_l,) = product([mine[0], *first], left_half, (None,), BF16, "product_far_l")
    far_l = lax.ppermute(far_l, "sample", Z_FAR)

    far, far_l, *rest = tie((far, far_l, *second, *third))
    second, third = rest[:3], rest[3:]
    far_other = lax.ppermute(far, "prompt", SWAP)
    third = across(third)
    up_l, down_l = product([mine[1], *second], left_half, (0, 1), BF16, "product_near_l")

    far_other, up_l, down_l = tie((far_other, up_l, down_l))
    right_half = [near_swapped, near_other_swapped, far, far_other]
    (far_r,) = product([mine[0], *first], right_half, (None,), BF16, "product_far_r")
    up_r, down_r = product([mine[1], *second], right_half, (0, 1), BF16, "product_near_r")
    query, far_r, up_r, down_r, *everyone = tie((query, far_r, up_r, down_r, *everyone))
    own_l, own_r = product([mine[2], *third], left_half + right_half, (None,), F32, "product_own")
    sums = [
        own_l,
        own_r,
        lax.ppermute(up_l, "sample", Z_UP),
        lax.ppermute(up_r, "sample", Z_UP),
        lax.ppermute(down_l, "sample", Z_DOWN),
        lax.ppermute(down_r, "sample", Z_DOWN),
        far_l,
        lax.ppermute(far_r, "sample", Z_FAR),
    ]

    queries_all, by_group, slots, alive = unpack(everyone)
    pool = pool_attention(slots, alive, queries_all, pool_pages[0, 0])
    local_alive = jnp.where(preempted[0] > 0, 0, comp_pages[0])
    local = local_attention(local_alive, query, new_kv[0], local_pages[0, 0])

    cache, packed = prefix_attention(prompt_pages, sums, by_group, pool)
    arrived = lax.all_to_all(packed, "sample", split_axis=0, concat_axis=0, tiled=True)
    attended = combine(arrived, local)
    return (cache, attended.reshape(1, 1, -1))


def solution(mesh):
    return jax.shard_map(
        per_device,
        mesh=mesh,
        in_specs=(
            P("prompt", None, "sample"),
            P("sample", "prompt"),
            P("prompt", "sample", None),
            P("prompt", "sample", None),
            P("prompt", "sample", None, None, None),
            P("prompt", "sample", None, None, None),
            P("prompt"),
            P("prompt", "sample"),
            P("prompt", "sample"),
            P("prompt", "sample", None),
        ),
        out_specs=(P("prompt", "sample", None), P("prompt", "sample", None)),
        check_vma=False,
    )
```

```python
import functools
import math

import jax
import jax.numpy as jnp
from jax import lax
from jax.experimental import pallas as pl
from jax.experimental.pallas import tpu as pltpu
from jax.sharding import PartitionSpec as P

QUERY_HEADS = 64
GROUPS = 8
HEADS = 8
HEAD_SIZE = 128
PAGE = 128
SAMPLES = 16
CMAX = 16
ROWS = 256
SLICE = 512
COLUMNS = 256
KVW = 2048
KEYS = GROUPS * HEAD_SIZE
PACK = QUERY_HEADS + HEADS
SENT = QUERY_HEADS + 16
LOW = -1e30
SCALE = 1.0 / math.sqrt(HEAD_SIZE)
MIB = 1 << 20
F32 = jnp.float32
BF16 = jnp.bfloat16

X_RIGHT = [(z * 4 + x, z * 4 + (x + 1) % 4) for z in range(4) for x in range(4)]
X_LEFT = [(z * 4 + x, z * 4 + (x + 3) % 4) for z in range(4) for x in range(4)]
X_FAR = [(z * 4 + x, z * 4 + (x + 2) % 4) for z in range(4) for x in range(4)]
Z_UP = [(z * 4 + x, (z + 1) % 4 * 4 + x) for z in range(4) for x in range(4)]
Z_DOWN = [(z * 4 + x, (z + 3) % 4 * 4 + x) for z in range(4) for x in range(4)]
Z_FAR = [(z * 4 + x, (z + 2) % 4 * 4 + x) for z in range(4) for x in range(4)]
SWAP = [(y * 2 + c, y * 2 + 1 - c) for y in range(4) for c in range(2)]
Y_SPLIT = [(y * 2 + c, (y + (1 if c == 0 else 3)) % 4 * 2 + c) for y in range(4) for c in range(2)]


def params(mib):
    return pltpu.CompilerParams(vmem_limit_bytes=mib * MIB)


def cost(flops, bytes_accessed):
    return pl.CostEstimate(flops=flops, bytes_accessed=bytes_accessed, transcendentals=0)


def nt_dot(a, b):
    return lax.dot_general(a, b, (((1,), (1,)), ((), ())), preferred_element_type=F32)


def put_lane(running, lane, column):
    at = lax.broadcasted_iota(jnp.int32, running.shape, len(running.shape) - 1)
    return jnp.where(at == lane, column, running)


HALF = QUERY_HEADS // 2
BLOCK = HALF + 8


def prepare_kernel(where, length, flag, query, sent, own):
    heads = [query[0, 0:1, h * HEAD_SIZE : (h + 1) * HEAD_SIZE].astype(F32) for h in range(QUERY_HEADS)]
    low, high = jnp.concatenate(heads[:HALF]), jnp.concatenate(heads[HALF:])
    own[:HALF] = low.astype(BF16)
    own[HALF:] = high.astype(BF16)
    sent[:HALF, :HEAD_SIZE] = low.astype(BF16)
    sent[:HALF, HEAD_SIZE:] = high.astype(BF16)
    plan = jnp.zeros((8, COLUMNS), F32)
    for c in range(CMAX):
        plan = put_lane(plan, c, where[0, 0, c].astype(F32))
    plan = put_lane(plan, CMAX, length[0, 0].astype(F32))
    plan = put_lane(plan, CMAX + 1, flag[0, 0].astype(F32))
    sent[HALF:] = plan.astype(BF16)


def prepare(query, where, length, flag):
    smem, vmem = pl.BlockSpec(memory_space=pltpu.SMEM), pl.BlockSpec(memory_space=pltpu.VMEM)
    return pl.pallas_call(
        prepare_kernel,
        out_shape=[
            jax.ShapeDtypeStruct((BLOCK, COLUMNS), BF16),
            jax.ShapeDtypeStruct((QUERY_HEADS, HEAD_SIZE), BF16),
        ],
        in_specs=[smem] * 3 + [vmem],
        out_specs=[vmem, vmem],
        compiler_params=params(16),
        cost_estimate=cost(1000, 1000),
        name="prepare",
    )(where, length, flag, query)


def unpack_kernel(*refs):
    arrived, (queries, by_group, slots, alive) = refs[:4], refs[4:]
    me = lax.axis_index("sample")

    def block_of(r):
        return arrived[r // 4][r % 4].astype(F32)

    plans = []
    for r in range(SAMPLES):
        block = block_of(r)
        for half in range(2):
            lanes = slice(half * HEAD_SIZE, (half + 1) * HEAD_SIZE)
            queries[r, half * HALF : (half + 1) * HALF] = block[:HALF, lanes].astype(BF16)
        plans.append(block[HALF : HALF + 1])
    for g in range(GROUPS):
        lanes = slice(g // 4 * HEAD_SIZE, (g // 4 + 1) * HEAD_SIZE)
        rows = slice(g % 4 * HEADS, (g % 4 + 1) * HEADS)
        parts = [block_of(r)[rows, lanes] for r in range(SAMPLES)]
        by_group[g] = jnp.concatenate(parts).astype(BF16)
    plan = jnp.concatenate(plans)
    lane = lax.broadcasted_iota(jnp.int32, plan.shape, 1)
    first = (me * CMAX).astype(F32)
    here = (lane < CMAX) & (plan >= first) & (plan < first + CMAX)
    live = here & (lane.astype(F32) < plan[:, CMAX : CMAX + 1]) & (plan[:, CMAX + 1 : CMAX + 2] > 0.5)
    slot = jnp.sum(jnp.where(here, plan - first, 0.0), axis=1, keepdims=True).astype(jnp.int32)
    some = jnp.max(jnp.where(live, 1.0, 0.0), axis=1, keepdims=True).astype(jnp.int32)
    for r in range(SAMPLES):
        slots[r] = slot[r, 0]
        alive[r] = some[r, 0]


def unpack(arrived):
    smem, vmem = pl.BlockSpec(memory_space=pltpu.SMEM), pl.BlockSpec(memory_space=pltpu.VMEM)
    return pl.pallas_call(
        unpack_kernel,
        out_shape=[
            jax.ShapeDtypeStruct((SAMPLES, QUERY_HEADS, HEAD_SIZE), BF16),
            jax.ShapeDtypeStruct((GROUPS, SAMPLES * HEADS, HEAD_SIZE), BF16),
            jax.ShapeDtypeStruct((SAMPLES,), jnp.int32),
            jax.ShapeDtypeStruct((SAMPLES,), jnp.int32),
        ],
        in_specs=[vmem] * 4,
        out_specs=[vmem, vmem, smem, smem],
        compiler_params=params(16),
        cost_estimate=cost(1000, 1000),
        name="unpack",
    )(*arrived)


STEPS = (0, 1, 3, 2)


def pick_kernel(states, *refs):
    outs, sems = refs[:8], refs[8]
    me = lax.axis_index("sample")
    z, x = me // 4, lax.rem(me, 4)
    copies = []
    for i, step in enumerate(STEPS):
        column = lax.rem(x + step, 4)
        for k, up in enumerate((2, 1, 3)):
            copies.append((states.at[lax.rem(z + up, 4), column], outs[i].at[k]))
        copies.append((states.at[z, column], outs[4 + i]))
    copies = [pltpu.make_async_copy(src, dst, sems.at[n]) for n, (src, dst) in enumerate(copies)]
    for copy in copies:
        copy.start()
    for copy in copies:
        copy.wait()


def pick(states):
    return pl.pallas_call(
        pick_kernel,
        out_shape=[jax.ShapeDtypeStruct((3, ROWS, SLICE), BF16)] * 4
        + [jax.ShapeDtypeStruct((ROWS, SLICE), BF16)] * 4,
        in_specs=[pl.BlockSpec(memory_space=pl.ANY)],
        out_specs=[pl.BlockSpec(memory_space=pltpu.VMEM)] * 8,
        scratch_shapes=[pltpu.SemaphoreType.DMA((16,))],
        compiler_params=params(50),
        cost_estimate=cost(1000, 1000),
        name="pick_rows",
    )(states)


def product_kernel(blocks, *refs):
    states, pieces, outs = refs[:4], refs[4:12], refs[12:]
    for j in range(8):
        for k, block in enumerate(blocks):
            total = jnp.zeros((ROWS, COLUMNS), F32)
            for d in range(4):
                left = states[d][...] if block is None else states[d][block]
                total += jnp.dot(left, pieces[j][d], preferred_element_type=F32)
            out = outs[k]
            out[:, j * COLUMNS : (j + 1) * COLUMNS] = total.astype(out.dtype)


def product(states, pieces, blocks, kind, name):
    vmem = pl.BlockSpec(memory_space=pltpu.VMEM)
    outs = [jax.ShapeDtypeStruct((ROWS, KVW), kind)] * len(blocks)
    return pl.pallas_call(
        functools.partial(product_kernel, blocks),
        out_shape=outs,
        in_specs=[vmem] * 12,
        out_specs=[vmem] * len(outs),
        compiler_params=params(20),
        cost_estimate=cost(1000, 1000),
        name=name,
    )(*states, *pieces)


def product_far_kernel(*refs):
    states, pieces, outs = refs[:4], refs[4:12], refs[12:]
    for j in range(8):
        total = jnp.zeros((ROWS, COLUMNS), F32)
        for d in range(4):
            total += jnp.dot(states[d][0], pieces[j][d], preferred_element_type=F32)
        outs[j // 4][:, (j % 4) * COLUMNS : (j % 4 + 1) * COLUMNS] = total.astype(BF16)


def product_far(states, pieces):
    vmem = pl.BlockSpec(memory_space=pltpu.VMEM)
    return pl.pallas_call(
        product_far_kernel,
        out_shape=[jax.ShapeDtypeStruct((ROWS, KVW // 2), BF16)] * 2,
        in_specs=[vmem] * 12,
        out_specs=[vmem] * 2,
        compiler_params=params(20),
        cost_estimate=cost(1000, 1000),
        name="product_far",
    )(*states, *pieces)


def relay_kernel(up, down, from_down, from_up, up_out, down_out):
    half = KVW // 2
    up_out[:, :half] = (up[:, :half].astype(F32) + from_down[...].astype(F32)).astype(BF16)
    up_out[:, half:] = up[:, half:]
    down_out[:, half:] = (down[:, half:].astype(F32) + from_up[...].astype(F32)).astype(BF16)
    down_out[:, :half] = down[:, :half]


def relay(up, down, from_down, from_up):
    vmem = pl.BlockSpec(memory_space=pltpu.VMEM)
    return pl.pallas_call(
        relay_kernel,
        out_shape=[jax.ShapeDtypeStruct((ROWS, KVW), BF16)] * 2,
        in_specs=[vmem] * 4,
        out_specs=[vmem] * 2,
        compiler_params=params(20),
        cost_estimate=cost(1000, 1000),
        name="relay_sums",
    )(up, down, from_down, from_up)


def log_rows(logs):
    out = jnp.full((HEADS, HEAD_SIZE), LOW, F32)
    for g in range(GROUPS):
        out = put_lane(out, g, logs[g * HEADS : (g + 1) * HEADS])
    return out


POOL_PAGES = 4


def page_kernel(slots, alive, query, *refs):
    pages, out = refs[:POOL_PAGES], refs[POOL_PAGES]
    step = pl.program_id(0)
    scores = []
    for k in range(POOL_PAGES):
        for g in range(GROUPS):
            keys = pages[k][0, :, g * HEAD_SIZE : (g + 1) * HEAD_SIZE]
            scores.append(nt_dot(query[k, g * HEADS : (g + 1) * HEADS], keys))
    scores = jnp.concatenate(scores) * SCALE
    top = jnp.max(scores, axis=-1, keepdims=True)
    exponent = jnp.exp(scores - top)
    total = jnp.sum(exponent, axis=-1, keepdims=True)
    logs, share = top + jnp.log(total), 1.0 / total
    for k in range(POOL_PAGES):
        live = alive[step * POOL_PAGES + k] != 0
        for g in range(GROUPS):
            rows = slice(k * QUERY_HEADS + g * HEADS, k * QUERY_HEADS + (g + 1) * HEADS)
            values = pages[k][0, :, KEYS + g * HEAD_SIZE : KEYS + (g + 1) * HEAD_SIZE]
            mixture = jnp.dot(exponent[rows].astype(BF16), values, preferred_element_type=F32)
            out[k, g * HEADS : (g + 1) * HEADS] = jnp.where(live, mixture * share[rows], 0.0)
        mine = log_rows(logs[k * QUERY_HEADS : (k + 1) * QUERY_HEADS])
        out[k, QUERY_HEADS:] = jnp.where(live, mine, LOW)


def pool_attention(slots, alive, queries_all, pool):
    def page_of(k):
        return lambda s, slots, alive: (slots[s * POOL_PAGES + k], 0, 0)

    return pl.pallas_call(
        page_kernel,
        out_shape=jax.ShapeDtypeStruct((SAMPLES, PACK, HEAD_SIZE), F32),
        grid_spec=pltpu.PrefetchScalarGridSpec(
            num_scalar_prefetch=2,
            grid=(SAMPLES // POOL_PAGES,),
            in_specs=[
                pl.BlockSpec(
                    (POOL_PAGES, QUERY_HEADS, HEAD_SIZE), lambda s, slots, alive: (s, 0, 0)
                )
            ]
            + [pl.BlockSpec((1, PAGE, KVW), page_of(k)) for k in range(POOL_PAGES)],
            out_specs=pl.BlockSpec(
                (POOL_PAGES, PACK, HEAD_SIZE), lambda s, slots, alive: (s, 0, 0)
            ),
        ),
        compiler_params=params(16),
        cost_estimate=cost(1000, 1000),
        name="pool_attention",
    )(slots, alive, queries_all, *[pool] * POOL_PAGES)


LOCAL_PAGES = 4


def local_kernel(pages_alive, query, new, pages, out, top_ref, sum_ref, mix_ref):
    step = pl.program_id(0)
    width = LOCAL_PAGES * PAGE

    @pl.when(step == 0)
    def _():
        for g in range(GROUPS):
            rows = slice(g * HEADS, (g + 1) * HEADS)
            lanes = slice(g * HEAD_SIZE, (g + 1) * HEAD_SIZE)
            value_lanes = slice(KEYS + g * HEAD_SIZE, KEYS + (g + 1) * HEAD_SIZE)
            products = query[rows].astype(F32) * new[0:1, lanes].astype(F32)
            top_ref[rows] = jnp.sum(products, axis=-1, keepdims=True) * SCALE
            sum_ref[rows] = jnp.ones((HEADS, 1), F32)
            mix_ref[rows] = jnp.broadcast_to(new[0:1, value_lanes].astype(F32), (HEADS, HEAD_SIZE))

    @pl.when(step * LOCAL_PAGES < pages_alive[0])
    def _():
        block = pages.reshape(width, KVW)
        at = step * width + lax.broadcasted_iota(jnp.int32, (QUERY_HEADS, width), 1)
        live = at < pages_alive[0] * PAGE
        scores = jnp.concatenate(
            [
                nt_dot(
                    query[g * HEADS : (g + 1) * HEADS],
                    block[:, g * HEAD_SIZE : (g + 1) * HEAD_SIZE],
                )
                for g in range(GROUPS)
            ]
        )
        scores = jnp.where(live, scores * SCALE, LOW)
        old = top_ref[...]
        top = jnp.maximum(old, jnp.max(scores, axis=-1, keepdims=True))
        shrink = jnp.exp(old - top)
        exponent = jnp.where(live, jnp.exp(scores - top), 0.0)
        top_ref[...] = top
        sum_ref[...] = sum_ref[...] * shrink + jnp.sum(exponent, axis=-1, keepdims=True)
        for g in range(GROUPS):
            rows = slice(g * HEADS, (g + 1) * HEADS)
            values = block[:, KEYS + g * HEAD_SIZE : KEYS + (g + 1) * HEAD_SIZE]
            mix_ref[rows] = mix_ref[rows] * shrink[rows] + jnp.dot(
                exponent[rows].astype(BF16), values, preferred_element_type=F32
            )

    @pl.when(step == CMAX // LOCAL_PAGES - 1)
    def _():
        out[:QUERY_HEADS] = mix_ref[...] / sum_ref[...]
        out[QUERY_HEADS:] = log_rows(top_ref[...] + jnp.log(sum_ref[...]))


def local_attention(pages_alive, query, new, pages):
    def block_of(step, alive):
        last = jnp.maximum(alive[0] - 1, 0) // LOCAL_PAGES
        return (jnp.minimum(step, last), 0, 0)

    return pl.pallas_call(
        local_kernel,
        out_shape=jax.ShapeDtypeStruct((PACK, HEAD_SIZE), F32),
        grid_spec=pltpu.PrefetchScalarGridSpec(
            num_scalar_prefetch=1,
            grid=(CMAX // LOCAL_PAGES,),
            in_specs=[
                pl.BlockSpec((QUERY_HEADS, HEAD_SIZE), lambda step, alive: (0, 0)),
                pl.BlockSpec((1, KVW), lambda step, alive: (0, 0)),
                pl.BlockSpec((LOCAL_PAGES, PAGE, KVW), block_of),
            ],
            out_specs=pl.BlockSpec((PACK, HEAD_SIZE), lambda step, alive: (0, 0)),
            scratch_shapes=[
                pltpu.VMEM((QUERY_HEADS, 1), F32),
                pltpu.VMEM((QUERY_HEADS, 1), F32),
                pltpu.VMEM((QUERY_HEADS, HEAD_SIZE), F32),
            ],
        ),
        compiler_params=params(16),
        cost_estimate=cost(1000, 1000),
        name="local_attention",
    )(pages_alive, query, new, pages)


def prefix_kernel(
    prompt_pages, own, up, down, queries, pool, cache, packed
):
    me, prompt = lax.axis_index("sample"), lax.axis_index("prompt")
    z, x = me // 4, lax.rem(me, 4)
    y, core = prompt // 2, lax.rem(prompt, 2)
    near = lax.rem(y + 3 - 2 * core, 4)
    other = lax.rem(y + 1 + 2 * core, 4)
    far = lax.rem(y + 2, 4)
    columns = (
        2 * y + core, 2 * y + 1 - core, 2 * near + core, 2 * near + 1 - core,
        2 * other + 1 - core, 2 * other + core, 2 * far + core, 2 * far + 1 - core,
    )
    for j in range(8):
        lanes = slice(j * COLUMNS, (j + 1) * COLUMNS)
        total = own[:, lanes] + up[:, lanes].astype(F32) + down[:, lanes].astype(F32)
        target = pl.ds(pl.multiple_of(columns[j] * COLUMNS, COLUMNS), COLUMNS)
        cache[0, :, target] = total.astype(BF16)
    sources = [
        lax.rem(z + 4 - dz, 4) * 4 + lax.rem(x + 4 - dx, 4) for dx in STEPS for dz in STEPS
    ]
    live = lax.broadcasted_iota(jnp.int32, (SAMPLES * HEADS, ROWS), 1) < prompt_pages[0] * PAGE - me * ROWS
    logs = jnp.full((SAMPLES * HEADS, HEAD_SIZE), LOW, F32)
    for g in range(GROUPS):
        keys = cache[0, :, g * HEAD_SIZE : (g + 1) * HEAD_SIZE]
        values = cache[0, :, KEYS + g * HEAD_SIZE : KEYS + (g + 1) * HEAD_SIZE]
        scores = jnp.where(live, nt_dot(queries[g], keys) * SCALE, LOW)
        top = jnp.max(scores, axis=-1, keepdims=True)
        exponent = jnp.where(live, jnp.exp(scores - top), 0.0)
        total = jnp.sum(exponent, axis=-1, keepdims=True)
        mixture = jnp.dot(exponent.astype(BF16), values, preferred_element_type=F32)
        some = total > 0.0
        total = jnp.where(some, total, 1.0)
        log = jnp.where(some, top + jnp.log(total), LOW)
        rows = slice(g * HEADS, (g + 1) * HEADS)
        pool_log = pool[:, QUERY_HEADS:, g : g + 1].reshape(SAMPLES * HEADS, 1)
        pool_mixture = pool[:, rows].reshape(SAMPLES * HEADS, HEAD_SIZE)
        high = jnp.maximum(log, pool_log)
        here, there = jnp.exp(log - high), jnp.exp(pool_log - high)
        both = here + there
        merged = mixture * (here / (total * both)) + pool_mixture * (there / both)
        for r, source in enumerate(sources):
            packed[source, rows] = merged[r * HEADS : (r + 1) * HEADS].astype(BF16)
        logs = put_lane(logs, g, high + jnp.log(both))
    first = logs.astype(BF16).astype(F32)
    second = (logs - first).astype(BF16).astype(F32)
    third = logs - first - second
    terms = jnp.zeros((SAMPLES * HEADS, HEAD_SIZE), F32)
    for g in range(GROUPS):
        for t, term in enumerate((first, second, third)):
            terms = put_lane(terms, t * GROUPS + g, term[:, g : g + 1])
    padding = jnp.zeros((SENT - QUERY_HEADS - HEADS, HEAD_SIZE), F32)
    for r, source in enumerate(sources):
        rows = jnp.concatenate([terms[r * HEADS : (r + 1) * HEADS], padding])
        packed[source, QUERY_HEADS:] = rows.astype(BF16)


def prefix_attention(prompt_pages, parts, queries, pool):
    smem, vmem = pl.BlockSpec(memory_space=pltpu.SMEM), pl.BlockSpec(memory_space=pltpu.VMEM)
    return pl.pallas_call(
        prefix_kernel,
        out_shape=[
            jax.ShapeDtypeStruct((1, ROWS, KVW), BF16),
            jax.ShapeDtypeStruct((SAMPLES, SENT, HEAD_SIZE), BF16),
        ],
        in_specs=[smem] + [vmem] * 5,
        out_specs=[vmem, vmem],
        compiler_params=params(20),
        cost_estimate=cost(300_000_000, 6 * MIB),
        name="prefix_attention",
    )(prompt_pages, *parts, queries, pool)


def combine_kernel(arrived, local, out):
    terms = arrived[:, QUERY_HEADS:].astype(F32)
    for g in range(GROUPS):
        rows = slice(g * HEADS, (g + 1) * HEADS)
        logs = sum(terms[:, :HEADS, lane : lane + 1] for lane in (g, g + GROUPS, g + 2 * GROUPS))
        local_log = local[QUERY_HEADS:, g : g + 1]
        high = jnp.maximum(jnp.max(logs, axis=0), local_log)
        shares = jnp.exp(logs - high[None])
        local_share = jnp.exp(local_log - high)
        total = jnp.sum(shares, axis=0) + local_share
        mixture = jnp.sum(arrived[:, rows].astype(F32) * shares, axis=0) + local[rows] * local_share
        out[rows] = (mixture / total).astype(BF16)


def combine(arrived, local):
    vmem = pl.BlockSpec(memory_space=pltpu.VMEM)
    return pl.pallas_call(
        combine_kernel,
        out_shape=jax.ShapeDtypeStruct((QUERY_HEADS, HEAD_SIZE), BF16),
        in_specs=[vmem, vmem],
        out_specs=vmem,
        compiler_params=params(16),
        cost_estimate=cost(1_000_000, MIB),
        name="combine",
    )(arrived, local)


def per_device(
    prompt_states,
    kv_weight,
    queries,
    new_kv,
    local_pages,
    pool_pages,
    prompt_pages,
    comp_pages,
    preempted,
    page_where,
):
    tie = lax.optimization_barrier

    weight_far = lax.ppermute(kv_weight, "sample", X_FAR)
    weight_right = lax.ppermute(kv_weight, "sample", X_RIGHT)
    weight_left = lax.ppermute(kv_weight, "sample", X_LEFT)
    block, query = prepare(queries, page_where, comp_pages, preempted)
    blocks = [block] + [lax.ppermute(block, "sample", to) for to in (Z_UP, Z_DOWN, Z_FAR)]
    states = prompt_states.reshape(4, 4, ROWS, SLICE)
    picked = pick(states)
    slices, picked = tie(((kv_weight, weight_right, weight_left, weight_far), picked))
    others, to_right, to_left, to_far = picked[:4]
    rows_far = lax.ppermute(to_far, "sample", X_FAR)
    to_right, to_left, rows_far, blocks = tie((to_right, to_left, rows_far, blocks))
    rows_right = lax.ppermute(to_right, "sample", X_RIGHT)
    rows_left = lax.ppermute(to_left, "sample", X_LEFT)
    of_column = jnp.stack(blocks)
    everyone = [of_column] + [
        lax.ppermute(of_column, "sample", to) for to in (X_RIGHT, X_LEFT, X_FAR)
    ]

    here = jnp.stack(slices)
    near = lax.ppermute(here, "prompt", Y_SPLIT)
    here_other = lax.ppermute(here, "prompt", SWAP)
    near_other = lax.ppermute(here_other, "prompt", Y_SPLIT)
    far = lax.ppermute(near, "prompt", Y_SPLIT)
    near_swapped = lax.ppermute(near, "prompt", SWAP)
    near_other_swapped = lax.ppermute(near_other, "prompt", SWAP)
    far, rows_right, rows_left, everyone = tie((far, rows_right, rows_left, everyone))
    far_other = lax.ppermute(far, "prompt", SWAP)
    others = [others, rows_right, rows_left, rows_far]
    pieces = [
        here, here_other, near, near_other,
        near_swapped, near_other_swapped, far, far_other,
    ]

    far_l, far_r = product_far(others, pieces)
    mine, to_right, to_left, to_far = picked[4:]
    to_right, to_left, to_far, far_l, far_r = tie((to_right, to_left, to_far, far_l, far_r))
    mine = [
        mine,
        lax.ppermute(to_right, "sample", X_RIGHT),
        lax.ppermute(to_left, "sample", X_LEFT),
        lax.ppermute(to_far, "sample", X_FAR),
    ]
    from_down = lax.ppermute(far_l, "sample", Z_UP)
    from_up = lax.ppermute(far_r, "sample", Z_DOWN)
    up, down = product(others, pieces, (1, 2), BF16, "product_near")
    up, down = relay(up, down, from_down, from_up)
    sums = [lax.ppermute(up, "sample", Z_UP), lax.ppermute(down, "sample", Z_DOWN)]

    everyone, query, up = tie((everyone, query, up))
    queries_all, by_group, slots, alive = unpack(everyone)
    pool = pool_attention(slots, alive, queries_all, pool_pages[0, 0])
    local_alive = jnp.where(preempted[0] > 0, 0, comp_pages[0])
    local = local_attention(local_alive, query, new_kv[0], local_pages[0, 0])
    mine, pool, local = tie((mine, pool, local))
    (own,) = product(mine, pieces, (None,), F32, "product_own")
    sums = [own, *sums]

    cache, packed = prefix_attention(prompt_pages, sums, by_group, pool)
    arrived = lax.all_to_all(packed, "sample", split_axis=0, concat_axis=0, tiled=True)
    attended = combine(arrived, local)
    return (cache, attended.reshape(1, 1, -1))


def solution(mesh):
    return jax.shard_map(
        per_device,
        mesh=mesh,
        in_specs=(
            P("prompt", None, "sample"),
            P("sample", "prompt"),
            P("prompt", "sample", None),
            P("prompt", "sample", None),
            P("prompt", "sample", None, None, None),
            P("prompt", "sample", None, None, None),
            P("prompt"),
            P("prompt", "sample"),
            P("prompt", "sample"),
            P("prompt", "sample", None),
        ),
        out_specs=(P("prompt", "sample", None), P("prompt", "sample", None)),
        check_vma=False,
    )
```

```python
import functools
import math

import jax
import jax.numpy as jnp
from jax import lax
from jax.experimental import pallas as pl
from jax.experimental.pallas import tpu as pltpu
from jax.sharding import PartitionSpec as P

QUERY_HEADS = 64
GROUPS = 8
HEADS = 8
HEAD_SIZE = 128
PAGE = 128
SAMPLES = 16
CMAX = 16
ROWS = 256
SLICE = 512
COLUMNS = 256
KVW = 2048
KEYS = GROUPS * HEAD_SIZE
PACK = QUERY_HEADS + HEADS
SENT = QUERY_HEADS + 16
LOW = -1e30
SCALE = 1.0 / math.sqrt(HEAD_SIZE)
MIB = 1 << 20
F32 = jnp.float32
BF16 = jnp.bfloat16

X_RIGHT = [(z * 4 + x, z * 4 + (x + 1) % 4) for z in range(4) for x in range(4)]
X_LEFT = [(z * 4 + x, z * 4 + (x + 3) % 4) for z in range(4) for x in range(4)]
X_FAR = [(z * 4 + x, z * 4 + (x + 2) % 4) for z in range(4) for x in range(4)]
Z_UP = [(z * 4 + x, (z + 1) % 4 * 4 + x) for z in range(4) for x in range(4)]
Z_DOWN = [(z * 4 + x, (z + 3) % 4 * 4 + x) for z in range(4) for x in range(4)]
Z_FAR = [(z * 4 + x, (z + 2) % 4 * 4 + x) for z in range(4) for x in range(4)]
SWAP = [(y * 2 + c, y * 2 + 1 - c) for y in range(4) for c in range(2)]
Y_SPLIT = [(y * 2 + c, (y + (1 if c == 0 else 3)) % 4 * 2 + c) for y in range(4) for c in range(2)]


def params(mib):
    return pltpu.CompilerParams(vmem_limit_bytes=mib * MIB)


def cost(flops, bytes_accessed):
    return pl.CostEstimate(flops=flops, bytes_accessed=bytes_accessed, transcendentals=0)


def nt_dot(a, b):
    return lax.dot_general(a, b, (((1,), (1,)), ((), ())), preferred_element_type=F32)


def put_lane(running, lane, column):
    at = lax.broadcasted_iota(jnp.int32, running.shape, len(running.shape) - 1)
    return jnp.where(at == lane, column, running)


HALF = QUERY_HEADS // 2
BLOCK = HALF + 8


def prepare_kernel(where, length, flag, query, sent, own):
    heads = [query[0, 0:1, h * HEAD_SIZE : (h + 1) * HEAD_SIZE].astype(F32) for h in range(QUERY_HEADS)]
    low, high = jnp.concatenate(heads[:HALF]), jnp.concatenate(heads[HALF:])
    own[:HALF] = low.astype(BF16)
    own[HALF:] = high.astype(BF16)
    sent[:HALF, :HEAD_SIZE] = low.astype(BF16)
    sent[:HALF, HEAD_SIZE:] = high.astype(BF16)
    plan = jnp.zeros((8, COLUMNS), F32)
    for c in range(CMAX):
        plan = put_lane(plan, c, where[0, 0, c].astype(F32))
    plan = put_lane(plan, CMAX, length[0, 0].astype(F32))
    plan = put_lane(plan, CMAX + 1, flag[0, 0].astype(F32))
    sent[HALF:] = plan.astype(BF16)


def prepare(query, where, length, flag):
    smem, vmem = pl.BlockSpec(memory_space=pltpu.SMEM), pl.BlockSpec(memory_space=pltpu.VMEM)
    return pl.pallas_call(
        prepare_kernel,
        out_shape=[
            jax.ShapeDtypeStruct((BLOCK, COLUMNS), BF16),
            jax.ShapeDtypeStruct((QUERY_HEADS, HEAD_SIZE), BF16),
        ],
        in_specs=[smem] * 3 + [vmem],
        out_specs=[vmem, vmem],
        compiler_params=params(16),
        cost_estimate=cost(1000, 1000),
        name="prepare",
    )(where, length, flag, query)


def unpack_kernel(*refs):
    arrived, (queries, by_group, slots, alive) = refs[:4], refs[4:]
    me = lax.axis_index("sample")

    def block_of(r):
        rows = slice(3 * ROWS + r % 4 // 2 * BLOCK, 3 * ROWS + (r % 4 // 2 + 1) * BLOCK)
        lanes = slice(r % 2 * COLUMNS, (r % 2 + 1) * COLUMNS)
        return arrived[r // 4][rows, lanes].astype(F32)

    plans = []
    for r in range(SAMPLES):
        block = block_of(r)
        for half in range(2):
            lanes = slice(half * HEAD_SIZE, (half + 1) * HEAD_SIZE)
            queries[r, half * HALF : (half + 1) * HALF] = block[:HALF, lanes].astype(BF16)
        plans.append(block[HALF : HALF + 1])
    for g in range(GROUPS):
        lanes = slice(g // 4 * HEAD_SIZE, (g // 4 + 1) * HEAD_SIZE)
        rows = slice(g % 4 * HEADS, (g % 4 + 1) * HEADS)
        parts = [block_of(r)[rows, lanes] for r in range(SAMPLES)]
        by_group[g] = jnp.concatenate(parts).astype(BF16)
    plan = jnp.concatenate(plans)
    lane = lax.broadcasted_iota(jnp.int32, plan.shape, 1)
    first = (me * CMAX).astype(F32)
    here = (lane < CMAX) & (plan >= first) & (plan < first + CMAX)
    live = here & (lane.astype(F32) < plan[:, CMAX : CMAX + 1]) & (plan[:, CMAX + 1 : CMAX + 2] > 0.5)
    slot = jnp.sum(jnp.where(here, plan - first, 0.0), axis=1, keepdims=True).astype(jnp.int32)
    some = jnp.max(jnp.where(live, 1.0, 0.0), axis=1, keepdims=True).astype(jnp.int32)
    for r in range(SAMPLES):
        slots[r] = slot[r, 0]
        alive[r] = some[r, 0]


def unpack(arrived):
    smem, vmem = pl.BlockSpec(memory_space=pltpu.SMEM), pl.BlockSpec(memory_space=pltpu.VMEM)
    return pl.pallas_call(
        unpack_kernel,
        out_shape=[
            jax.ShapeDtypeStruct((SAMPLES, QUERY_HEADS, HEAD_SIZE), BF16),
            jax.ShapeDtypeStruct((GROUPS, SAMPLES * HEADS, HEAD_SIZE), BF16),
            jax.ShapeDtypeStruct((SAMPLES,), jnp.int32),
            jax.ShapeDtypeStruct((SAMPLES,), jnp.int32),
        ],
        in_specs=[vmem] * 4,
        out_specs=[vmem, vmem, smem, smem],
        compiler_params=params(16),
        cost_estimate=cost(1000, 1000),
        name="unpack",
    )(*arrived)


STEPS = (0, 1, 3, 2)


def pick_kernel(states, *refs):
    blocks, outs, sems = refs[:4], refs[4:12], refs[12]
    me = lax.axis_index("sample")
    z, x = me // 4, lax.rem(me, 4)
    copies = []
    for i, step in enumerate(STEPS):
        column = lax.rem(x + step, 4)
        for k, up in enumerate((2, 1, 3)):
            copies.append((states.at[lax.rem(z + up, 4), column], outs[i].at[pl.ds(k * ROWS, ROWS)]))
        copies.append((states.at[z, column], outs[4 + i]))
    copies = [pltpu.make_async_copy(src, dst, sems.at[n]) for n, (src, dst) in enumerate(copies)]
    for copy in copies:
        copy.start()
    for out in outs[:4]:
        for r, block in enumerate(blocks):
            rows = slice(3 * ROWS + r // 2 * BLOCK, 3 * ROWS + (r // 2 + 1) * BLOCK)
            out[rows, r % 2 * COLUMNS : (r % 2 + 1) * COLUMNS] = block[...]
    for copy in copies:
        copy.wait()


def pick(states, blocks):
    return pl.pallas_call(
        pick_kernel,
        out_shape=[jax.ShapeDtypeStruct((3 * ROWS + 2 * BLOCK, SLICE), BF16)] * 4
        + [jax.ShapeDtypeStruct((ROWS, SLICE), BF16)] * 4,
        in_specs=[pl.BlockSpec(memory_space=pl.ANY)] + [pl.BlockSpec(memory_space=pltpu.VMEM)] * 4,
        out_specs=[pl.BlockSpec(memory_space=pltpu.VMEM)] * 8,
        scratch_shapes=[pltpu.SemaphoreType.DMA((16,))],
        compiler_params=params(50),
        cost_estimate=cost(1000, 1000),
        name="pick_rows",
    )(states, *blocks)


def product_kernel(blocks, *refs):
    states, pieces, outs = refs[:4], refs[4:12], refs[12:]
    for j in range(8):
        for k, block in enumerate(blocks):
            total = jnp.zeros((ROWS, COLUMNS), F32)
            for d in range(4):
                left = states[d][...] if block is None else states[d][block * ROWS : (block + 1) * ROWS]
                total += jnp.dot(left, pieces[j][d], preferred_element_type=F32)
            out = outs[2 * k + j // 4]
            out[:, (j % 4) * COLUMNS : (j % 4 + 1) * COLUMNS] = total.astype(out.dtype)


def product(states, pieces, blocks, kind, name):
    vmem = pl.BlockSpec(memory_space=pltpu.VMEM)
    outs = [jax.ShapeDtypeStruct((ROWS, KVW // 2), kind)] * (2 * len(blocks))
    return pl.pallas_call(
        functools.partial(product_kernel, blocks),
        out_shape=outs,
        in_specs=[vmem] * 12,
        out_specs=[vmem] * len(outs),
        compiler_params=params(20),
        cost_estimate=cost(1000, 1000),
        name=name,
    )(*states, *pieces)


def product_far_kernel(*refs):
    states, pieces, outs = refs[:4], refs[4:12], refs[12:]
    for j in range(8):
        total = jnp.zeros((ROWS, COLUMNS), F32)
        for d in range(4):
            total += jnp.dot(states[d][:ROWS], pieces[j][d], preferred_element_type=F32)
        outs[j // 4][:, (j % 4) * COLUMNS : (j % 4 + 1) * COLUMNS] = total.astype(BF16)


def product_far(states, pieces):
    vmem = pl.BlockSpec(memory_space=pltpu.VMEM)
    return pl.pallas_call(
        product_far_kernel,
        out_shape=[jax.ShapeDtypeStruct((ROWS, KVW // 2), BF16)] * 2,
        in_specs=[vmem] * 12,
        out_specs=[vmem] * 2,
        compiler_params=params(20),
        cost_estimate=cost(1000, 1000),
        name="product_far",
    )(*states, *pieces)


def relay_kernel(up, down, from_down, from_up, up_out, down_out):
    up_out[...] = (up[...].astype(F32) + from_down[...].astype(F32)).astype(BF16)
    down_out[...] = (down[...].astype(F32) + from_up[...].astype(F32)).astype(BF16)


def relay(up, down, from_down, from_up):
    vmem = pl.BlockSpec(memory_space=pltpu.VMEM)
    return pl.pallas_call(
        relay_kernel,
        out_shape=[jax.ShapeDtypeStruct((ROWS, KVW // 2), BF16)] * 2,
        in_specs=[vmem] * 4,
        out_specs=[vmem] * 2,
        compiler_params=params(16),
        cost_estimate=cost(1000, 1000),
        name="relay_sums",
    )(up, down, from_down, from_up)


def log_rows(logs):
    out = jnp.full((HEADS, HEAD_SIZE), LOW, F32)
    for g in range(GROUPS):
        out = put_lane(out, g, logs[g * HEADS : (g + 1) * HEADS])
    return out


POOL_PAGES = 4


def page_kernel(slots, alive, query, *refs):
    pages, out = refs[:POOL_PAGES], refs[POOL_PAGES]
    step = pl.program_id(0)
    scores = []
    for k in range(POOL_PAGES):
        for g in range(GROUPS):
            keys = pages[k][0, :, g * HEAD_SIZE : (g + 1) * HEAD_SIZE]
            scores.append(nt_dot(query[k, g * HEADS : (g + 1) * HEADS], keys))
    scores = jnp.concatenate(scores) * SCALE
    top = jnp.max(scores, axis=-1, keepdims=True)
    exponent = jnp.exp(scores - top)
    total = jnp.sum(exponent, axis=-1, keepdims=True)
    logs, share = top + jnp.log(total), 1.0 / total
    for k in range(POOL_PAGES):
        live = alive[step * POOL_PAGES + k] != 0
        for g in range(GROUPS):
            rows = slice(k * QUERY_HEADS + g * HEADS, k * QUERY_HEADS + (g + 1) * HEADS)
            values = pages[k][0, :, KEYS + g * HEAD_SIZE : KEYS + (g + 1) * HEAD_SIZE]
            mixture = jnp.dot(exponent[rows].astype(BF16), values, preferred_element_type=F32)
            out[k, g * HEADS : (g + 1) * HEADS] = jnp.where(live, mixture * share[rows], 0.0)
        mine = log_rows(logs[k * QUERY_HEADS : (k + 1) * QUERY_HEADS])
        out[k, QUERY_HEADS:] = jnp.where(live, mine, LOW)


def pool_attention(slots, alive, queries_all, pool):
    def page_of(k):
        return lambda s, slots, alive: (slots[s * POOL_PAGES + k], 0, 0)

    return pl.pallas_call(
        page_kernel,
        out_shape=jax.ShapeDtypeStruct((SAMPLES, PACK, HEAD_SIZE), F32),
        grid_spec=pltpu.PrefetchScalarGridSpec(
            num_scalar_prefetch=2,
            grid=(SAMPLES // POOL_PAGES,),
            in_specs=[
                pl.BlockSpec(
                    (POOL_PAGES, QUERY_HEADS, HEAD_SIZE), lambda s, slots, alive: (s, 0, 0)
                )
            ]
            + [pl.BlockSpec((1, PAGE, KVW), page_of(k)) for k in range(POOL_PAGES)],
            out_specs=pl.BlockSpec(
                (POOL_PAGES, PACK, HEAD_SIZE), lambda s, slots, alive: (s, 0, 0)
            ),
        ),
        compiler_params=params(16),
        cost_estimate=cost(1000, 1000),
        name="pool_attention",
    )(slots, alive, queries_all, *[pool] * POOL_PAGES)


LOCAL_PAGES = 4


def local_kernel(pages_alive, query, new, pages, out, top_ref, sum_ref, mix_ref):
    step = pl.program_id(0)
    width = LOCAL_PAGES * PAGE

    @pl.when(step == 0)
    def _():
        for g in range(GROUPS):
            rows = slice(g * HEADS, (g + 1) * HEADS)
            lanes = slice(g * HEAD_SIZE, (g + 1) * HEAD_SIZE)
            value_lanes = slice(KEYS + g * HEAD_SIZE, KEYS + (g + 1) * HEAD_SIZE)
            products = query[rows].astype(F32) * new[0:1, lanes].astype(F32)
            top_ref[rows] = jnp.sum(products, axis=-1, keepdims=True) * SCALE
            sum_ref[rows] = jnp.ones((HEADS, 1), F32)
            mix_ref[rows] = jnp.broadcast_to(new[0:1, value_lanes].astype(F32), (HEADS, HEAD_SIZE))

    @pl.when(step * LOCAL_PAGES < pages_alive[0])
    def _():
        block = pages.reshape(width, KVW)
        at = step * width + lax.broadcasted_iota(jnp.int32, (QUERY_HEADS, width), 1)
        live = at < pages_alive[0] * PAGE
        scores = jnp.concatenate(
            [
                nt_dot(
                    query[g * HEADS : (g + 1) * HEADS],
                    block[:, g * HEAD_SIZE : (g + 1) * HEAD_SIZE],
                )
                for g in range(GROUPS)
            ]
        )
        scores = jnp.where(live, scores * SCALE, LOW)
        old = top_ref[...]
        top = jnp.maximum(old, jnp.max(scores, axis=-1, keepdims=True))
        shrink = jnp.exp(old - top)
        exponent = jnp.where(live, jnp.exp(scores - top), 0.0)
        top_ref[...] = top
        sum_ref[...] = sum_ref[...] * shrink + jnp.sum(exponent, axis=-1, keepdims=True)
        for g in range(GROUPS):
            rows = slice(g * HEADS, (g + 1) * HEADS)
            values = block[:, KEYS + g * HEAD_SIZE : KEYS + (g + 1) * HEAD_SIZE]
            mix_ref[rows] = mix_ref[rows] * shrink[rows] + jnp.dot(
                exponent[rows].astype(BF16), values, preferred_element_type=F32
            )

    @pl.when(step == CMAX // LOCAL_PAGES - 1)
    def _():
        out[:QUERY_HEADS] = mix_ref[...] / sum_ref[...]
        out[QUERY_HEADS:] = log_rows(top_ref[...] + jnp.log(sum_ref[...]))


def local_attention(pages_alive, query, new, pages):
    def block_of(step, alive):
        last = jnp.maximum(alive[0] - 1, 0) // LOCAL_PAGES
        return (jnp.minimum(step, last), 0, 0)

    return pl.pallas_call(
        local_kernel,
        out_shape=jax.ShapeDtypeStruct((PACK, HEAD_SIZE), F32),
        grid_spec=pltpu.PrefetchScalarGridSpec(
            num_scalar_prefetch=1,
            grid=(CMAX // LOCAL_PAGES,),
            in_specs=[
                pl.BlockSpec((QUERY_HEADS, HEAD_SIZE), lambda step, alive: (0, 0)),
                pl.BlockSpec((1, KVW), lambda step, alive: (0, 0)),
                pl.BlockSpec((LOCAL_PAGES, PAGE, KVW), block_of),
            ],
            out_specs=pl.BlockSpec((PACK, HEAD_SIZE), lambda step, alive: (0, 0)),
            scratch_shapes=[
                pltpu.VMEM((QUERY_HEADS, 1), F32),
                pltpu.VMEM((QUERY_HEADS, 1), F32),
                pltpu.VMEM((QUERY_HEADS, HEAD_SIZE), F32),
            ],
        ),
        compiler_params=params(16),
        cost_estimate=cost(1000, 1000),
        name="local_attention",
    )(pages_alive, query, new, pages)


def prefix_kernel(
    prompt_pages, own_l, own_r, up_l, up_r, down_l, down_r, queries, pool, cache, packed
):
    me, prompt = lax.axis_index("sample"), lax.axis_index("prompt")
    z, x = me // 4, lax.rem(me, 4)
    y, core = prompt // 2, lax.rem(prompt, 2)
    near = lax.rem(y + 3 - 2 * core, 4)
    other = lax.rem(y + 1 + 2 * core, 4)
    far = lax.rem(y + 2, 4)
    columns = (
        2 * y + core, 2 * y + 1 - core, 2 * near + core, 2 * near + 1 - core,
        2 * other + 1 - core, 2 * other + core, 2 * far + core, 2 * far + 1 - core,
    )
    for j in range(8):
        lanes = slice((j % 4) * COLUMNS, (j % 4 + 1) * COLUMNS)
        own, up, down = (own_l, up_l, down_l) if j < 4 else (own_r, up_r, down_r)
        total = own[:, lanes] + up[:, lanes].astype(F32) + down[:, lanes].astype(F32)
        target = pl.ds(pl.multiple_of(columns[j] * COLUMNS, COLUMNS), COLUMNS)
        cache[0, :, target] = total.astype(BF16)
    sources = [
        lax.rem(z + 4 - dz, 4) * 4 + lax.rem(x + 4 - dx, 4) for dx in STEPS for dz in STEPS
    ]
    live = lax.broadcasted_iota(jnp.int32, (SAMPLES * HEADS, ROWS), 1) < prompt_pages[0] * PAGE - me * ROWS
    logs = jnp.full((SAMPLES * HEADS, HEAD_SIZE), LOW, F32)
    for g in range(GROUPS):
        keys = cache[0, :, g * HEAD_SIZE : (g + 1) * HEAD_SIZE]
        values = cache[0, :, KEYS + g * HEAD_SIZE : KEYS + (g + 1) * HEAD_SIZE]
        scores = jnp.where(live, nt_dot(queries[g], keys) * SCALE, LOW)
        top = jnp.max(scores, axis=-1, keepdims=True)
        exponent = jnp.where(live, jnp.exp(scores - top), 0.0)
        total = jnp.sum(exponent, axis=-1, keepdims=True)
        mixture = jnp.dot(exponent.astype(BF16), values, preferred_element_type=F32)
        some = total > 0.0
        total = jnp.where(some, total, 1.0)
        log = jnp.where(some, top + jnp.log(total), LOW)
        rows = slice(g * HEADS, (g + 1) * HEADS)
        pool_log = pool[:, QUERY_HEADS:, g : g + 1].reshape(SAMPLES * HEADS, 1)
        pool_mixture = pool[:, rows].reshape(SAMPLES * HEADS, HEAD_SIZE)
        high = jnp.maximum(log, pool_log)
        here, there = jnp.exp(log - high), jnp.exp(pool_log - high)
        both = here + there
        merged = mixture * (here / (total * both)) + pool_mixture * (there / both)
        for r, source in enumerate(sources):
            packed[source, rows] = merged[r * HEADS : (r + 1) * HEADS].astype(BF16)
        logs = put_lane(logs, g, high + jnp.log(both))
    first = logs.astype(BF16).astype(F32)
    second = (logs - first).astype(BF16).astype(F32)
    third = logs - first - second
    terms = jnp.zeros((SAMPLES * HEADS, HEAD_SIZE), F32)
    for g in range(GROUPS):
        for t, term in enumerate((first, second, third)):
            terms = put_lane(terms, t * GROUPS + g, term[:, g : g + 1])
    padding = jnp.zeros((SENT - QUERY_HEADS - HEADS, HEAD_SIZE), F32)
    for r, source in enumerate(sources):
        rows = jnp.concatenate([terms[r * HEADS : (r + 1) * HEADS], padding])
        packed[source, QUERY_HEADS:] = rows.astype(BF16)


def prefix_attention(prompt_pages, parts, queries, pool):
    smem, vmem = pl.BlockSpec(memory_space=pltpu.SMEM), pl.BlockSpec(memory_space=pltpu.VMEM)
    return pl.pallas_call(
        prefix_kernel,
        out_shape=[
            jax.ShapeDtypeStruct((1, ROWS, KVW), BF16),
            jax.ShapeDtypeStruct((SAMPLES, SENT, HEAD_SIZE), BF16),
        ],
        in_specs=[smem] + [vmem] * 8,
        out_specs=[vmem, vmem],
        compiler_params=params(20),
        cost_estimate=cost(300_000_000, 6 * MIB),
        name="prefix_attention",
    )(prompt_pages, *parts, queries, pool)


def combine_kernel(arrived, local, out):
    terms = arrived[:, QUERY_HEADS:].astype(F32)
    for g in range(GROUPS):
        rows = slice(g * HEADS, (g + 1) * HEADS)
        logs = sum(terms[:, :HEADS, lane : lane + 1] for lane in (g, g + GROUPS, g + 2 * GROUPS))
        local_log = local[QUERY_HEADS:, g : g + 1]
        high = jnp.maximum(jnp.max(logs, axis=0), local_log)
        shares = jnp.exp(logs - high[None])
        local_share = jnp.exp(local_log - high)
        total = jnp.sum(shares, axis=0) + local_share
        mixture = jnp.sum(arrived[:, rows].astype(F32) * shares, axis=0) + local[rows] * local_share
        out[rows] = (mixture / total).astype(BF16)


def combine(arrived, local):
    vmem = pl.BlockSpec(memory_space=pltpu.VMEM)
    return pl.pallas_call(
        combine_kernel,
        out_shape=jax.ShapeDtypeStruct((QUERY_HEADS, HEAD_SIZE), BF16),
        in_specs=[vmem, vmem],
        out_specs=vmem,
        compiler_params=params(16),
        cost_estimate=cost(1_000_000, MIB),
        name="combine",
    )(arrived, local)


def per_device(
    prompt_states,
    kv_weight,
    queries,
    new_kv,
    local_pages,
    pool_pages,
    prompt_pages,
    comp_pages,
    preempted,
    page_where,
):
    tie = lax.optimization_barrier

    weight_far = lax.ppermute(kv_weight, "sample", X_FAR)
    weight_right = lax.ppermute(kv_weight, "sample", X_RIGHT)
    weight_left = lax.ppermute(kv_weight, "sample", X_LEFT)
    block, query = prepare(queries, page_where, comp_pages, preempted)
    blocks = [block] + [lax.ppermute(block, "sample", to) for to in (Z_UP, Z_DOWN, Z_FAR)]
    states = prompt_states.reshape(4, 4, ROWS, SLICE)
    picked = pick(states, blocks)
    slices, picked = tie(((kv_weight, weight_right, weight_left, weight_far), picked))
    others, to_right, to_left, to_far = picked[:4]
    rows_far = lax.ppermute(to_far, "sample", X_FAR)
    to_right, to_left, rows_far = tie((to_right, to_left, rows_far))
    rows_right = lax.ppermute(to_right, "sample", X_RIGHT)
    rows_left = lax.ppermute(to_left, "sample", X_LEFT)

    here = jnp.stack(slices)
    near = lax.ppermute(here, "prompt", Y_SPLIT)
    here_other = lax.ppermute(here, "prompt", SWAP)
    near_other = lax.ppermute(here_other, "prompt", Y_SPLIT)
    far = lax.ppermute(near, "prompt", Y_SPLIT)
    near_swapped = lax.ppermute(near, "prompt", SWAP)
    near_other_swapped = lax.ppermute(near_other, "prompt", SWAP)
    far, rows_right, rows_left = tie((far, rows_right, rows_left))
    far_other = lax.ppermute(far, "prompt", SWAP)
    others = [others, rows_right, rows_left, rows_far]
    pieces = [
        here, here_other, near, near_other,
        near_swapped, near_other_swapped, far, far_other,
    ]

    far_l, far_r = product_far(others, pieces)
    mine, to_right, to_left, to_far = picked[4:]
    to_right, to_left, to_far, far_l, far_r = tie((to_right, to_left, to_far, far_l, far_r))
    mine = [
        mine,
        lax.ppermute(to_right, "sample", X_RIGHT),
        lax.ppermute(to_left, "sample", X_LEFT),
        lax.ppermute(to_far, "sample", X_FAR),
    ]
    from_down = lax.ppermute(far_l, "sample", Z_UP)
    from_up = lax.ppermute(far_r, "sample", Z_DOWN)
    up_l, up_r, down_l, down_r = product(others, pieces, (1, 2), BF16, "product_near")
    up_r, down_l, from_down, from_up = (
        lax.ppermute(up_r, "sample", Z_UP), lax.ppermute(down_l, "sample", Z_DOWN), from_down, from_up,
    )
    up_l, down_r = relay(up_l, down_r, from_down, from_up)
    sums = [
        lax.ppermute(up_l, "sample", Z_UP),
        up_r,
        down_l,
        lax.ppermute(down_r, "sample", Z_DOWN),
    ]

    arrived, query, up_l = tie((others, query, up_l))
    queries_all, by_group, slots, alive = unpack(arrived)
    pool = pool_attention(slots, alive, queries_all, pool_pages[0, 0])
    local_alive = jnp.where(preempted[0] > 0, 0, comp_pages[0])
    local = local_attention(local_alive, query, new_kv[0], local_pages[0, 0])
    mine, pool, local = tie((mine, pool, local))
    sums = [*product(mine, pieces, (None,), F32, "product_own"), *sums]

    cache, packed = prefix_attention(prompt_pages, sums, by_group, pool)
    arrived = lax.all_to_all(packed, "sample", split_axis=0, concat_axis=0, tiled=True)
    attended = combine(arrived, local)
    return (cache, attended.reshape(1, 1, -1))


def solution(mesh):
    return jax.shard_map(
        per_device,
        mesh=mesh,
        in_specs=(
            P("prompt", None, "sample"),
            P("sample", "prompt"),
            P("prompt", "sample", None),
            P("prompt", "sample", None),
            P("prompt", "sample", None, None, None),
            P("prompt", "sample", None, None, None),
            P("prompt"),
            P("prompt", "sample"),
            P("prompt", "sample"),
            P("prompt", "sample", None),
        ),
        out_specs=(P("prompt", "sample", None), P("prompt", "sample", None)),
        check_vma=False,
    )
```

```python
import functools
import math

import jax
import jax.numpy as jnp
from jax import lax
from jax.experimental import pallas as pl
from jax.experimental.pallas import tpu as pltpu
from jax.sharding import PartitionSpec as P

QUERY_HEADS = 64
GROUPS = 8
HEADS = 8
HEAD_SIZE = 128
PAGE = 128
SAMPLES = 16
CMAX = 16
ROWS = 256
SLICE = 512
COLUMNS = 256
KVW = 2048
KEYS = GROUPS * HEAD_SIZE
PACK = QUERY_HEADS + HEADS
SENT = QUERY_HEADS + 16
LOW = -1e30
SCALE = 1.0 / math.sqrt(HEAD_SIZE)
MIB = 1 << 20
F32 = jnp.float32
BF16 = jnp.bfloat16

X_RIGHT = [(z * 4 + x, z * 4 + (x + 1) % 4) for z in range(4) for x in range(4)]
X_LEFT = [(z * 4 + x, z * 4 + (x + 3) % 4) for z in range(4) for x in range(4)]
X_FAR = [(z * 4 + x, z * 4 + (x + 2) % 4) for z in range(4) for x in range(4)]
Z_UP = [(z * 4 + x, (z + 1) % 4 * 4 + x) for z in range(4) for x in range(4)]
Z_DOWN = [(z * 4 + x, (z + 3) % 4 * 4 + x) for z in range(4) for x in range(4)]
Z_FAR = [(z * 4 + x, (z + 2) % 4 * 4 + x) for z in range(4) for x in range(4)]
SWAP = [(y * 2 + c, y * 2 + 1 - c) for y in range(4) for c in range(2)]
Y_SPLIT = [(y * 2 + c, (y + (1 if c == 0 else 3)) % 4 * 2 + c) for y in range(4) for c in range(2)]


def params(mib):
    return pltpu.CompilerParams(vmem_limit_bytes=mib * MIB)


def cost(flops, bytes_accessed):
    return pl.CostEstimate(flops=flops, bytes_accessed=bytes_accessed, transcendentals=0)


def nt_dot(a, b):
    return lax.dot_general(a, b, (((1,), (1,)), ((), ())), preferred_element_type=F32)


def put_lane(running, lane, column):
    at = lax.broadcasted_iota(jnp.int32, running.shape, len(running.shape) - 1)
    return jnp.where(at == lane, column, running)


HALF = QUERY_HEADS // 2
BLOCK = HALF + 8


def prepare_kernel(where, length, flag, query, sent, own):
    heads = [query[0, 0:1, h * HEAD_SIZE : (h + 1) * HEAD_SIZE].astype(F32) for h in range(QUERY_HEADS)]
    low, high = jnp.concatenate(heads[:HALF]), jnp.concatenate(heads[HALF:])
    own[:HALF] = low.astype(BF16)
    own[HALF:] = high.astype(BF16)
    sent[:HALF, :HEAD_SIZE] = low.astype(BF16)
    sent[:HALF, HEAD_SIZE:] = high.astype(BF16)
    plan = jnp.zeros((8, COLUMNS), F32)
    for c in range(CMAX):
        plan = put_lane(plan, c, where[0, 0, c].astype(F32))
    plan = put_lane(plan, CMAX, length[0, 0].astype(F32))
    plan = put_lane(plan, CMAX + 1, flag[0, 0].astype(F32))
    sent[HALF:] = plan.astype(BF16)


def prepare(query, where, length, flag):
    smem, vmem = pl.BlockSpec(memory_space=pltpu.SMEM), pl.BlockSpec(memory_space=pltpu.VMEM)
    return pl.pallas_call(
        prepare_kernel,
        out_shape=[
            jax.ShapeDtypeStruct((BLOCK, COLUMNS), BF16),
            jax.ShapeDtypeStruct((QUERY_HEADS, HEAD_SIZE), BF16),
        ],
        in_specs=[smem] * 3 + [vmem],
        out_specs=[vmem, vmem],
        compiler_params=params(16),
        cost_estimate=cost(1000, 1000),
        name="prepare",
    )(where, length, flag, query)


def unpack_kernel(*refs):
    own, arrived, (queries, by_group, slots, alive) = refs[:4], refs[4:7], refs[7:]
    me = lax.axis_index("sample")

    def block_of(r):
        if r < 4:
            return own[r][...].astype(F32)
        source = arrived[r // 4 - 1]
        first = source.shape[0] - 2 * BLOCK + r % 4 // 2 * BLOCK
        lanes = slice(r % 2 * COLUMNS, (r % 2 + 1) * COLUMNS)
        return source[first : first + BLOCK, lanes].astype(F32)

    plans = []
    for r in range(SAMPLES):
        block = block_of(r)
        for half in range(2):
            lanes = slice(half * HEAD_SIZE, (half + 1) * HEAD_SIZE)
            queries[r, half * HALF : (half + 1) * HALF] = block[:HALF, lanes].astype(BF16)
        plans.append(block[HALF : HALF + 1])
    for g in range(GROUPS):
        lanes = slice(g // 4 * HEAD_SIZE, (g // 4 + 1) * HEAD_SIZE)
        rows = slice(g % 4 * HEADS, (g % 4 + 1) * HEADS)
        parts = [block_of(r)[rows, lanes] for r in range(SAMPLES)]
        by_group[g] = jnp.concatenate(parts).astype(BF16)
    plan = jnp.concatenate(plans)
    lane = lax.broadcasted_iota(jnp.int32, plan.shape, 1)
    first = (me * CMAX).astype(F32)
    here = (lane < CMAX) & (plan >= first) & (plan < first + CMAX)
    live = here & (lane.astype(F32) < plan[:, CMAX : CMAX + 1]) & (plan[:, CMAX + 1 : CMAX + 2] > 0.5)
    slot = jnp.sum(jnp.where(here, plan - first, 0.0), axis=1, keepdims=True).astype(jnp.int32)
    some = jnp.max(jnp.where(live, 1.0, 0.0), axis=1, keepdims=True).astype(jnp.int32)
    for r in range(SAMPLES):
        slots[r] = slot[r, 0]
        alive[r] = some[r, 0]


def unpack(own, arrived):
    smem, vmem = pl.BlockSpec(memory_space=pltpu.SMEM), pl.BlockSpec(memory_space=pltpu.VMEM)
    return pl.pallas_call(
        unpack_kernel,
        out_shape=[
            jax.ShapeDtypeStruct((SAMPLES, QUERY_HEADS, HEAD_SIZE), BF16),
            jax.ShapeDtypeStruct((GROUPS, SAMPLES * HEADS, HEAD_SIZE), BF16),
            jax.ShapeDtypeStruct((SAMPLES,), jnp.int32),
            jax.ShapeDtypeStruct((SAMPLES,), jnp.int32),
        ],
        in_specs=[vmem] * 7,
        out_specs=[vmem, vmem, smem, smem],
        compiler_params=params(16),
        cost_estimate=cost(1000, 1000),
        name="unpack",
    )(*own, *arrived)


STEPS = (0, 1, 3, 2)
NEXT = (2, 1, 3, 0)


def copy_rows(states, sems, wanted):
    me = lax.axis_index("sample")
    z, x = me // 4, lax.rem(me, 4)
    copies = [
        pltpu.make_async_copy(
            states.at[lax.rem(z + NEXT[k], 4), lax.rem(x + step, 4)], target, sems.at[n]
        )
        for n, (step, k, target) in enumerate(wanted)
    ]
    for copy in copies:
        copy.start()
    return copies


def block_rows(k):
    return pl.ds(k * ROWS, ROWS)


def pick_far_kernel(states, own, far, sems):
    wanted = [(2, k, far.at[block_rows(k)]) for k in range(3)]
    wanted += [(0, k, own.at[block_rows(k)]) for k in range(4)]
    for copy in copy_rows(states, sems, wanted):
        copy.wait()


def pick_far(states):
    vmem = pl.BlockSpec(memory_space=pltpu.VMEM)
    return pl.pallas_call(
        pick_far_kernel,
        out_shape=[
            jax.ShapeDtypeStruct((4 * ROWS, SLICE), BF16),
            jax.ShapeDtypeStruct((3 * ROWS, SLICE), BF16),
        ],
        in_specs=[pl.BlockSpec(memory_space=pl.ANY)],
        out_specs=[vmem] * 2,
        scratch_shapes=[pltpu.SemaphoreType.DMA((7,))],
        compiler_params=params(50),
        cost_estimate=cost(1000, 1000),
        name="pick_far",
    )(states)


def put_blocks(target, first, blocks):
    for r, block in enumerate(blocks):
        rows = slice(first + r // 2 * BLOCK, first + (r // 2 + 1) * BLOCK)
        target[rows, r % 2 * COLUMNS : (r % 2 + 1) * COLUMNS] = block[...]


def pick_near_kernel(states, *refs):
    blocks, (right, left, last), sems = refs[:4], refs[4:7], refs[7]
    wanted = [(1, k, right.at[block_rows(k)]) for k in range(4)]
    wanted += [(3, k, left.at[block_rows(k)]) for k in range(4)]
    wanted += [(2, 3, last.at[block_rows(0)])]
    copies = copy_rows(states, sems, wanted)
    put_blocks(right, 4 * ROWS, blocks)
    put_blocks(left, 4 * ROWS, blocks)
    put_blocks(last, ROWS, blocks)
    for copy in copies:
        copy.wait()


def pick_near(states, blocks):
    vmem = pl.BlockSpec(memory_space=pltpu.VMEM)
    return pl.pallas_call(
        pick_near_kernel,
        out_shape=[jax.ShapeDtypeStruct((4 * ROWS + 2 * BLOCK, SLICE), BF16)] * 2
        + [jax.ShapeDtypeStruct((ROWS + 2 * BLOCK, SLICE), BF16)],
        in_specs=[pl.BlockSpec(memory_space=pl.ANY)] + [vmem] * 4,
        out_specs=[vmem] * 3,
        scratch_shapes=[pltpu.SemaphoreType.DMA((9,))],
        compiler_params=params(44),
        cost_estimate=cost(1000, 1000),
        name="pick_near",
    )(states, *blocks)


def product_kernel(blocks, *refs):
    states, pieces, outs = refs[:4], refs[4:12], refs[12:]
    for j in range(8):
        for k, block in enumerate(blocks):
            total = jnp.zeros((ROWS, COLUMNS), F32)
            for d in range(4):
                at = block[d] * ROWS
                total += jnp.dot(
                    states[d][at : at + ROWS], pieces[j][d], preferred_element_type=F32
                )
            out = outs[2 * k + j // 4]
            out[:, (j % 4) * COLUMNS : (j % 4 + 1) * COLUMNS] = total.astype(out.dtype)


def product(states, pieces, blocks, kind, name):
    vmem = pl.BlockSpec(memory_space=pltpu.VMEM)
    outs = [jax.ShapeDtypeStruct((ROWS, KVW // 2), kind)] * (2 * len(blocks))
    return pl.pallas_call(
        functools.partial(product_kernel, blocks),
        out_shape=outs,
        in_specs=[vmem] * 12,
        out_specs=[vmem] * len(outs),
        compiler_params=params(20),
        cost_estimate=cost(1000, 1000),
        name=name,
    )(*states, *pieces)


def product_far_kernel(*refs):
    states, pieces, outs = refs[:4], refs[4:12], refs[12:]
    for j in range(8):
        total = jnp.zeros((ROWS, COLUMNS), F32)
        for d in range(4):
            total += jnp.dot(states[d][:ROWS], pieces[j][d], preferred_element_type=F32)
        outs[j // 4][:, (j % 4) * COLUMNS : (j % 4 + 1) * COLUMNS] = total.astype(BF16)


def product_far(states, pieces):
    vmem = pl.BlockSpec(memory_space=pltpu.VMEM)
    return pl.pallas_call(
        product_far_kernel,
        out_shape=[jax.ShapeDtypeStruct((ROWS, KVW // 2), BF16)] * 2,
        in_specs=[vmem] * 12,
        out_specs=[vmem] * 2,
        compiler_params=params(20),
        cost_estimate=cost(1000, 1000),
        name="product_far",
    )(*states, *pieces)


def relay_kernel(up, down, from_down, from_up, up_out, down_out):
    up_out[...] = (up[...].astype(F32) + from_down[...].astype(F32)).astype(BF16)
    down_out[...] = (down[...].astype(F32) + from_up[...].astype(F32)).astype(BF16)


def relay(up, down, from_down, from_up):
    vmem = pl.BlockSpec(memory_space=pltpu.VMEM)
    return pl.pallas_call(
        relay_kernel,
        out_shape=[jax.ShapeDtypeStruct((ROWS, KVW // 2), BF16)] * 2,
        in_specs=[vmem] * 4,
        out_specs=[vmem] * 2,
        compiler_params=params(16),
        cost_estimate=cost(1000, 1000),
        name="relay_sums",
    )(up, down, from_down, from_up)


def log_rows(logs):
    out = jnp.full((HEADS, HEAD_SIZE), LOW, F32)
    for g in range(GROUPS):
        out = put_lane(out, g, logs[g * HEADS : (g + 1) * HEADS])
    return out


POOL_PAGES = 4


def page_kernel(slots, alive, query, *refs):
    pages, out = refs[:POOL_PAGES], refs[POOL_PAGES]
    step = pl.program_id(0)
    scores = []
    for k in range(POOL_PAGES):
        for g in range(GROUPS):
            keys = pages[k][0, :, g * HEAD_SIZE : (g + 1) * HEAD_SIZE]
            scores.append(nt_dot(query[k, g * HEADS : (g + 1) * HEADS], keys))
    scores = jnp.concatenate(scores) * SCALE
    top = jnp.max(scores, axis=-1, keepdims=True)
    exponent = jnp.exp(scores - top)
    total = jnp.sum(exponent, axis=-1, keepdims=True)
    logs, share = top + jnp.log(total), 1.0 / total
    for k in range(POOL_PAGES):
        live = alive[step * POOL_PAGES + k] != 0
        for g in range(GROUPS):
            rows = slice(k * QUERY_HEADS + g * HEADS, k * QUERY_HEADS + (g + 1) * HEADS)
            values = pages[k][0, :, KEYS + g * HEAD_SIZE : KEYS + (g + 1) * HEAD_SIZE]
            mixture = jnp.dot(exponent[rows].astype(BF16), values, preferred_element_type=F32)
            out[k, g * HEADS : (g + 1) * HEADS] = jnp.where(live, mixture * share[rows], 0.0)
        mine = log_rows(logs[k * QUERY_HEADS : (k + 1) * QUERY_HEADS])
        out[k, QUERY_HEADS:] = jnp.where(live, mine, LOW)


def pool_attention(slots, alive, queries_all, pool):
    def page_of(k):
        return lambda s, slots, alive: (slots[s * POOL_PAGES + k], 0, 0)

    return pl.pallas_call(
        page_kernel,
        out_shape=jax.ShapeDtypeStruct((SAMPLES, PACK, HEAD_SIZE), F32),
        grid_spec=pltpu.PrefetchScalarGridSpec(
            num_scalar_prefetch=2,
            grid=(SAMPLES // POOL_PAGES,),
            in_specs=[
                pl.BlockSpec(
                    (POOL_PAGES, QUERY_HEADS, HEAD_SIZE), lambda s, slots, alive: (s, 0, 0)
                )
            ]
            + [pl.BlockSpec((1, PAGE, KVW), page_of(k)) for k in range(POOL_PAGES)],
            out_specs=pl.BlockSpec(
                (POOL_PAGES, PACK, HEAD_SIZE), lambda s, slots, alive: (s, 0, 0)
            ),
        ),
        compiler_params=params(16),
        cost_estimate=cost(1000, 1000),
        name="pool_attention",
    )(slots, alive, queries_all, *[pool] * POOL_PAGES)


LOCAL_PAGES = 4


def local_kernel(pages_alive, query, new, pages, out, top_ref, sum_ref, mix_ref):
    step = pl.program_id(0)
    width = LOCAL_PAGES * PAGE

    @pl.when(step == 0)
    def _():
        for g in range(GROUPS):
            rows = slice(g * HEADS, (g + 1) * HEADS)
            lanes = slice(g * HEAD_SIZE, (g + 1) * HEAD_SIZE)
            value_lanes = slice(KEYS + g * HEAD_SIZE, KEYS + (g + 1) * HEAD_SIZE)
            products = query[rows].astype(F32) * new[0:1, lanes].astype(F32)
            top_ref[rows] = jnp.sum(products, axis=-1, keepdims=True) * SCALE
            sum_ref[rows] = jnp.ones((HEADS, 1), F32)
            mix_ref[rows] = jnp.broadcast_to(new[0:1, value_lanes].astype(F32), (HEADS, HEAD_SIZE))

    @pl.when(step * LOCAL_PAGES < pages_alive[0])
    def _():
        block = pages.reshape(width, KVW)
        at = step * width + lax.broadcasted_iota(jnp.int32, (QUERY_HEADS, width), 1)
        live = at < pages_alive[0] * PAGE
        scores = jnp.concatenate(
            [
                nt_dot(
                    query[g * HEADS : (g + 1) * HEADS],
                    block[:, g * HEAD_SIZE : (g + 1) * HEAD_SIZE],
                )
                for g in range(GROUPS)
            ]
        )
        scores = jnp.where(live, scores * SCALE, LOW)
        old = top_ref[...]
        top = jnp.maximum(old, jnp.max(scores, axis=-1, keepdims=True))
        shrink = jnp.exp(old - top)
        exponent = jnp.where(live, jnp.exp(scores - top), 0.0)
        top_ref[...] = top
        sum_ref[...] = sum_ref[...] * shrink + jnp.sum(exponent, axis=-1, keepdims=True)
        for g in range(GROUPS):
            rows = slice(g * HEADS, (g + 1) * HEADS)
            values = block[:, KEYS + g * HEAD_SIZE : KEYS + (g + 1) * HEAD_SIZE]
            mix_ref[rows] = mix_ref[rows] * shrink[rows] + jnp.dot(
                exponent[rows].astype(BF16), values, preferred_element_type=F32
            )

    @pl.when(step == CMAX // LOCAL_PAGES - 1)
    def _():
        out[:QUERY_HEADS] = mix_ref[...] / sum_ref[...]
        out[QUERY_HEADS:] = log_rows(top_ref[...] + jnp.log(sum_ref[...]))


def local_attention(pages_alive, query, new, pages):
    def block_of(step, alive):
        last = jnp.maximum(alive[0] - 1, 0) // LOCAL_PAGES
        return (jnp.minimum(step, last), 0, 0)

    return pl.pallas_call(
        local_kernel,
        out_shape=jax.ShapeDtypeStruct((PACK, HEAD_SIZE), F32),
        grid_spec=pltpu.PrefetchScalarGridSpec(
            num_scalar_prefetch=1,
            grid=(CMAX // LOCAL_PAGES,),
            in_specs=[
                pl.BlockSpec((QUERY_HEADS, HEAD_SIZE), lambda step, alive: (0, 0)),
                pl.BlockSpec((1, KVW), lambda step, alive: (0, 0)),
                pl.BlockSpec((LOCAL_PAGES, PAGE, KVW), block_of),
            ],
            out_specs=pl.BlockSpec((PACK, HEAD_SIZE), lambda step, alive: (0, 0)),
            scratch_shapes=[
                pltpu.VMEM((QUERY_HEADS, 1), F32),
                pltpu.VMEM((QUERY_HEADS, 1), F32),
                pltpu.VMEM((QUERY_HEADS, HEAD_SIZE), F32),
            ],
        ),
        compiler_params=params(16),
        cost_estimate=cost(1000, 1000),
        name="local_attention",
    )(pages_alive, query, new, pages)


def prefix_kernel(
    prompt_pages, own_l, own_r, up_l, up_r, down_l, down_r, queries, pool, cache, packed
):
    me, prompt = lax.axis_index("sample"), lax.axis_index("prompt")
    z, x = me // 4, lax.rem(me, 4)
    y, core = prompt // 2, lax.rem(prompt, 2)
    near = lax.rem(y + 3 - 2 * core, 4)
    other = lax.rem(y + 1 + 2 * core, 4)
    far = lax.rem(y + 2, 4)
    columns = (
        2 * y + core, 2 * y + 1 - core, 2 * near + core, 2 * near + 1 - core,
        2 * other + 1 - core, 2 * other + core, 2 * far + core, 2 * far + 1 - core,
    )
    for j in range(8):
        lanes = slice((j % 4) * COLUMNS, (j % 4 + 1) * COLUMNS)
        own, up, down = (own_l, up_l, down_l) if j < 4 else (own_r, up_r, down_r)
        total = own[:, lanes] + up[:, lanes].astype(F32) + down[:, lanes].astype(F32)
        target = pl.ds(pl.multiple_of(columns[j] * COLUMNS, COLUMNS), COLUMNS)
        cache[0, :, target] = total.astype(BF16)
    sources = [
        lax.rem(z + 4 - dz, 4) * 4 + lax.rem(x + 4 - dx, 4) for dx in STEPS for dz in STEPS
    ]
    live = lax.broadcasted_iota(jnp.int32, (SAMPLES * HEADS, ROWS), 1) < prompt_pages[0] * PAGE - me * ROWS
    logs = jnp.full((SAMPLES * HEADS, HEAD_SIZE), LOW, F32)
    for g in range(GROUPS):
        keys = cache[0, :, g * HEAD_SIZE : (g + 1) * HEAD_SIZE]
        values = cache[0, :, KEYS + g * HEAD_SIZE : KEYS + (g + 1) * HEAD_SIZE]
        scores = jnp.where(live, nt_dot(queries[g], keys) * SCALE, LOW)
        top = jnp.max(scores, axis=-1, keepdims=True)
        exponent = jnp.where(live, jnp.exp(scores - top), 0.0)
        total = jnp.sum(exponent, axis=-1, keepdims=True)
        mixture = jnp.dot(exponent.astype(BF16), values, preferred_element_type=F32)
        some = total > 0.0
        total = jnp.where(some, total, 1.0)
        log = jnp.where(some, top + jnp.log(total), LOW)
        rows = slice(g * HEADS, (g + 1) * HEADS)
        pool_log = pool[:, QUERY_HEADS:, g : g + 1].reshape(SAMPLES * HEADS, 1)
        pool_mixture = pool[:, rows].reshape(SAMPLES * HEADS, HEAD_SIZE)
        high = jnp.maximum(log, pool_log)
        here, there = jnp.exp(log - high), jnp.exp(pool_log - high)
        both = here + there
        merged = mixture * (here / (total * both)) + pool_mixture * (there / both)
        for r, source in enumerate(sources):
            packed[source, rows] = merged[r * HEADS : (r + 1) * HEADS].astype(BF16)
        logs = put_lane(logs, g, high + jnp.log(both))
    first = logs.astype(BF16).astype(F32)
    second = (logs - first).astype(BF16).astype(F32)
    third = logs - first - second
    terms = jnp.zeros((SAMPLES * HEADS, HEAD_SIZE), F32)
    for g in range(GROUPS):
        for t, term in enumerate((first, second, third)):
            terms = put_lane(terms, t * GROUPS + g, term[:, g : g + 1])
    padding = jnp.zeros((SENT - QUERY_HEADS - HEADS, HEAD_SIZE), F32)
    for r, source in enumerate(sources):
        rows = jnp.concatenate([terms[r * HEADS : (r + 1) * HEADS], padding])
        packed[source, QUERY_HEADS:] = rows.astype(BF16)


def prefix_attention(prompt_pages, parts, queries, pool):
    smem, vmem = pl.BlockSpec(memory_space=pltpu.SMEM), pl.BlockSpec(memory_space=pltpu.VMEM)
    return pl.pallas_call(
        prefix_kernel,
        out_shape=[
            jax.ShapeDtypeStruct((1, ROWS, KVW), BF16),
            jax.ShapeDtypeStruct((SAMPLES, SENT, HEAD_SIZE), BF16),
        ],
        in_specs=[smem] + [vmem] * 8,
        out_specs=[vmem, vmem],
        compiler_params=params(20),
        cost_estimate=cost(300_000_000, 6 * MIB),
        name="prefix_attention",
    )(prompt_pages, *parts, queries, pool)


def combine_kernel(arrived, local, out):
    terms = arrived[:, QUERY_HEADS:].astype(F32)
    for g in range(GROUPS):
        rows = slice(g * HEADS, (g + 1) * HEADS)
        logs = sum(terms[:, :HEADS, lane : lane + 1] for lane in (g, g + GROUPS, g + 2 * GROUPS))
        local_log = local[QUERY_HEADS:, g : g + 1]
        high = jnp.maximum(jnp.max(logs, axis=0), local_log)
        shares = jnp.exp(logs - high[None])
        local_share = jnp.exp(local_log - high)
        total = jnp.sum(shares, axis=0) + local_share
        mixture = jnp.sum(arrived[:, rows].astype(F32) * shares, axis=0) + local[rows] * local_share
        out[rows] = (mixture / total).astype(BF16)


def combine(arrived, local):
    vmem = pl.BlockSpec(memory_space=pltpu.VMEM)
    return pl.pallas_call(
        combine_kernel,
        out_shape=jax.ShapeDtypeStruct((QUERY_HEADS, HEAD_SIZE), BF16),
        in_specs=[vmem, vmem],
        out_specs=vmem,
        compiler_params=params(16),
        cost_estimate=cost(1_000_000, MIB),
        name="combine",
    )(arrived, local)


def per_device(
    prompt_states,
    kv_weight,
    queries,
    new_kv,
    local_pages,
    pool_pages,
    prompt_pages,
    comp_pages,
    preempted,
    page_where,
):
    tie = lax.optimization_barrier

    weight_far = lax.ppermute(kv_weight, "sample", X_FAR)
    weight_right = lax.ppermute(kv_weight, "sample", X_RIGHT)
    weight_left = lax.ppermute(kv_weight, "sample", X_LEFT)
    block, query = prepare(queries, page_where, comp_pages, preempted)
    states = prompt_states.reshape(4, 4, ROWS, SLICE)
    own_states, to_far = pick_far(states)
    slices, own_states, to_far, block = tie(
        ((kv_weight, weight_right, weight_left, weight_far), own_states, to_far, block)
    )
    blocks = [block] + [lax.ppermute(block, "sample", to) for to in (Z_UP, Z_DOWN, Z_FAR)]
    to_right, to_left, last_far = pick_near(states, blocks)
    rows_far = lax.ppermute(to_far, "sample", X_FAR)
    rows_right = lax.ppermute(to_right, "sample", X_RIGHT)
    rows_left = lax.ppermute(to_left, "sample", X_LEFT)

    here = jnp.stack(slices)
    near = lax.ppermute(here, "prompt", Y_SPLIT)
    here_other = lax.ppermute(here, "prompt", SWAP)
    near_other = lax.ppermute(here_other, "prompt", Y_SPLIT)
    near, near_other, rows_far = tie((near, near_other, rows_far))
    far = lax.ppermute(near, "prompt", Y_SPLIT)
    near_swapped = lax.ppermute(near, "prompt", SWAP)
    near_other_swapped = lax.ppermute(near_other, "prompt", SWAP)
    far, rows_right, rows_left = tie((far, rows_right, rows_left))
    far_other = lax.ppermute(far, "prompt", SWAP)
    others = [own_states, rows_right, rows_left, rows_far]
    pieces = [
        here, here_other, near, near_other,
        near_swapped, near_other_swapped, far, far_other,
    ]

    far_l, far_r = product_far(others, pieces)
    last_far, rows_right = tie((last_far, rows_right))
    last_far = lax.ppermute(last_far, "sample", X_FAR)
    from_down = lax.ppermute(far_l, "sample", Z_UP)
    from_up = lax.ppermute(far_r, "sample", Z_DOWN)
    up_l, up_r, down_l, down_r = product(others, pieces, ((1,) * 4, (2,) * 4), BF16, "product_near")
    up_r, down_l, last_far = tie((up_r, down_l, last_far))
    up_r, down_l = lax.ppermute(up_r, "sample", Z_UP), lax.ppermute(down_l, "sample", Z_DOWN)
    up_l, down_r = relay(up_l, down_r, from_down, from_up)
    sums = [
        lax.ppermute(up_l, "sample", Z_UP),
        up_r,
        down_l,
        lax.ppermute(down_r, "sample", Z_DOWN),
    ]

    arrived, query, up_l = tie(([rows_right, rows_left, last_far], query, up_l))
    queries_all, by_group, slots, alive = unpack(blocks, arrived)
    pool = pool_attention(slots, alive, queries_all, pool_pages[0, 0])
    local_alive = jnp.where(preempted[0] > 0, 0, comp_pages[0])
    local = local_attention(local_alive, query, new_kv[0], local_pages[0, 0])
    mine, pool, local = tie(([own_states, *arrived], pool, local))
    sums = [*product(mine, pieces, ((3, 3, 3, 0),), F32, "product_own"), *sums]

    cache, packed = prefix_attention(prompt_pages, sums, by_group, pool)
    arrived = lax.all_to_all(packed, "sample", split_axis=0, concat_axis=0, tiled=True)
    attended = combine(arrived, local)
    return (cache, attended.reshape(1, 1, -1))


def solution(mesh):
    return jax.shard_map(
        per_device,
        mesh=mesh,
        in_specs=(
            P("prompt", None, "sample"),
            P("sample", "prompt"),
            P("prompt", "sample", None),
            P("prompt", "sample", None),
            P("prompt", "sample", None, None, None),
            P("prompt", "sample", None, None, None),
            P("prompt"),
            P("prompt", "sample"),
            P("prompt", "sample"),
            P("prompt", "sample", None),
        ),
        out_specs=(P("prompt", "sample", None), P("prompt", "sample", None)),
        check_vma=False,
    )
```

```python
import functools
import math

import jax
import jax.numpy as jnp
from jax import lax
from jax.experimental import pallas as pl
from jax.experimental.pallas import tpu as pltpu
from jax.sharding import PartitionSpec as P

QUERY_HEADS = 64
GROUPS = 8
HEADS = 8
HEAD_SIZE = 128
PAGE = 128
SAMPLES = 16
CMAX = 16
ROWS = 256
SLICE = 512
COLUMNS = 256
KVW = 2048
KEYS = GROUPS * HEAD_SIZE
PACK = QUERY_HEADS + HEADS
SENT = QUERY_HEADS + 16
LOW = -1e30
SCALE = 1.0 / math.sqrt(HEAD_SIZE)
MIB = 1 << 20
F32 = jnp.float32
BF16 = jnp.bfloat16

X_RIGHT = [(z * 4 + x, z * 4 + (x + 1) % 4) for z in range(4) for x in range(4)]
X_LEFT = [(z * 4 + x, z * 4 + (x + 3) % 4) for z in range(4) for x in range(4)]
X_FAR = [(z * 4 + x, z * 4 + (x + 2) % 4) for z in range(4) for x in range(4)]
Z_UP = [(z * 4 + x, (z + 1) % 4 * 4 + x) for z in range(4) for x in range(4)]
Z_DOWN = [(z * 4 + x, (z + 3) % 4 * 4 + x) for z in range(4) for x in range(4)]
Z_FAR = [(z * 4 + x, (z + 2) % 4 * 4 + x) for z in range(4) for x in range(4)]
SWAP = [(y * 2 + c, y * 2 + 1 - c) for y in range(4) for c in range(2)]
Y_SPLIT = [(y * 2 + c, (y + (1 if c == 0 else 3)) % 4 * 2 + c) for y in range(4) for c in range(2)]


def params(mib):
    return pltpu.CompilerParams(vmem_limit_bytes=mib * MIB)


def cost(flops, bytes_accessed):
    return pl.CostEstimate(flops=flops, bytes_accessed=bytes_accessed, transcendentals=0)


def nt_dot(a, b):
    return lax.dot_general(a, b, (((1,), (1,)), ((), ())), preferred_element_type=F32)


def put_lane(running, lane, column):
    at = lax.broadcasted_iota(jnp.int32, running.shape, len(running.shape) - 1)
    return jnp.where(at == lane, column, running)


HALF = QUERY_HEADS // 2
BLOCK = HALF + 8


def prepare_kernel(where, length, flag, query, sent, own):
    heads = [query[0, 0:1, h * HEAD_SIZE : (h + 1) * HEAD_SIZE].astype(F32) for h in range(QUERY_HEADS)]
    low, high = jnp.concatenate(heads[:HALF]), jnp.concatenate(heads[HALF:])
    own[:HALF] = low.astype(BF16)
    own[HALF:] = high.astype(BF16)
    sent[:HALF, :HEAD_SIZE] = low.astype(BF16)
    sent[:HALF, HEAD_SIZE:] = high.astype(BF16)
    plan = jnp.zeros((8, COLUMNS), F32)
    for c in range(CMAX):
        plan = put_lane(plan, c, where[0, 0, c].astype(F32))
    plan = put_lane(plan, CMAX, length[0, 0].astype(F32))
    plan = put_lane(plan, CMAX + 1, flag[0, 0].astype(F32))
    sent[HALF:] = plan.astype(BF16)


def prepare(query, where, length, flag):
    smem, vmem = pl.BlockSpec(memory_space=pltpu.SMEM), pl.BlockSpec(memory_space=pltpu.VMEM)
    return pl.pallas_call(
        prepare_kernel,
        out_shape=[
            jax.ShapeDtypeStruct((BLOCK, COLUMNS), BF16),
            jax.ShapeDtypeStruct((QUERY_HEADS, HEAD_SIZE), BF16),
        ],
        in_specs=[smem] * 3 + [vmem],
        out_specs=[vmem, vmem],
        compiler_params=params(16),
        cost_estimate=cost(1000, 1000),
        name="prepare",
    )(where, length, flag, query)


def unpack_kernel(*refs):
    own, arrived, (queries, by_group, slots, alive) = refs[:4], refs[4:7], refs[7:]
    me = lax.axis_index("sample")

    def block_of(r):
        if r < 4:
            return own[r][...].astype(F32)
        source = arrived[r // 4 - 1]
        first = source.shape[0] - 2 * BLOCK + r % 4 // 2 * BLOCK
        lanes = slice(r % 2 * COLUMNS, (r % 2 + 1) * COLUMNS)
        return source[first : first + BLOCK, lanes].astype(F32)

    plans = []
    for r in range(SAMPLES):
        block = block_of(r)
        for half in range(2):
            lanes = slice(half * HEAD_SIZE, (half + 1) * HEAD_SIZE)
            queries[r, half * HALF : (half + 1) * HALF] = block[:HALF, lanes].astype(BF16)
        plans.append(block[HALF : HALF + 1])
    for g in range(GROUPS):
        lanes = slice(g // 4 * HEAD_SIZE, (g // 4 + 1) * HEAD_SIZE)
        rows = slice(g % 4 * HEADS, (g % 4 + 1) * HEADS)
        parts = [block_of(r)[rows, lanes] for r in range(SAMPLES)]
        by_group[g] = jnp.concatenate(parts).astype(BF16)
    plan = jnp.concatenate(plans)
    lane = lax.broadcasted_iota(jnp.int32, plan.shape, 1)
    first = (me * CMAX).astype(F32)
    here = (lane < CMAX) & (plan >= first) & (plan < first + CMAX)
    live = here & (lane.astype(F32) < plan[:, CMAX : CMAX + 1]) & (plan[:, CMAX + 1 : CMAX + 2] > 0.5)
    slot = jnp.sum(jnp.where(here, plan - first, 0.0), axis=1, keepdims=True).astype(jnp.int32)
    some = jnp.max(jnp.where(live, 1.0, 0.0), axis=1, keepdims=True).astype(jnp.int32)
    for r in range(SAMPLES):
        slots[r] = slot[r, 0]
        alive[r] = some[r, 0]


def unpack(own, arrived):
    smem, vmem = pl.BlockSpec(memory_space=pltpu.SMEM), pl.BlockSpec(memory_space=pltpu.VMEM)
    return pl.pallas_call(
        unpack_kernel,
        out_shape=[
            jax.ShapeDtypeStruct((SAMPLES, QUERY_HEADS, HEAD_SIZE), BF16),
            jax.ShapeDtypeStruct((GROUPS, SAMPLES * HEADS, HEAD_SIZE), BF16),
            jax.ShapeDtypeStruct((SAMPLES,), jnp.int32),
            jax.ShapeDtypeStruct((SAMPLES,), jnp.int32),
        ],
        in_specs=[vmem] * 7,
        out_specs=[vmem, vmem, smem, smem],
        compiler_params=params(16),
        cost_estimate=cost(1000, 1000),
        name="unpack",
    )(*own, *arrived)


STEPS = (0, 1, 3, 2)
NEXT = (2, 1, 3, 0)


def copy_rows(states, sems, wanted):
    me = lax.axis_index("sample")
    z, x = me // 4, lax.rem(me, 4)
    copies = [
        pltpu.make_async_copy(
            states.at[lax.rem(z + NEXT[k], 4), lax.rem(x + step, 4)], target, sems.at[n]
        )
        for n, (step, k, target) in enumerate(wanted)
    ]
    for copy in copies:
        copy.start()
    return copies


def block_rows(k):
    return pl.ds(k * ROWS, ROWS)


def pick_far_kernel(states, own, far, sems):
    wanted = [(2, k, far.at[block_rows(k)]) for k in range(3)]
    wanted += [(0, k, own.at[block_rows(k)]) for k in range(4)]
    for copy in copy_rows(states, sems, wanted):
        copy.wait()


def pick_far(states):
    vmem = pl.BlockSpec(memory_space=pltpu.VMEM)
    return pl.pallas_call(
        pick_far_kernel,
        out_shape=[
            jax.ShapeDtypeStruct((4 * ROWS, SLICE), BF16),
            jax.ShapeDtypeStruct((3 * ROWS, SLICE), BF16),
        ],
        in_specs=[pl.BlockSpec(memory_space=pl.ANY)],
        out_specs=[vmem] * 2,
        scratch_shapes=[pltpu.SemaphoreType.DMA((7,))],
        compiler_params=params(50),
        cost_estimate=cost(1000, 1000),
        name="pick_far",
    )(states)


def put_blocks(target, first, blocks):
    for r, block in enumerate(blocks):
        rows = slice(first + r // 2 * BLOCK, first + (r // 2 + 1) * BLOCK)
        target[rows, r % 2 * COLUMNS : (r % 2 + 1) * COLUMNS] = block[...]


def pick_near_kernel(states, *refs):
    blocks, (right, left, last), sems = refs[:4], refs[4:7], refs[7]
    wanted = [(1, k, right.at[block_rows(k)]) for k in range(4)]
    wanted += [(3, k, left.at[block_rows(k)]) for k in range(4)]
    wanted += [(2, 3, last.at[block_rows(0)])]
    copies = copy_rows(states, sems, wanted)
    put_blocks(right, 4 * ROWS, blocks)
    put_blocks(left, 4 * ROWS, blocks)
    put_blocks(last, ROWS, blocks)
    for copy in copies:
        copy.wait()


def pick_near(states, blocks):
    vmem = pl.BlockSpec(memory_space=pltpu.VMEM)
    return pl.pallas_call(
        pick_near_kernel,
        out_shape=[jax.ShapeDtypeStruct((4 * ROWS + 2 * BLOCK, SLICE), BF16)] * 2
        + [jax.ShapeDtypeStruct((ROWS + 2 * BLOCK, SLICE), BF16)],
        in_specs=[pl.BlockSpec(memory_space=pl.ANY)] + [vmem] * 4,
        out_specs=[vmem] * 3,
        scratch_shapes=[pltpu.SemaphoreType.DMA((9,))],
        compiler_params=params(44),
        cost_estimate=cost(1000, 1000),
        name="pick_near",
    )(states, *blocks)


def product_kernel(blocks, *refs):
    states, pieces, outs = refs[:4], refs[4:12], refs[12:]
    for j in range(8):
        for k, block in enumerate(blocks):
            total = jnp.zeros((ROWS, COLUMNS), F32)
            for d in range(4):
                at = block[d] * ROWS
                total += jnp.dot(
                    states[d][at : at + ROWS], pieces[j][d], preferred_element_type=F32
                )
            out = outs[2 * k + j // 4]
            out[:, (j % 4) * COLUMNS : (j % 4 + 1) * COLUMNS] = total.astype(out.dtype)


def product(states, pieces, blocks, kind, name):
    vmem = pl.BlockSpec(memory_space=pltpu.VMEM)
    outs = [jax.ShapeDtypeStruct((ROWS, KVW // 2), kind)] * (2 * len(blocks))
    return pl.pallas_call(
        functools.partial(product_kernel, blocks),
        out_shape=outs,
        in_specs=[vmem] * 12,
        out_specs=[vmem] * len(outs),
        compiler_params=params(20),
        cost_estimate=cost(1000, 1000),
        name=name,
    )(*states, *pieces)


def product_far_kernel(*refs):
    states, pieces, outs = refs[:4], refs[4:12], refs[12:]
    for j in range(8):
        total = jnp.zeros((ROWS, COLUMNS), F32)
        for d in range(4):
            total += jnp.dot(states[d][:ROWS], pieces[j][d], preferred_element_type=F32)
        outs[j // 4][:, (j % 4) * COLUMNS : (j % 4 + 1) * COLUMNS] = total.astype(BF16)


def product_far(states, pieces):
    vmem = pl.BlockSpec(memory_space=pltpu.VMEM)
    return pl.pallas_call(
        product_far_kernel,
        out_shape=[jax.ShapeDtypeStruct((ROWS, KVW // 2), BF16)] * 2,
        in_specs=[vmem] * 12,
        out_specs=[vmem] * 2,
        compiler_params=params(20),
        cost_estimate=cost(1000, 1000),
        name="product_far",
    )(*states, *pieces)


def relay_kernel(up, down, from_down, from_up, up_out, down_out):
    up_out[...] = (up[...].astype(F32) + from_down[...].astype(F32)).astype(BF16)
    down_out[...] = (down[...].astype(F32) + from_up[...].astype(F32)).astype(BF16)


def relay(up, down, from_down, from_up):
    vmem = pl.BlockSpec(memory_space=pltpu.VMEM)
    return pl.pallas_call(
        relay_kernel,
        out_shape=[jax.ShapeDtypeStruct((ROWS, KVW // 2), BF16)] * 2,
        in_specs=[vmem] * 4,
        out_specs=[vmem] * 2,
        compiler_params=params(16),
        cost_estimate=cost(1000, 1000),
        name="relay_sums",
    )(up, down, from_down, from_up)


def log_rows(logs):
    out = jnp.full((HEADS, HEAD_SIZE), LOW, F32)
    for g in range(GROUPS):
        out = put_lane(out, g, logs[g * HEADS : (g + 1) * HEADS])
    return out


POOL_PAGES = 4


def page_kernel(slots, alive, query, *refs):
    pages, out = refs[:POOL_PAGES], refs[POOL_PAGES]
    step = pl.program_id(0)
    scores = []
    for k in range(POOL_PAGES):
        for g in range(GROUPS):
            keys = pages[k][0, :, g * HEAD_SIZE : (g + 1) * HEAD_SIZE]
            scores.append(nt_dot(query[k, g * HEADS : (g + 1) * HEADS], keys))
    scores = jnp.concatenate(scores) * SCALE
    top = jnp.max(scores, axis=-1, keepdims=True)
    exponent = jnp.exp(scores - top)
    total = jnp.sum(exponent, axis=-1, keepdims=True)
    logs, share = top + jnp.log(total), 1.0 / total
    for k in range(POOL_PAGES):
        live = alive[step * POOL_PAGES + k] != 0
        for g in range(GROUPS):
            rows = slice(k * QUERY_HEADS + g * HEADS, k * QUERY_HEADS + (g + 1) * HEADS)
            values = pages[k][0, :, KEYS + g * HEAD_SIZE : KEYS + (g + 1) * HEAD_SIZE]
            mixture = jnp.dot(exponent[rows].astype(BF16), values, preferred_element_type=F32)
            out[k, g * HEADS : (g + 1) * HEADS] = jnp.where(live, mixture * share[rows], 0.0)
        mine = log_rows(logs[k * QUERY_HEADS : (k + 1) * QUERY_HEADS])
        out[k, QUERY_HEADS:] = jnp.where(live, mine, LOW)


def pool_attention(slots, alive, queries_all, pool):
    def page_of(k):
        return lambda s, slots, alive: (slots[s * POOL_PAGES + k], 0, 0)

    return pl.pallas_call(
        page_kernel,
        out_shape=jax.ShapeDtypeStruct((SAMPLES, PACK, HEAD_SIZE), F32),
        grid_spec=pltpu.PrefetchScalarGridSpec(
            num_scalar_prefetch=2,
            grid=(SAMPLES // POOL_PAGES,),
            in_specs=[
                pl.BlockSpec(
                    (POOL_PAGES, QUERY_HEADS, HEAD_SIZE), lambda s, slots, alive: (s, 0, 0)
                )
            ]
            + [pl.BlockSpec((1, PAGE, KVW), page_of(k)) for k in range(POOL_PAGES)],
            out_specs=pl.BlockSpec(
                (POOL_PAGES, PACK, HEAD_SIZE), lambda s, slots, alive: (s, 0, 0)
            ),
        ),
        compiler_params=params(16),
        cost_estimate=cost(1000, 1000),
        name="pool_attention",
    )(slots, alive, queries_all, *[pool] * POOL_PAGES)


LOCAL_PAGES = 4


def local_kernel(pages_alive, query, new, pages, out, top_ref, sum_ref, mix_ref):
    step = pl.program_id(0)
    width = LOCAL_PAGES * PAGE

    @pl.when(step == 0)
    def _():
        for g in range(GROUPS):
            rows = slice(g * HEADS, (g + 1) * HEADS)
            lanes = slice(g * HEAD_SIZE, (g + 1) * HEAD_SIZE)
            value_lanes = slice(KEYS + g * HEAD_SIZE, KEYS + (g + 1) * HEAD_SIZE)
            products = query[rows].astype(F32) * new[0:1, lanes].astype(F32)
            top_ref[rows] = jnp.sum(products, axis=-1, keepdims=True) * SCALE
            sum_ref[rows] = jnp.ones((HEADS, 1), F32)
            mix_ref[rows] = jnp.broadcast_to(new[0:1, value_lanes].astype(F32), (HEADS, HEAD_SIZE))

    @pl.when(step * LOCAL_PAGES < pages_alive[0])
    def _():
        block = pages.reshape(width, KVW)
        at = step * width + lax.broadcasted_iota(jnp.int32, (QUERY_HEADS, width), 1)
        live = at < pages_alive[0] * PAGE
        scores = jnp.concatenate(
            [
                nt_dot(
                    query[g * HEADS : (g + 1) * HEADS],
                    block[:, g * HEAD_SIZE : (g + 1) * HEAD_SIZE],
                )
                for g in range(GROUPS)
            ]
        )
        scores = jnp.where(live, scores * SCALE, LOW)
        old = top_ref[...]
        top = jnp.maximum(old, jnp.max(scores, axis=-1, keepdims=True))
        shrink = jnp.exp(old - top)
        exponent = jnp.where(live, jnp.exp(scores - top), 0.0)
        top_ref[...] = top
        sum_ref[...] = sum_ref[...] * shrink + jnp.sum(exponent, axis=-1, keepdims=True)
        for g in range(GROUPS):
            rows = slice(g * HEADS, (g + 1) * HEADS)
            values = block[:, KEYS + g * HEAD_SIZE : KEYS + (g + 1) * HEAD_SIZE]
            mix_ref[rows] = mix_ref[rows] * shrink[rows] + jnp.dot(
                exponent[rows].astype(BF16), values, preferred_element_type=F32
            )

    @pl.when(step == CMAX // LOCAL_PAGES - 1)
    def _():
        out[:QUERY_HEADS] = mix_ref[...] / sum_ref[...]
        out[QUERY_HEADS:] = log_rows(top_ref[...] + jnp.log(sum_ref[...]))


def local_attention(pages_alive, query, new, pages):
    def block_of(step, alive):
        last = jnp.maximum(alive[0] - 1, 0) // LOCAL_PAGES
        return (jnp.minimum(step, last), 0, 0)

    return pl.pallas_call(
        local_kernel,
        out_shape=jax.ShapeDtypeStruct((PACK, HEAD_SIZE), F32),
        grid_spec=pltpu.PrefetchScalarGridSpec(
            num_scalar_prefetch=1,
            grid=(CMAX // LOCAL_PAGES,),
            in_specs=[
                pl.BlockSpec((QUERY_HEADS, HEAD_SIZE), lambda step, alive: (0, 0)),
                pl.BlockSpec((1, KVW), lambda step, alive: (0, 0)),
                pl.BlockSpec((LOCAL_PAGES, PAGE, KVW), block_of),
            ],
            out_specs=pl.BlockSpec((PACK, HEAD_SIZE), lambda step, alive: (0, 0)),
            scratch_shapes=[
                pltpu.VMEM((QUERY_HEADS, 1), F32),
                pltpu.VMEM((QUERY_HEADS, 1), F32),
                pltpu.VMEM((QUERY_HEADS, HEAD_SIZE), F32),
            ],
        ),
        compiler_params=params(16),
        cost_estimate=cost(1000, 1000),
        name="local_attention",
    )(pages_alive, query, new, pages)


def prefix_kernel(
    prompt_pages, own_l, own_r, up_l, up_r, down_l, down_r, queries, pool, cache, packed
):
    me, prompt = lax.axis_index("sample"), lax.axis_index("prompt")
    z, x = me // 4, lax.rem(me, 4)
    y, core = prompt // 2, lax.rem(prompt, 2)
    near = lax.rem(y + 3 - 2 * core, 4)
    other = lax.rem(y + 1 + 2 * core, 4)
    far = lax.rem(y + 2, 4)
    columns = (
        2 * y + core, 2 * y + 1 - core, 2 * near + core, 2 * near + 1 - core,
        2 * other + 1 - core, 2 * other + core, 2 * far + core, 2 * far + 1 - core,
    )
    for j in range(8):
        lanes = slice((j % 4) * COLUMNS, (j % 4 + 1) * COLUMNS)
        own, up, down = (own_l, up_l, down_l) if j < 4 else (own_r, up_r, down_r)
        total = own[:, lanes] + up[:, lanes].astype(F32) + down[:, lanes].astype(F32)
        target = pl.ds(pl.multiple_of(columns[j] * COLUMNS, COLUMNS), COLUMNS)
        cache[0, :, target] = total.astype(BF16)
    sources = [
        lax.rem(z + 4 - dz, 4) * 4 + lax.rem(x + 4 - dx, 4) for dx in STEPS for dz in STEPS
    ]
    live = lax.broadcasted_iota(jnp.int32, (SAMPLES * HEADS, ROWS), 1) < prompt_pages[0] * PAGE - me * ROWS
    logs = jnp.full((SAMPLES * HEADS, HEAD_SIZE), LOW, F32)
    for g in range(GROUPS):
        keys = cache[0, :, g * HEAD_SIZE : (g + 1) * HEAD_SIZE]
        values = cache[0, :, KEYS + g * HEAD_SIZE : KEYS + (g + 1) * HEAD_SIZE]
        scores = jnp.where(live, nt_dot(queries[g], keys) * SCALE, LOW)
        top = jnp.max(scores, axis=-1, keepdims=True)
        exponent = jnp.where(live, jnp.exp(scores - top), 0.0)
        total = jnp.sum(exponent, axis=-1, keepdims=True)
        mixture = jnp.dot(exponent.astype(BF16), values, preferred_element_type=F32)
        some = total > 0.0
        total = jnp.where(some, total, 1.0)
        log = jnp.where(some, top + jnp.log(total), LOW)
        rows = slice(g * HEADS, (g + 1) * HEADS)
        pool_log = pool[:, QUERY_HEADS:, g : g + 1].reshape(SAMPLES * HEADS, 1)
        pool_mixture = pool[:, rows].reshape(SAMPLES * HEADS, HEAD_SIZE)
        high = jnp.maximum(log, pool_log)
        here, there = jnp.exp(log - high), jnp.exp(pool_log - high)
        both = here + there
        merged = mixture * (here / (total * both)) + pool_mixture * (there / both)
        for r, source in enumerate(sources):
            packed[source, rows] = merged[r * HEADS : (r + 1) * HEADS].astype(BF16)
        logs = put_lane(logs, g, high + jnp.log(both))
    first = logs.astype(BF16).astype(F32)
    second = (logs - first).astype(BF16).astype(F32)
    third = logs - first - second
    terms = jnp.zeros((SAMPLES * HEADS, HEAD_SIZE), F32)
    for g in range(GROUPS):
        for t, term in enumerate((first, second, third)):
            terms = put_lane(terms, t * GROUPS + g, term[:, g : g + 1])
    padding = jnp.zeros((SENT - QUERY_HEADS - HEADS, HEAD_SIZE), F32)
    for r, source in enumerate(sources):
        rows = jnp.concatenate([terms[r * HEADS : (r + 1) * HEADS], padding])
        packed[source, QUERY_HEADS:] = rows.astype(BF16)


def prefix_attention(prompt_pages, parts, queries, pool):
    smem, vmem = pl.BlockSpec(memory_space=pltpu.SMEM), pl.BlockSpec(memory_space=pltpu.VMEM)
    return pl.pallas_call(
        prefix_kernel,
        out_shape=[
            jax.ShapeDtypeStruct((1, ROWS, KVW), BF16),
            jax.ShapeDtypeStruct((SAMPLES, SENT, HEAD_SIZE), BF16),
        ],
        in_specs=[smem] + [vmem] * 8,
        out_specs=[vmem, vmem],
        compiler_params=params(20),
        cost_estimate=cost(300_000_000, 6 * MIB),
        name="prefix_attention",
    )(prompt_pages, *parts, queries, pool)


def combine_kernel(arrived, local, out):
    terms = arrived[:, QUERY_HEADS:].astype(F32)
    for g in range(GROUPS):
        rows = slice(g * HEADS, (g + 1) * HEADS)
        logs = sum(terms[:, :HEADS, lane : lane + 1] for lane in (g, g + GROUPS, g + 2 * GROUPS))
        local_log = local[QUERY_HEADS:, g : g + 1]
        high = jnp.maximum(jnp.max(logs, axis=0), local_log)
        shares = jnp.exp(logs - high[None])
        local_share = jnp.exp(local_log - high)
        total = jnp.sum(shares, axis=0) + local_share
        mixture = jnp.sum(arrived[:, rows].astype(F32) * shares, axis=0) + local[rows] * local_share
        out[rows] = (mixture / total).astype(BF16)


def combine(arrived, local):
    vmem = pl.BlockSpec(memory_space=pltpu.VMEM)
    return pl.pallas_call(
        combine_kernel,
        out_shape=jax.ShapeDtypeStruct((QUERY_HEADS, HEAD_SIZE), BF16),
        in_specs=[vmem, vmem],
        out_specs=vmem,
        compiler_params=params(16),
        cost_estimate=cost(1_000_000, MIB),
        name="combine",
    )(arrived, local)


def per_device(
    prompt_states,
    kv_weight,
    queries,
    new_kv,
    local_pages,
    pool_pages,
    prompt_pages,
    comp_pages,
    preempted,
    page_where,
):
    tie = lax.optimization_barrier

    weight_far = lax.ppermute(kv_weight, "sample", X_FAR)
    weight_right = lax.ppermute(kv_weight, "sample", X_RIGHT)
    weight_left = lax.ppermute(kv_weight, "sample", X_LEFT)
    block, query = prepare(queries, page_where, comp_pages, preempted)
    states = prompt_states.reshape(4, 4, ROWS, SLICE)
    own_states, to_far = pick_far(states)
    slices, own_states, to_far, block = tie(
        ((kv_weight, weight_right, weight_left, weight_far), own_states, to_far, block)
    )
    blocks = [block] + [lax.ppermute(block, "sample", to) for to in (Z_UP, Z_DOWN, Z_FAR)]
    to_right, to_left, last_far = pick_near(states, blocks)
    rows_far = lax.ppermute(to_far, "sample", X_FAR)
    rows_right = lax.ppermute(to_right, "sample", X_RIGHT)
    rows_left = lax.ppermute(to_left, "sample", X_LEFT)

    here = jnp.stack(slices)
    near = lax.ppermute(here, "prompt", Y_SPLIT)
    here_other = lax.ppermute(here, "prompt", SWAP)
    near_other = lax.ppermute(here_other, "prompt", Y_SPLIT)
    near, near_other, rows_far = tie((near, near_other, rows_far))
    far = lax.ppermute(near, "prompt", Y_SPLIT)
    near_swapped = lax.ppermute(near, "prompt", SWAP)
    near_other_swapped = lax.ppermute(near_other, "prompt", SWAP)
    far, rows_right, rows_left = tie((far, rows_right, rows_left))
    far_other = lax.ppermute(far, "prompt", SWAP)
    others = [own_states, rows_right, rows_left, rows_far]
    pieces = [
        here, here_other, near, near_other,
        near_swapped, near_other_swapped, far, far_other,
    ]

    far_l, far_r = product_far(others, pieces)
    last_far, rows_right = tie((last_far, rows_right))
    last_far = lax.ppermute(last_far, "sample", X_FAR)
    from_down = lax.ppermute(far_l, "sample", Z_UP)
    from_up = lax.ppermute(far_r, "sample", Z_DOWN)
    up_l, up_r, down_l, down_r = product(others, pieces, ((1,) * 4, (2,) * 4), BF16, "product_near")
    up_r, down_l = lax.ppermute(up_r, "sample", Z_UP), lax.ppermute(down_l, "sample", Z_DOWN)
    up_l, down_r = relay(up_l, down_r, from_down, from_up)
    sums = [
        lax.ppermute(up_l, "sample", Z_UP),
        up_r,
        down_l,
        lax.ppermute(down_r, "sample", Z_DOWN),
    ]

    query, up_l = tie((query, up_l))
    local_alive = jnp.where(preempted[0] > 0, 0, comp_pages[0])
    local = local_attention(local_alive, query, new_kv[0], local_pages[0, 0])
    arrived, local = tie(([rows_right, rows_left, last_far], local))
    queries_all, by_group, slots, alive = unpack(blocks, arrived)
    pool = pool_attention(slots, alive, queries_all, pool_pages[0, 0])
    mine, pool, local = tie(([own_states, *arrived], pool, local))
    sums = [*product(mine, pieces, ((3, 3, 3, 0),), F32, "product_own"), *sums]

    cache, packed = prefix_attention(prompt_pages, sums, by_group, pool)
    arrived = lax.all_to_all(packed, "sample", split_axis=0, concat_axis=0, tiled=True)
    attended = combine(arrived, local)
    return (cache, attended.reshape(1, 1, -1))


def solution(mesh):
    return jax.shard_map(
        per_device,
        mesh=mesh,
        in_specs=(
            P("prompt", None, "sample"),
            P("sample", "prompt"),
            P("prompt", "sample", None),
            P("prompt", "sample", None),
            P("prompt", "sample", None, None, None),
            P("prompt", "sample", None, None, None),
            P("prompt"),
            P("prompt", "sample"),
            P("prompt", "sample"),
            P("prompt", "sample", None),
        ),
        out_specs=(P("prompt", "sample", None), P("prompt", "sample", None)),
        check_vma=False,
    )
```

```python
import functools
import math

import jax
import jax.numpy as jnp
from jax import lax
from jax.experimental import pallas as pl
from jax.experimental.pallas import tpu as pltpu
from jax.sharding import PartitionSpec as P

QUERY_HEADS = 64
GROUPS = 8
HEADS = 8
HEAD_SIZE = 128
PAGE = 128
SAMPLES = 16
CMAX = 16
ROWS = 256
SLICE = 512
COLUMNS = 256
KVW = 2048
KEYS = GROUPS * HEAD_SIZE
PACK = QUERY_HEADS + HEADS
SENT = QUERY_HEADS + 16
LOW = -1e30
SCALE = 1.0 / math.sqrt(HEAD_SIZE)
MIB = 1 << 20
F32 = jnp.float32
BF16 = jnp.bfloat16

X_RIGHT = [(z * 4 + x, z * 4 + (x + 1) % 4) for z in range(4) for x in range(4)]
X_LEFT = [(z * 4 + x, z * 4 + (x + 3) % 4) for z in range(4) for x in range(4)]
X_FAR = [(z * 4 + x, z * 4 + (x + 2) % 4) for z in range(4) for x in range(4)]
Z_UP = [(z * 4 + x, (z + 1) % 4 * 4 + x) for z in range(4) for x in range(4)]
Z_DOWN = [(z * 4 + x, (z + 3) % 4 * 4 + x) for z in range(4) for x in range(4)]
Z_FAR = [(z * 4 + x, (z + 2) % 4 * 4 + x) for z in range(4) for x in range(4)]
SWAP = [(y * 2 + c, y * 2 + 1 - c) for y in range(4) for c in range(2)]
Y_SPLIT = [(y * 2 + c, (y + (1 if c == 0 else 3)) % 4 * 2 + c) for y in range(4) for c in range(2)]


def params(mib):
    return pltpu.CompilerParams(vmem_limit_bytes=mib * MIB)


def cost(flops, bytes_accessed):
    return pl.CostEstimate(flops=flops, bytes_accessed=bytes_accessed, transcendentals=0)


def nt_dot(a, b):
    return lax.dot_general(a, b, (((1,), (1,)), ((), ())), preferred_element_type=F32)


def put_lane(running, lane, column):
    at = lax.broadcasted_iota(jnp.int32, running.shape, len(running.shape) - 1)
    return jnp.where(at == lane, column, running)


HALF = QUERY_HEADS // 2
BLOCK = HALF + 8


def prepare_kernel(where, length, flag, query, sent, own):
    heads = [query[0, 0:1, h * HEAD_SIZE : (h + 1) * HEAD_SIZE].astype(F32) for h in range(QUERY_HEADS)]
    low, high = jnp.concatenate(heads[:HALF]), jnp.concatenate(heads[HALF:])
    own[:HALF] = low.astype(BF16)
    own[HALF:] = high.astype(BF16)
    sent[:HALF, :HEAD_SIZE] = low.astype(BF16)
    sent[:HALF, HEAD_SIZE:] = high.astype(BF16)
    plan = jnp.zeros((8, COLUMNS), F32)
    for c in range(CMAX):
        plan = put_lane(plan, c, where[0, 0, c].astype(F32))
    plan = put_lane(plan, CMAX, length[0, 0].astype(F32))
    plan = put_lane(plan, CMAX + 1, flag[0, 0].astype(F32))
    sent[HALF:] = plan.astype(BF16)


def prepare(query, where, length, flag):
    smem, vmem = pl.BlockSpec(memory_space=pltpu.SMEM), pl.BlockSpec(memory_space=pltpu.VMEM)
    return pl.pallas_call(
        prepare_kernel,
        out_shape=[
            jax.ShapeDtypeStruct((BLOCK, COLUMNS), BF16),
            jax.ShapeDtypeStruct((QUERY_HEADS, HEAD_SIZE), BF16),
        ],
        in_specs=[smem] * 3 + [vmem],
        out_specs=[vmem, vmem],
        compiler_params=params(16),
        cost_estimate=cost(1000, 1000),
        name="prepare",
    )(where, length, flag, query)


def unpack_kernel(*refs):
    own, arrived, (queries, by_group, slots, alive) = refs[:4], refs[4:7], refs[7:]
    me = lax.axis_index("sample")

    def block_of(r):
        if r < 4:
            return own[r][...].astype(F32)
        source = arrived[r // 4 - 1]
        first = source.shape[0] - 2 * BLOCK + r % 4 // 2 * BLOCK
        lanes = slice(r % 2 * COLUMNS, (r % 2 + 1) * COLUMNS)
        return source[first : first + BLOCK, lanes].astype(F32)

    plans = []
    for r in range(SAMPLES):
        block = block_of(r)
        for half in range(2):
            lanes = slice(half * HEAD_SIZE, (half + 1) * HEAD_SIZE)
            queries[r, half * HALF : (half + 1) * HALF] = block[:HALF, lanes].astype(BF16)
        plans.append(block[HALF : HALF + 1])
    for g in range(GROUPS):
        lanes = slice(g // 4 * HEAD_SIZE, (g // 4 + 1) * HEAD_SIZE)
        rows = slice(g % 4 * HEADS, (g % 4 + 1) * HEADS)
        parts = [block_of(r)[rows, lanes] for r in range(SAMPLES)]
        by_group[g] = jnp.concatenate(parts).astype(BF16)
    plan = jnp.concatenate(plans)
    lane = lax.broadcasted_iota(jnp.int32, plan.shape, 1)
    first = (me * CMAX).astype(F32)
    here = (lane < CMAX) & (plan >= first) & (plan < first + CMAX)
    live = here & (lane.astype(F32) < plan[:, CMAX : CMAX + 1]) & (plan[:, CMAX + 1 : CMAX + 2] > 0.5)
    slot = jnp.sum(jnp.where(here, plan - first, 0.0), axis=1, keepdims=True).astype(jnp.int32)
    some = jnp.max(jnp.where(live, 1.0, 0.0), axis=1, keepdims=True).astype(jnp.int32)
    for r in range(SAMPLES):
        slots[r] = slot[r, 0]
        alive[r] = some[r, 0]


def unpack(own, arrived):
    smem, vmem = pl.BlockSpec(memory_space=pltpu.SMEM), pl.BlockSpec(memory_space=pltpu.VMEM)
    return pl.pallas_call(
        unpack_kernel,
        out_shape=[
            jax.ShapeDtypeStruct((SAMPLES, QUERY_HEADS, HEAD_SIZE), BF16),
            jax.ShapeDtypeStruct((GROUPS, SAMPLES * HEADS, HEAD_SIZE), BF16),
            jax.ShapeDtypeStruct((SAMPLES,), jnp.int32),
            jax.ShapeDtypeStruct((SAMPLES,), jnp.int32),
        ],
        in_specs=[vmem] * 7,
        out_specs=[vmem, vmem, smem, smem],
        compiler_params=params(16),
        cost_estimate=cost(1000, 1000),
        name="unpack",
    )(*own, *arrived)


STEPS = (0, 1, 3, 2)
NEXT = (2, 1, 3, 0)


def copy_rows(states, sems, wanted):
    me = lax.axis_index("sample")
    z, x = me // 4, lax.rem(me, 4)
    copies = [
        pltpu.make_async_copy(
            states.at[lax.rem(z + NEXT[k], 4), lax.rem(x + step, 4)], target, sems.at[n]
        )
        for n, (step, k, target) in enumerate(wanted)
    ]
    for copy in copies:
        copy.start()
    return copies


def block_rows(k):
    return pl.ds(k * ROWS, ROWS)


def pick_far_kernel(states, own, far, sems):
    wanted = [(2, k, far.at[block_rows(k)]) for k in range(3)]
    wanted += [(0, k, own.at[block_rows(k)]) for k in range(4)]
    for copy in copy_rows(states, sems, wanted):
        copy.wait()


def pick_far(states):
    vmem = pl.BlockSpec(memory_space=pltpu.VMEM)
    return pl.pallas_call(
        pick_far_kernel,
        out_shape=[
            jax.ShapeDtypeStruct((4 * ROWS, SLICE), BF16),
            jax.ShapeDtypeStruct((3 * ROWS, SLICE), BF16),
        ],
        in_specs=[pl.BlockSpec(memory_space=pl.ANY)],
        out_specs=[vmem] * 2,
        scratch_shapes=[pltpu.SemaphoreType.DMA((7,))],
        compiler_params=params(50),
        cost_estimate=cost(1000, 1000),
        name="pick_far",
    )(states)


def put_blocks(target, first, blocks):
    for r, block in enumerate(blocks):
        rows = slice(first + r // 2 * BLOCK, first + (r // 2 + 1) * BLOCK)
        target[rows, r % 2 * COLUMNS : (r % 2 + 1) * COLUMNS] = block[...]


def pick_near_kernel(states, *refs):
    blocks, (first_right, first_left, right, left, last), sems = refs[:4], refs[4:9], refs[9]
    wanted = [(1, 0, first_right), (3, 0, first_left)]
    wanted += [(1, k + 1, right.at[block_rows(k)]) for k in range(3)]
    wanted += [(3, k + 1, left.at[block_rows(k)]) for k in range(3)]
    wanted += [(2, 3, last.at[block_rows(0)])]
    copies = copy_rows(states, sems, wanted)
    put_blocks(right, 3 * ROWS, blocks)
    put_blocks(left, 3 * ROWS, blocks)
    put_blocks(last, ROWS, blocks)
    for copy in copies:
        copy.wait()


def pick_near(states, blocks):
    vmem = pl.BlockSpec(memory_space=pltpu.VMEM)
    return pl.pallas_call(
        pick_near_kernel,
        out_shape=[jax.ShapeDtypeStruct((ROWS, SLICE), BF16)] * 2
        + [jax.ShapeDtypeStruct((3 * ROWS + 2 * BLOCK, SLICE), BF16)] * 2
        + [jax.ShapeDtypeStruct((ROWS + 2 * BLOCK, SLICE), BF16)],
        in_specs=[pl.BlockSpec(memory_space=pl.ANY)] + [vmem] * 4,
        out_specs=[vmem] * 5,
        scratch_shapes=[pltpu.SemaphoreType.DMA((9,))],
        compiler_params=params(44),
        cost_estimate=cost(1000, 1000),
        name="pick_near",
    )(states, *blocks)


def weight_of(pieces, j, d):
    return pieces[j][d] if j < 7 else pieces[7 + d // 2][d % 2]


def product_kernel(blocks, *refs):
    states, pieces, outs = refs[:4], refs[4:13], refs[13:]
    for j in range(8):
        for k, block in enumerate(blocks):
            total = jnp.zeros((ROWS, COLUMNS), F32)
            for d in range(4):
                at = block[d] * ROWS
                total += jnp.dot(
                    states[d][at : at + ROWS], weight_of(pieces, j, d), preferred_element_type=F32
                )
            out = outs[2 * k + j // 4]
            out[:, (j % 4) * COLUMNS : (j % 4 + 1) * COLUMNS] = total.astype(out.dtype)


def product(states, pieces, blocks, kind, name):
    vmem = pl.BlockSpec(memory_space=pltpu.VMEM)
    outs = [jax.ShapeDtypeStruct((ROWS, KVW // 2), kind)] * (2 * len(blocks))
    return pl.pallas_call(
        functools.partial(product_kernel, blocks),
        out_shape=outs,
        in_specs=[vmem] * 13,
        out_specs=[vmem] * len(outs),
        compiler_params=params(20),
        cost_estimate=cost(1000, 1000),
        name=name,
    )(*states, *pieces)


def product_far_kernel(*refs):
    states, pieces, outs = refs[:4], refs[4:13], refs[13:]
    for j in range(8):
        total = jnp.zeros((ROWS, COLUMNS), F32)
        for d in range(4):
            total += jnp.dot(
                states[d][:ROWS], weight_of(pieces, j, d), preferred_element_type=F32
            )
        outs[j // 4][:, (j % 4) * COLUMNS : (j % 4 + 1) * COLUMNS] = total.astype(BF16)


def product_far(states, pieces):
    vmem = pl.BlockSpec(memory_space=pltpu.VMEM)
    return pl.pallas_call(
        product_far_kernel,
        out_shape=[jax.ShapeDtypeStruct((ROWS, KVW // 2), BF16)] * 2,
        in_specs=[vmem] * 13,
        out_specs=[vmem] * 2,
        compiler_params=params(20),
        cost_estimate=cost(1000, 1000),
        name="product_far",
    )(*states, *pieces)


def relay_kernel(up, down, from_down, from_up, up_out, down_out):
    up_out[...] = (up[...].astype(F32) + from_down[...].astype(F32)).astype(BF16)
    down_out[...] = (down[...].astype(F32) + from_up[...].astype(F32)).astype(BF16)


def relay(up, down, from_down, from_up):
    vmem = pl.BlockSpec(memory_space=pltpu.VMEM)
    return pl.pallas_call(
        relay_kernel,
        out_shape=[jax.ShapeDtypeStruct((ROWS, KVW // 2), BF16)] * 2,
        in_specs=[vmem] * 4,
        out_specs=[vmem] * 2,
        compiler_params=params(16),
        cost_estimate=cost(1000, 1000),
        name="relay_sums",
    )(up, down, from_down, from_up)


def log_rows(logs):
    out = jnp.full((HEADS, HEAD_SIZE), LOW, F32)
    for g in range(GROUPS):
        out = put_lane(out, g, logs[g * HEADS : (g + 1) * HEADS])
    return out


POOL_PAGES = 4


def page_kernel(slots, alive, query, *refs):
    pages, out = refs[:POOL_PAGES], refs[POOL_PAGES]
    step = pl.program_id(0)
    scores = []
    for k in range(POOL_PAGES):
        for g in range(GROUPS):
            keys = pages[k][0, :, g * HEAD_SIZE : (g + 1) * HEAD_SIZE]
            scores.append(nt_dot(query[k, g * HEADS : (g + 1) * HEADS], keys))
    scores = jnp.concatenate(scores) * SCALE
    top = jnp.max(scores, axis=-1, keepdims=True)
    exponent = jnp.exp(scores - top)
    total = jnp.sum(exponent, axis=-1, keepdims=True)
    logs, share = top + jnp.log(total), 1.0 / total
    for k in range(POOL_PAGES):
        live = alive[step * POOL_PAGES + k] != 0
        for g in range(GROUPS):
            rows = slice(k * QUERY_HEADS + g * HEADS, k * QUERY_HEADS + (g + 1) * HEADS)
            values = pages[k][0, :, KEYS + g * HEAD_SIZE : KEYS + (g + 1) * HEAD_SIZE]
            mixture = jnp.dot(exponent[rows].astype(BF16), values, preferred_element_type=F32)
            out[k, g * HEADS : (g + 1) * HEADS] = jnp.where(live, mixture * share[rows], 0.0)
        mine = log_rows(logs[k * QUERY_HEADS : (k + 1) * QUERY_HEADS])
        out[k, QUERY_HEADS:] = jnp.where(live, mine, LOW)


def pool_attention(slots, alive, queries_all, pool):
    def page_of(k):
        return lambda s, slots, alive: (slots[s * POOL_PAGES + k], 0, 0)

    return pl.pallas_call(
        page_kernel,
        out_shape=jax.ShapeDtypeStruct((SAMPLES, PACK, HEAD_SIZE), F32),
        grid_spec=pltpu.PrefetchScalarGridSpec(
            num_scalar_prefetch=2,
            grid=(SAMPLES // POOL_PAGES,),
            in_specs=[
                pl.BlockSpec(
                    (POOL_PAGES, QUERY_HEADS, HEAD_SIZE), lambda s, slots, alive: (s, 0, 0)
                )
            ]
            + [pl.BlockSpec((1, PAGE, KVW), page_of(k)) for k in range(POOL_PAGES)],
            out_specs=pl.BlockSpec(
                (POOL_PAGES, PACK, HEAD_SIZE), lambda s, slots, alive: (s, 0, 0)
            ),
        ),
        compiler_params=params(16),
        cost_estimate=cost(1000, 1000),
        name="pool_attention",
    )(slots, alive, queries_all, *[pool] * POOL_PAGES)


LOCAL_PAGES = 4


def local_kernel(pages_alive, query, new, pages, out, top_ref, sum_ref, mix_ref):
    step = pl.program_id(0)
    width = LOCAL_PAGES * PAGE

    @pl.when(step == 0)
    def _():
        for g in range(GROUPS):
            rows = slice(g * HEADS, (g + 1) * HEADS)
            lanes = slice(g * HEAD_SIZE, (g + 1) * HEAD_SIZE)
            value_lanes = slice(KEYS + g * HEAD_SIZE, KEYS + (g + 1) * HEAD_SIZE)
            products = query[rows].astype(F32) * new[0:1, lanes].astype(F32)
            top_ref[rows] = jnp.sum(products, axis=-1, keepdims=True) * SCALE
            sum_ref[rows] = jnp.ones((HEADS, 1), F32)
            mix_ref[rows] = jnp.broadcast_to(new[0:1, value_lanes].astype(F32), (HEADS, HEAD_SIZE))

    @pl.when(step * LOCAL_PAGES < pages_alive[0])
    def _():
        block = pages.reshape(width, KVW)
        at = step * width + lax.broadcasted_iota(jnp.int32, (QUERY_HEADS, width), 1)
        live = at < pages_alive[0] * PAGE
        scores = jnp.concatenate(
            [
                nt_dot(
                    query[g * HEADS : (g + 1) * HEADS],
                    block[:, g * HEAD_SIZE : (g + 1) * HEAD_SIZE],
                )
                for g in range(GROUPS)
            ]
        )
        scores = jnp.where(live, scores * SCALE, LOW)
        old = top_ref[...]
        top = jnp.maximum(old, jnp.max(scores, axis=-1, keepdims=True))
        shrink = jnp.exp(old - top)
        exponent = jnp.where(live, jnp.exp(scores - top), 0.0)
        top_ref[...] = top
        sum_ref[...] = sum_ref[...] * shrink + jnp.sum(exponent, axis=-1, keepdims=True)
        for g in range(GROUPS):
            rows = slice(g * HEADS, (g + 1) * HEADS)
            values = block[:, KEYS + g * HEAD_SIZE : KEYS + (g + 1) * HEAD_SIZE]
            mix_ref[rows] = mix_ref[rows] * shrink[rows] + jnp.dot(
                exponent[rows].astype(BF16), values, preferred_element_type=F32
            )

    @pl.when(step == CMAX // LOCAL_PAGES - 1)
    def _():
        out[:QUERY_HEADS] = mix_ref[...] / sum_ref[...]
        out[QUERY_HEADS:] = log_rows(top_ref[...] + jnp.log(sum_ref[...]))


def local_attention(pages_alive, query, new, pages):
    def block_of(step, alive):
        last = jnp.maximum(alive[0] - 1, 0) // LOCAL_PAGES
        return (jnp.minimum(step, last), 0, 0)

    return pl.pallas_call(
        local_kernel,
        out_shape=jax.ShapeDtypeStruct((PACK, HEAD_SIZE), F32),
        grid_spec=pltpu.PrefetchScalarGridSpec(
            num_scalar_prefetch=1,
            grid=(CMAX // LOCAL_PAGES,),
            in_specs=[
                pl.BlockSpec((QUERY_HEADS, HEAD_SIZE), lambda step, alive: (0, 0)),
                pl.BlockSpec((1, KVW), lambda step, alive: (0, 0)),
                pl.BlockSpec((LOCAL_PAGES, PAGE, KVW), block_of),
            ],
            out_specs=pl.BlockSpec((PACK, HEAD_SIZE), lambda step, alive: (0, 0)),
            scratch_shapes=[
                pltpu.VMEM((QUERY_HEADS, 1), F32),
                pltpu.VMEM((QUERY_HEADS, 1), F32),
                pltpu.VMEM((QUERY_HEADS, HEAD_SIZE), F32),
            ],
        ),
        compiler_params=params(16),
        cost_estimate=cost(1000, 1000),
        name="local_attention",
    )(pages_alive, query, new, pages)


def prefix_kernel(
    prompt_pages, own_l, own_r, up_l, up_r, down_l, down_r, queries, pool, cache, packed
):
    me, prompt = lax.axis_index("sample"), lax.axis_index("prompt")
    z, x = me // 4, lax.rem(me, 4)
    y, core = prompt // 2, lax.rem(prompt, 2)
    near = lax.rem(y + 3 - 2 * core, 4)
    other = lax.rem(y + 1 + 2 * core, 4)
    far = lax.rem(y + 2, 4)
    columns = (
        2 * y + core, 2 * y + 1 - core, 2 * near + core, 2 * near + 1 - core,
        2 * other + 1 - core, 2 * other + core, 2 * far + core, 2 * far + 1 - core,
    )
    for j in range(8):
        lanes = slice((j % 4) * COLUMNS, (j % 4 + 1) * COLUMNS)
        own, up, down = (own_l, up_l, down_l) if j < 4 else (own_r, up_r, down_r)
        total = own[:, lanes] + up[:, lanes].astype(F32) + down[:, lanes].astype(F32)
        target = pl.ds(pl.multiple_of(columns[j] * COLUMNS, COLUMNS), COLUMNS)
        cache[0, :, target] = total.astype(BF16)
    sources = [
        lax.rem(z + 4 - dz, 4) * 4 + lax.rem(x + 4 - dx, 4) for dx in STEPS for dz in STEPS
    ]
    live = lax.broadcasted_iota(jnp.int32, (SAMPLES * HEADS, ROWS), 1) < prompt_pages[0] * PAGE - me * ROWS
    logs = jnp.full((SAMPLES * HEADS, HEAD_SIZE), LOW, F32)
    for g in range(GROUPS):
        keys = cache[0, :, g * HEAD_SIZE : (g + 1) * HEAD_SIZE]
        values = cache[0, :, KEYS + g * HEAD_SIZE : KEYS + (g + 1) * HEAD_SIZE]
        scores = jnp.where(live, nt_dot(queries[g], keys) * SCALE, LOW)
        top = jnp.max(scores, axis=-1, keepdims=True)
        exponent = jnp.where(live, jnp.exp(scores - top), 0.0)
        total = jnp.sum(exponent, axis=-1, keepdims=True)
        mixture = jnp.dot(exponent.astype(BF16), values, preferred_element_type=F32)
        some = total > 0.0
        total = jnp.where(some, total, 1.0)
        log = jnp.where(some, top + jnp.log(total), LOW)
        rows = slice(g * HEADS, (g + 1) * HEADS)
        pool_log = pool[:, QUERY_HEADS:, g : g + 1].reshape(SAMPLES * HEADS, 1)
        pool_mixture = pool[:, rows].reshape(SAMPLES * HEADS, HEAD_SIZE)
        high = jnp.maximum(log, pool_log)
        here, there = jnp.exp(log - high), jnp.exp(pool_log - high)
        both = here + there
        merged = mixture * (here / (total * both)) + pool_mixture * (there / both)
        for r, source in enumerate(sources):
            packed[source, rows] = merged[r * HEADS : (r + 1) * HEADS].astype(BF16)
        logs = put_lane(logs, g, high + jnp.log(both))
    first = logs.astype(BF16).astype(F32)
    second = (logs - first).astype(BF16).astype(F32)
    third = logs - first - second
    terms = jnp.zeros((SAMPLES * HEADS, HEAD_SIZE), F32)
    for g in range(GROUPS):
        for t, term in enumerate((first, second, third)):
            terms = put_lane(terms, t * GROUPS + g, term[:, g : g + 1])
    padding = jnp.zeros((SENT - QUERY_HEADS - HEADS, HEAD_SIZE), F32)
    for r, source in enumerate(sources):
        rows = jnp.concatenate([terms[r * HEADS : (r + 1) * HEADS], padding])
        packed[source, QUERY_HEADS:] = rows.astype(BF16)


def prefix_attention(prompt_pages, parts, queries, pool):
    smem, vmem = pl.BlockSpec(memory_space=pltpu.SMEM), pl.BlockSpec(memory_space=pltpu.VMEM)
    return pl.pallas_call(
        prefix_kernel,
        out_shape=[
            jax.ShapeDtypeStruct((1, ROWS, KVW), BF16),
            jax.ShapeDtypeStruct((SAMPLES, SENT, HEAD_SIZE), BF16),
        ],
        in_specs=[smem] + [vmem] * 8,
        out_specs=[vmem, vmem],
        compiler_params=params(20),
        cost_estimate=cost(300_000_000, 6 * MIB),
        name="prefix_attention",
    )(prompt_pages, *parts, queries, pool)


def combine_kernel(arrived, local, out):
    terms = arrived[:, QUERY_HEADS:].astype(F32)
    for g in range(GROUPS):
        rows = slice(g * HEADS, (g + 1) * HEADS)
        logs = sum(terms[:, :HEADS, lane : lane + 1] for lane in (g, g + GROUPS, g + 2 * GROUPS))
        local_log = local[QUERY_HEADS:, g : g + 1]
        high = jnp.maximum(jnp.max(logs, axis=0), local_log)
        shares = jnp.exp(logs - high[None])
        local_share = jnp.exp(local_log - high)
        total = jnp.sum(shares, axis=0) + local_share
        mixture = jnp.sum(arrived[:, rows].astype(F32) * shares, axis=0) + local[rows] * local_share
        mixture = (mixture / total).astype(BF16)
        for h in range(HEADS):
            lanes = slice((g * HEADS + h) * HEAD_SIZE, (g * HEADS + h + 1) * HEAD_SIZE)
            out[0, :, lanes] = mixture[h : h + 1]


def combine(arrived, local):
    vmem = pl.BlockSpec(memory_space=pltpu.VMEM)
    return pl.pallas_call(
        combine_kernel,
        out_shape=jax.ShapeDtypeStruct((1, 1, QUERY_HEADS * HEAD_SIZE), BF16),
        in_specs=[vmem, vmem],
        out_specs=vmem,
        compiler_params=params(16),
        cost_estimate=cost(1_000_000, MIB),
        name="combine",
    )(arrived, local)


def per_device(
    prompt_states,
    kv_weight,
    queries,
    new_kv,
    local_pages,
    pool_pages,
    prompt_pages,
    comp_pages,
    preempted,
    page_where,
):
    tie = lax.optimization_barrier

    weight_far = lax.ppermute(kv_weight, "sample", X_FAR)
    weight_right = lax.ppermute(kv_weight, "sample", X_RIGHT)
    weight_left = lax.ppermute(kv_weight, "sample", X_LEFT)
    block, query = prepare(queries, page_where, comp_pages, preempted)
    states = prompt_states.reshape(4, 4, ROWS, SLICE)
    own_states, to_far = pick_far(states)
    slices, own_states, to_far, block = tie(
        ((kv_weight, weight_right, weight_left, weight_far), own_states, to_far, block)
    )
    blocks = [block] + [lax.ppermute(block, "sample", to) for to in (Z_UP, Z_DOWN, Z_FAR)]
    first_right, first_left, to_right, to_left, last_far = pick_near(states, blocks)
    rows_far = lax.ppermute(to_far, "sample", X_FAR)
    first_right = lax.ppermute(first_right, "sample", X_RIGHT)
    first_left = lax.ppermute(first_left, "sample", X_LEFT)
    rows_right = lax.ppermute(to_right, "sample", X_RIGHT)
    rows_left = lax.ppermute(to_left, "sample", X_LEFT)

    here = jnp.stack(slices)
    near = lax.ppermute(here, "prompt", Y_SPLIT)
    here_other = lax.ppermute(here, "prompt", SWAP)
    near_other = lax.ppermute(here_other, "prompt", Y_SPLIT)
    near, near_other, rows_far, first_right, first_left = tie(
        (near, near_other, rows_far, first_right, first_left)
    )
    far = lax.ppermute(near, "prompt", Y_SPLIT)
    near_swapped = lax.ppermute(near, "prompt", SWAP)
    near_other_swapped = lax.ppermute(near_other, "prompt", SWAP)
    query, near_swapped = tie((query, near_swapped))
    local_alive = jnp.where(preempted[0] > 0, 0, comp_pages[0])
    local = local_attention(local_alive, query, new_kv[0], local_pages[0, 0])
    far, local = tie((far, local))
    far_other = [lax.ppermute(half, "prompt", SWAP) for half in (far[:2], far[2:])]
    pieces = [
        here, here_other, near, near_other,
        near_swapped, near_other_swapped, far, *far_other,
    ]

    first_right, rows_right, rows_left = tie((first_right, rows_right, rows_left))

    far_l, far_r = product_far([own_states, first_right, first_left, rows_far], pieces)
    from_down = lax.ppermute(far_l, "sample", Z_UP)
    from_up = lax.ppermute(far_r, "sample", Z_DOWN)
    last_far, rows_right = tie((last_far, rows_right))
    last_far = lax.ppermute(last_far, "sample", X_FAR)
    others = [own_states, rows_right, rows_left, rows_far]
    up_l, up_r, down_l, down_r = product(
        others, pieces, ((1, 0, 0, 1), (2, 1, 1, 2)), BF16, "product_near"
    )
    up_r, down_l = lax.ppermute(up_r, "sample", Z_UP), lax.ppermute(down_l, "sample", Z_DOWN)
    up_l, down_r = relay(up_l, down_r, from_down, from_up)
    sums = [
        lax.ppermute(up_l, "sample", Z_UP),
        up_r,
        down_l,
        lax.ppermute(down_r, "sample", Z_DOWN),
    ]

    arrived, up_l = tie(([rows_right, rows_left, last_far], up_l))
    queries_all, by_group, slots, alive = unpack(blocks, arrived)
    pool = pool_attention(slots, alive, queries_all, pool_pages[0, 0])
    mine, pool = tie(([own_states, *arrived], pool))
    sums = [*product(mine, pieces, ((3, 2, 2, 0),), F32, "product_own"), *sums]

    cache, packed = prefix_attention(prompt_pages, sums, by_group, pool)
    arrived = lax.all_to_all(packed, "sample", split_axis=0, concat_axis=0, tiled=True)
    attended = combine(arrived, local)
    return (cache, attended)


def solution(mesh):
    return jax.shard_map(
        per_device,
        mesh=mesh,
        in_specs=(
            P("prompt", None, "sample"),
            P("sample", "prompt"),
            P("prompt", "sample", None),
            P("prompt", "sample", None),
            P("prompt", "sample", None, None, None),
            P("prompt", "sample", None, None, None),
            P("prompt"),
            P("prompt", "sample"),
            P("prompt", "sample"),
            P("prompt", "sample", None),
        ),
        out_specs=(P("prompt", "sample", None), P("prompt", "sample", None)),
        check_vma=False,
    )
```

```python
import functools
import math

import jax
import jax.numpy as jnp
from jax import lax
from jax.experimental import pallas as pl
from jax.experimental.pallas import tpu as pltpu
from jax.sharding import PartitionSpec as P

QUERY_HEADS = 64
GROUPS = 8
HEADS = 8
HEAD_SIZE = 128
PAGE = 128
SAMPLES = 16
CMAX = 16
ROWS = 256
SLICE = 512
COLUMNS = 256
KVW = 2048
KEYS = GROUPS * HEAD_SIZE
PACK = QUERY_HEADS + HEADS
SENT = QUERY_HEADS + 16
LOW = -1e30
SCALE = 1.0 / math.sqrt(HEAD_SIZE)
MIB = 1 << 20
F32 = jnp.float32
BF16 = jnp.bfloat16

X_RIGHT = [(z * 4 + x, z * 4 + (x + 1) % 4) for z in range(4) for x in range(4)]
X_LEFT = [(z * 4 + x, z * 4 + (x + 3) % 4) for z in range(4) for x in range(4)]
X_FAR = [(z * 4 + x, z * 4 + (x + 2) % 4) for z in range(4) for x in range(4)]
Z_UP = [(z * 4 + x, (z + 1) % 4 * 4 + x) for z in range(4) for x in range(4)]
Z_DOWN = [(z * 4 + x, (z + 3) % 4 * 4 + x) for z in range(4) for x in range(4)]
Z_FAR = [(z * 4 + x, (z + 2) % 4 * 4 + x) for z in range(4) for x in range(4)]
SWAP = [(y * 2 + c, y * 2 + 1 - c) for y in range(4) for c in range(2)]
Y_SPLIT = [(y * 2 + c, (y + (1 if c == 0 else 3)) % 4 * 2 + c) for y in range(4) for c in range(2)]


def params(mib):
    return pltpu.CompilerParams(vmem_limit_bytes=mib * MIB)


def cost(flops, bytes_accessed):
    return pl.CostEstimate(flops=flops, bytes_accessed=bytes_accessed, transcendentals=0)


def nt_dot(a, b):
    return lax.dot_general(a, b, (((1,), (1,)), ((), ())), preferred_element_type=F32)


def put_lane(running, lane, column):
    at = lax.broadcasted_iota(jnp.int32, running.shape, len(running.shape) - 1)
    return jnp.where(at == lane, column, running)


HALF = QUERY_HEADS // 2
BLOCK = HALF + 8


def prepare_kernel(where, length, flag, query, sent, own):
    heads = [query[0, 0:1, h * HEAD_SIZE : (h + 1) * HEAD_SIZE].astype(F32) for h in range(QUERY_HEADS)]
    low, high = jnp.concatenate(heads[:HALF]), jnp.concatenate(heads[HALF:])
    own[:HALF] = low.astype(BF16)
    own[HALF:] = high.astype(BF16)
    sent[:HALF, :HEAD_SIZE] = low.astype(BF16)
    sent[:HALF, HEAD_SIZE:] = high.astype(BF16)
    plan = jnp.zeros((8, COLUMNS), F32)
    for c in range(CMAX):
        plan = put_lane(plan, c, where[0, 0, c].astype(F32))
    plan = put_lane(plan, CMAX, length[0, 0].astype(F32))
    plan = put_lane(plan, CMAX + 1, flag[0, 0].astype(F32))
    sent[HALF:] = plan.astype(BF16)


def prepare(query, where, length, flag):
    smem, vmem = pl.BlockSpec(memory_space=pltpu.SMEM), pl.BlockSpec(memory_space=pltpu.VMEM)
    return pl.pallas_call(
        prepare_kernel,
        out_shape=[
            jax.ShapeDtypeStruct((BLOCK, COLUMNS), BF16),
            jax.ShapeDtypeStruct((QUERY_HEADS, HEAD_SIZE), BF16),
        ],
        in_specs=[smem] * 3 + [vmem],
        out_specs=[vmem, vmem],
        compiler_params=params(16),
        cost_estimate=cost(1000, 1000),
        name="prepare",
    )(where, length, flag, query)


def unpack_kernel(*refs):
    own, arrived, (queries, by_group, slots, alive) = refs[:4], refs[4:7], refs[7:]
    me = lax.axis_index("sample")

    def block_of(r):
        if r < 4:
            return own[r][...].astype(F32)
        source = arrived[r // 4 - 1]
        first = source.shape[0] - 2 * BLOCK + r % 4 // 2 * BLOCK
        lanes = slice(r % 2 * COLUMNS, (r % 2 + 1) * COLUMNS)
        return source[first : first + BLOCK, lanes].astype(F32)

    plans = []
    for r in range(SAMPLES):
        block = block_of(r)
        for half in range(2):
            lanes = slice(half * HEAD_SIZE, (half + 1) * HEAD_SIZE)
            queries[r, half * HALF : (half + 1) * HALF] = block[:HALF, lanes].astype(BF16)
        plans.append(block[HALF : HALF + 1])
    for g in range(GROUPS):
        lanes = slice(g // 4 * HEAD_SIZE, (g // 4 + 1) * HEAD_SIZE)
        rows = slice(g % 4 * HEADS, (g % 4 + 1) * HEADS)
        parts = [block_of(r)[rows, lanes] for r in range(SAMPLES)]
        by_group[g] = jnp.concatenate(parts).astype(BF16)
    plan = jnp.concatenate(plans)
    lane = lax.broadcasted_iota(jnp.int32, plan.shape, 1)
    first = (me * CMAX).astype(F32)
    here = (lane < CMAX) & (plan >= first) & (plan < first + CMAX)
    live = here & (lane.astype(F32) < plan[:, CMAX : CMAX + 1]) & (plan[:, CMAX + 1 : CMAX + 2] > 0.5)
    slot = jnp.sum(jnp.where(here, plan - first, 0.0), axis=1, keepdims=True).astype(jnp.int32)
    some = jnp.max(jnp.where(live, 1.0, 0.0), axis=1, keepdims=True).astype(jnp.int32)
    for r in range(SAMPLES):
        slots[r] = slot[r, 0]
        alive[r] = some[r, 0]


def unpack(own, arrived):
    smem, vmem = pl.BlockSpec(memory_space=pltpu.SMEM), pl.BlockSpec(memory_space=pltpu.VMEM)
    return pl.pallas_call(
        unpack_kernel,
        out_shape=[
            jax.ShapeDtypeStruct((SAMPLES, QUERY_HEADS, HEAD_SIZE), BF16),
            jax.ShapeDtypeStruct((GROUPS, SAMPLES * HEADS, HEAD_SIZE), BF16),
            jax.ShapeDtypeStruct((SAMPLES,), jnp.int32),
            jax.ShapeDtypeStruct((SAMPLES,), jnp.int32),
        ],
        in_specs=[vmem] * 7,
        out_specs=[vmem, vmem, smem, smem],
        compiler_params=params(16),
        cost_estimate=cost(1000, 1000),
        name="unpack",
    )(*own, *arrived)


STEPS = (0, 1, 3, 2)
NEXT = (2, 1, 3, 0)


def copy_rows(states, sems, wanted):
    me = lax.axis_index("sample")
    z, x = me // 4, lax.rem(me, 4)
    copies = [
        pltpu.make_async_copy(
            states.at[lax.rem(z + NEXT[k], 4), lax.rem(x + step, 4)], target, sems.at[n]
        )
        for n, (step, k, target) in enumerate(wanted)
    ]
    for copy in copies:
        copy.start()
    return copies


def block_rows(k):
    return pl.ds(k * ROWS, ROWS)


def pick_far_kernel(states, own, far, sems):
    wanted = [(2, k, far.at[block_rows(k)]) for k in range(3)]
    wanted += [(0, k, own.at[block_rows(k)]) for k in range(4)]
    for copy in copy_rows(states, sems, wanted):
        copy.wait()


def pick_far(states):
    vmem = pl.BlockSpec(memory_space=pltpu.VMEM)
    return pl.pallas_call(
        pick_far_kernel,
        out_shape=[
            jax.ShapeDtypeStruct((4 * ROWS, SLICE), BF16),
            jax.ShapeDtypeStruct((3 * ROWS, SLICE), BF16),
        ],
        in_specs=[pl.BlockSpec(memory_space=pl.ANY)],
        out_specs=[vmem] * 2,
        scratch_shapes=[pltpu.SemaphoreType.DMA((7,))],
        compiler_params=params(50),
        cost_estimate=cost(1000, 1000),
        name="pick_far",
    )(states)


def put_blocks(target, first, blocks):
    for r, block in enumerate(blocks):
        rows = slice(first + r // 2 * BLOCK, first + (r // 2 + 1) * BLOCK)
        target[rows, r % 2 * COLUMNS : (r % 2 + 1) * COLUMNS] = block[...]


def pick_near_kernel(states, *refs):
    blocks, (right, left, last_far), sems = refs[:4], refs[4:7], refs[7]
    wanted = [(1, k, right.at[block_rows(k)]) for k in range(4)]
    wanted += [(3, k, left.at[block_rows(k)]) for k in range(4)]
    wanted += [(2, 3, last_far.at[block_rows(0)])]
    copies = copy_rows(states, sems, wanted)
    put_blocks(right, 4 * ROWS, blocks)
    put_blocks(left, 4 * ROWS, blocks)
    put_blocks(last_far, ROWS, blocks)
    for copy in copies:
        copy.wait()


def pick_near(states, blocks):
    vmem = pl.BlockSpec(memory_space=pltpu.VMEM)
    return pl.pallas_call(
        pick_near_kernel,
        out_shape=[jax.ShapeDtypeStruct((4 * ROWS + 2 * BLOCK, SLICE), BF16)] * 2
        + [jax.ShapeDtypeStruct((ROWS + 2 * BLOCK, SLICE), BF16)],
        in_specs=[pl.BlockSpec(memory_space=pl.ANY)] + [vmem] * 4,
        out_specs=[vmem] * 3,
        scratch_shapes=[pltpu.SemaphoreType.DMA((9,))],
        compiler_params=params(44),
        cost_estimate=cost(1000, 1000),
        name="pick_near",
    )(states, *blocks)


def product_kernel(blocks, *refs):
    states, pieces, outs = refs[:4], refs[4:12], refs[12:]
    for j in range(8):
        for k, block in enumerate(blocks):
            total = jnp.zeros((ROWS, COLUMNS), F32)
            for d in range(4):
                at = block[d] * ROWS
                total += jnp.dot(
                    states[d][at : at + ROWS], pieces[j][d], preferred_element_type=F32
                )
            out = outs[2 * k + j // 4]
            out[:, (j % 4) * COLUMNS : (j % 4 + 1) * COLUMNS] = total.astype(out.dtype)


def product(states, pieces, blocks, kind, name):
    vmem = pl.BlockSpec(memory_space=pltpu.VMEM)
    outs = [jax.ShapeDtypeStruct((ROWS, KVW // 2), kind)] * (2 * len(blocks))
    return pl.pallas_call(
        functools.partial(product_kernel, blocks),
        out_shape=outs,
        in_specs=[vmem] * 12,
        out_specs=[vmem] * len(outs),
        compiler_params=params(20),
        cost_estimate=cost(1000, 1000),
        name=name,
    )(*states, *pieces)


def product_far_kernel(*refs):
    states, pieces, outs = refs[:4], refs[4:12], refs[12:]
    for j in range(8):
        total = jnp.zeros((ROWS, COLUMNS), F32)
        for d in range(4):
            total += jnp.dot(
                states[d][:ROWS], pieces[j][d], preferred_element_type=F32
            )
        outs[j // 4][:, (j % 4) * COLUMNS : (j % 4 + 1) * COLUMNS] = total.astype(BF16)


def product_far(states, pieces):
    vmem = pl.BlockSpec(memory_space=pltpu.VMEM)
    return pl.pallas_call(
        product_far_kernel,
        out_shape=[jax.ShapeDtypeStruct((ROWS, KVW // 2), BF16)] * 2,
        in_specs=[vmem] * 12,
        out_specs=[vmem] * 2,
        compiler_params=params(20),
        cost_estimate=cost(1000, 1000),
        name="product_far",
    )(*states, *pieces)


def relay_kernel(up, down, from_down, from_up, up_out, down_out):
    up_out[...] = (up[...].astype(F32) + from_down[...].astype(F32)).astype(BF16)
    down_out[...] = (down[...].astype(F32) + from_up[...].astype(F32)).astype(BF16)


def relay(up, down, from_down, from_up):
    vmem = pl.BlockSpec(memory_space=pltpu.VMEM)
    return pl.pallas_call(
        relay_kernel,
        out_shape=[jax.ShapeDtypeStruct((ROWS, KVW // 2), BF16)] * 2,
        in_specs=[vmem] * 4,
        out_specs=[vmem] * 2,
        compiler_params=params(16),
        cost_estimate=cost(1000, 1000),
        name="relay_sums",
    )(up, down, from_down, from_up)


def log_rows(logs):
    out = jnp.full((HEADS, HEAD_SIZE), LOW, F32)
    for g in range(GROUPS):
        out = put_lane(out, g, logs[g * HEADS : (g + 1) * HEADS])
    return out


POOL_PAGES = 4


def page_kernel(slots, alive, query, *refs):
    pages, out = refs[:POOL_PAGES], refs[POOL_PAGES]
    step = pl.program_id(0)
    scores = []
    for k in range(POOL_PAGES):
        for g in range(GROUPS):
            keys = pages[k][0, :, g * HEAD_SIZE : (g + 1) * HEAD_SIZE]
            scores.append(nt_dot(query[k, g * HEADS : (g + 1) * HEADS], keys))
    scores = jnp.concatenate(scores) * SCALE
    top = jnp.max(scores, axis=-1, keepdims=True)
    exponent = jnp.exp(scores - top)
    total = jnp.sum(exponent, axis=-1, keepdims=True)
    logs, share = top + jnp.log(total), 1.0 / total
    for k in range(POOL_PAGES):
        live = alive[step * POOL_PAGES + k] != 0
        for g in range(GROUPS):
            rows = slice(k * QUERY_HEADS + g * HEADS, k * QUERY_HEADS + (g + 1) * HEADS)
            values = pages[k][0, :, KEYS + g * HEAD_SIZE : KEYS + (g + 1) * HEAD_SIZE]
            mixture = jnp.dot(exponent[rows].astype(BF16), values, preferred_element_type=F32)
            out[k, g * HEADS : (g + 1) * HEADS] = jnp.where(live, mixture * share[rows], 0.0)
        mine = log_rows(logs[k * QUERY_HEADS : (k + 1) * QUERY_HEADS])
        out[k, QUERY_HEADS:] = jnp.where(live, mine, LOW)


def pool_attention(slots, alive, queries_all, pool):
    def page_of(k):
        return lambda s, slots, alive: (slots[s * POOL_PAGES + k], 0, 0)

    return pl.pallas_call(
        page_kernel,
        out_shape=jax.ShapeDtypeStruct((SAMPLES, PACK, HEAD_SIZE), F32),
        grid_spec=pltpu.PrefetchScalarGridSpec(
            num_scalar_prefetch=2,
            grid=(SAMPLES // POOL_PAGES,),
            in_specs=[
                pl.BlockSpec(
                    (POOL_PAGES, QUERY_HEADS, HEAD_SIZE), lambda s, slots, alive: (s, 0, 0)
                )
            ]
            + [pl.BlockSpec((1, PAGE, KVW), page_of(k)) for k in range(POOL_PAGES)],
            out_specs=pl.BlockSpec(
                (POOL_PAGES, PACK, HEAD_SIZE), lambda s, slots, alive: (s, 0, 0)
            ),
        ),
        compiler_params=params(16),
        cost_estimate=cost(1000, 1000),
        name="pool_attention",
    )(slots, alive, queries_all, *[pool] * POOL_PAGES)


LOCAL_PAGES = 4


def local_kernel(pages_alive, query, new, pages, out, top_ref, sum_ref, mix_ref):
    step = pl.program_id(0)
    width = LOCAL_PAGES * PAGE

    @pl.when(step == 0)
    def _():
        for g in range(GROUPS):
            rows = slice(g * HEADS, (g + 1) * HEADS)
            lanes = slice(g * HEAD_SIZE, (g + 1) * HEAD_SIZE)
            value_lanes = slice(KEYS + g * HEAD_SIZE, KEYS + (g + 1) * HEAD_SIZE)
            products = query[rows].astype(F32) * new[0:1, lanes].astype(F32)
            top_ref[rows] = jnp.sum(products, axis=-1, keepdims=True) * SCALE
            sum_ref[rows] = jnp.ones((HEADS, 1), F32)
            mix_ref[rows] = jnp.broadcast_to(new[0:1, value_lanes].astype(F32), (HEADS, HEAD_SIZE))

    @pl.when(step * LOCAL_PAGES < pages_alive[0])
    def _():
        block = pages.reshape(width, KVW)
        at = step * width + lax.broadcasted_iota(jnp.int32, (QUERY_HEADS, width), 1)
        live = at < pages_alive[0] * PAGE
        scores = jnp.concatenate(
            [
                nt_dot(
                    query[g * HEADS : (g + 1) * HEADS],
                    block[:, g * HEAD_SIZE : (g + 1) * HEAD_SIZE],
                )
                for g in range(GROUPS)
            ]
        )
        scores = jnp.where(live, scores * SCALE, LOW)
        old = top_ref[...]
        top = jnp.maximum(old, jnp.max(scores, axis=-1, keepdims=True))
        shrink = jnp.exp(old - top)
        exponent = jnp.where(live, jnp.exp(scores - top), 0.0)
        top_ref[...] = top
        sum_ref[...] = sum_ref[...] * shrink + jnp.sum(exponent, axis=-1, keepdims=True)
        for g in range(GROUPS):
            rows = slice(g * HEADS, (g + 1) * HEADS)
            values = block[:, KEYS + g * HEAD_SIZE : KEYS + (g + 1) * HEAD_SIZE]
            mix_ref[rows] = mix_ref[rows] * shrink[rows] + jnp.dot(
                exponent[rows].astype(BF16), values, preferred_element_type=F32
            )

    @pl.when(step == CMAX // LOCAL_PAGES - 1)
    def _():
        out[:QUERY_HEADS] = mix_ref[...] / sum_ref[...]
        out[QUERY_HEADS:] = log_rows(top_ref[...] + jnp.log(sum_ref[...]))


def local_attention(pages_alive, query, new, pages):
    def block_of(step, alive):
        last = jnp.maximum(alive[0] - 1, 0) // LOCAL_PAGES
        return (jnp.minimum(step, last), 0, 0)

    return pl.pallas_call(
        local_kernel,
        out_shape=jax.ShapeDtypeStruct((PACK, HEAD_SIZE), F32),
        grid_spec=pltpu.PrefetchScalarGridSpec(
            num_scalar_prefetch=1,
            grid=(CMAX // LOCAL_PAGES,),
            in_specs=[
                pl.BlockSpec((QUERY_HEADS, HEAD_SIZE), lambda step, alive: (0, 0)),
                pl.BlockSpec((1, KVW), lambda step, alive: (0, 0)),
                pl.BlockSpec((LOCAL_PAGES, PAGE, KVW), block_of),
            ],
            out_specs=pl.BlockSpec((PACK, HEAD_SIZE), lambda step, alive: (0, 0)),
            scratch_shapes=[
                pltpu.VMEM((QUERY_HEADS, 1), F32),
                pltpu.VMEM((QUERY_HEADS, 1), F32),
                pltpu.VMEM((QUERY_HEADS, HEAD_SIZE), F32),
            ],
        ),
        compiler_params=params(16),
        cost_estimate=cost(1000, 1000),
        name="local_attention",
    )(pages_alive, query, new, pages)


def prefix_kernel(
    prompt_pages, own_l, own_r, up_l, up_r, down_l, down_r, queries, pool, cache, packed
):
    me, prompt = lax.axis_index("sample"), lax.axis_index("prompt")
    z, x = me // 4, lax.rem(me, 4)
    y, core = prompt // 2, lax.rem(prompt, 2)
    near = lax.rem(y + 3 - 2 * core, 4)
    other = lax.rem(y + 1 + 2 * core, 4)
    far = lax.rem(y + 2, 4)
    columns = (
        2 * y + core, 2 * y + 1 - core, 2 * near + core, 2 * near + 1 - core,
        2 * other + 1 - core, 2 * other + core, 2 * far + core, 2 * far + 1 - core,
    )
    for j in range(8):
        lanes = slice((j % 4) * COLUMNS, (j % 4 + 1) * COLUMNS)
        own, up, down = (own_l, up_l, down_l) if j < 4 else (own_r, up_r, down_r)
        total = own[:, lanes] + up[:, lanes].astype(F32) + down[:, lanes].astype(F32)
        target = pl.ds(pl.multiple_of(columns[j] * COLUMNS, COLUMNS), COLUMNS)
        cache[0, :, target] = total.astype(BF16)
    sources = [
        lax.rem(z + 4 - dz, 4) * 4 + lax.rem(x + 4 - dx, 4) for dx in STEPS for dz in STEPS
    ]
    live = lax.broadcasted_iota(jnp.int32, (SAMPLES * HEADS, ROWS), 1) < prompt_pages[0] * PAGE - me * ROWS
    logs = jnp.full((SAMPLES * HEADS, HEAD_SIZE), LOW, F32)
    for g in range(GROUPS):
        keys = cache[0, :, g * HEAD_SIZE : (g + 1) * HEAD_SIZE]
        values = cache[0, :, KEYS + g * HEAD_SIZE : KEYS + (g + 1) * HEAD_SIZE]
        scores = jnp.where(live, nt_dot(queries[g], keys) * SCALE, LOW)
        top = jnp.max(scores, axis=-1, keepdims=True)
        exponent = jnp.where(live, jnp.exp(scores - top), 0.0)
        total = jnp.sum(exponent, axis=-1, keepdims=True)
        mixture = jnp.dot(exponent.astype(BF16), values, preferred_element_type=F32)
        some = total > 0.0
        total = jnp.where(some, total, 1.0)
        log = jnp.where(some, top + jnp.log(total), LOW)
        rows = slice(g * HEADS, (g + 1) * HEADS)
        pool_log = pool[:, QUERY_HEADS:, g : g + 1].reshape(SAMPLES * HEADS, 1)
        pool_mixture = pool[:, rows].reshape(SAMPLES * HEADS, HEAD_SIZE)
        high = jnp.maximum(log, pool_log)
        here, there = jnp.exp(log - high), jnp.exp(pool_log - high)
        both = here + there
        merged = mixture * (here / (total * both)) + pool_mixture * (there / both)
        for r, source in enumerate(sources):
            packed[source, rows] = merged[r * HEADS : (r + 1) * HEADS].astype(BF16)
        logs = put_lane(logs, g, high + jnp.log(both))
    first = logs.astype(BF16).astype(F32)
    second = (logs - first).astype(BF16).astype(F32)
    third = logs - first - second
    terms = jnp.zeros((SAMPLES * HEADS, HEAD_SIZE), F32)
    for g in range(GROUPS):
        for t, term in enumerate((first, second, third)):
            terms = put_lane(terms, t * GROUPS + g, term[:, g : g + 1])
    padding = jnp.zeros((SENT - QUERY_HEADS - HEADS, HEAD_SIZE), F32)
    for r, source in enumerate(sources):
        rows = jnp.concatenate([terms[r * HEADS : (r + 1) * HEADS], padding])
        packed[source, QUERY_HEADS:] = rows.astype(BF16)


def prefix_attention(prompt_pages, parts, queries, pool):
    smem, vmem = pl.BlockSpec(memory_space=pltpu.SMEM), pl.BlockSpec(memory_space=pltpu.VMEM)
    return pl.pallas_call(
        prefix_kernel,
        out_shape=[
            jax.ShapeDtypeStruct((1, ROWS, KVW), BF16),
            jax.ShapeDtypeStruct((SAMPLES, SENT, HEAD_SIZE), BF16),
        ],
        in_specs=[smem] + [vmem] * 8,
        out_specs=[vmem, vmem],
        compiler_params=params(20),
        cost_estimate=cost(300_000_000, 6 * MIB),
        name="prefix_attention",
    )(prompt_pages, *parts, queries, pool)


def combine_kernel(arrived, local, out):
    terms = arrived[:, QUERY_HEADS:].astype(F32)
    for g in range(GROUPS):
        rows = slice(g * HEADS, (g + 1) * HEADS)
        logs = sum(terms[:, :HEADS, lane : lane + 1] for lane in (g, g + GROUPS, g + 2 * GROUPS))
        local_log = local[QUERY_HEADS:, g : g + 1]
        high = jnp.maximum(jnp.max(logs, axis=0), local_log)
        shares = jnp.exp(logs - high[None])
        local_share = jnp.exp(local_log - high)
        total = jnp.sum(shares, axis=0) + local_share
        mixture = jnp.sum(arrived[:, rows].astype(F32) * shares, axis=0) + local[rows] * local_share
        mixture = (mixture / total).astype(BF16)
        for h in range(HEADS):
            lanes = slice((g * HEADS + h) * HEAD_SIZE, (g * HEADS + h + 1) * HEAD_SIZE)
            out[0, :, lanes] = mixture[h : h + 1]


def combine(arrived, local):
    vmem = pl.BlockSpec(memory_space=pltpu.VMEM)
    return pl.pallas_call(
        combine_kernel,
        out_shape=jax.ShapeDtypeStruct((1, 1, QUERY_HEADS * HEAD_SIZE), BF16),
        in_specs=[vmem, vmem],
        out_specs=vmem,
        compiler_params=params(16),
        cost_estimate=cost(1_000_000, MIB),
        name="combine",
    )(arrived, local)


def per_device(
    prompt_states,
    kv_weight,
    queries,
    new_kv,
    local_pages,
    pool_pages,
    prompt_pages,
    comp_pages,
    preempted,
    page_where,
):
    tie = lax.optimization_barrier

    weight_far = lax.ppermute(kv_weight, "sample", X_FAR)
    weight_right = lax.ppermute(kv_weight, "sample", X_RIGHT)
    weight_left = lax.ppermute(kv_weight, "sample", X_LEFT)
    block, query = prepare(queries, page_where, comp_pages, preempted)
    states = prompt_states.reshape(4, 4, ROWS, SLICE)
    own_states, to_far = pick_far(states)
    slices, own_states, to_far, block = tie(
        ((kv_weight, weight_right, weight_left, weight_far), own_states, to_far, block)
    )
    blocks = [block] + [lax.ppermute(block, "sample", to) for to in (Z_UP, Z_DOWN, Z_FAR)]
    to_right, to_left, last_far = pick_near(states, blocks)
    rows_far = lax.ppermute(to_far, "sample", X_FAR)
    rows_right = lax.ppermute(to_right, "sample", X_RIGHT)
    rows_left = lax.ppermute(to_left, "sample", X_LEFT)

    here = jnp.stack(slices)
    near = lax.ppermute(here, "prompt", Y_SPLIT)
    here_other = lax.ppermute(here, "prompt", SWAP)
    near_other = lax.ppermute(here_other, "prompt", Y_SPLIT)
    near, near_other, rows_far = tie((near, near_other, rows_far))
    far = lax.ppermute(near, "prompt", Y_SPLIT)
    near_swapped = lax.ppermute(near, "prompt", SWAP)
    near_other_swapped = lax.ppermute(near_other, "prompt", SWAP)
    local_alive = jnp.where(preempted[0] > 0, 0, comp_pages[0])
    local = local_attention(local_alive, query, new_kv[0], local_pages[0, 0])
    far, rows_right, rows_left, local = tie((far, rows_right, rows_left, local))
    far_other = lax.ppermute(far, "prompt", SWAP)
    pieces = [
        here, here_other, near, near_other, near_swapped, near_other_swapped, far, far_other,
    ]
    others = [own_states, rows_right, rows_left, rows_far]

    far_l, far_r = product_far(others, pieces)
    from_down = lax.ppermute(far_l, "sample", Z_UP)
    from_up = lax.ppermute(far_r, "sample", Z_DOWN)
    last_far, rows_right = tie((last_far, rows_right))
    last_far = lax.ppermute(last_far, "sample", X_FAR)
    up_l, up_r, down_l, down_r = product(
        others, pieces, ((1,) * 4, (2,) * 4), BF16, "product_near"
    )
    up_r, down_l = lax.ppermute(up_r, "sample", Z_UP), lax.ppermute(down_l, "sample", Z_DOWN)
    from_down, from_up, last_far = tie((from_down, from_up, last_far))
    up_l, down_r = relay(up_l, down_r, from_down, from_up)
    sums = [
        lax.ppermute(up_l, "sample", Z_UP),
        up_r,
        down_l,
        lax.ppermute(down_r, "sample", Z_DOWN),
    ]

    arrived, up_l = tie(([rows_right, rows_left, last_far], up_l))
    queries_all, by_group, slots, alive = unpack(blocks, arrived)
    pool = pool_attention(slots, alive, queries_all, pool_pages[0, 0])
    mine, pool = tie(([own_states, *arrived], pool))
    sums = [*product(mine, pieces, ((3, 3, 3, 0),), F32, "product_own"), *sums]

    cache, packed = prefix_attention(prompt_pages, sums, by_group, pool)
    arrived = lax.all_to_all(packed, "sample", split_axis=0, concat_axis=0, tiled=True)
    attended = combine(arrived, local)
    return (cache, attended)


def solution(mesh):
    return jax.shard_map(
        per_device,
        mesh=mesh,
        in_specs=(
            P("prompt", None, "sample"),
            P("sample", "prompt"),
            P("prompt", "sample", None),
            P("prompt", "sample", None),
            P("prompt", "sample", None, None, None),
            P("prompt", "sample", None, None, None),
            P("prompt"),
            P("prompt", "sample"),
            P("prompt", "sample"),
            P("prompt", "sample", None),
        ),
        out_specs=(P("prompt", "sample", None), P("prompt", "sample", None)),
        check_vma=False,
    )
```

```python
import functools
import math

import jax
import jax.numpy as jnp
from jax import lax
from jax.experimental import pallas as pl
from jax.experimental.pallas import tpu as pltpu
from jax.sharding import PartitionSpec as P

QUERY_HEADS = 64
GROUPS = 8
HEADS = 8
HEAD_SIZE = 128
PAGE = 128
SAMPLES = 16
CMAX = 16
ROWS = 256
SLICE = 512
COLUMNS = 256
KVW = 2048
KEYS = GROUPS * HEAD_SIZE
PACK = QUERY_HEADS + HEADS
SENT = QUERY_HEADS + 16
LOW = -1e30
SCALE = 1.0 / math.sqrt(HEAD_SIZE)
MIB = 1 << 20
F32 = jnp.float32
BF16 = jnp.bfloat16

X_RIGHT = [(z * 4 + x, z * 4 + (x + 1) % 4) for z in range(4) for x in range(4)]
X_LEFT = [(z * 4 + x, z * 4 + (x + 3) % 4) for z in range(4) for x in range(4)]
X_FAR = [(z * 4 + x, z * 4 + (x + 2) % 4) for z in range(4) for x in range(4)]
Z_UP = [(z * 4 + x, (z + 1) % 4 * 4 + x) for z in range(4) for x in range(4)]
Z_DOWN = [(z * 4 + x, (z + 3) % 4 * 4 + x) for z in range(4) for x in range(4)]
Z_FAR = [(z * 4 + x, (z + 2) % 4 * 4 + x) for z in range(4) for x in range(4)]
SWAP = [(y * 2 + c, y * 2 + 1 - c) for y in range(4) for c in range(2)]
Y_SPLIT = [(y * 2 + c, (y + (1 if c == 0 else 3)) % 4 * 2 + c) for y in range(4) for c in range(2)]


def params(mib):
    return pltpu.CompilerParams(vmem_limit_bytes=mib * MIB)


def cost(flops, bytes_accessed):
    return pl.CostEstimate(flops=flops, bytes_accessed=bytes_accessed, transcendentals=0)


def nt_dot(a, b):
    return lax.dot_general(a, b, (((1,), (1,)), ((), ())), preferred_element_type=F32)


def put_lane(running, lane, column):
    at = lax.broadcasted_iota(jnp.int32, running.shape, len(running.shape) - 1)
    return jnp.where(at == lane, column, running)


HALF = QUERY_HEADS // 2
BLOCK = HALF + 8


def prepare_kernel(where, length, flag, query, sent, own):
    heads = [query[0, 0:1, h * HEAD_SIZE : (h + 1) * HEAD_SIZE].astype(F32) for h in range(QUERY_HEADS)]
    low, high = jnp.concatenate(heads[:HALF]), jnp.concatenate(heads[HALF:])
    own[:HALF] = low.astype(BF16)
    own[HALF:] = high.astype(BF16)
    sent[:HALF, :HEAD_SIZE] = low.astype(BF16)
    sent[:HALF, HEAD_SIZE:] = high.astype(BF16)
    plan = jnp.zeros((8, COLUMNS), F32)
    for c in range(CMAX):
        plan = put_lane(plan, c, where[0, 0, c].astype(F32))
    plan = put_lane(plan, CMAX, length[0, 0].astype(F32))
    plan = put_lane(plan, CMAX + 1, flag[0, 0].astype(F32))
    sent[HALF:] = plan.astype(BF16)


def prepare(query, where, length, flag):
    smem, vmem = pl.BlockSpec(memory_space=pltpu.SMEM), pl.BlockSpec(memory_space=pltpu.VMEM)
    return pl.pallas_call(
        prepare_kernel,
        out_shape=[
            jax.ShapeDtypeStruct((BLOCK, COLUMNS), BF16),
            jax.ShapeDtypeStruct((QUERY_HEADS, HEAD_SIZE), BF16),
        ],
        in_specs=[smem] * 3 + [vmem],
        out_specs=[vmem, vmem],
        compiler_params=params(16),
        cost_estimate=cost(1000, 1000),
        name="prepare",
    )(where, length, flag, query)


def unpack_kernel(*refs):
    own, arrived, (queries, by_group, slots, alive) = refs[:4], refs[4:7], refs[7:]
    me = lax.axis_index("sample")

    def block_of(r):
        if r < 4:
            return own[r][...].astype(F32)
        source = arrived[r // 4 - 1]
        first = source.shape[0] - 2 * BLOCK + r % 4 // 2 * BLOCK
        lanes = slice(r % 2 * COLUMNS, (r % 2 + 1) * COLUMNS)
        return source[first : first + BLOCK, lanes].astype(F32)

    plans = []
    for r in range(SAMPLES):
        block = block_of(r)
        for half in range(2):
            lanes = slice(half * HEAD_SIZE, (half + 1) * HEAD_SIZE)
            queries[r, half * HALF : (half + 1) * HALF] = block[:HALF, lanes].astype(BF16)
        plans.append(block[HALF : HALF + 1])
    for g in range(GROUPS):
        lanes = slice(g // 4 * HEAD_SIZE, (g // 4 + 1) * HEAD_SIZE)
        rows = slice(g % 4 * HEADS, (g % 4 + 1) * HEADS)
        parts = [block_of(r)[rows, lanes] for r in range(SAMPLES)]
        by_group[g] = jnp.concatenate(parts).astype(BF16)
    plan = jnp.concatenate(plans)
    lane = lax.broadcasted_iota(jnp.int32, plan.shape, 1)
    first = (me * CMAX).astype(F32)
    here = (lane < CMAX) & (plan >= first) & (plan < first + CMAX)
    live = here & (lane.astype(F32) < plan[:, CMAX : CMAX + 1]) & (plan[:, CMAX + 1 : CMAX + 2] > 0.5)
    slot = jnp.sum(jnp.where(here, plan - first, 0.0), axis=1, keepdims=True).astype(jnp.int32)
    some = jnp.max(jnp.where(live, 1.0, 0.0), axis=1, keepdims=True).astype(jnp.int32)
    for r in range(SAMPLES):
        slots[r] = slot[r, 0]
        alive[r] = some[r, 0]


def unpack(own, arrived):
    smem, vmem = pl.BlockSpec(memory_space=pltpu.SMEM), pl.BlockSpec(memory_space=pltpu.VMEM)
    return pl.pallas_call(
        unpack_kernel,
        out_shape=[
            jax.ShapeDtypeStruct((SAMPLES, QUERY_HEADS, HEAD_SIZE), BF16),
            jax.ShapeDtypeStruct((GROUPS, SAMPLES * HEADS, HEAD_SIZE), BF16),
            jax.ShapeDtypeStruct((SAMPLES,), jnp.int32),
            jax.ShapeDtypeStruct((SAMPLES,), jnp.int32),
        ],
        in_specs=[vmem] * 7,
        out_specs=[vmem, vmem, smem, smem],
        compiler_params=params(16),
        cost_estimate=cost(1000, 1000),
        name="unpack",
    )(*own, *arrived)


STEPS = (0, 1, 3, 2)
NEXT = (2, 1, 3, 0)


def copy_rows(states, sems, wanted):
    me = lax.axis_index("sample")
    z, x = me // 4, lax.rem(me, 4)
    copies = [
        pltpu.make_async_copy(
            states.at[lax.rem(z + NEXT[k], 4), lax.rem(x + step, 4)], target, sems.at[n]
        )
        for n, (step, k, target) in enumerate(wanted)
    ]
    for copy in copies:
        copy.start()
    return copies


def block_rows(k):
    return pl.ds(k * ROWS, ROWS)


def pick_far_kernel(states, own, far, sems):
    wanted = [(2, k, far.at[block_rows(k)]) for k in range(3)]
    wanted += [(0, k, own.at[block_rows(k)]) for k in range(4)]
    for copy in copy_rows(states, sems, wanted):
        copy.wait()


def pick_far(states):
    vmem = pl.BlockSpec(memory_space=pltpu.VMEM)
    return pl.pallas_call(
        pick_far_kernel,
        out_shape=[
            jax.ShapeDtypeStruct((4 * ROWS, SLICE), BF16),
            jax.ShapeDtypeStruct((3 * ROWS, SLICE), BF16),
        ],
        in_specs=[pl.BlockSpec(memory_space=pl.ANY)],
        out_specs=[vmem] * 2,
        scratch_shapes=[pltpu.SemaphoreType.DMA((7,))],
        compiler_params=params(50),
        cost_estimate=cost(1000, 1000),
        name="pick_far",
    )(states)


def put_blocks(target, first, blocks):
    for r, block in enumerate(blocks):
        rows = slice(first + r // 2 * BLOCK, first + (r // 2 + 1) * BLOCK)
        target[rows, r % 2 * COLUMNS : (r % 2 + 1) * COLUMNS] = block[...]


def pick_near_kernel(states, *refs):
    blocks, (right, left, last_right, last_left, last_far), sems = refs[:4], refs[4:9], refs[9]
    wanted = [(1, k, right.at[block_rows(k)]) for k in range(3)]
    wanted += [(3, k, left.at[block_rows(k)]) for k in range(3)]
    wanted += [(1, 3, last_right), (3, 3, last_left), (2, 3, last_far.at[block_rows(0)])]
    copies = copy_rows(states, sems, wanted)
    put_blocks(right, 3 * ROWS, blocks)
    put_blocks(left, 3 * ROWS, blocks)
    put_blocks(last_far, ROWS, blocks)
    for copy in copies:
        copy.wait()


def pick_near(states, blocks):
    vmem = pl.BlockSpec(memory_space=pltpu.VMEM)
    return pl.pallas_call(
        pick_near_kernel,
        out_shape=[jax.ShapeDtypeStruct((3 * ROWS + 2 * BLOCK, SLICE), BF16)] * 2
        + [jax.ShapeDtypeStruct((ROWS, SLICE), BF16)] * 2
        + [jax.ShapeDtypeStruct((ROWS + 2 * BLOCK, SLICE), BF16)],
        in_specs=[pl.BlockSpec(memory_space=pl.ANY)] + [vmem] * 4,
        out_specs=[vmem] * 5,
        scratch_shapes=[pltpu.SemaphoreType.DMA((9,))],
        compiler_params=params(44),
        cost_estimate=cost(1000, 1000),
        name="pick_near",
    )(states, *blocks)


def weight_of(pieces, j, d):
    return pieces[j][d] if j < 6 else pieces[2 * j - 6 + d // 2][d % 2]


def product_kernel(blocks, *refs):
    states, pieces, outs = refs[:4], refs[4:14], refs[14:]
    for j in range(8):
        for k, block in enumerate(blocks):
            total = jnp.zeros((ROWS, COLUMNS), F32)
            for d in range(4):
                at = block[d] * ROWS
                total += jnp.dot(
                    states[d][at : at + ROWS], weight_of(pieces, j, d), preferred_element_type=F32
                )
            out = outs[2 * k + j // 4]
            out[:, (j % 4) * COLUMNS : (j % 4 + 1) * COLUMNS] = total.astype(out.dtype)


def product(states, pieces, blocks, kind, name):
    vmem = pl.BlockSpec(memory_space=pltpu.VMEM)
    outs = [jax.ShapeDtypeStruct((ROWS, KVW // 2), kind)] * (2 * len(blocks))
    return pl.pallas_call(
        functools.partial(product_kernel, blocks),
        out_shape=outs,
        in_specs=[vmem] * 14,
        out_specs=[vmem] * len(outs),
        compiler_params=params(20),
        cost_estimate=cost(1000, 1000),
        name=name,
    )(*states, *pieces)


def product_far_kernel(*refs):
    states, pieces, outs = refs[:4], refs[4:14], refs[14:]
    for j in range(8):
        total = jnp.zeros((ROWS, COLUMNS), F32)
        for d in range(4):
            total += jnp.dot(
                states[d][:ROWS], weight_of(pieces, j, d), preferred_element_type=F32
            )
        outs[j // 4][:, (j % 4) * COLUMNS : (j % 4 + 1) * COLUMNS] = total.astype(BF16)


def product_far(states, pieces):
    vmem = pl.BlockSpec(memory_space=pltpu.VMEM)
    return pl.pallas_call(
        product_far_kernel,
        out_shape=[jax.ShapeDtypeStruct((ROWS, KVW // 2), BF16)] * 2,
        in_specs=[vmem] * 14,
        out_specs=[vmem] * 2,
        compiler_params=params(20),
        cost_estimate=cost(1000, 1000),
        name="product_far",
    )(*states, *pieces)


def relay_kernel(up, down, from_down, from_up, up_out, down_out):
    up_out[...] = (up[...].astype(F32) + from_down[...].astype(F32)).astype(BF16)
    down_out[...] = (down[...].astype(F32) + from_up[...].astype(F32)).astype(BF16)


def relay(up, down, from_down, from_up):
    vmem = pl.BlockSpec(memory_space=pltpu.VMEM)
    return pl.pallas_call(
        relay_kernel,
        out_shape=[jax.ShapeDtypeStruct((ROWS, KVW // 2), BF16)] * 2,
        in_specs=[vmem] * 4,
        out_specs=[vmem] * 2,
        compiler_params=params(16),
        cost_estimate=cost(1000, 1000),
        name="relay_sums",
    )(up, down, from_down, from_up)


def log_rows(logs):
    out = jnp.full((HEADS, HEAD_SIZE), LOW, F32)
    for g in range(GROUPS):
        out = put_lane(out, g, logs[g * HEADS : (g + 1) * HEADS])
    return out


POOL_PAGES = 4


def page_kernel(slots, alive, query, *refs):
    pages, out = refs[:POOL_PAGES], refs[POOL_PAGES]
    step = pl.program_id(0)
    scores = []
    for k in range(POOL_PAGES):
        for g in range(GROUPS):
            keys = pages[k][0, :, g * HEAD_SIZE : (g + 1) * HEAD_SIZE]
            scores.append(nt_dot(query[k, g * HEADS : (g + 1) * HEADS], keys))
    scores = jnp.concatenate(scores) * SCALE
    top = jnp.max(scores, axis=-1, keepdims=True)
    exponent = jnp.exp(scores - top)
    total = jnp.sum(exponent, axis=-1, keepdims=True)
    logs, share = top + jnp.log(total), 1.0 / total
    for k in range(POOL_PAGES):
        live = alive[step * POOL_PAGES + k] != 0
        for g in range(GROUPS):
            rows = slice(k * QUERY_HEADS + g * HEADS, k * QUERY_HEADS + (g + 1) * HEADS)
            values = pages[k][0, :, KEYS + g * HEAD_SIZE : KEYS + (g + 1) * HEAD_SIZE]
            mixture = jnp.dot(exponent[rows].astype(BF16), values, preferred_element_type=F32)
            out[k, g * HEADS : (g + 1) * HEADS] = jnp.where(live, mixture * share[rows], 0.0)
        mine = log_rows(logs[k * QUERY_HEADS : (k + 1) * QUERY_HEADS])
        out[k, QUERY_HEADS:] = jnp.where(live, mine, LOW)


def pool_attention(slots, alive, queries_all, pool):
    def page_of(k):
        return lambda s, slots, alive: (slots[s * POOL_PAGES + k], 0, 0)

    return pl.pallas_call(
        page_kernel,
        out_shape=jax.ShapeDtypeStruct((SAMPLES, PACK, HEAD_SIZE), F32),
        grid_spec=pltpu.PrefetchScalarGridSpec(
            num_scalar_prefetch=2,
            grid=(SAMPLES // POOL_PAGES,),
            in_specs=[
                pl.BlockSpec(
                    (POOL_PAGES, QUERY_HEADS, HEAD_SIZE), lambda s, slots, alive: (s, 0, 0)
                )
            ]
            + [pl.BlockSpec((1, PAGE, KVW), page_of(k)) for k in range(POOL_PAGES)],
            out_specs=pl.BlockSpec(
                (POOL_PAGES, PACK, HEAD_SIZE), lambda s, slots, alive: (s, 0, 0)
            ),
        ),
        compiler_params=params(16),
        cost_estimate=cost(1000, 1000),
        name="pool_attention",
    )(slots, alive, queries_all, *[pool] * POOL_PAGES)


LOCAL_PAGES = 4


def local_kernel(pages_alive, query, new, pages, out, top_ref, sum_ref, mix_ref):
    step = pl.program_id(0)
    width = LOCAL_PAGES * PAGE

    @pl.when(step == 0)
    def _():
        for g in range(GROUPS):
            rows = slice(g * HEADS, (g + 1) * HEADS)
            lanes = slice(g * HEAD_SIZE, (g + 1) * HEAD_SIZE)
            value_lanes = slice(KEYS + g * HEAD_SIZE, KEYS + (g + 1) * HEAD_SIZE)
            products = query[rows].astype(F32) * new[0:1, lanes].astype(F32)
            top_ref[rows] = jnp.sum(products, axis=-1, keepdims=True) * SCALE
            sum_ref[rows] = jnp.ones((HEADS, 1), F32)
            mix_ref[rows] = jnp.broadcast_to(new[0:1, value_lanes].astype(F32), (HEADS, HEAD_SIZE))

    @pl.when(step * LOCAL_PAGES < pages_alive[0])
    def _():
        block = pages.reshape(width, KVW)
        at = step * width + lax.broadcasted_iota(jnp.int32, (QUERY_HEADS, width), 1)
        live = at < pages_alive[0] * PAGE
        scores = jnp.concatenate(
            [
                nt_dot(
                    query[g * HEADS : (g + 1) * HEADS],
                    block[:, g * HEAD_SIZE : (g + 1) * HEAD_SIZE],
                )
                for g in range(GROUPS)
            ]
        )
        scores = jnp.where(live, scores * SCALE, LOW)
        old = top_ref[...]
        top = jnp.maximum(old, jnp.max(scores, axis=-1, keepdims=True))
        shrink = jnp.exp(old - top)
        exponent = jnp.where(live, jnp.exp(scores - top), 0.0)
        top_ref[...] = top
        sum_ref[...] = sum_ref[...] * shrink + jnp.sum(exponent, axis=-1, keepdims=True)
        for g in range(GROUPS):
            rows = slice(g * HEADS, (g + 1) * HEADS)
            values = block[:, KEYS + g * HEAD_SIZE : KEYS + (g + 1) * HEAD_SIZE]
            mix_ref[rows] = mix_ref[rows] * shrink[rows] + jnp.dot(
                exponent[rows].astype(BF16), values, preferred_element_type=F32
            )

    @pl.when(step == CMAX // LOCAL_PAGES - 1)
    def _():
        out[:QUERY_HEADS] = mix_ref[...] / sum_ref[...]
        out[QUERY_HEADS:] = log_rows(top_ref[...] + jnp.log(sum_ref[...]))


def local_attention(pages_alive, query, new, pages):
    def block_of(step, alive):
        last = jnp.maximum(alive[0] - 1, 0) // LOCAL_PAGES
        return (jnp.minimum(step, last), 0, 0)

    return pl.pallas_call(
        local_kernel,
        out_shape=jax.ShapeDtypeStruct((PACK, HEAD_SIZE), F32),
        grid_spec=pltpu.PrefetchScalarGridSpec(
            num_scalar_prefetch=1,
            grid=(CMAX // LOCAL_PAGES,),
            in_specs=[
                pl.BlockSpec((QUERY_HEADS, HEAD_SIZE), lambda step, alive: (0, 0)),
                pl.BlockSpec((1, KVW), lambda step, alive: (0, 0)),
                pl.BlockSpec((LOCAL_PAGES, PAGE, KVW), block_of),
            ],
            out_specs=pl.BlockSpec((PACK, HEAD_SIZE), lambda step, alive: (0, 0)),
            scratch_shapes=[
                pltpu.VMEM((QUERY_HEADS, 1), F32),
                pltpu.VMEM((QUERY_HEADS, 1), F32),
                pltpu.VMEM((QUERY_HEADS, HEAD_SIZE), F32),
            ],
        ),
        compiler_params=params(16),
        cost_estimate=cost(1000, 1000),
        name="local_attention",
    )(pages_alive, query, new, pages)


def prefix_kernel(
    prompt_pages, own_l, own_r, up_l, up_r, down_l, down_r, queries, pool, cache, packed
):
    me, prompt = lax.axis_index("sample"), lax.axis_index("prompt")
    z, x = me // 4, lax.rem(me, 4)
    y, core = prompt // 2, lax.rem(prompt, 2)
    near = lax.rem(y + 3 - 2 * core, 4)
    other = lax.rem(y + 1 + 2 * core, 4)
    far = lax.rem(y + 2, 4)
    columns = (
        2 * y + core, 2 * y + 1 - core, 2 * near + core, 2 * near + 1 - core,
        2 * other + 1 - core, 2 * other + core, 2 * far + core, 2 * far + 1 - core,
    )
    for j in range(8):
        lanes = slice((j % 4) * COLUMNS, (j % 4 + 1) * COLUMNS)
        own, up, down = (own_l, up_l, down_l) if j < 4 else (own_r, up_r, down_r)
        total = own[:, lanes] + up[:, lanes].astype(F32) + down[:, lanes].astype(F32)
        target = pl.ds(pl.multiple_of(columns[j] * COLUMNS, COLUMNS), COLUMNS)
        cache[0, :, target] = total.astype(BF16)
    sources = [
        lax.rem(z + 4 - dz, 4) * 4 + lax.rem(x + 4 - dx, 4) for dx in STEPS for dz in STEPS
    ]
    live = lax.broadcasted_iota(jnp.int32, (SAMPLES * HEADS, ROWS), 1) < prompt_pages[0] * PAGE - me * ROWS
    logs = jnp.full((SAMPLES * HEADS, HEAD_SIZE), LOW, F32)
    for g in range(GROUPS):
        keys = cache[0, :, g * HEAD_SIZE : (g + 1) * HEAD_SIZE]
        values = cache[0, :, KEYS + g * HEAD_SIZE : KEYS + (g + 1) * HEAD_SIZE]
        scores = jnp.where(live, nt_dot(queries[g], keys) * SCALE, LOW)
        top = jnp.max(scores, axis=-1, keepdims=True)
        exponent = jnp.where(live, jnp.exp(scores - top), 0.0)
        total = jnp.sum(exponent, axis=-1, keepdims=True)
        mixture = jnp.dot(exponent.astype(BF16), values, preferred_element_type=F32)
        some = total > 0.0
        total = jnp.where(some, total, 1.0)
        log = jnp.where(some, top + jnp.log(total), LOW)
        rows = slice(g * HEADS, (g + 1) * HEADS)
        pool_log = pool[:, QUERY_HEADS:, g : g + 1].reshape(SAMPLES * HEADS, 1)
        pool_mixture = pool[:, rows].reshape(SAMPLES * HEADS, HEAD_SIZE)
        high = jnp.maximum(log, pool_log)
        here, there = jnp.exp(log - high), jnp.exp(pool_log - high)
        both = here + there
        merged = mixture * (here / (total * both)) + pool_mixture * (there / both)
        for r, source in enumerate(sources):
            packed[source, rows] = merged[r * HEADS : (r + 1) * HEADS].astype(BF16)
        logs = put_lane(logs, g, high + jnp.log(both))
    first = logs.astype(BF16).astype(F32)
    second = (logs - first).astype(BF16).astype(F32)
    third = logs - first - second
    terms = jnp.zeros((SAMPLES * HEADS, HEAD_SIZE), F32)
    for g in range(GROUPS):
        for t, term in enumerate((first, second, third)):
            terms = put_lane(terms, t * GROUPS + g, term[:, g : g + 1])
    padding = jnp.zeros((SENT - QUERY_HEADS - HEADS, HEAD_SIZE), F32)
    for r, source in enumerate(sources):
        rows = jnp.concatenate([terms[r * HEADS : (r + 1) * HEADS], padding])
        packed[source, QUERY_HEADS:] = rows.astype(BF16)


def prefix_attention(prompt_pages, parts, queries, pool):
    smem, vmem = pl.BlockSpec(memory_space=pltpu.SMEM), pl.BlockSpec(memory_space=pltpu.VMEM)
    return pl.pallas_call(
        prefix_kernel,
        out_shape=[
            jax.ShapeDtypeStruct((1, ROWS, KVW), BF16),
            jax.ShapeDtypeStruct((SAMPLES, SENT, HEAD_SIZE), BF16),
        ],
        in_specs=[smem] + [vmem] * 8,
        out_specs=[vmem, vmem],
        compiler_params=params(20),
        cost_estimate=cost(300_000_000, 6 * MIB),
        name="prefix_attention",
    )(prompt_pages, *parts, queries, pool)


def combine_kernel(arrived, local, out):
    terms = arrived[:, QUERY_HEADS:].astype(F32)
    for g in range(GROUPS):
        rows = slice(g * HEADS, (g + 1) * HEADS)
        logs = sum(terms[:, :HEADS, lane : lane + 1] for lane in (g, g + GROUPS, g + 2 * GROUPS))
        local_log = local[QUERY_HEADS:, g : g + 1]
        high = jnp.maximum(jnp.max(logs, axis=0), local_log)
        shares = jnp.exp(logs - high[None])
        local_share = jnp.exp(local_log - high)
        total = jnp.sum(shares, axis=0) + local_share
        mixture = jnp.sum(arrived[:, rows].astype(F32) * shares, axis=0) + local[rows] * local_share
        mixture = (mixture / total).astype(BF16)
        for h in range(HEADS):
            lanes = slice((g * HEADS + h) * HEAD_SIZE, (g * HEADS + h + 1) * HEAD_SIZE)
            out[0, :, lanes] = mixture[h : h + 1]


def combine(arrived, local):
    vmem = pl.BlockSpec(memory_space=pltpu.VMEM)
    return pl.pallas_call(
        combine_kernel,
        out_shape=jax.ShapeDtypeStruct((1, 1, QUERY_HEADS * HEAD_SIZE), BF16),
        in_specs=[vmem, vmem],
        out_specs=vmem,
        compiler_params=params(16),
        cost_estimate=cost(1_000_000, MIB),
        name="combine",
    )(arrived, local)


def per_device(
    prompt_states,
    kv_weight,
    queries,
    new_kv,
    local_pages,
    pool_pages,
    prompt_pages,
    comp_pages,
    preempted,
    page_where,
):
    tie = lax.optimization_barrier

    weight_far = lax.ppermute(kv_weight, "sample", X_FAR)
    weight_right = lax.ppermute(kv_weight, "sample", X_RIGHT)
    weight_left = lax.ppermute(kv_weight, "sample", X_LEFT)
    block, query = prepare(queries, page_where, comp_pages, preempted)
    states = prompt_states.reshape(4, 4, ROWS, SLICE)
    own_states, to_far = pick_far(states)
    slices, own_states, to_far, block = tie(
        ((kv_weight, weight_right, weight_left, weight_far), own_states, to_far, block)
    )
    blocks = [block] + [lax.ppermute(block, "sample", to) for to in (Z_UP, Z_DOWN, Z_FAR)]
    to_right, to_left, last_right, last_left, last_far = pick_near(states, blocks)
    rows_far = lax.ppermute(to_far, "sample", X_FAR)
    rows_right = lax.ppermute(to_right, "sample", X_RIGHT)
    rows_left = lax.ppermute(to_left, "sample", X_LEFT)

    here = jnp.stack(slices)
    near = lax.ppermute(here, "prompt", Y_SPLIT)
    here_other = lax.ppermute(here, "prompt", SWAP)
    near_other = lax.ppermute(here_other, "prompt", Y_SPLIT)
    local_alive = jnp.where(preempted[0] > 0, 0, comp_pages[0])
    local = local_attention(local_alive, query, new_kv[0], local_pages[0, 0])
    near, near_other, rows_far, local = tie((near, near_other, rows_far, local))
    far = [lax.ppermute(half, "prompt", Y_SPLIT) for half in (near[:2], near[2:])]
    near_swapped = lax.ppermute(near, "prompt", SWAP)
    near_other_swapped = lax.ppermute(near_other, "prompt", SWAP)
    far, rows_right, rows_left = tie((far, rows_right, rows_left))
    far_other = [lax.ppermute(half, "prompt", SWAP) for half in far]
    pieces = [
        here, here_other, near, near_other, near_swapped, near_other_swapped, *far, *far_other,
    ]
    others = [own_states, rows_right, rows_left, rows_far]

    far_l, far_r = product_far(others, pieces)
    from_down = lax.ppermute(far_l, "sample", Z_UP)
    from_up = lax.ppermute(far_r, "sample", Z_DOWN)
    last_far, rows_right = tie((last_far, rows_right))
    last_far = lax.ppermute(last_far, "sample", X_FAR)
    up_l, up_r, down_l, down_r = product(
        others, pieces, ((1,) * 4, (2,) * 4), BF16, "product_near"
    )
    up_r, down_l = lax.ppermute(up_r, "sample", Z_UP), lax.ppermute(down_l, "sample", Z_DOWN)
    from_down, from_up, last_far = tie((from_down, from_up, last_far))
    up_l, down_r = relay(up_l, down_r, from_down, from_up)
    sums = [
        lax.ppermute(up_l, "sample", Z_UP),
        up_r,
        down_l,
        lax.ppermute(down_r, "sample", Z_DOWN),
    ]

    arrived, up_l = tie(([rows_right, rows_left, last_far], up_l))
    queries_all, by_group, slots, alive = unpack(blocks, arrived)
    pool = pool_attention(slots, alive, queries_all, pool_pages[0, 0])
    last_right = lax.ppermute(last_right, "sample", X_RIGHT)
    last_left = lax.ppermute(last_left, "sample", X_LEFT)
    mine, pool = tie(([own_states, last_right, last_left, last_far], pool))
    sums = [*product(mine, pieces, ((3, 0, 0, 0),), F32, "product_own"), *sums]

    cache, packed = prefix_attention(prompt_pages, sums, by_group, pool)
    arrived = lax.all_to_all(packed, "sample", split_axis=0, concat_axis=0, tiled=True)
    attended = combine(arrived, local)
    return (cache, attended)


def solution(mesh):
    return jax.shard_map(
        per_device,
        mesh=mesh,
        in_specs=(
            P("prompt", None, "sample"),
            P("sample", "prompt"),
            P("prompt", "sample", None),
            P("prompt", "sample", None),
            P("prompt", "sample", None, None, None),
            P("prompt", "sample", None, None, None),
            P("prompt"),
            P("prompt", "sample"),
            P("prompt", "sample"),
            P("prompt", "sample", None),
        ),
        out_specs=(P("prompt", "sample", None), P("prompt", "sample", None)),
        check_vma=False,
    )
```

```python
import functools
import math

import jax
import jax.numpy as jnp
from jax import lax
from jax.experimental import pallas as pl
from jax.experimental.pallas import tpu as pltpu
from jax.sharding import PartitionSpec as P

QUERY_HEADS = 64
GROUPS = 8
HEADS = 8
HEAD_SIZE = 128
PAGE = 128
SAMPLES = 16
CMAX = 16
ROWS = 256
SLICE = 512
COLUMNS = 256
KVW = 2048
KEYS = GROUPS * HEAD_SIZE
PACK = QUERY_HEADS + HEADS
SENT = QUERY_HEADS + 16
LOW = -1e30
SCALE = 1.0 / math.sqrt(HEAD_SIZE)
MIB = 1 << 20
F32 = jnp.float32
BF16 = jnp.bfloat16

X_RIGHT = [(z * 4 + x, z * 4 + (x + 1) % 4) for z in range(4) for x in range(4)]
X_LEFT = [(z * 4 + x, z * 4 + (x + 3) % 4) for z in range(4) for x in range(4)]
X_FAR = [(z * 4 + x, z * 4 + (x + 2) % 4) for z in range(4) for x in range(4)]
Z_UP = [(z * 4 + x, (z + 1) % 4 * 4 + x) for z in range(4) for x in range(4)]
Z_DOWN = [(z * 4 + x, (z + 3) % 4 * 4 + x) for z in range(4) for x in range(4)]
Z_FAR = [(z * 4 + x, (z + 2) % 4 * 4 + x) for z in range(4) for x in range(4)]
SWAP = [(y * 2 + c, y * 2 + 1 - c) for y in range(4) for c in range(2)]
Y_SPLIT = [(y * 2 + c, (y + (1 if c == 0 else 3)) % 4 * 2 + c) for y in range(4) for c in range(2)]


def params(mib):
    return pltpu.CompilerParams(vmem_limit_bytes=mib * MIB)


def cost(flops, bytes_accessed):
    return pl.CostEstimate(flops=flops, bytes_accessed=bytes_accessed, transcendentals=0)


def nt_dot(a, b):
    return lax.dot_general(a, b, (((1,), (1,)), ((), ())), preferred_element_type=F32)


def put_lane(running, lane, column):
    at = lax.broadcasted_iota(jnp.int32, running.shape, len(running.shape) - 1)
    return jnp.where(at == lane, column, running)


HALF = QUERY_HEADS // 2
BLOCK = HALF + 8


def prepare_kernel(where, length, flag, query, sent, own):
    heads = [query[0, 0:1, h * HEAD_SIZE : (h + 1) * HEAD_SIZE].astype(F32) for h in range(QUERY_HEADS)]
    low, high = jnp.concatenate(heads[:HALF]), jnp.concatenate(heads[HALF:])
    own[:HALF] = low.astype(BF16)
    own[HALF:] = high.astype(BF16)
    sent[:HALF, :HEAD_SIZE] = low.astype(BF16)
    sent[:HALF, HEAD_SIZE:] = high.astype(BF16)
    plan = jnp.zeros((8, COLUMNS), F32)
    for c in range(CMAX):
        plan = put_lane(plan, c, where[0, 0, c].astype(F32))
    plan = put_lane(plan, CMAX, length[0, 0].astype(F32))
    plan = put_lane(plan, CMAX + 1, flag[0, 0].astype(F32))
    sent[HALF:] = plan.astype(BF16)


def prepare(query, where, length, flag):
    smem, vmem = pl.BlockSpec(memory_space=pltpu.SMEM), pl.BlockSpec(memory_space=pltpu.VMEM)
    return pl.pallas_call(
        prepare_kernel,
        out_shape=[
            jax.ShapeDtypeStruct((BLOCK, COLUMNS), BF16),
            jax.ShapeDtypeStruct((QUERY_HEADS, HEAD_SIZE), BF16),
        ],
        in_specs=[smem] * 3 + [vmem],
        out_specs=[vmem, vmem],
        compiler_params=params(16),
        cost_estimate=cost(1000, 1000),
        name="prepare",
    )(where, length, flag, query)


def unpack_kernel(*refs):
    own, arrived, (queries, by_group, slots, alive) = refs[:4], refs[4:7], refs[7:]
    me = lax.axis_index("sample")

    def block_of(r):
        if r < 4:
            return own[r][...].astype(F32)
        source = arrived[r // 4 - 1]
        first = source.shape[0] - 2 * BLOCK + r % 4 // 2 * BLOCK
        lanes = slice(r % 2 * COLUMNS, (r % 2 + 1) * COLUMNS)
        return source[first : first + BLOCK, lanes].astype(F32)

    plans = []
    for r in range(SAMPLES):
        block = block_of(r)
        for half in range(2):
            lanes = slice(half * HEAD_SIZE, (half + 1) * HEAD_SIZE)
            queries[r, half * HALF : (half + 1) * HALF] = block[:HALF, lanes].astype(BF16)
        plans.append(block[HALF : HALF + 1])
    for g in range(GROUPS):
        lanes = slice(g // 4 * HEAD_SIZE, (g // 4 + 1) * HEAD_SIZE)
        rows = slice(g % 4 * HEADS, (g % 4 + 1) * HEADS)
        parts = [block_of(r)[rows, lanes] for r in range(SAMPLES)]
        by_group[g] = jnp.concatenate(parts).astype(BF16)
    plan = jnp.concatenate(plans)
    lane = lax.broadcasted_iota(jnp.int32, plan.shape, 1)
    first = (me * CMAX).astype(F32)
    here = (lane < CMAX) & (plan >= first) & (plan < first + CMAX)
    live = here & (lane.astype(F32) < plan[:, CMAX : CMAX + 1]) & (plan[:, CMAX + 1 : CMAX + 2] > 0.5)
    slot = jnp.sum(jnp.where(here, plan - first, 0.0), axis=1, keepdims=True).astype(jnp.int32)
    some = jnp.max(jnp.where(live, 1.0, 0.0), axis=1, keepdims=True).astype(jnp.int32)
    for r in range(SAMPLES):
        slots[r] = slot[r, 0]
        alive[r] = some[r, 0]


def unpack(own, arrived):
    smem, vmem = pl.BlockSpec(memory_space=pltpu.SMEM), pl.BlockSpec(memory_space=pltpu.VMEM)
    return pl.pallas_call(
        unpack_kernel,
        out_shape=[
            jax.ShapeDtypeStruct((SAMPLES, QUERY_HEADS, HEAD_SIZE), BF16),
            jax.ShapeDtypeStruct((GROUPS, SAMPLES * HEADS, HEAD_SIZE), BF16),
            jax.ShapeDtypeStruct((SAMPLES,), jnp.int32),
            jax.ShapeDtypeStruct((SAMPLES,), jnp.int32),
        ],
        in_specs=[vmem] * 7,
        out_specs=[vmem, vmem, smem, smem],
        compiler_params=params(16),
        cost_estimate=cost(1000, 1000),
        name="unpack",
    )(*own, *arrived)


STEPS = (0, 1, 3, 2)
NEXT = (2, 1, 3, 0)


PAD = 16


def copy_rows(states, sems, wanted):
    me = lax.axis_index("sample")
    z, x = me // 4, lax.rem(me, 4)
    copies = [
        pltpu.make_async_copy(
            states.at[lax.rem(z + NEXT[k], 4), lax.rem(x + step, 4)], target, sems.at[n]
        )
        for n, (step, k, target) in enumerate(wanted)
    ]
    for copy in copies:
        copy.start()
    return copies


def block_rows(k):
    return pl.ds(k * ROWS, ROWS)


def pick_far_kernel(states, own, far, sems):
    wanted = [(2, k, far.at[block_rows(k)]) for k in range(4)]
    wanted += [(0, k, own.at[block_rows(k)]) for k in range(4)]
    copies = copy_rows(states, sems, wanted)
    far[4 * ROWS :] = jnp.zeros((PAD, SLICE), BF16)
    for copy in copies:
        copy.wait()


def pick_far(states):
    vmem = pl.BlockSpec(memory_space=pltpu.VMEM)
    return pl.pallas_call(
        pick_far_kernel,
        out_shape=[
            jax.ShapeDtypeStruct((4 * ROWS, SLICE), BF16),
            jax.ShapeDtypeStruct((4 * ROWS + PAD, SLICE), BF16),
        ],
        in_specs=[pl.BlockSpec(memory_space=pl.ANY)],
        out_specs=[vmem] * 2,
        scratch_shapes=[pltpu.SemaphoreType.DMA((8,))],
        compiler_params=params(50),
        cost_estimate=cost(1000, 1000),
        name="pick_far",
    )(states)


def put_blocks(target, first, blocks):
    for r, block in enumerate(blocks):
        rows = slice(first + r // 2 * BLOCK, first + (r // 2 + 1) * BLOCK)
        target[rows, r % 2 * COLUMNS : (r % 2 + 1) * COLUMNS] = block[...]


def pick_near_kernel(states, *refs):
    blocks, (right, left, last_right, last_left, far_blocks), sems = refs[:4], refs[4:9], refs[9]
    wanted = [(1, k, right.at[block_rows(k)]) for k in range(3)]
    wanted += [(3, k, left.at[block_rows(k)]) for k in range(3)]
    wanted += [(1, 3, last_right), (3, 3, last_left)]
    copies = copy_rows(states, sems, wanted)
    put_blocks(right, 3 * ROWS, blocks)
    put_blocks(left, 3 * ROWS, blocks)
    put_blocks(far_blocks, 0, blocks)
    for copy in copies:
        copy.wait()


def pick_near(states, blocks):
    vmem = pl.BlockSpec(memory_space=pltpu.VMEM)
    return pl.pallas_call(
        pick_near_kernel,
        out_shape=[jax.ShapeDtypeStruct((3 * ROWS + 2 * BLOCK, SLICE), BF16)] * 2
        + [jax.ShapeDtypeStruct((ROWS, SLICE), BF16)] * 2
        + [jax.ShapeDtypeStruct((2 * BLOCK, SLICE), BF16)],
        in_specs=[pl.BlockSpec(memory_space=pl.ANY)] + [vmem] * 4,
        out_specs=[vmem] * 5,
        scratch_shapes=[pltpu.SemaphoreType.DMA((8,))],
        compiler_params=params(44),
        cost_estimate=cost(1000, 1000),
        name="pick_near",
    )(states, *blocks)


def weight_of(pieces, j, d):
    return pieces[j][d] if j < 6 else pieces[2 * j - 6 + d // 2][d % 2]


def product_kernel(blocks, *refs):
    states, pieces, outs = refs[:4], refs[4:14], refs[14:]
    for j in range(8):
        for k, block in enumerate(blocks):
            total = jnp.zeros((ROWS, COLUMNS), F32)
            for d in range(4):
                at = block[d] * ROWS
                total += jnp.dot(
                    states[d][at : at + ROWS], weight_of(pieces, j, d), preferred_element_type=F32
                )
            out = outs[2 * k + j // 4]
            out[:, (j % 4) * COLUMNS : (j % 4 + 1) * COLUMNS] = total.astype(out.dtype)


def product(states, pieces, blocks, kind, name):
    vmem = pl.BlockSpec(memory_space=pltpu.VMEM)
    outs = [jax.ShapeDtypeStruct((ROWS, KVW // 2), kind)] * (2 * len(blocks))
    return pl.pallas_call(
        functools.partial(product_kernel, blocks),
        out_shape=outs,
        in_specs=[vmem] * 14,
        out_specs=[vmem] * len(outs),
        compiler_params=params(20),
        cost_estimate=cost(1000, 1000),
        name=name,
    )(*states, *pieces)


def product_far_kernel(first, *refs):
    states, pieces, out = refs[:4], refs[4:-1], refs[-1]
    for j in range(4):
        total = jnp.zeros((ROWS, COLUMNS), F32)
        for d in range(4):
            part = pieces[j][d] if first + j < 6 else weight_of((None,) * 4 + pieces, first + j, d)
            total += jnp.dot(states[d][:ROWS], part, preferred_element_type=F32)
        out[:, j * COLUMNS : (j + 1) * COLUMNS] = total.astype(BF16)


def product_far(states, pieces, first, name):
    vmem = pl.BlockSpec(memory_space=pltpu.VMEM)
    return pl.pallas_call(
        functools.partial(product_far_kernel, first),
        out_shape=jax.ShapeDtypeStruct((ROWS, KVW // 2), BF16),
        in_specs=[vmem] * (4 + len(pieces)),
        out_specs=vmem,
        compiler_params=params(20),
        cost_estimate=cost(1000, 1000),
        name=name,
    )(*states, *pieces)


def relay_kernel(up, down, from_down, from_up, up_out, down_out):
    up_out[...] = (up[...].astype(F32) + from_down[...].astype(F32)).astype(BF16)
    down_out[...] = (down[...].astype(F32) + from_up[...].astype(F32)).astype(BF16)


def relay(up, down, from_down, from_up):
    vmem = pl.BlockSpec(memory_space=pltpu.VMEM)
    return pl.pallas_call(
        relay_kernel,
        out_shape=[jax.ShapeDtypeStruct((ROWS, KVW // 2), BF16)] * 2,
        in_specs=[vmem] * 4,
        out_specs=[vmem] * 2,
        compiler_params=params(16),
        cost_estimate=cost(1000, 1000),
        name="relay_sums",
    )(up, down, from_down, from_up)


def log_rows(logs):
    out = jnp.full((HEADS, HEAD_SIZE), LOW, F32)
    for g in range(GROUPS):
        out = put_lane(out, g, logs[g * HEADS : (g + 1) * HEADS])
    return out


POOL_PAGES = 4


def page_kernel(slots, alive, query, *refs):
    pages, out = refs[:POOL_PAGES], refs[POOL_PAGES]
    step = pl.program_id(0)
    scores = []
    for k in range(POOL_PAGES):
        for g in range(GROUPS):
            keys = pages[k][0, :, g * HEAD_SIZE : (g + 1) * HEAD_SIZE]
            scores.append(nt_dot(query[k, g * HEADS : (g + 1) * HEADS], keys))
    scores = jnp.concatenate(scores) * SCALE
    top = jnp.max(scores, axis=-1, keepdims=True)
    exponent = jnp.exp(scores - top)
    total = jnp.sum(exponent, axis=-1, keepdims=True)
    logs, share = top + jnp.log(total), 1.0 / total
    for k in range(POOL_PAGES):
        live = alive[step * POOL_PAGES + k] != 0
        for g in range(GROUPS):
            rows = slice(k * QUERY_HEADS + g * HEADS, k * QUERY_HEADS + (g + 1) * HEADS)
            values = pages[k][0, :, KEYS + g * HEAD_SIZE : KEYS + (g + 1) * HEAD_SIZE]
            mixture = jnp.dot(exponent[rows].astype(BF16), values, preferred_element_type=F32)
            out[k, g * HEADS : (g + 1) * HEADS] = jnp.where(live, mixture * share[rows], 0.0)
        mine = log_rows(logs[k * QUERY_HEADS : (k + 1) * QUERY_HEADS])
        out[k, QUERY_HEADS:] = jnp.where(live, mine, LOW)


def pool_attention(slots, alive, queries_all, pool):
    def page_of(k):
        return lambda s, slots, alive: (slots[s * POOL_PAGES + k], 0, 0)

    return pl.pallas_call(
        page_kernel,
        out_shape=jax.ShapeDtypeStruct((SAMPLES, PACK, HEAD_SIZE), F32),
        grid_spec=pltpu.PrefetchScalarGridSpec(
            num_scalar_prefetch=2,
            grid=(SAMPLES // POOL_PAGES,),
            in_specs=[
                pl.BlockSpec(
                    (POOL_PAGES, QUERY_HEADS, HEAD_SIZE), lambda s, slots, alive: (s, 0, 0)
                )
            ]
            + [pl.BlockSpec((1, PAGE, KVW), page_of(k)) for k in range(POOL_PAGES)],
            out_specs=pl.BlockSpec(
                (POOL_PAGES, PACK, HEAD_SIZE), lambda s, slots, alive: (s, 0, 0)
            ),
        ),
        compiler_params=params(16),
        cost_estimate=cost(1000, 1000),
        name="pool_attention",
    )(slots, alive, queries_all, *[pool] * POOL_PAGES)


LOCAL_PAGES = 4


def local_kernel(pages_alive, query, new, pages, out, top_ref, sum_ref, mix_ref):
    step = pl.program_id(0)
    width = LOCAL_PAGES * PAGE

    @pl.when(step == 0)
    def _():
        for g in range(GROUPS):
            rows = slice(g * HEADS, (g + 1) * HEADS)
            lanes = slice(g * HEAD_SIZE, (g + 1) * HEAD_SIZE)
            value_lanes = slice(KEYS + g * HEAD_SIZE, KEYS + (g + 1) * HEAD_SIZE)
            products = query[rows].astype(F32) * new[0:1, lanes].astype(F32)
            top_ref[rows] = jnp.sum(products, axis=-1, keepdims=True) * SCALE
            sum_ref[rows] = jnp.ones((HEADS, 1), F32)
            mix_ref[rows] = jnp.broadcast_to(new[0:1, value_lanes].astype(F32), (HEADS, HEAD_SIZE))

    @pl.when(step * LOCAL_PAGES < pages_alive[0])
    def _():
        block = pages.reshape(width, KVW)
        at = step * width + lax.broadcasted_iota(jnp.int32, (QUERY_HEADS, width), 1)
        live = at < pages_alive[0] * PAGE
        scores = jnp.concatenate(
            [
                nt_dot(
                    query[g * HEADS : (g + 1) * HEADS],
                    block[:, g * HEAD_SIZE : (g + 1) * HEAD_SIZE],
                )
                for g in range(GROUPS)
            ]
        )
        scores = jnp.where(live, scores * SCALE, LOW)
        old = top_ref[...]
        top = jnp.maximum(old, jnp.max(scores, axis=-1, keepdims=True))
        shrink = jnp.exp(old - top)
        exponent = jnp.where(live, jnp.exp(scores - top), 0.0)
        top_ref[...] = top
        sum_ref[...] = sum_ref[...] * shrink + jnp.sum(exponent, axis=-1, keepdims=True)
        for g in range(GROUPS):
            rows = slice(g * HEADS, (g + 1) * HEADS)
            values = block[:, KEYS + g * HEAD_SIZE : KEYS + (g + 1) * HEAD_SIZE]
            mix_ref[rows] = mix_ref[rows] * shrink[rows] + jnp.dot(
                exponent[rows].astype(BF16), values, preferred_element_type=F32
            )

    @pl.when(step == CMAX // LOCAL_PAGES - 1)
    def _():
        out[:QUERY_HEADS] = mix_ref[...] / sum_ref[...]
        out[QUERY_HEADS:] = log_rows(top_ref[...] + jnp.log(sum_ref[...]))


def local_attention(pages_alive, query, new, pages):
    def block_of(step, alive):
        last = jnp.maximum(alive[0] - 1, 0) // LOCAL_PAGES
        return (jnp.minimum(step, last), 0, 0)

    return pl.pallas_call(
        local_kernel,
        out_shape=jax.ShapeDtypeStruct((PACK, HEAD_SIZE), F32),
        grid_spec=pltpu.PrefetchScalarGridSpec(
            num_scalar_prefetch=1,
            grid=(CMAX // LOCAL_PAGES,),
            in_specs=[
                pl.BlockSpec((QUERY_HEADS, HEAD_SIZE), lambda step, alive: (0, 0)),
                pl.BlockSpec((1, KVW), lambda step, alive: (0, 0)),
                pl.BlockSpec((LOCAL_PAGES, PAGE, KVW), block_of),
            ],
            out_specs=pl.BlockSpec((PACK, HEAD_SIZE), lambda step, alive: (0, 0)),
            scratch_shapes=[
                pltpu.VMEM((QUERY_HEADS, 1), F32),
                pltpu.VMEM((QUERY_HEADS, 1), F32),
                pltpu.VMEM((QUERY_HEADS, HEAD_SIZE), F32),
            ],
        ),
        compiler_params=params(16),
        cost_estimate=cost(1000, 1000),
        name="local_attention",
    )(pages_alive, query, new, pages)


def prefix_kernel(
    prompt_pages, own_l, own_r, up_l, up_r, down_l, down_r, queries, pool, cache, packed
):
    me, prompt = lax.axis_index("sample"), lax.axis_index("prompt")
    z, x = me // 4, lax.rem(me, 4)
    y, core = prompt // 2, lax.rem(prompt, 2)
    near = lax.rem(y + 3 - 2 * core, 4)
    other = lax.rem(y + 1 + 2 * core, 4)
    far = lax.rem(y + 2, 4)
    columns = (
        2 * y + core, 2 * y + 1 - core, 2 * near + core, 2 * near + 1 - core,
        2 * other + 1 - core, 2 * other + core, 2 * far + core, 2 * far + 1 - core,
    )
    for j in range(8):
        lanes = slice((j % 4) * COLUMNS, (j % 4 + 1) * COLUMNS)
        own, up, down = (own_l, up_l, down_l) if j < 4 else (own_r, up_r, down_r)
        total = own[:, lanes] + up[:, lanes].astype(F32) + down[:, lanes].astype(F32)
        target = pl.ds(pl.multiple_of(columns[j] * COLUMNS, COLUMNS), COLUMNS)
        cache[0, :, target] = total.astype(BF16)
    sources = [
        lax.rem(z + 4 - dz, 4) * 4 + lax.rem(x + 4 - dx, 4) for dx in STEPS for dz in STEPS
    ]
    live = lax.broadcasted_iota(jnp.int32, (SAMPLES * HEADS, ROWS), 1) < prompt_pages[0] * PAGE - me * ROWS
    logs = jnp.full((SAMPLES * HEADS, HEAD_SIZE), LOW, F32)
    for g in range(GROUPS):
        keys = cache[0, :, g * HEAD_SIZE : (g + 1) * HEAD_SIZE]
        values = cache[0, :, KEYS + g * HEAD_SIZE : KEYS + (g + 1) * HEAD_SIZE]
        scores = jnp.where(live, nt_dot(queries[g], keys) * SCALE, LOW)
        top = jnp.max(scores, axis=-1, keepdims=True)
        exponent = jnp.where(live, jnp.exp(scores - top), 0.0)
        total = jnp.sum(exponent, axis=-1, keepdims=True)
        mixture = jnp.dot(exponent.astype(BF16), values, preferred_element_type=F32)
        some = total > 0.0
        total = jnp.where(some, total, 1.0)
        log = jnp.where(some, top + jnp.log(total), LOW)
        rows = slice(g * HEADS, (g + 1) * HEADS)
        pool_log = pool[:, QUERY_HEADS:, g : g + 1].reshape(SAMPLES * HEADS, 1)
        pool_mixture = pool[:, rows].reshape(SAMPLES * HEADS, HEAD_SIZE)
        high = jnp.maximum(log, pool_log)
        here, there = jnp.exp(log - high), jnp.exp(pool_log - high)
        both = here + there
        merged = mixture * (here / (total * both)) + pool_mixture * (there / both)
        for r, source in enumerate(sources):
            packed[source, rows] = merged[r * HEADS : (r + 1) * HEADS].astype(BF16)
        logs = put_lane(logs, g, high + jnp.log(both))
    first = logs.astype(BF16).astype(F32)
    second = (logs - first).astype(BF16).astype(F32)
    third = logs - first - second
    terms = jnp.zeros((SAMPLES * HEADS, HEAD_SIZE), F32)
    for g in range(GROUPS):
        for t, term in enumerate((first, second, third)):
            terms = put_lane(terms, t * GROUPS + g, term[:, g : g + 1])
    padding = jnp.zeros((SENT - QUERY_HEADS - HEADS, HEAD_SIZE), F32)
    for r, source in enumerate(sources):
        rows = jnp.concatenate([terms[r * HEADS : (r + 1) * HEADS], padding])
        packed[source, QUERY_HEADS:] = rows.astype(BF16)


def prefix_attention(prompt_pages, parts, queries, pool):
    smem, vmem = pl.BlockSpec(memory_space=pltpu.SMEM), pl.BlockSpec(memory_space=pltpu.VMEM)
    return pl.pallas_call(
        prefix_kernel,
        out_shape=[
            jax.ShapeDtypeStruct((1, ROWS, KVW), BF16),
            jax.ShapeDtypeStruct((SAMPLES, SENT, HEAD_SIZE), BF16),
        ],
        in_specs=[smem] + [vmem] * 8,
        out_specs=[vmem, vmem],
        compiler_params=params(20),
        cost_estimate=cost(300_000_000, 6 * MIB),
        name="prefix_attention",
    )(prompt_pages, *parts, queries, pool)


def combine_kernel(arrived, local, out):
    terms = arrived[:, QUERY_HEADS:].astype(F32)
    for g in range(GROUPS):
        rows = slice(g * HEADS, (g + 1) * HEADS)
        logs = sum(terms[:, :HEADS, lane : lane + 1] for lane in (g, g + GROUPS, g + 2 * GROUPS))
        local_log = local[QUERY_HEADS:, g : g + 1]
        high = jnp.maximum(jnp.max(logs, axis=0), local_log)
        shares = jnp.exp(logs - high[None])
        local_share = jnp.exp(local_log - high)
        total = jnp.sum(shares, axis=0) + local_share
        mixture = jnp.sum(arrived[:, rows].astype(F32) * shares, axis=0) + local[rows] * local_share
        mixture = (mixture / total).astype(BF16)
        for h in range(HEADS):
            lanes = slice((g * HEADS + h) * HEAD_SIZE, (g * HEADS + h + 1) * HEAD_SIZE)
            out[0, :, lanes] = mixture[h : h + 1]


def combine(arrived, local):
    vmem = pl.BlockSpec(memory_space=pltpu.VMEM)
    return pl.pallas_call(
        combine_kernel,
        out_shape=jax.ShapeDtypeStruct((1, 1, QUERY_HEADS * HEAD_SIZE), BF16),
        in_specs=[vmem, vmem],
        out_specs=vmem,
        compiler_params=params(16),
        cost_estimate=cost(1_000_000, MIB),
        name="combine",
    )(arrived, local)


def per_device(
    prompt_states,
    kv_weight,
    queries,
    new_kv,
    local_pages,
    pool_pages,
    prompt_pages,
    comp_pages,
    preempted,
    page_where,
):
    tie = lax.optimization_barrier

    weight_far = lax.ppermute(kv_weight, "sample", X_FAR)
    weight_right = lax.ppermute(kv_weight, "sample", X_RIGHT)
    weight_left = lax.ppermute(kv_weight, "sample", X_LEFT)
    block, query = prepare(queries, page_where, comp_pages, preempted)
    states = prompt_states.reshape(4, 4, ROWS, SLICE)
    own_states, to_far = pick_far(states)
    slices, own_states, to_far, block = tie(
        ((kv_weight, weight_right, weight_left, weight_far), own_states, to_far, block)
    )
    blocks = [block] + [lax.ppermute(block, "sample", to) for to in (Z_UP, Z_DOWN, Z_FAR)]
    to_right, to_left, last_right, last_left, far_blocks = pick_near(states, blocks)
    rows_far = lax.ppermute(to_far, "sample", X_FAR)
    rows_right = lax.ppermute(to_right, "sample", X_RIGHT)
    rows_left = lax.ppermute(to_left, "sample", X_LEFT)

    here = jnp.stack(slices)
    near = lax.ppermute(here, "prompt", Y_SPLIT)
    here_other = lax.ppermute(here, "prompt", SWAP)
    near_other = lax.ppermute(here_other, "prompt", Y_SPLIT)
    local_alive = jnp.where(preempted[0] > 0, 0, comp_pages[0])
    local = local_attention(local_alive, query, new_kv[0], local_pages[0, 0])
    near, near_other, rows_far, local = tie((near, near_other, rows_far, local))
    far = [lax.ppermute(half, "prompt", Y_SPLIT) for half in (near[:2], near[2:])]
    near_swapped = lax.ppermute(near, "prompt", SWAP)
    near_other_swapped = lax.ppermute(near_other, "prompt", SWAP)
    far, rows_right, rows_left = tie((far, rows_right, rows_left))
    far_other = [lax.ppermute(half, "prompt", SWAP) for half in far]
    pieces = [
        here, here_other, near, near_other, near_swapped, near_other_swapped, *far, *far_other,
    ]
    others = [own_states, rows_right, rows_left, rows_far]

    far_l = product_far(others, pieces[:4], 0, "product_far_l")
    far_other[0], far_l = tie((far_other[0], far_l))
    pieces[8] = far_other[0]
    far_r = product_far(others, pieces[4:], 4, "product_far_r")
    from_down = lax.ppermute(far_l, "sample", Z_UP)
    from_up = lax.ppermute(far_r, "sample", Z_DOWN)
    far_blocks, rows_right = tie((far_blocks, rows_right))
    far_blocks = lax.ppermute(far_blocks, "sample", X_FAR)
    up_l, up_r, down_l, down_r = product(
        others, pieces, ((1,) * 4, (2,) * 4), BF16, "product_near"
    )
    up_r, down_l = lax.ppermute(up_r, "sample", Z_UP), lax.ppermute(down_l, "sample", Z_DOWN)
    from_down, from_up, far_blocks = tie((from_down, from_up, far_blocks))
    up_l, down_r = relay(up_l, down_r, from_down, from_up)
    sums = [
        lax.ppermute(up_l, "sample", Z_UP),
        up_r,
        down_l,
        lax.ppermute(down_r, "sample", Z_DOWN),
    ]

    arrived, up_l = tie(([rows_right, rows_left, far_blocks], up_l))
    queries_all, by_group, slots, alive = unpack(blocks, arrived)
    pool = pool_attention(slots, alive, queries_all, pool_pages[0, 0])
    last_right = lax.ppermute(last_right, "sample", X_RIGHT)
    last_left = lax.ppermute(last_left, "sample", X_LEFT)
    mine, pool = tie(([own_states, last_right, last_left, rows_far], pool))
    sums = [*product(mine, pieces, ((3, 0, 0, 3),), F32, "product_own"), *sums]

    cache, packed = prefix_attention(prompt_pages, sums, by_group, pool)
    arrived = lax.all_to_all(packed, "sample", split_axis=0, concat_axis=0, tiled=True)
    attended = combine(arrived, local)
    return (cache, attended)


def solution(mesh):
    return jax.shard_map(
        per_device,
        mesh=mesh,
        in_specs=(
            P("prompt", None, "sample"),
            P("sample", "prompt"),
            P("prompt", "sample", None),
            P("prompt", "sample", None),
            P("prompt", "sample", None, None, None),
            P("prompt", "sample", None, None, None),
            P("prompt"),
            P("prompt", "sample"),
            P("prompt", "sample"),
            P("prompt", "sample", None),
        ),
        out_specs=(P("prompt", "sample", None), P("prompt", "sample", None)),
        check_vma=False,
    )
```

```python
import functools
import math

import jax
import jax.numpy as jnp
from jax import lax
from jax.experimental import pallas as pl
from jax.experimental.pallas import tpu as pltpu
from jax.sharding import PartitionSpec as P

QUERY_HEADS = 64
GROUPS = 8
HEADS = 8
HEAD_SIZE = 128
PAGE = 128
SAMPLES = 16
CMAX = 16
ROWS = 256
SLICE = 512
COLUMNS = 256
KVW = 2048
KEYS = GROUPS * HEAD_SIZE
PACK = QUERY_HEADS + HEADS
SENT = QUERY_HEADS + 16
LOW = -1e30
SCALE = 1.0 / math.sqrt(HEAD_SIZE)
MIB = 1 << 20
F32 = jnp.float32
BF16 = jnp.bfloat16

X_RIGHT = [(z * 4 + x, z * 4 + (x + 1) % 4) for z in range(4) for x in range(4)]
X_LEFT = [(z * 4 + x, z * 4 + (x + 3) % 4) for z in range(4) for x in range(4)]
X_FAR = [(z * 4 + x, z * 4 + (x + 2) % 4) for z in range(4) for x in range(4)]
Z_UP = [(z * 4 + x, (z + 1) % 4 * 4 + x) for z in range(4) for x in range(4)]
Z_DOWN = [(z * 4 + x, (z + 3) % 4 * 4 + x) for z in range(4) for x in range(4)]
Z_FAR = [(z * 4 + x, (z + 2) % 4 * 4 + x) for z in range(4) for x in range(4)]
SWAP = [(y * 2 + c, y * 2 + 1 - c) for y in range(4) for c in range(2)]
Y_SPLIT = [(y * 2 + c, (y + (1 if c == 0 else 3)) % 4 * 2 + c) for y in range(4) for c in range(2)]


def params(mib):
    return pltpu.CompilerParams(vmem_limit_bytes=mib * MIB)


def cost(flops, bytes_accessed):
    return pl.CostEstimate(flops=flops, bytes_accessed=bytes_accessed, transcendentals=0)


def nt_dot(a, b):
    return lax.dot_general(a, b, (((1,), (1,)), ((), ())), preferred_element_type=F32)


def put_lane(running, lane, column):
    at = lax.broadcasted_iota(jnp.int32, running.shape, len(running.shape) - 1)
    return jnp.where(at == lane, column, running)


HALF = QUERY_HEADS // 2
BLOCK = HALF + 8


def prepare_kernel(where, length, flag, query, sent, own):
    heads = [query[0, 0:1, h * HEAD_SIZE : (h + 1) * HEAD_SIZE].astype(F32) for h in range(QUERY_HEADS)]
    low, high = jnp.concatenate(heads[:HALF]), jnp.concatenate(heads[HALF:])
    own[:HALF] = low.astype(BF16)
    own[HALF:] = high.astype(BF16)
    sent[:HALF, :HEAD_SIZE] = low.astype(BF16)
    sent[:HALF, HEAD_SIZE:] = high.astype(BF16)
    plan = jnp.zeros((8, COLUMNS), F32)
    for c in range(CMAX):
        plan = put_lane(plan, c, where[0, 0, c].astype(F32))
    plan = put_lane(plan, CMAX, length[0, 0].astype(F32))
    plan = put_lane(plan, CMAX + 1, flag[0, 0].astype(F32))
    sent[HALF:] = plan.astype(BF16)


def prepare(query, where, length, flag):
    smem, vmem = pl.BlockSpec(memory_space=pltpu.SMEM), pl.BlockSpec(memory_space=pltpu.VMEM)
    return pl.pallas_call(
        prepare_kernel,
        out_shape=[
            jax.ShapeDtypeStruct((BLOCK, COLUMNS), BF16),
            jax.ShapeDtypeStruct((QUERY_HEADS, HEAD_SIZE), BF16),
        ],
        in_specs=[smem] * 3 + [vmem],
        out_specs=[vmem, vmem],
        compiler_params=params(16),
        cost_estimate=cost(1000, 1000),
        name="prepare",
    )(where, length, flag, query)


def unpack_kernel(*refs):
    own, arrived, (queries, by_group, slots, alive) = refs[:4], refs[4:7], refs[7:]
    me = lax.axis_index("sample")

    def block_of(r):
        if r < 4:
            return own[r][...].astype(F32)
        source = arrived[r // 4 - 1]
        first = source.shape[0] - 2 * BLOCK + r % 4 // 2 * BLOCK
        lanes = slice(r % 2 * COLUMNS, (r % 2 + 1) * COLUMNS)
        return source[first : first + BLOCK, lanes].astype(F32)

    plans = []
    for r in range(SAMPLES):
        block = block_of(r)
        for half in range(2):
            lanes = slice(half * HEAD_SIZE, (half + 1) * HEAD_SIZE)
            queries[r, half * HALF : (half + 1) * HALF] = block[:HALF, lanes].astype(BF16)
        plans.append(block[HALF : HALF + 1])
    for g in range(GROUPS):
        lanes = slice(g // 4 * HEAD_SIZE, (g // 4 + 1) * HEAD_SIZE)
        rows = slice(g % 4 * HEADS, (g % 4 + 1) * HEADS)
        parts = [block_of(r)[rows, lanes] for r in range(SAMPLES)]
        by_group[g] = jnp.concatenate(parts).astype(BF16)
    plan = jnp.concatenate(plans)
    lane = lax.broadcasted_iota(jnp.int32, plan.shape, 1)
    first = (me * CMAX).astype(F32)
    here = (lane < CMAX) & (plan >= first) & (plan < first + CMAX)
    live = here & (lane.astype(F32) < plan[:, CMAX : CMAX + 1]) & (plan[:, CMAX + 1 : CMAX + 2] > 0.5)
    slot = jnp.sum(jnp.where(here, plan - first, 0.0), axis=1, keepdims=True).astype(jnp.int32)
    some = jnp.max(jnp.where(live, 1.0, 0.0), axis=1, keepdims=True).astype(jnp.int32)
    for r in range(SAMPLES):
        slots[r] = slot[r, 0]
        alive[r] = some[r, 0]


def unpack(own, arrived):
    smem, vmem = pl.BlockSpec(memory_space=pltpu.SMEM), pl.BlockSpec(memory_space=pltpu.VMEM)
    return pl.pallas_call(
        unpack_kernel,
        out_shape=[
            jax.ShapeDtypeStruct((SAMPLES, QUERY_HEADS, HEAD_SIZE), BF16),
            jax.ShapeDtypeStruct((GROUPS, SAMPLES * HEADS, HEAD_SIZE), BF16),
            jax.ShapeDtypeStruct((SAMPLES,), jnp.int32),
            jax.ShapeDtypeStruct((SAMPLES,), jnp.int32),
        ],
        in_specs=[vmem] * 7,
        out_specs=[vmem, vmem, smem, smem],
        compiler_params=params(16),
        cost_estimate=cost(1000, 1000),
        name="unpack",
    )(*own, *arrived)


STEPS = (0, 1, 3, 2)
NEXT = (2, 1, 3, 0)


PAD = 16


def copy_rows(states, sems, wanted):
    me = lax.axis_index("sample")
    z, x = me // 4, lax.rem(me, 4)
    copies = [
        pltpu.make_async_copy(
            states.at[lax.rem(z + NEXT[k], 4), lax.rem(x + step, 4)], target, sems.at[n]
        )
        for n, (step, k, target) in enumerate(wanted)
    ]
    for copy in copies:
        copy.start()
    return copies


def block_rows(k):
    return pl.ds(k * ROWS, ROWS)


def pick_far_kernel(states, own, far, sems):
    wanted = [(2, k, far.at[block_rows(k)]) for k in range(4)]
    wanted += [(0, k, own.at[block_rows(k)]) for k in range(4)]
    copies = copy_rows(states, sems, wanted)
    far[4 * ROWS :] = jnp.zeros((PAD, SLICE), BF16)
    for copy in copies:
        copy.wait()


def pick_far(states):
    vmem = pl.BlockSpec(memory_space=pltpu.VMEM)
    return pl.pallas_call(
        pick_far_kernel,
        out_shape=[
            jax.ShapeDtypeStruct((4 * ROWS, SLICE), BF16),
            jax.ShapeDtypeStruct((4 * ROWS + PAD, SLICE), BF16),
        ],
        in_specs=[pl.BlockSpec(memory_space=pl.ANY)],
        out_specs=[vmem] * 2,
        scratch_shapes=[pltpu.SemaphoreType.DMA((8,))],
        compiler_params=params(50),
        cost_estimate=cost(1000, 1000),
        name="pick_far",
    )(states)


def put_blocks(target, first, blocks):
    for r, block in enumerate(blocks):
        rows = slice(first + r // 2 * BLOCK, first + (r // 2 + 1) * BLOCK)
        target[rows, r % 2 * COLUMNS : (r % 2 + 1) * COLUMNS] = block[...]


def pick_near_kernel(states, *refs):
    blocks, (right, left, last_right, last_left, far_blocks), sems = refs[:4], refs[4:9], refs[9]
    wanted = [(1, k, right.at[block_rows(k)]) for k in range(3)]
    wanted += [(3, k, left.at[block_rows(k)]) for k in range(3)]
    wanted += [(1, 3, last_right.at[block_rows(0)]), (3, 3, last_left.at[block_rows(0)])]
    copies = copy_rows(states, sems, wanted)
    put_blocks(last_right, ROWS, blocks)
    put_blocks(last_left, ROWS, blocks)
    put_blocks(far_blocks, 0, blocks)
    for copy in copies:
        copy.wait()


def pick_near(states, blocks):
    vmem = pl.BlockSpec(memory_space=pltpu.VMEM)
    return pl.pallas_call(
        pick_near_kernel,
        out_shape=[jax.ShapeDtypeStruct((3 * ROWS, SLICE), BF16)] * 2
        + [jax.ShapeDtypeStruct((ROWS + 2 * BLOCK, SLICE), BF16)] * 2
        + [jax.ShapeDtypeStruct((2 * BLOCK, SLICE), BF16)],
        in_specs=[pl.BlockSpec(memory_space=pl.ANY)] + [vmem] * 4,
        out_specs=[vmem] * 5,
        scratch_shapes=[pltpu.SemaphoreType.DMA((8,))],
        compiler_params=params(44),
        cost_estimate=cost(1000, 1000),
        name="pick_near",
    )(states, *blocks)


def weight_of(pieces, j, d):
    return pieces[j][d] if j < 6 else pieces[2 * j - 6 + d // 2][d % 2]


def product_kernel(blocks, *refs):
    states, pieces, outs = refs[:4], refs[4:14], refs[14:]
    for j in range(8):
        for k, block in enumerate(blocks):
            total = jnp.zeros((ROWS, COLUMNS), F32)
            for d in range(4):
                at = block[d] * ROWS
                total += jnp.dot(
                    states[d][at : at + ROWS], weight_of(pieces, j, d), preferred_element_type=F32
                )
            out = outs[2 * k + j // 4]
            out[:, (j % 4) * COLUMNS : (j % 4 + 1) * COLUMNS] = total.astype(out.dtype)


def product(states, pieces, blocks, kind, name):
    vmem = pl.BlockSpec(memory_space=pltpu.VMEM)
    outs = [jax.ShapeDtypeStruct((ROWS, KVW // 2), kind)] * (2 * len(blocks))
    return pl.pallas_call(
        functools.partial(product_kernel, blocks),
        out_shape=outs,
        in_specs=[vmem] * 14,
        out_specs=[vmem] * len(outs),
        compiler_params=params(20),
        cost_estimate=cost(1000, 1000),
        name=name,
    )(*states, *pieces)


def product_far_kernel(first, *refs):
    states, pieces, out = refs[:4], refs[4:-1], refs[-1]
    for j in range(4):
        total = jnp.zeros((ROWS, COLUMNS), F32)
        for d in range(4):
            part = pieces[j][d] if first + j < 6 else weight_of((None,) * 4 + pieces, first + j, d)
            total += jnp.dot(states[d][:ROWS], part, preferred_element_type=F32)
        out[:, j * COLUMNS : (j + 1) * COLUMNS] = total.astype(BF16)


def product_far(states, pieces, first, name):
    vmem = pl.BlockSpec(memory_space=pltpu.VMEM)
    return pl.pallas_call(
        functools.partial(product_far_kernel, first),
        out_shape=jax.ShapeDtypeStruct((ROWS, KVW // 2), BF16),
        in_specs=[vmem] * (4 + len(pieces)),
        out_specs=vmem,
        compiler_params=params(20),
        cost_estimate=cost(1000, 1000),
        name=name,
    )(*states, *pieces)


def relay_kernel(up, down, from_down, from_up, up_out, down_out):
    up_out[...] = (up[...].astype(F32) + from_down[...].astype(F32)).astype(BF16)
    down_out[...] = (down[...].astype(F32) + from_up[...].astype(F32)).astype(BF16)


def relay(up, down, from_down, from_up):
    vmem = pl.BlockSpec(memory_space=pltpu.VMEM)
    return pl.pallas_call(
        relay_kernel,
        out_shape=[jax.ShapeDtypeStruct((ROWS, KVW // 2), BF16)] * 2,
        in_specs=[vmem] * 4,
        out_specs=[vmem] * 2,
        compiler_params=params(16),
        cost_estimate=cost(1000, 1000),
        name="relay_sums",
    )(up, down, from_down, from_up)


def log_rows(logs):
    out = jnp.full((HEADS, HEAD_SIZE), LOW, F32)
    for g in range(GROUPS):
        out = put_lane(out, g, logs[g * HEADS : (g + 1) * HEADS])
    return out


POOL_PAGES = 4


def page_kernel(slots, alive, query, *refs):
    pages, out = refs[:POOL_PAGES], refs[POOL_PAGES]
    step = pl.program_id(0)
    scores = []
    for k in range(POOL_PAGES):
        for g in range(GROUPS):
            keys = pages[k][0, :, g * HEAD_SIZE : (g + 1) * HEAD_SIZE]
            scores.append(nt_dot(query[k, g * HEADS : (g + 1) * HEADS], keys))
    scores = jnp.concatenate(scores) * SCALE
    top = jnp.max(scores, axis=-1, keepdims=True)
    exponent = jnp.exp(scores - top)
    total = jnp.sum(exponent, axis=-1, keepdims=True)
    logs, share = top + jnp.log(total), 1.0 / total
    for k in range(POOL_PAGES):
        live = alive[step * POOL_PAGES + k] != 0
        for g in range(GROUPS):
            rows = slice(k * QUERY_HEADS + g * HEADS, k * QUERY_HEADS + (g + 1) * HEADS)
            values = pages[k][0, :, KEYS + g * HEAD_SIZE : KEYS + (g + 1) * HEAD_SIZE]
            mixture = jnp.dot(exponent[rows].astype(BF16), values, preferred_element_type=F32)
            out[k, g * HEADS : (g + 1) * HEADS] = jnp.where(live, mixture * share[rows], 0.0)
        mine = log_rows(logs[k * QUERY_HEADS : (k + 1) * QUERY_HEADS])
        out[k, QUERY_HEADS:] = jnp.where(live, mine, LOW)


def pool_attention(slots, alive, queries_all, pool):
    def page_of(k):
        return lambda s, slots, alive: (slots[s * POOL_PAGES + k], 0, 0)

    return pl.pallas_call(
        page_kernel,
        out_shape=jax.ShapeDtypeStruct((SAMPLES, PACK, HEAD_SIZE), F32),
        grid_spec=pltpu.PrefetchScalarGridSpec(
            num_scalar_prefetch=2,
            grid=(SAMPLES // POOL_PAGES,),
            in_specs=[
                pl.BlockSpec(
                    (POOL_PAGES, QUERY_HEADS, HEAD_SIZE), lambda s, slots, alive: (s, 0, 0)
                )
            ]
            + [pl.BlockSpec((1, PAGE, KVW), page_of(k)) for k in range(POOL_PAGES)],
            out_specs=pl.BlockSpec(
                (POOL_PAGES, PACK, HEAD_SIZE), lambda s, slots, alive: (s, 0, 0)
            ),
        ),
        compiler_params=params(16),
        cost_estimate=cost(1000, 1000),
        name="pool_attention",
    )(slots, alive, queries_all, *[pool] * POOL_PAGES)


LOCAL_PAGES = 4


def local_kernel(pages_alive, query, new, pages, out, top_ref, sum_ref, mix_ref):
    step = pl.program_id(0)
    width = LOCAL_PAGES * PAGE

    @pl.when(step == 0)
    def _():
        for g in range(GROUPS):
            rows = slice(g * HEADS, (g + 1) * HEADS)
            lanes = slice(g * HEAD_SIZE, (g + 1) * HEAD_SIZE)
            value_lanes = slice(KEYS + g * HEAD_SIZE, KEYS + (g + 1) * HEAD_SIZE)
            products = query[rows].astype(F32) * new[0:1, lanes].astype(F32)
            top_ref[rows] = jnp.sum(products, axis=-1, keepdims=True) * SCALE
            sum_ref[rows] = jnp.ones((HEADS, 1), F32)
            mix_ref[rows] = jnp.broadcast_to(new[0:1, value_lanes].astype(F32), (HEADS, HEAD_SIZE))

    @pl.when(step * LOCAL_PAGES < pages_alive[0])
    def _():
        block = pages.reshape(width, KVW)
        at = step * width + lax.broadcasted_iota(jnp.int32, (QUERY_HEADS, width), 1)
        live = at < pages_alive[0] * PAGE
        scores = jnp.concatenate(
            [
                nt_dot(
                    query[g * HEADS : (g + 1) * HEADS],
                    block[:, g * HEAD_SIZE : (g + 1) * HEAD_SIZE],
                )
                for g in range(GROUPS)
            ]
        )
        scores = jnp.where(live, scores * SCALE, LOW)
        old = top_ref[...]
        top = jnp.maximum(old, jnp.max(scores, axis=-1, keepdims=True))
        shrink = jnp.exp(old - top)
        exponent = jnp.where(live, jnp.exp(scores - top), 0.0)
        top_ref[...] = top
        sum_ref[...] = sum_ref[...] * shrink + jnp.sum(exponent, axis=-1, keepdims=True)
        for g in range(GROUPS):
            rows = slice(g * HEADS, (g + 1) * HEADS)
            values = block[:, KEYS + g * HEAD_SIZE : KEYS + (g + 1) * HEAD_SIZE]
            mix_ref[rows] = mix_ref[rows] * shrink[rows] + jnp.dot(
                exponent[rows].astype(BF16), values, preferred_element_type=F32
            )

    @pl.when(step == CMAX // LOCAL_PAGES - 1)
    def _():
        out[:QUERY_HEADS] = mix_ref[...] / sum_ref[...]
        out[QUERY_HEADS:] = log_rows(top_ref[...] + jnp.log(sum_ref[...]))


def local_attention(pages_alive, query, new, pages):
    def block_of(step, alive):
        last = jnp.maximum(alive[0] - 1, 0) // LOCAL_PAGES
        return (jnp.minimum(step, last), 0, 0)

    return pl.pallas_call(
        local_kernel,
        out_shape=jax.ShapeDtypeStruct((PACK, HEAD_SIZE), F32),
        grid_spec=pltpu.PrefetchScalarGridSpec(
            num_scalar_prefetch=1,
            grid=(CMAX // LOCAL_PAGES,),
            in_specs=[
                pl.BlockSpec((QUERY_HEADS, HEAD_SIZE), lambda step, alive: (0, 0)),
                pl.BlockSpec((1, KVW), lambda step, alive: (0, 0)),
                pl.BlockSpec((LOCAL_PAGES, PAGE, KVW), block_of),
            ],
            out_specs=pl.BlockSpec((PACK, HEAD_SIZE), lambda step, alive: (0, 0)),
            scratch_shapes=[
                pltpu.VMEM((QUERY_HEADS, 1), F32),
                pltpu.VMEM((QUERY_HEADS, 1), F32),
                pltpu.VMEM((QUERY_HEADS, HEAD_SIZE), F32),
            ],
        ),
        compiler_params=params(16),
        cost_estimate=cost(1000, 1000),
        name="local_attention",
    )(pages_alive, query, new, pages)


def prefix_kernel(
    prompt_pages, own_l, own_r, up_l, up_r, down_l, down_r, queries, pool, cache, packed
):
    me, prompt = lax.axis_index("sample"), lax.axis_index("prompt")
    z, x = me // 4, lax.rem(me, 4)
    y, core = prompt // 2, lax.rem(prompt, 2)
    near = lax.rem(y + 3 - 2 * core, 4)
    other = lax.rem(y + 1 + 2 * core, 4)
    far = lax.rem(y + 2, 4)
    columns = (
        2 * y + core, 2 * y + 1 - core, 2 * near + core, 2 * near + 1 - core,
        2 * other + 1 - core, 2 * other + core, 2 * far + core, 2 * far + 1 - core,
    )
    for j in range(8):
        lanes = slice((j % 4) * COLUMNS, (j % 4 + 1) * COLUMNS)
        own, up, down = (own_l, up_l, down_l) if j < 4 else (own_r, up_r, down_r)
        total = own[:, lanes] + up[:, lanes].astype(F32) + down[:, lanes].astype(F32)
        target = pl.ds(pl.multiple_of(columns[j] * COLUMNS, COLUMNS), COLUMNS)
        cache[0, :, target] = total.astype(BF16)
    sources = [
        lax.rem(z + 4 - dz, 4) * 4 + lax.rem(x + 4 - dx, 4) for dx in STEPS for dz in STEPS
    ]
    live = lax.broadcasted_iota(jnp.int32, (SAMPLES * HEADS, ROWS), 1) < prompt_pages[0] * PAGE - me * ROWS
    logs = jnp.full((SAMPLES * HEADS, HEAD_SIZE), LOW, F32)
    for g in range(GROUPS):
        keys = cache[0, :, g * HEAD_SIZE : (g + 1) * HEAD_SIZE]
        values = cache[0, :, KEYS + g * HEAD_SIZE : KEYS + (g + 1) * HEAD_SIZE]
        scores = jnp.where(live, nt_dot(queries[g], keys) * SCALE, LOW)
        top = jnp.max(scores, axis=-1, keepdims=True)
        exponent = jnp.where(live, jnp.exp(scores - top), 0.0)
        total = jnp.sum(exponent, axis=-1, keepdims=True)
        mixture = jnp.dot(exponent.astype(BF16), values, preferred_element_type=F32)
        some = total > 0.0
        total = jnp.where(some, total, 1.0)
        log = jnp.where(some, top + jnp.log(total), LOW)
        rows = slice(g * HEADS, (g + 1) * HEADS)
        pool_log = pool[:, QUERY_HEADS:, g : g + 1].reshape(SAMPLES * HEADS, 1)
        pool_mixture = pool[:, rows].reshape(SAMPLES * HEADS, HEAD_SIZE)
        high = jnp.maximum(log, pool_log)
        here, there = jnp.exp(log - high), jnp.exp(pool_log - high)
        both = here + there
        merged = mixture * (here / (total * both)) + pool_mixture * (there / both)
        for r, source in enumerate(sources):
            packed[source, rows] = merged[r * HEADS : (r + 1) * HEADS].astype(BF16)
        logs = put_lane(logs, g, high + jnp.log(both))
    first = logs.astype(BF16).astype(F32)
    second = (logs - first).astype(BF16).astype(F32)
    third = logs - first - second
    lane = lax.broadcasted_iota(jnp.int32, logs.shape, 1)
    later = jnp.where(lane < 2 * GROUPS, pltpu.roll(second, GROUPS, 1), pltpu.roll(third, 2 * GROUPS, 1))
    terms = jnp.where(lane < GROUPS, first, jnp.where(lane < 3 * GROUPS, later, 0.0))
    padding = jnp.zeros((SENT - QUERY_HEADS - HEADS, HEAD_SIZE), F32)
    for r, source in enumerate(sources):
        rows = jnp.concatenate([terms[r * HEADS : (r + 1) * HEADS], padding])
        packed[source, QUERY_HEADS:] = rows.astype(BF16)


def prefix_attention(prompt_pages, parts, queries, pool):
    smem, vmem = pl.BlockSpec(memory_space=pltpu.SMEM), pl.BlockSpec(memory_space=pltpu.VMEM)
    return pl.pallas_call(
        prefix_kernel,
        out_shape=[
            jax.ShapeDtypeStruct((1, ROWS, KVW), BF16),
            jax.ShapeDtypeStruct((SAMPLES, SENT, HEAD_SIZE), BF16),
        ],
        in_specs=[smem] + [vmem] * 8,
        out_specs=[vmem, vmem],
        compiler_params=params(20),
        cost_estimate=cost(300_000_000, 6 * MIB),
        name="prefix_attention",
    )(prompt_pages, *parts, queries, pool)


def combine_kernel(arrived, local, out):
    terms = arrived[:, QUERY_HEADS:].astype(F32)
    for g in range(GROUPS):
        rows = slice(g * HEADS, (g + 1) * HEADS)
        logs = sum(terms[:, :HEADS, lane : lane + 1] for lane in (g, g + GROUPS, g + 2 * GROUPS))
        local_log = local[QUERY_HEADS:, g : g + 1]
        high = jnp.maximum(jnp.max(logs, axis=0), local_log)
        shares = jnp.exp(logs - high[None])
        local_share = jnp.exp(local_log - high)
        total = jnp.sum(shares, axis=0) + local_share
        mixture = jnp.sum(arrived[:, rows].astype(F32) * shares, axis=0) + local[rows] * local_share
        mixture = (mixture / total).astype(BF16)
        for h in range(HEADS):
            lanes = slice((g * HEADS + h) * HEAD_SIZE, (g * HEADS + h + 1) * HEAD_SIZE)
            out[0, :, lanes] = mixture[h : h + 1]


def combine(arrived, local):
    vmem = pl.BlockSpec(memory_space=pltpu.VMEM)
    return pl.pallas_call(
        combine_kernel,
        out_shape=jax.ShapeDtypeStruct((1, 1, QUERY_HEADS * HEAD_SIZE), BF16),
        in_specs=[vmem, vmem],
        out_specs=vmem,
        compiler_params=params(16),
        cost_estimate=cost(1_000_000, MIB),
        name="combine",
    )(arrived, local)


def per_device(
    prompt_states,
    kv_weight,
    queries,
    new_kv,
    local_pages,
    pool_pages,
    prompt_pages,
    comp_pages,
    preempted,
    page_where,
):
    tie = lax.optimization_barrier

    weight_far = lax.ppermute(kv_weight, "sample", X_FAR)
    weight_right = lax.ppermute(kv_weight, "sample", X_RIGHT)
    weight_left = lax.ppermute(kv_weight, "sample", X_LEFT)
    block, query = prepare(queries, page_where, comp_pages, preempted)
    states = prompt_states.reshape(4, 4, ROWS, SLICE)
    own_states, to_far = pick_far(states)
    slices, own_states, to_far, block = tie(
        ((kv_weight, weight_right, weight_left, weight_far), own_states, to_far, block)
    )
    blocks = [block] + [lax.ppermute(block, "sample", to) for to in (Z_UP, Z_DOWN, Z_FAR)]
    to_right, to_left, last_right, last_left, far_blocks = pick_near(states, blocks)
    rows_far = lax.ppermute(to_far, "sample", X_FAR)
    rows_right = lax.ppermute(to_right, "sample", X_RIGHT)
    rows_left = lax.ppermute(to_left, "sample", X_LEFT)

    here = jnp.stack(slices)
    near = lax.ppermute(here, "prompt", Y_SPLIT)
    here_other = lax.ppermute(here, "prompt", SWAP)
    near_other = lax.ppermute(here_other, "prompt", Y_SPLIT)
    local_alive = jnp.where(preempted[0] > 0, 0, comp_pages[0])
    local = local_attention(local_alive, query, new_kv[0], local_pages[0, 0])
    near, near_other, rows_far, local = tie((near, near_other, rows_far, local))
    far = [lax.ppermute(half, "prompt", Y_SPLIT) for half in (near[:2], near[2:])]
    near_swapped = lax.ppermute(near, "prompt", SWAP)
    near_other_swapped = lax.ppermute(near_other, "prompt", SWAP)
    far, rows_right, rows_left = tie((far, rows_right, rows_left))
    far_other = [lax.ppermute(half, "prompt", SWAP) for half in far]
    pieces = [
        here, here_other, near, near_other, near_swapped, near_other_swapped, *far, *far_other,
    ]
    others = [own_states, rows_right, rows_left, rows_far]

    far_l = product_far(others, pieces[:4], 0, "product_far_l")
    far_other[0], far_l = tie((far_other[0], far_l))
    pieces[8] = far_other[0]
    far_r = product_far(others, pieces[4:], 4, "product_far_r")
    from_down = lax.ppermute(far_l, "sample", Z_UP)
    from_up = lax.ppermute(far_r, "sample", Z_DOWN)
    far_blocks, rows_right = tie((far_blocks, rows_right))
    far_blocks = lax.ppermute(far_blocks, "sample", X_FAR)
    up_l, up_r, down_l, down_r = product(
        others, pieces, ((1,) * 4, (2,) * 4), BF16, "product_near"
    )
    up_r, down_l = lax.ppermute(up_r, "sample", Z_UP), lax.ppermute(down_l, "sample", Z_DOWN)
    from_down, from_up, far_blocks = tie((from_down, from_up, far_blocks))
    up_l, down_r = relay(up_l, down_r, from_down, from_up)
    sums = [
        lax.ppermute(up_l, "sample", Z_UP),
        up_r,
        down_l,
        lax.ppermute(down_r, "sample", Z_DOWN),
    ]

    last_right = lax.ppermute(last_right, "sample", X_RIGHT)
    last_left = lax.ppermute(last_left, "sample", X_LEFT)
    queries_all, by_group, slots, alive = unpack(blocks, [last_right, last_left, far_blocks])
    pool = pool_attention(slots, alive, queries_all, pool_pages[0, 0])
    mine, pool = tie(([own_states, last_right, last_left, rows_far], pool))
    sums = [*product(mine, pieces, ((3, 0, 0, 3),), F32, "product_own"), *sums]

    cache, packed = prefix_attention(prompt_pages, sums, by_group, pool)
    arrived = lax.all_to_all(packed, "sample", split_axis=0, concat_axis=0, tiled=True)
    attended = combine(arrived, local)
    return (cache, attended)


def solution(mesh):
    return jax.shard_map(
        per_device,
        mesh=mesh,
        in_specs=(
            P("prompt", None, "sample"),
            P("sample", "prompt"),
            P("prompt", "sample", None),
            P("prompt", "sample", None),
            P("prompt", "sample", None, None, None),
            P("prompt", "sample", None, None, None),
            P("prompt"),
            P("prompt", "sample"),
            P("prompt", "sample"),
            P("prompt", "sample", None),
        ),
        out_specs=(P("prompt", "sample", None), P("prompt", "sample", None)),
        check_vma=False,
    )
```

```python
import functools
import math

import jax
import jax.numpy as jnp
from jax import lax
from jax.experimental import pallas as pl
from jax.experimental.pallas import tpu as pltpu
from jax.sharding import PartitionSpec as P

QUERY_HEADS = 64
GROUPS = 8
HEADS = 8
HEAD_SIZE = 128
PAGE = 128
SAMPLES = 16
CMAX = 16
ROWS = 256
SLICE = 512
COLUMNS = 256
KVW = 2048
KEYS = GROUPS * HEAD_SIZE
PACK = QUERY_HEADS + HEADS
SENT = QUERY_HEADS + 16
LOW = -1e30
SCALE = 1.0 / math.sqrt(HEAD_SIZE)
MIB = 1 << 20
F32 = jnp.float32
BF16 = jnp.bfloat16

X_RIGHT = [(z * 4 + x, z * 4 + (x + 1) % 4) for z in range(4) for x in range(4)]
X_LEFT = [(z * 4 + x, z * 4 + (x + 3) % 4) for z in range(4) for x in range(4)]
X_FAR = [(z * 4 + x, z * 4 + (x + 2) % 4) for z in range(4) for x in range(4)]
Z_UP = [(z * 4 + x, (z + 1) % 4 * 4 + x) for z in range(4) for x in range(4)]
Z_DOWN = [(z * 4 + x, (z + 3) % 4 * 4 + x) for z in range(4) for x in range(4)]
Z_FAR = [(z * 4 + x, (z + 2) % 4 * 4 + x) for z in range(4) for x in range(4)]
SWAP = [(y * 2 + c, y * 2 + 1 - c) for y in range(4) for c in range(2)]
Y_SPLIT = [(y * 2 + c, (y + (1 if c == 0 else 3)) % 4 * 2 + c) for y in range(4) for c in range(2)]


def params(mib):
    return pltpu.CompilerParams(vmem_limit_bytes=mib * MIB)


def cost(flops, bytes_accessed):
    return pl.CostEstimate(flops=flops, bytes_accessed=bytes_accessed, transcendentals=0)


def nt_dot(a, b):
    return lax.dot_general(a, b, (((1,), (1,)), ((), ())), preferred_element_type=F32)


def put_lane(running, lane, column):
    at = lax.broadcasted_iota(jnp.int32, running.shape, len(running.shape) - 1)
    return jnp.where(at == lane, column, running)


HALF = QUERY_HEADS // 2
BLOCK = HALF + 8


def prepare_kernel(where, length, flag, query, sent, own):
    heads = [query[0, 0:1, h * HEAD_SIZE : (h + 1) * HEAD_SIZE].astype(F32) for h in range(QUERY_HEADS)]
    low, high = jnp.concatenate(heads[:HALF]), jnp.concatenate(heads[HALF:])
    own[:HALF] = low.astype(BF16)
    own[HALF:] = high.astype(BF16)
    sent[:HALF, :HEAD_SIZE] = low.astype(BF16)
    sent[:HALF, HEAD_SIZE:] = high.astype(BF16)
    plan = jnp.zeros((8, COLUMNS), F32)
    for c in range(CMAX):
        plan = put_lane(plan, c, where[0, 0, c].astype(F32))
    plan = put_lane(plan, CMAX, length[0, 0].astype(F32))
    plan = put_lane(plan, CMAX + 1, flag[0, 0].astype(F32))
    sent[HALF:] = plan.astype(BF16)


def prepare(query, where, length, flag):
    smem, vmem = pl.BlockSpec(memory_space=pltpu.SMEM), pl.BlockSpec(memory_space=pltpu.VMEM)
    return pl.pallas_call(
        prepare_kernel,
        out_shape=[
            jax.ShapeDtypeStruct((BLOCK, COLUMNS), BF16),
            jax.ShapeDtypeStruct((QUERY_HEADS, HEAD_SIZE), BF16),
        ],
        in_specs=[smem] * 3 + [vmem],
        out_specs=[vmem, vmem],
        compiler_params=params(16),
        cost_estimate=cost(1000, 1000),
        name="prepare",
    )(where, length, flag, query)


def unpack_kernel(*refs):
    own, arrived, (queries, by_group, slots, alive) = refs[:4], refs[4:7], refs[7:]
    me = lax.axis_index("sample")

    def block_of(r):
        if r < 4:
            return own[r][...].astype(F32)
        source = arrived[r // 4 - 1]
        first = source.shape[0] - 2 * BLOCK + r % 4 // 2 * BLOCK
        lanes = slice(r % 2 * COLUMNS, (r % 2 + 1) * COLUMNS)
        return source[first : first + BLOCK, lanes].astype(F32)

    plans = []
    for r in range(SAMPLES):
        block = block_of(r)
        for half in range(2):
            lanes = slice(half * HEAD_SIZE, (half + 1) * HEAD_SIZE)
            queries[r, half * HALF : (half + 1) * HALF] = block[:HALF, lanes].astype(BF16)
        plans.append(block[HALF : HALF + 1])
    for g in range(GROUPS):
        lanes = slice(g // 4 * HEAD_SIZE, (g // 4 + 1) * HEAD_SIZE)
        rows = slice(g % 4 * HEADS, (g % 4 + 1) * HEADS)
        parts = [block_of(r)[rows, lanes] for r in range(SAMPLES)]
        by_group[g] = jnp.concatenate(parts).astype(BF16)
    plan = jnp.concatenate(plans)
    lane = lax.broadcasted_iota(jnp.int32, plan.shape, 1)
    first = (me * CMAX).astype(F32)
    here = (lane < CMAX) & (plan >= first) & (plan < first + CMAX)
    live = here & (lane.astype(F32) < plan[:, CMAX : CMAX + 1]) & (plan[:, CMAX + 1 : CMAX + 2] > 0.5)
    slot = jnp.sum(jnp.where(here, plan - first, 0.0), axis=1, keepdims=True).astype(jnp.int32)
    some = jnp.max(jnp.where(live, 1.0, 0.0), axis=1, keepdims=True).astype(jnp.int32)
    for r in range(SAMPLES):
        slots[r] = slot[r, 0]
        alive[r] = some[r, 0]


def unpack(own, arrived):
    smem, vmem = pl.BlockSpec(memory_space=pltpu.SMEM), pl.BlockSpec(memory_space=pltpu.VMEM)
    return pl.pallas_call(
        unpack_kernel,
        out_shape=[
            jax.ShapeDtypeStruct((SAMPLES, QUERY_HEADS, HEAD_SIZE), BF16),
            jax.ShapeDtypeStruct((GROUPS, SAMPLES * HEADS, HEAD_SIZE), BF16),
            jax.ShapeDtypeStruct((SAMPLES,), jnp.int32),
            jax.ShapeDtypeStruct((SAMPLES,), jnp.int32),
        ],
        in_specs=[vmem] * 7,
        out_specs=[vmem, vmem, smem, smem],
        compiler_params=params(16),
        cost_estimate=cost(1000, 1000),
        name="unpack",
    )(*own, *arrived)


STEPS = (0, 1, 3, 2)
NEXT = (2, 1, 3, 0)


PAD = 16


def copy_rows(states, sems, wanted):
    me = lax.axis_index("sample")
    z, x = me // 4, lax.rem(me, 4)
    copies = [
        pltpu.make_async_copy(
            states.at[lax.rem(z + NEXT[k], 4), lax.rem(x + step, 4)], target, sems.at[n]
        )
        for n, (step, k, target) in enumerate(wanted)
    ]
    for copy in copies:
        copy.start()
    return copies


def block_rows(k):
    return pl.ds(k * ROWS, ROWS)


def pick_far_kernel(states, own, far, sems):
    wanted = [(2, k, far.at[block_rows(k)]) for k in range(4)]
    wanted += [(0, k, own.at[block_rows(k)]) for k in range(4)]
    copies = copy_rows(states, sems, wanted)
    far[4 * ROWS :] = jnp.zeros((PAD, SLICE), BF16)
    for copy in copies:
        copy.wait()


def pick_far(states):
    vmem = pl.BlockSpec(memory_space=pltpu.VMEM)
    return pl.pallas_call(
        pick_far_kernel,
        out_shape=[
            jax.ShapeDtypeStruct((4 * ROWS, SLICE), BF16),
            jax.ShapeDtypeStruct((4 * ROWS + PAD, SLICE), BF16),
        ],
        in_specs=[pl.BlockSpec(memory_space=pl.ANY)],
        out_specs=[vmem] * 2,
        scratch_shapes=[pltpu.SemaphoreType.DMA((8,))],
        compiler_params=params(50),
        cost_estimate=cost(1000, 1000),
        name="pick_far",
    )(states)


def put_blocks(target, first, blocks):
    for r, block in enumerate(blocks):
        rows = slice(first + r // 2 * BLOCK, first + (r // 2 + 1) * BLOCK)
        target[rows, r % 2 * COLUMNS : (r % 2 + 1) * COLUMNS] = block[...]


def pick_near_kernel(states, *refs):
    blocks, (right, left, last_right, last_left, far_blocks), sems = refs[:4], refs[4:9], refs[9]
    wanted = [(1, k, right.at[block_rows(k)]) for k in range(3)]
    wanted += [(3, k, left.at[block_rows(k)]) for k in range(3)]
    wanted += [(1, 3, last_right.at[block_rows(0)]), (3, 3, last_left.at[block_rows(0)])]
    copies = copy_rows(states, sems, wanted)
    put_blocks(last_right, ROWS, blocks)
    put_blocks(last_left, ROWS, blocks)
    put_blocks(far_blocks, 0, blocks)
    for copy in copies:
        copy.wait()


def pick_near(states, blocks):
    vmem = pl.BlockSpec(memory_space=pltpu.VMEM)
    return pl.pallas_call(
        pick_near_kernel,
        out_shape=[jax.ShapeDtypeStruct((3 * ROWS, SLICE), BF16)] * 2
        + [jax.ShapeDtypeStruct((ROWS + 2 * BLOCK, SLICE), BF16)] * 2
        + [jax.ShapeDtypeStruct((2 * BLOCK, SLICE), BF16)],
        in_specs=[pl.BlockSpec(memory_space=pl.ANY)] + [vmem] * 4,
        out_specs=[vmem] * 5,
        scratch_shapes=[pltpu.SemaphoreType.DMA((8,))],
        compiler_params=params(44),
        cost_estimate=cost(1000, 1000),
        name="pick_near",
    )(states, *blocks)


def weight_of(pieces, j, d):
    return pieces[j][d] if j < 6 else pieces[2 * j - 6 + d // 2][d % 2]


def product_kernel(blocks, *refs):
    states, pieces, outs = refs[:4], refs[4:14], refs[14:]
    for j in range(8):
        for k, block in enumerate(blocks):
            total = jnp.zeros((ROWS, COLUMNS), F32)
            for d in range(4):
                at = block[d] * ROWS
                total += jnp.dot(
                    states[d][at : at + ROWS], weight_of(pieces, j, d), preferred_element_type=F32
                )
            out = outs[2 * k + j // 4]
            out[:, (j % 4) * COLUMNS : (j % 4 + 1) * COLUMNS] = total.astype(out.dtype)


def product(states, pieces, blocks, kind, name):
    vmem = pl.BlockSpec(memory_space=pltpu.VMEM)
    outs = [jax.ShapeDtypeStruct((ROWS, KVW // 2), kind)] * (2 * len(blocks))
    return pl.pallas_call(
        functools.partial(product_kernel, blocks),
        out_shape=outs,
        in_specs=[vmem] * 14,
        out_specs=[vmem] * len(outs),
        compiler_params=params(20),
        cost_estimate=cost(1000, 1000),
        name=name,
    )(*states, *pieces)


def product_far_kernel(first, *refs):
    states, pieces, out = refs[:4], refs[4:-1], refs[-1]
    for j in range(4):
        total = jnp.zeros((ROWS, COLUMNS), F32)
        for d in range(4):
            part = pieces[j][d] if first + j < 6 else weight_of((None,) * 4 + pieces, first + j, d)
            total += jnp.dot(states[d][:ROWS], part, preferred_element_type=F32)
        out[:, j * COLUMNS : (j + 1) * COLUMNS] = total.astype(BF16)


def product_far(states, pieces, first, name):
    vmem = pl.BlockSpec(memory_space=pltpu.VMEM)
    return pl.pallas_call(
        functools.partial(product_far_kernel, first),
        out_shape=jax.ShapeDtypeStruct((ROWS, KVW // 2), BF16),
        in_specs=[vmem] * (4 + len(pieces)),
        out_specs=vmem,
        compiler_params=params(20),
        cost_estimate=cost(1000, 1000),
        name=name,
    )(*states, *pieces)


def relay_kernel(up, down, from_down, from_up, up_out, down_out):
    up_out[...] = (up[...].astype(F32) + from_down[...].astype(F32)).astype(BF16)
    down_out[...] = (down[...].astype(F32) + from_up[...].astype(F32)).astype(BF16)


def relay(up, down, from_down, from_up):
    vmem = pl.BlockSpec(memory_space=pltpu.VMEM)
    return pl.pallas_call(
        relay_kernel,
        out_shape=[jax.ShapeDtypeStruct((ROWS, KVW // 2), BF16)] * 2,
        in_specs=[vmem] * 4,
        out_specs=[vmem] * 2,
        compiler_params=params(16),
        cost_estimate=cost(1000, 1000),
        name="relay_sums",
    )(up, down, from_down, from_up)


def log_rows(logs):
    out = jnp.full((HEADS, HEAD_SIZE), LOW, F32)
    for g in range(GROUPS):
        out = put_lane(out, g, logs[g * HEADS : (g + 1) * HEADS])
    return out


POOL_PAGES = 4


def page_kernel(slots, alive, query, *refs):
    pages, out = refs[:POOL_PAGES], refs[POOL_PAGES]
    step = pl.program_id(0)
    scores = []
    for k in range(POOL_PAGES):
        for g in range(GROUPS):
            keys = pages[k][0, :, g * HEAD_SIZE : (g + 1) * HEAD_SIZE]
            scores.append(nt_dot(query[k, g * HEADS : (g + 1) * HEADS], keys))
    scores = jnp.concatenate(scores) * SCALE
    top = jnp.max(scores, axis=-1, keepdims=True)
    exponent = jnp.exp(scores - top)
    total = jnp.sum(exponent, axis=-1, keepdims=True)
    logs, share = top + jnp.log(total), 1.0 / total
    for k in range(POOL_PAGES):
        live = alive[step * POOL_PAGES + k] != 0
        for g in range(GROUPS):
            rows = slice(k * QUERY_HEADS + g * HEADS, k * QUERY_HEADS + (g + 1) * HEADS)
            values = pages[k][0, :, KEYS + g * HEAD_SIZE : KEYS + (g + 1) * HEAD_SIZE]
            mixture = jnp.dot(exponent[rows].astype(BF16), values, preferred_element_type=F32)
            out[k, g * HEADS : (g + 1) * HEADS] = jnp.where(live, mixture * share[rows], 0.0)
        mine = log_rows(logs[k * QUERY_HEADS : (k + 1) * QUERY_HEADS])
        out[k, QUERY_HEADS:] = jnp.where(live, mine, LOW)


def pool_attention(slots, alive, queries_all, pool):
    def page_of(k):
        return lambda s, slots, alive: (slots[s * POOL_PAGES + k], 0, 0)

    return pl.pallas_call(
        page_kernel,
        out_shape=jax.ShapeDtypeStruct((SAMPLES, PACK, HEAD_SIZE), F32),
        grid_spec=pltpu.PrefetchScalarGridSpec(
            num_scalar_prefetch=2,
            grid=(SAMPLES // POOL_PAGES,),
            in_specs=[
                pl.BlockSpec(
                    (POOL_PAGES, QUERY_HEADS, HEAD_SIZE), lambda s, slots, alive: (s, 0, 0)
                )
            ]
            + [pl.BlockSpec((1, PAGE, KVW), page_of(k)) for k in range(POOL_PAGES)],
            out_specs=pl.BlockSpec(
                (POOL_PAGES, PACK, HEAD_SIZE), lambda s, slots, alive: (s, 0, 0)
            ),
        ),
        compiler_params=params(16),
        cost_estimate=cost(1000, 1000),
        name="pool_attention",
    )(slots, alive, queries_all, *[pool] * POOL_PAGES)


LOCAL_PAGES = 4


def local_kernel(pages_alive, query, new, pages, out, top_ref, sum_ref, mix_ref):
    step = pl.program_id(0)
    width = LOCAL_PAGES * PAGE

    @pl.when(step == 0)
    def _():
        for g in range(GROUPS):
            rows = slice(g * HEADS, (g + 1) * HEADS)
            lanes = slice(g * HEAD_SIZE, (g + 1) * HEAD_SIZE)
            value_lanes = slice(KEYS + g * HEAD_SIZE, KEYS + (g + 1) * HEAD_SIZE)
            products = query[rows].astype(F32) * new[0:1, lanes].astype(F32)
            top_ref[rows] = jnp.sum(products, axis=-1, keepdims=True) * SCALE
            sum_ref[rows] = jnp.ones((HEADS, 1), F32)
            mix_ref[rows] = jnp.broadcast_to(new[0:1, value_lanes].astype(F32), (HEADS, HEAD_SIZE))

    @pl.when(step * LOCAL_PAGES < pages_alive[0])
    def _():
        block = pages.reshape(width, KVW)
        at = step * width + lax.broadcasted_iota(jnp.int32, (QUERY_HEADS, width), 1)
        live = at < pages_alive[0] * PAGE
        scores = jnp.concatenate(
            [
                nt_dot(
                    query[g * HEADS : (g + 1) * HEADS],
                    block[:, g * HEAD_SIZE : (g + 1) * HEAD_SIZE],
                )
                for g in range(GROUPS)
            ]
        )
        scores = jnp.where(live, scores * SCALE, LOW)
        old = top_ref[...]
        top = jnp.maximum(old, jnp.max(scores, axis=-1, keepdims=True))
        shrink = jnp.exp(old - top)
        exponent = jnp.where(live, jnp.exp(scores - top), 0.0)
        top_ref[...] = top
        sum_ref[...] = sum_ref[...] * shrink + jnp.sum(exponent, axis=-1, keepdims=True)
        for g in range(GROUPS):
            rows = slice(g * HEADS, (g + 1) * HEADS)
            values = block[:, KEYS + g * HEAD_SIZE : KEYS + (g + 1) * HEAD_SIZE]
            mix_ref[rows] = mix_ref[rows] * shrink[rows] + jnp.dot(
                exponent[rows].astype(BF16), values, preferred_element_type=F32
            )

    @pl.when(step == CMAX // LOCAL_PAGES - 1)
    def _():
        out[:QUERY_HEADS] = mix_ref[...] / sum_ref[...]
        out[QUERY_HEADS:] = log_rows(top_ref[...] + jnp.log(sum_ref[...]))


def local_attention(pages_alive, query, new, pages):
    def block_of(step, alive):
        last = jnp.maximum(alive[0] - 1, 0) // LOCAL_PAGES
        return (jnp.minimum(step, last), 0, 0)

    return pl.pallas_call(
        local_kernel,
        out_shape=jax.ShapeDtypeStruct((PACK, HEAD_SIZE), F32),
        grid_spec=pltpu.PrefetchScalarGridSpec(
            num_scalar_prefetch=1,
            grid=(CMAX // LOCAL_PAGES,),
            in_specs=[
                pl.BlockSpec((QUERY_HEADS, HEAD_SIZE), lambda step, alive: (0, 0)),
                pl.BlockSpec((1, KVW), lambda step, alive: (0, 0)),
                pl.BlockSpec((LOCAL_PAGES, PAGE, KVW), block_of),
            ],
            out_specs=pl.BlockSpec((PACK, HEAD_SIZE), lambda step, alive: (0, 0)),
            scratch_shapes=[
                pltpu.VMEM((QUERY_HEADS, 1), F32),
                pltpu.VMEM((QUERY_HEADS, 1), F32),
                pltpu.VMEM((QUERY_HEADS, HEAD_SIZE), F32),
            ],
        ),
        compiler_params=params(16),
        cost_estimate=cost(1000, 1000),
        name="local_attention",
    )(pages_alive, query, new, pages)


def prefix_kernel(
    prompt_pages, own_l, own_r, up_l, up_r, down_l, down_r, queries, pool, cache, packed
):
    me, prompt = lax.axis_index("sample"), lax.axis_index("prompt")
    z, x = me // 4, lax.rem(me, 4)
    y, core = prompt // 2, lax.rem(prompt, 2)
    near = lax.rem(y + 3 - 2 * core, 4)
    other = lax.rem(y + 1 + 2 * core, 4)
    far = lax.rem(y + 2, 4)
    columns = (
        2 * y + core, 2 * y + 1 - core, 2 * near + core, 2 * near + 1 - core,
        2 * other + 1 - core, 2 * other + core, 2 * far + core, 2 * far + 1 - core,
    )
    for j in range(8):
        lanes = slice((j % 4) * COLUMNS, (j % 4 + 1) * COLUMNS)
        own, up, down = (own_l, up_l, down_l) if j < 4 else (own_r, up_r, down_r)
        total = own[:, lanes] + up[:, lanes].astype(F32) + down[:, lanes].astype(F32)
        target = pl.ds(pl.multiple_of(columns[j] * COLUMNS, COLUMNS), COLUMNS)
        cache[0, :, target] = total.astype(BF16)
    sources = [
        lax.rem(z + 4 - dz, 4) * 4 + lax.rem(x + 4 - dx, 4) for dx in STEPS for dz in STEPS
    ]
    live = lax.broadcasted_iota(jnp.int32, (SAMPLES * HEADS, ROWS), 1) < prompt_pages[0] * PAGE - me * ROWS
    logs = jnp.full((SAMPLES * HEADS, HEAD_SIZE), LOW, F32)
    for g in range(GROUPS):
        keys = cache[0, :, g * HEAD_SIZE : (g + 1) * HEAD_SIZE]
        values = cache[0, :, KEYS + g * HEAD_SIZE : KEYS + (g + 1) * HEAD_SIZE]
        scores = jnp.where(live, nt_dot(queries[g], keys) * SCALE, LOW)
        top = jnp.max(scores, axis=-1, keepdims=True)
        exponent = jnp.where(live, jnp.exp(scores - top), 0.0)
        total = jnp.sum(exponent, axis=-1, keepdims=True)
        mixture = jnp.dot(exponent.astype(BF16), values, preferred_element_type=F32)
        some = total > 0.0
        total = jnp.where(some, total, 1.0)
        log = jnp.where(some, top + jnp.log(total), LOW)
        rows = slice(g * HEADS, (g + 1) * HEADS)
        pool_log = pool[:, QUERY_HEADS:, g : g + 1].reshape(SAMPLES * HEADS, 1)
        pool_mixture = pool[:, rows].reshape(SAMPLES * HEADS, HEAD_SIZE)
        high = jnp.maximum(log, pool_log)
        here, there = jnp.exp(log - high), jnp.exp(pool_log - high)
        both = here + there
        merged = mixture * (here / (total * both)) + pool_mixture * (there / both)
        for r, source in enumerate(sources):
            packed[source, rows] = merged[r * HEADS : (r + 1) * HEADS].astype(BF16)
        logs = put_lane(logs, g, high + jnp.log(both))
    first = logs.astype(BF16).astype(F32)
    second = (logs - first).astype(BF16).astype(F32)
    third = logs - first - second
    lane = lax.broadcasted_iota(jnp.int32, logs.shape, 1)
    later = jnp.where(lane < 2 * GROUPS, pltpu.roll(second, GROUPS, 1), pltpu.roll(third, 2 * GROUPS, 1))
    terms = jnp.where(lane < GROUPS, first, jnp.where(lane < 3 * GROUPS, later, 0.0))
    padding = jnp.zeros((SENT - QUERY_HEADS - HEADS, HEAD_SIZE), F32)
    for r, source in enumerate(sources):
        rows = jnp.concatenate([terms[r * HEADS : (r + 1) * HEADS], padding])
        packed[source, QUERY_HEADS:] = rows.astype(BF16)


def prefix_attention(prompt_pages, parts, queries, pool):
    smem, vmem = pl.BlockSpec(memory_space=pltpu.SMEM), pl.BlockSpec(memory_space=pltpu.VMEM)
    return pl.pallas_call(
        prefix_kernel,
        out_shape=[
            jax.ShapeDtypeStruct((1, ROWS, KVW), BF16),
            jax.ShapeDtypeStruct((SAMPLES, SENT, HEAD_SIZE), BF16),
        ],
        in_specs=[smem] + [vmem] * 8,
        out_specs=[vmem, vmem],
        compiler_params=params(20),
        cost_estimate=cost(300_000_000, 6 * MIB),
        name="prefix_attention",
    )(prompt_pages, *parts, queries, pool)


def combine_kernel(arrived, local, out):
    terms = arrived[:, QUERY_HEADS:].astype(F32)
    for g in range(GROUPS):
        rows = slice(g * HEADS, (g + 1) * HEADS)
        logs = sum(terms[:, :HEADS, lane : lane + 1] for lane in (g, g + GROUPS, g + 2 * GROUPS))
        local_log = local[QUERY_HEADS:, g : g + 1]
        high = jnp.maximum(jnp.max(logs, axis=0), local_log)
        shares = jnp.exp(logs - high[None])
        local_share = jnp.exp(local_log - high)
        total = jnp.sum(shares, axis=0) + local_share
        mixture = jnp.sum(arrived[:, rows].astype(F32) * shares, axis=0) + local[rows] * local_share
        mixture = (mixture / total).astype(BF16)
        for h in range(HEADS):
            lanes = slice((g * HEADS + h) * HEAD_SIZE, (g * HEADS + h + 1) * HEAD_SIZE)
            out[0, :, lanes] = mixture[h : h + 1]


def combine(arrived, local):
    vmem = pl.BlockSpec(memory_space=pltpu.VMEM)
    return pl.pallas_call(
        combine_kernel,
        out_shape=jax.ShapeDtypeStruct((1, 1, QUERY_HEADS * HEAD_SIZE), BF16),
        in_specs=[vmem, vmem],
        out_specs=vmem,
        compiler_params=params(16),
        cost_estimate=cost(1_000_000, MIB),
        name="combine",
    )(arrived, local)


def per_device(
    prompt_states,
    kv_weight,
    queries,
    new_kv,
    local_pages,
    pool_pages,
    prompt_pages,
    comp_pages,
    preempted,
    page_where,
):
    tie = lax.optimization_barrier

    weight_far = lax.ppermute(kv_weight, "sample", X_FAR)
    weight_right = lax.ppermute(kv_weight, "sample", X_RIGHT)
    weight_left = lax.ppermute(kv_weight, "sample", X_LEFT)
    block, query = prepare(queries, page_where, comp_pages, preempted)
    states = prompt_states.reshape(4, 4, ROWS, SLICE)
    own_states, to_far = pick_far(states)
    slices, own_states, to_far, block = tie(
        ((kv_weight, weight_right, weight_left, weight_far), own_states, to_far, block)
    )
    blocks = [block] + [lax.ppermute(block, "sample", to) for to in (Z_UP, Z_DOWN, Z_FAR)]
    to_right, to_left, last_right, last_left, far_blocks = pick_near(states, blocks)
    rows_far = lax.ppermute(to_far, "sample", X_FAR)
    rows_right = lax.ppermute(to_right, "sample", X_RIGHT)
    rows_left = lax.ppermute(to_left, "sample", X_LEFT)

    here = jnp.stack(slices)
    near = lax.ppermute(here, "prompt", Y_SPLIT)
    here_other = lax.ppermute(here, "prompt", SWAP)
    near_other = lax.ppermute(here_other, "prompt", Y_SPLIT)
    local_alive = jnp.where(preempted[0] > 0, 0, comp_pages[0])
    local = local_attention(local_alive, query, new_kv[0], local_pages[0, 0])
    near, near_other, rows_far, local = tie((near, near_other, rows_far, local))
    far = [lax.ppermute(half, "prompt", Y_SPLIT) for half in (near[:2], near[2:])]
    near_swapped = lax.ppermute(near, "prompt", SWAP)
    near_other_swapped = lax.ppermute(near_other, "prompt", SWAP)
    far, rows_right, rows_left = tie((far, rows_right, rows_left))
    far_other = [lax.ppermute(half, "prompt", SWAP) for half in far]
    pieces = [
        here, here_other, near, near_other, near_swapped, near_other_swapped, *far, *far_other,
    ]
    others = [own_states, rows_right, rows_left, rows_far]

    far_l = product_far(others, pieces[:4], 0, "product_far_l")
    far_other[0], far_l = tie((far_other[0], far_l))
    pieces[8] = far_other[0]
    far_r = product_far(others, pieces[4:], 4, "product_far_r")
    from_down = lax.ppermute(far_l, "sample", Z_UP)
    from_up = lax.ppermute(far_r, "sample", Z_DOWN)
    far_blocks, rows_right = tie((far_blocks, rows_right))
    far_blocks = lax.ppermute(far_blocks, "sample", X_FAR)
    others[1], last_right, last_left, far_blocks = tie(
        (others[1], last_right, last_left, far_blocks)
    )
    up_l, up_r, down_l, down_r = product(
        others, pieces, ((1,) * 4, (2,) * 4), BF16, "product_near"
    )
    up_r, down_l = lax.ppermute(up_r, "sample", Z_UP), lax.ppermute(down_l, "sample", Z_DOWN)
    up_l, down_r = relay(up_l, down_r, from_down, from_up)
    sums = [
        lax.ppermute(up_l, "sample", Z_UP),
        up_r,
        down_l,
        lax.ppermute(down_r, "sample", Z_DOWN),
    ]

    last_right = lax.ppermute(last_right, "sample", X_RIGHT)
    last_left = lax.ppermute(last_left, "sample", X_LEFT)
    queries_all, by_group, slots, alive = unpack(blocks, [last_right, last_left, far_blocks])
    pool = pool_attention(slots, alive, queries_all, pool_pages[0, 0])
    mine, pool = tie(([own_states, last_right, last_left, rows_far], pool))
    sums = [*product(mine, pieces, ((3, 0, 0, 3),), F32, "product_own"), *sums]

    cache, packed = prefix_attention(prompt_pages, sums, by_group, pool)
    arrived = lax.all_to_all(packed, "sample", split_axis=0, concat_axis=0, tiled=True)
    attended = combine(arrived, local)
    return (cache, attended)


def solution(mesh):
    return jax.shard_map(
        per_device,
        mesh=mesh,
        in_specs=(
            P("prompt", None, "sample"),
            P("sample", "prompt"),
            P("prompt", "sample", None),
            P("prompt", "sample", None),
            P("prompt", "sample", None, None, None),
            P("prompt", "sample", None, None, None),
            P("prompt"),
            P("prompt", "sample"),
            P("prompt", "sample"),
            P("prompt", "sample", None),
        ),
        out_specs=(P("prompt", "sample", None), P("prompt", "sample", None)),
        check_vma=False,
    )
```

```python
import functools
import math

import jax
import jax.numpy as jnp
from jax import lax
from jax.experimental import pallas as pl
from jax.experimental.pallas import tpu as pltpu
from jax.sharding import PartitionSpec as P

QUERY_HEADS = 64
GROUPS = 8
HEADS = 8
HEAD_SIZE = 128
PAGE = 128
SAMPLES = 16
CMAX = 16
ROWS = 256
SLICE = 512
COLUMNS = 256
KVW = 2048
KEYS = GROUPS * HEAD_SIZE
PACK = QUERY_HEADS + HEADS
SENT = QUERY_HEADS + 16
LOW = -1e30
SCALE = 1.0 / math.sqrt(HEAD_SIZE)
MIB = 1 << 20
F32 = jnp.float32
BF16 = jnp.bfloat16

X_RIGHT = [(z * 4 + x, z * 4 + (x + 1) % 4) for z in range(4) for x in range(4)]
X_LEFT = [(z * 4 + x, z * 4 + (x + 3) % 4) for z in range(4) for x in range(4)]
X_FAR = [(z * 4 + x, z * 4 + (x + 2) % 4) for z in range(4) for x in range(4)]
Z_UP = [(z * 4 + x, (z + 1) % 4 * 4 + x) for z in range(4) for x in range(4)]
Z_DOWN = [(z * 4 + x, (z + 3) % 4 * 4 + x) for z in range(4) for x in range(4)]
Z_FAR = [(z * 4 + x, (z + 2) % 4 * 4 + x) for z in range(4) for x in range(4)]
SWAP = [(y * 2 + c, y * 2 + 1 - c) for y in range(4) for c in range(2)]
Y_SPLIT = [(y * 2 + c, (y + (1 if c == 0 else 3)) % 4 * 2 + c) for y in range(4) for c in range(2)]


def params(mib):
    return pltpu.CompilerParams(vmem_limit_bytes=mib * MIB)


def cost(flops, bytes_accessed):
    return pl.CostEstimate(flops=flops, bytes_accessed=bytes_accessed, transcendentals=0)


def nt_dot(a, b):
    return lax.dot_general(a, b, (((1,), (1,)), ((), ())), preferred_element_type=F32)


def put_lane(running, lane, column):
    at = lax.broadcasted_iota(jnp.int32, running.shape, len(running.shape) - 1)
    return jnp.where(at == lane, column, running)


HALF = QUERY_HEADS // 2
BLOCK = HALF + 8


def prepare_kernel(where, length, flag, query, sent, own):
    heads = [query[0, 0:1, h * HEAD_SIZE : (h + 1) * HEAD_SIZE].astype(F32) for h in range(QUERY_HEADS)]
    low, high = jnp.concatenate(heads[:HALF]), jnp.concatenate(heads[HALF:])
    own[:HALF] = low.astype(BF16)
    own[HALF:] = high.astype(BF16)
    sent[:HALF, :HEAD_SIZE] = low.astype(BF16)
    sent[:HALF, HEAD_SIZE:] = high.astype(BF16)
    plan = jnp.zeros((8, COLUMNS), F32)
    for c in range(CMAX):
        plan = put_lane(plan, c, where[0, 0, c].astype(F32))
    plan = put_lane(plan, CMAX, length[0, 0].astype(F32))
    plan = put_lane(plan, CMAX + 1, flag[0, 0].astype(F32))
    sent[HALF:] = plan.astype(BF16)


def prepare(query, where, length, flag):
    smem, vmem = pl.BlockSpec(memory_space=pltpu.SMEM), pl.BlockSpec(memory_space=pltpu.VMEM)
    return pl.pallas_call(
        prepare_kernel,
        out_shape=[
            jax.ShapeDtypeStruct((BLOCK, COLUMNS), BF16),
            jax.ShapeDtypeStruct((QUERY_HEADS, HEAD_SIZE), BF16),
        ],
        in_specs=[smem] * 3 + [vmem],
        out_specs=[vmem, vmem],
        compiler_params=params(16),
        cost_estimate=cost(1000, 1000),
        name="prepare",
    )(where, length, flag, query)


def unpack_kernel(*refs):
    own, arrived, (queries, by_group, slots, alive) = refs[:4], refs[4:7], refs[7:]
    me = lax.axis_index("sample")

    def block_of(r):
        if r < 4:
            return own[r][...].astype(F32)
        source = arrived[r // 4 - 1]
        first = source.shape[0] - 2 * BLOCK + r % 4 // 2 * BLOCK
        lanes = slice(r % 2 * COLUMNS, (r % 2 + 1) * COLUMNS)
        return source[first : first + BLOCK, lanes].astype(F32)

    plans = []
    for r in range(SAMPLES):
        block = block_of(r)
        for half in range(2):
            lanes = slice(half * HEAD_SIZE, (half + 1) * HEAD_SIZE)
            queries[r, half * HALF : (half + 1) * HALF] = block[:HALF, lanes].astype(BF16)
        plans.append(block[HALF : HALF + 1])
    for g in range(GROUPS):
        lanes = slice(g // 4 * HEAD_SIZE, (g // 4 + 1) * HEAD_SIZE)
        rows = slice(g % 4 * HEADS, (g % 4 + 1) * HEADS)
        parts = [block_of(r)[rows, lanes] for r in range(SAMPLES)]
        by_group[g] = jnp.concatenate(parts).astype(BF16)
    plan = jnp.concatenate(plans)
    lane = lax.broadcasted_iota(jnp.int32, plan.shape, 1)
    first = (me * CMAX).astype(F32)
    here = (lane < CMAX) & (plan >= first) & (plan < first + CMAX)
    live = here & (lane.astype(F32) < plan[:, CMAX : CMAX + 1]) & (plan[:, CMAX + 1 : CMAX + 2] > 0.5)
    slot = jnp.sum(jnp.where(here, plan - first, 0.0), axis=1, keepdims=True).astype(jnp.int32)
    some = jnp.max(jnp.where(live, 1.0, 0.0), axis=1, keepdims=True).astype(jnp.int32)
    for r in range(SAMPLES):
        slots[r] = slot[r, 0]
        alive[r] = some[r, 0]


def unpack(own, arrived):
    smem, vmem = pl.BlockSpec(memory_space=pltpu.SMEM), pl.BlockSpec(memory_space=pltpu.VMEM)
    return pl.pallas_call(
        unpack_kernel,
        out_shape=[
            jax.ShapeDtypeStruct((SAMPLES, QUERY_HEADS, HEAD_SIZE), BF16),
            jax.ShapeDtypeStruct((GROUPS, SAMPLES * HEADS, HEAD_SIZE), BF16),
            jax.ShapeDtypeStruct((SAMPLES,), jnp.int32),
            jax.ShapeDtypeStruct((SAMPLES,), jnp.int32),
        ],
        in_specs=[vmem] * 7,
        out_specs=[vmem, vmem, smem, smem],
        compiler_params=params(16),
        cost_estimate=cost(1000, 1000),
        name="unpack",
    )(*own, *arrived)


STEPS = (0, 1, 3, 2)
NEXT = (2, 1, 3, 0)


def copy_rows(states, sems, wanted):
    me = lax.axis_index("sample")
    z, x = me // 4, lax.rem(me, 4)
    copies = [
        pltpu.make_async_copy(
            states.at[lax.rem(z + NEXT[k], 4), lax.rem(x + step, 4)], target, sems.at[n]
        )
        for n, (step, k, target) in enumerate(wanted)
    ]
    for copy in copies:
        copy.start()
    return copies


def block_rows(k):
    return pl.ds(k * ROWS, ROWS)


def pick_far_kernel(states, own, far, sems):
    wanted = [(2, k, far.at[block_rows(k)]) for k in range(3)]
    wanted += [(0, k, own.at[block_rows(k)]) for k in range(4)]
    for copy in copy_rows(states, sems, wanted):
        copy.wait()


def pick_far(states):
    vmem = pl.BlockSpec(memory_space=pltpu.VMEM)
    return pl.pallas_call(
        pick_far_kernel,
        out_shape=[
            jax.ShapeDtypeStruct((4 * ROWS, SLICE), BF16),
            jax.ShapeDtypeStruct((3 * ROWS, SLICE), BF16),
        ],
        in_specs=[pl.BlockSpec(memory_space=pl.ANY)],
        out_specs=[vmem] * 2,
        scratch_shapes=[pltpu.SemaphoreType.DMA((7,))],
        compiler_params=params(50),
        cost_estimate=cost(1000, 1000),
        name="pick_far",
    )(states)


def put_blocks(target, first, blocks):
    for r, block in enumerate(blocks):
        rows = slice(first + r // 2 * BLOCK, first + (r // 2 + 1) * BLOCK)
        target[rows, r % 2 * COLUMNS : (r % 2 + 1) * COLUMNS] = block[...]


def pick_near_kernel(states, *refs):
    blocks, (right, left, last_right, last_left, last_far), sems = refs[:4], refs[4:9], refs[9]
    wanted = [(1, k, right.at[block_rows(k)]) for k in range(3)]
    wanted += [(3, k, left.at[block_rows(k)]) for k in range(3)]
    wanted += [(1, 3, last_right), (3, 3, last_left), (2, 3, last_far.at[block_rows(0)])]
    copies = copy_rows(states, sems, wanted)
    put_blocks(right, 3 * ROWS, blocks)
    put_blocks(left, 3 * ROWS, blocks)
    put_blocks(last_far, ROWS, blocks)
    for copy in copies:
        copy.wait()


def pick_near(states, blocks):
    vmem = pl.BlockSpec(memory_space=pltpu.VMEM)
    return pl.pallas_call(
        pick_near_kernel,
        out_shape=[jax.ShapeDtypeStruct((3 * ROWS + 2 * BLOCK, SLICE), BF16)] * 2
        + [jax.ShapeDtypeStruct((ROWS, SLICE), BF16)] * 2
        + [jax.ShapeDtypeStruct((ROWS + 2 * BLOCK, SLICE), BF16)],
        in_specs=[pl.BlockSpec(memory_space=pl.ANY)] + [vmem] * 4,
        out_specs=[vmem] * 5,
        scratch_shapes=[pltpu.SemaphoreType.DMA((9,))],
        compiler_params=params(44),
        cost_estimate=cost(1000, 1000),
        name="pick_near",
    )(states, *blocks)


def weight_of(pieces, j, d):
    return pieces[j][d] if j < 6 else pieces[2 * j - 6 + d // 2][d % 2]


def product_kernel(blocks, *refs):
    states, pieces, outs = refs[:4], refs[4:14], refs[14:]
    for j in range(8):
        for k, block in enumerate(blocks):
            total = jnp.zeros((ROWS, COLUMNS), F32)
            for d in range(4):
                at = block[d] * ROWS
                total += jnp.dot(
                    states[d][at : at + ROWS], weight_of(pieces, j, d), preferred_element_type=F32
                )
            out = outs[2 * k + j // 4]
            out[:, (j % 4) * COLUMNS : (j % 4 + 1) * COLUMNS] = total.astype(out.dtype)


def product(states, pieces, blocks, kind, name):
    vmem = pl.BlockSpec(memory_space=pltpu.VMEM)
    outs = [jax.ShapeDtypeStruct((ROWS, KVW // 2), kind)] * (2 * len(blocks))
    return pl.pallas_call(
        functools.partial(product_kernel, blocks),
        out_shape=outs,
        in_specs=[vmem] * 14,
        out_specs=[vmem] * len(outs),
        compiler_params=params(20),
        cost_estimate=cost(1000, 1000),
        name=name,
    )(*states, *pieces)


def product_far_kernel(first, *refs):
    states, pieces, out = refs[:4], refs[4:-1], refs[-1]
    for j in range(4):
        total = jnp.zeros((ROWS, COLUMNS), F32)
        for d in range(4):
            part = pieces[j][d] if first + j < 6 else weight_of((None,) * 4 + pieces, first + j, d)
            total += jnp.dot(states[d][:ROWS], part, preferred_element_type=F32)
        out[:, j * COLUMNS : (j + 1) * COLUMNS] = total.astype(BF16)


def product_far(states, pieces, first, name):
    vmem = pl.BlockSpec(memory_space=pltpu.VMEM)
    return pl.pallas_call(
        functools.partial(product_far_kernel, first),
        out_shape=jax.ShapeDtypeStruct((ROWS, KVW // 2), BF16),
        in_specs=[vmem] * (4 + len(pieces)),
        out_specs=vmem,
        compiler_params=params(20),
        cost_estimate=cost(1000, 1000),
        name=name,
    )(*states, *pieces)


def relay_kernel(up, down, from_down, from_up, up_out, down_out):
    up_out[...] = (up[...].astype(F32) + from_down[...].astype(F32)).astype(BF16)
    down_out[...] = (down[...].astype(F32) + from_up[...].astype(F32)).astype(BF16)


def relay(up, down, from_down, from_up):
    vmem = pl.BlockSpec(memory_space=pltpu.VMEM)
    return pl.pallas_call(
        relay_kernel,
        out_shape=[jax.ShapeDtypeStruct((ROWS, KVW // 2), BF16)] * 2,
        in_specs=[vmem] * 4,
        out_specs=[vmem] * 2,
        compiler_params=params(16),
        cost_estimate=cost(1000, 1000),
        name="relay_sums",
    )(up, down, from_down, from_up)


def log_rows(logs):
    out = jnp.full((HEADS, HEAD_SIZE), LOW, F32)
    for g in range(GROUPS):
        out = put_lane(out, g, logs[g * HEADS : (g + 1) * HEADS])
    return out


POOL_PAGES = 4


def page_kernel(slots, alive, query, *refs):
    pages, out = refs[:POOL_PAGES], refs[POOL_PAGES]
    step = pl.program_id(0)
    scores = []
    for k in range(POOL_PAGES):
        for g in range(GROUPS):
            keys = pages[k][0, :, g * HEAD_SIZE : (g + 1) * HEAD_SIZE]
            scores.append(nt_dot(query[k, g * HEADS : (g + 1) * HEADS], keys))
    scores = jnp.concatenate(scores) * SCALE
    top = jnp.max(scores, axis=-1, keepdims=True)
    exponent = jnp.exp(scores - top)
    total = jnp.sum(exponent, axis=-1, keepdims=True)
    logs, share = top + jnp.log(total), 1.0 / total
    for k in range(POOL_PAGES):
        live = alive[step * POOL_PAGES + k] != 0
        for g in range(GROUPS):
            rows = slice(k * QUERY_HEADS + g * HEADS, k * QUERY_HEADS + (g + 1) * HEADS)
            values = pages[k][0, :, KEYS + g * HEAD_SIZE : KEYS + (g + 1) * HEAD_SIZE]
            mixture = jnp.dot(exponent[rows].astype(BF16), values, preferred_element_type=F32)
            out[k, g * HEADS : (g + 1) * HEADS] = jnp.where(live, mixture * share[rows], 0.0)
        mine = log_rows(logs[k * QUERY_HEADS : (k + 1) * QUERY_HEADS])
        out[k, QUERY_HEADS:] = jnp.where(live, mine, LOW)


def pool_attention(slots, alive, queries_all, pool):
    def page_of(k):
        return lambda s, slots, alive: (slots[s * POOL_PAGES + k], 0, 0)

    return pl.pallas_call(
        page_kernel,
        out_shape=jax.ShapeDtypeStruct((SAMPLES, PACK, HEAD_SIZE), F32),
        grid_spec=pltpu.PrefetchScalarGridSpec(
            num_scalar_prefetch=2,
            grid=(SAMPLES // POOL_PAGES,),
            in_specs=[
                pl.BlockSpec(
                    (POOL_PAGES, QUERY_HEADS, HEAD_SIZE), lambda s, slots, alive: (s, 0, 0)
                )
            ]
            + [pl.BlockSpec((1, PAGE, KVW), page_of(k)) for k in range(POOL_PAGES)],
            out_specs=pl.BlockSpec(
                (POOL_PAGES, PACK, HEAD_SIZE), lambda s, slots, alive: (s, 0, 0)
            ),
        ),
        compiler_params=params(16),
        cost_estimate=cost(1000, 1000),
        name="pool_attention",
    )(slots, alive, queries_all, *[pool] * POOL_PAGES)


LOCAL_PAGES = 4


def local_kernel(pages_alive, query, new, pages, out, top_ref, sum_ref, mix_ref):
    step = pl.program_id(0)
    width = LOCAL_PAGES * PAGE

    @pl.when(step == 0)
    def _():
        for g in range(GROUPS):
            rows = slice(g * HEADS, (g + 1) * HEADS)
            lanes = slice(g * HEAD_SIZE, (g + 1) * HEAD_SIZE)
            value_lanes = slice(KEYS + g * HEAD_SIZE, KEYS + (g + 1) * HEAD_SIZE)
            products = query[rows].astype(F32) * new[0:1, lanes].astype(F32)
            top_ref[rows] = jnp.sum(products, axis=-1, keepdims=True) * SCALE
            sum_ref[rows] = jnp.ones((HEADS, 1), F32)
            mix_ref[rows] = jnp.broadcast_to(new[0:1, value_lanes].astype(F32), (HEADS, HEAD_SIZE))

    @pl.when(step * LOCAL_PAGES < pages_alive[0])
    def _():
        block = pages.reshape(width, KVW)
        at = step * width + lax.broadcasted_iota(jnp.int32, (QUERY_HEADS, width), 1)
        live = at < pages_alive[0] * PAGE
        scores = jnp.concatenate(
            [
                nt_dot(
                    query[g * HEADS : (g + 1) * HEADS],
                    block[:, g * HEAD_SIZE : (g + 1) * HEAD_SIZE],
                )
                for g in range(GROUPS)
            ]
        )
        scores = jnp.where(live, scores * SCALE, LOW)
        old = top_ref[...]
        top = jnp.maximum(old, jnp.max(scores, axis=-1, keepdims=True))
        shrink = jnp.exp(old - top)
        exponent = jnp.where(live, jnp.exp(scores - top), 0.0)
        top_ref[...] = top
        sum_ref[...] = sum_ref[...] * shrink + jnp.sum(exponent, axis=-1, keepdims=True)
        for g in range(GROUPS):
            rows = slice(g * HEADS, (g + 1) * HEADS)
            values = block[:, KEYS + g * HEAD_SIZE : KEYS + (g + 1) * HEAD_SIZE]
            mix_ref[rows] = mix_ref[rows] * shrink[rows] + jnp.dot(
                exponent[rows].astype(BF16), values, preferred_element_type=F32
            )

    @pl.when(step == CMAX // LOCAL_PAGES - 1)
    def _():
        out[:QUERY_HEADS] = mix_ref[...] / sum_ref[...]
        out[QUERY_HEADS:] = log_rows(top_ref[...] + jnp.log(sum_ref[...]))


def local_attention(pages_alive, query, new, pages):
    def block_of(step, alive):
        last = jnp.maximum(alive[0] - 1, 0) // LOCAL_PAGES
        return (jnp.minimum(step, last), 0, 0)

    return pl.pallas_call(
        local_kernel,
        out_shape=jax.ShapeDtypeStruct((PACK, HEAD_SIZE), F32),
        grid_spec=pltpu.PrefetchScalarGridSpec(
            num_scalar_prefetch=1,
            grid=(CMAX // LOCAL_PAGES,),
            in_specs=[
                pl.BlockSpec((QUERY_HEADS, HEAD_SIZE), lambda step, alive: (0, 0)),
                pl.BlockSpec((1, KVW), lambda step, alive: (0, 0)),
                pl.BlockSpec((LOCAL_PAGES, PAGE, KVW), block_of),
            ],
            out_specs=pl.BlockSpec((PACK, HEAD_SIZE), lambda step, alive: (0, 0)),
            scratch_shapes=[
                pltpu.VMEM((QUERY_HEADS, 1), F32),
                pltpu.VMEM((QUERY_HEADS, 1), F32),
                pltpu.VMEM((QUERY_HEADS, HEAD_SIZE), F32),
            ],
        ),
        compiler_params=params(16),
        cost_estimate=cost(1000, 1000),
        name="local_attention",
    )(pages_alive, query, new, pages)


def prefix_kernel(
    prompt_pages, own_l, own_r, up_l, up_r, down_l, down_r, queries, pool, cache, packed
):
    me, prompt = lax.axis_index("sample"), lax.axis_index("prompt")
    z, x = me // 4, lax.rem(me, 4)
    y, core = prompt // 2, lax.rem(prompt, 2)
    near = lax.rem(y + 3 - 2 * core, 4)
    other = lax.rem(y + 1 + 2 * core, 4)
    far = lax.rem(y + 2, 4)
    columns = (
        2 * y + core, 2 * y + 1 - core, 2 * near + core, 2 * near + 1 - core,
        2 * other + 1 - core, 2 * other + core, 2 * far + core, 2 * far + 1 - core,
    )
    for j in range(8):
        lanes = slice((j % 4) * COLUMNS, (j % 4 + 1) * COLUMNS)
        own, up, down = (own_l, up_l, down_l) if j < 4 else (own_r, up_r, down_r)
        total = own[:, lanes] + up[:, lanes].astype(F32) + down[:, lanes].astype(F32)
        target = pl.ds(pl.multiple_of(columns[j] * COLUMNS, COLUMNS), COLUMNS)
        cache[0, :, target] = total.astype(BF16)
    sources = [
        lax.rem(z + 4 - dz, 4) * 4 + lax.rem(x + 4 - dx, 4) for dx in STEPS for dz in STEPS
    ]
    live = lax.broadcasted_iota(jnp.int32, (SAMPLES * HEADS, ROWS), 1) < prompt_pages[0] * PAGE - me * ROWS
    logs = jnp.full((SAMPLES * HEADS, HEAD_SIZE), LOW, F32)
    for g in range(GROUPS):
        keys = cache[0, :, g * HEAD_SIZE : (g + 1) * HEAD_SIZE]
        values = cache[0, :, KEYS + g * HEAD_SIZE : KEYS + (g + 1) * HEAD_SIZE]
        scores = jnp.where(live, nt_dot(queries[g], keys) * SCALE, LOW)
        top = jnp.max(scores, axis=-1, keepdims=True)
        exponent = jnp.where(live, jnp.exp(scores - top), 0.0)
        total = jnp.sum(exponent, axis=-1, keepdims=True)
        mixture = jnp.dot(exponent.astype(BF16), values, preferred_element_type=F32)
        some = total > 0.0
        total = jnp.where(some, total, 1.0)
        log = jnp.where(some, top + jnp.log(total), LOW)
        rows = slice(g * HEADS, (g + 1) * HEADS)
        pool_log = pool[:, QUERY_HEADS:, g : g + 1].reshape(SAMPLES * HEADS, 1)
        pool_mixture = pool[:, rows].reshape(SAMPLES * HEADS, HEAD_SIZE)
        high = jnp.maximum(log, pool_log)
        here, there = jnp.exp(log - high), jnp.exp(pool_log - high)
        both = here + there
        merged = mixture * (here / (total * both)) + pool_mixture * (there / both)
        for r, source in enumerate(sources):
            packed[source, rows] = merged[r * HEADS : (r + 1) * HEADS].astype(BF16)
        logs = put_lane(logs, g, high + jnp.log(both))
    first = logs.astype(BF16).astype(F32)
    second = (logs - first).astype(BF16).astype(F32)
    third = logs - first - second
    lane = lax.broadcasted_iota(jnp.int32, logs.shape, 1)
    later = jnp.where(lane < 2 * GROUPS, pltpu.roll(second, GROUPS, 1), pltpu.roll(third, 2 * GROUPS, 1))
    terms = jnp.where(lane < GROUPS, first, jnp.where(lane < 3 * GROUPS, later, 0.0))
    padding = jnp.zeros((SENT - QUERY_HEADS - HEADS, HEAD_SIZE), F32)
    for r, source in enumerate(sources):
        rows = jnp.concatenate([terms[r * HEADS : (r + 1) * HEADS], padding])
        packed[source, QUERY_HEADS:] = rows.astype(BF16)


def prefix_attention(prompt_pages, parts, queries, pool):
    smem, vmem = pl.BlockSpec(memory_space=pltpu.SMEM), pl.BlockSpec(memory_space=pltpu.VMEM)
    return pl.pallas_call(
        prefix_kernel,
        out_shape=[
            jax.ShapeDtypeStruct((1, ROWS, KVW), BF16),
            jax.ShapeDtypeStruct((SAMPLES, SENT, HEAD_SIZE), BF16),
        ],
        in_specs=[smem] + [vmem] * 8,
        out_specs=[vmem, vmem],
        compiler_params=params(20),
        cost_estimate=cost(300_000_000, 6 * MIB),
        name="prefix_attention",
    )(prompt_pages, *parts, queries, pool)


def combine_kernel(arrived, local, out):
    terms = arrived[:, QUERY_HEADS:].astype(F32)
    for g in range(GROUPS):
        rows = slice(g * HEADS, (g + 1) * HEADS)
        logs = sum(terms[:, :HEADS, lane : lane + 1] for lane in (g, g + GROUPS, g + 2 * GROUPS))
        local_log = local[QUERY_HEADS:, g : g + 1]
        high = jnp.maximum(jnp.max(logs, axis=0), local_log)
        shares = jnp.exp(logs - high[None])
        local_share = jnp.exp(local_log - high)
        total = jnp.sum(shares, axis=0) + local_share
        mixture = jnp.sum(arrived[:, rows].astype(F32) * shares, axis=0) + local[rows] * local_share
        mixture = (mixture / total).astype(BF16)
        for h in range(HEADS):
            lanes = slice((g * HEADS + h) * HEAD_SIZE, (g * HEADS + h + 1) * HEAD_SIZE)
            out[0, :, lanes] = mixture[h : h + 1]


def combine(arrived, local):
    vmem = pl.BlockSpec(memory_space=pltpu.VMEM)
    return pl.pallas_call(
        combine_kernel,
        out_shape=jax.ShapeDtypeStruct((1, 1, QUERY_HEADS * HEAD_SIZE), BF16),
        in_specs=[vmem, vmem],
        out_specs=vmem,
        compiler_params=params(16),
        cost_estimate=cost(1_000_000, MIB),
        name="combine",
    )(arrived, local)


def per_device(
    prompt_states,
    kv_weight,
    queries,
    new_kv,
    local_pages,
    pool_pages,
    prompt_pages,
    comp_pages,
    preempted,
    page_where,
):
    tie = lax.optimization_barrier

    weight_far = lax.ppermute(kv_weight, "sample", X_FAR)
    weight_right = lax.ppermute(kv_weight, "sample", X_RIGHT)
    weight_left = lax.ppermute(kv_weight, "sample", X_LEFT)
    block, query = prepare(queries, page_where, comp_pages, preempted)
    states = prompt_states.reshape(4, 4, ROWS, SLICE)
    own_states, to_far = pick_far(states)
    slices, own_states, to_far, block = tie(
        ((kv_weight, weight_right, weight_left, weight_far), own_states, to_far, block)
    )
    blocks = [block] + [lax.ppermute(block, "sample", to) for to in (Z_UP, Z_DOWN, Z_FAR)]
    to_right, to_left, last_right, last_left, last_far = pick_near(states, blocks)
    rows_far = lax.ppermute(to_far, "sample", X_FAR)
    rows_right = lax.ppermute(to_right, "sample", X_RIGHT)
    rows_left = lax.ppermute(to_left, "sample", X_LEFT)

    here = jnp.stack(slices)
    near = lax.ppermute(here, "prompt", Y_SPLIT)
    here_other = lax.ppermute(here, "prompt", SWAP)
    near_other = lax.ppermute(here_other, "prompt", Y_SPLIT)
    local_alive = jnp.where(preempted[0] > 0, 0, comp_pages[0])
    local = local_attention(local_alive, query, new_kv[0], local_pages[0, 0])
    near, near_other, rows_far, local = tie((near, near_other, rows_far, local))
    far = [lax.ppermute(half, "prompt", Y_SPLIT) for half in (near[:2], near[2:])]
    near_swapped = lax.ppermute(near, "prompt", SWAP)
    near_other_swapped = lax.ppermute(near_other, "prompt", SWAP)
    far, rows_right, rows_left = tie((far, rows_right, rows_left))
    far_other = [lax.ppermute(half, "prompt", SWAP) for half in far]
    pieces = [
        here, here_other, near, near_other, near_swapped, near_other_swapped, *far, *far_other,
    ]
    others = [own_states, rows_right, rows_left, rows_far]

    far_l = product_far(others, pieces[:4], 0, "product_far_l")
    far_other[0], far_l = tie((far_other[0], far_l))
    pieces[8] = far_other[0]
    far_r = product_far(others, pieces[4:], 4, "product_far_r")
    from_down = lax.ppermute(far_l, "sample", Z_UP)
    from_up = lax.ppermute(far_r, "sample", Z_DOWN)
    last_far, rows_right = tie((last_far, rows_right))
    last_far = lax.ppermute(last_far, "sample", X_FAR)
    up_l, up_r, down_l, down_r = product(
        others, pieces, ((1,) * 4, (2,) * 4), BF16, "product_near"
    )
    up_r, down_l = lax.ppermute(up_r, "sample", Z_UP), lax.ppermute(down_l, "sample", Z_DOWN)
    from_down, from_up, last_far = tie((from_down, from_up, last_far))
    up_l, down_r = relay(up_l, down_r, from_down, from_up)
    sums = [
        lax.ppermute(up_l, "sample", Z_UP),
        up_r,
        down_l,
        lax.ppermute(down_r, "sample", Z_DOWN),
    ]

    arrived, up_l = tie(([rows_right, rows_left, last_far], up_l))
    queries_all, by_group, slots, alive = unpack(blocks, arrived)
    pool = pool_attention(slots, alive, queries_all, pool_pages[0, 0])
    last_right = lax.ppermute(last_right, "sample", X_RIGHT)
    last_left = lax.ppermute(last_left, "sample", X_LEFT)
    mine, pool = tie(([own_states, last_right, last_left, last_far], pool))
    sums = [*product(mine, pieces, ((3, 0, 0, 0),), F32, "product_own"), *sums]

    cache, packed = prefix_attention(prompt_pages, sums, by_group, pool)
    arrived = lax.all_to_all(packed, "sample", split_axis=0, concat_axis=0, tiled=True)
    attended = combine(arrived, local)
    return (cache, attended)


def solution(mesh):
    return jax.shard_map(
        per_device,
        mesh=mesh,
        in_specs=(
            P("prompt", None, "sample"),
            P("sample", "prompt"),
            P("prompt", "sample", None),
            P("prompt", "sample", None),
            P("prompt", "sample", None, None, None),
            P("prompt", "sample", None, None, None),
            P("prompt"),
            P("prompt", "sample"),
            P("prompt", "sample"),
            P("prompt", "sample", None),
        ),
        out_specs=(P("prompt", "sample", None), P("prompt", "sample", None)),
        check_vma=False,
    )
```
